32 devices in a mesh: seq: 8 (over z, y), rep: 4 (over x, core).
Axes of the slice: x: 2, y: 2, z: 4, core: 2. Of those that a mesh axis runs over, the one named last changes fastest.
Arguments:
- mixed: bfloat16 [4, 16, 512, 1024], P('rep', None, None, 'seq'), may hold values from -6 to 6
- decay_in: bfloat16 [4, 16, 2, 1024], P('rep', None, None, 'seq'), may hold values from -6 to 13.8
- beta_in: bfloat16 [4, 16, 2, 1024], P('rep', None, None, 'seq'), may hold values from -6 to 6
- gate_z: bfloat16 [4, 16, 256, 1024], P('rep', None, None, 'seq'), may hold values from -6 to 6
- conv_weight: bfloat16 [4, 16, 512], P(None, 'seq'), may hold values from -3 to 3
- a_log: float32 [32], P('seq'), may hold values from -10 to 3
- dt_bias: float32 [32], P('seq'), may hold values from -5.5 to -3.5
- norm_gain: float32 [128], replicated, may hold values from 0.5 to 1.5
- req_blocks: int32 [4, 8], P('rep'), may hold values from 1 to 4, 16 in all within a row
- replica_of: int32 [4, 8], P('rep'), may hold values from 0 to 3, as said below
- finished: int32 [4, 8], P('rep'), may hold values from 0 to 1
Outputs:
- mixer_out: bfloat16 [4, 16, 256, 1024], P('rep', None, None, 'seq')
- states_out: float32 [4, 8, 32, 128, 128], P('rep', None, 'seq')
- tails_out: bfloat16 [4, 8, 3, 16, 512], P('rep', None, None, 'seq')
The draws below stay inside these ranges and needn't reach their ends.
Inputs may be any that keep to these rules, and one draw needn't show every extreme that they name: `req_blocks`: blocks of 64 tokens of each of the 8 requests of a pack; together they fill the pack. `replica_of`: at most 2 finished requests of one pack, and at most 8 finished requests of all packs together, name the same replica.
All inputs are finite; a program needn't handle non-finite values.
Results may differ from the reference program's by a relative error of at most 0.012.
Values may be sent and summed in bfloat16 or wider, within the bound.
No kernel may reach another device: no remote copies, remote signals or barrier semaphores. Data moves between devices by JAX's collectives and lax.ppermute only.
A program may use at most 64 MiB of HBM per device.

```python
import math
import jax
import jax.numpy as jnp
import numpy as np
from jax import lax

HK = 16
HV = 32
DK = 128
DV = 128
KERNEL = 4
SPAN = 64
REQS = 8
CAP = 2
RATIO = 2
GROUP_CH = 512
SEQ_LEN = 1024
NBLOCKS = 16
MOST_BLOCKS = 4
SLOTS = 8
N_REP = 4


def draw_a_log(key, part):
    linked_tokens = MOST_BLOCKS * SPAN
    pick_key, slow_key, fast_key = jax.random.split(jax.random.fold_in(key, 11), 3)
    quick = jax.random.uniform(pick_key, (HV,)) < 0.5
    slow_rate = jax.random.uniform(slow_key, (HV,), minval=0.25, maxval=1.0) / (0.05 * linked_tokens)
    fast_rate = jnp.exp(jax.random.uniform(fast_key, (HV,), minval=jnp.log(2.0), maxval=jnp.log(8.0)))
    return jnp.log(jnp.where(quick, fast_rate, slow_rate)).astype(jnp.float32)


def draw_decay_in(key, part):
    linked_tokens = MOST_BLOCKS * SPAN
    full_shape = (N_REP, HK, RATIO, SEQ_LEN)
    base_key, random_spot_key, height_key = jax.random.split(jax.random.fold_in(key, 13), 3)
    base_offset = jnp.clip(jax.random.normal(base_key, full_shape), -6.0, 6.0)
    request_runs = jax.random.uniform(random_spot_key, full_shape) < 3.0 / linked_tokens
    block_height = jax.random.uniform(height_key, full_shape, minval=0.02, maxval=0.05) * linked_tokens
    return jnp.where(request_runs, block_height, base_offset).astype(jnp.float32).astype(jnp.bfloat16)


def replica_table(key):
    busy_key, pair_key, offset_key, done_key, order_key = jax.random.split(jax.random.fold_in(key, 7), 5)
    pair_count = REQS // CAP
    busy = jax.random.randint(busy_key, (), 0, N_REP)
    busy_pair = jax.random.randint(pair_key, (N_REP, 1), 0, pair_count)
    offsets = jax.random.randint(offset_key, (N_REP, 1), 0, N_REP - 1)
    request_index = jnp.arange(REQS, dtype=jnp.int32)[None, :]
    pair_index = request_index // CAP
    other_index = pair_index - (pair_index > busy_pair).astype(jnp.int32)
    other_dest = (busy + 1 + (offsets + other_index) % (N_REP - 1)) % N_REP
    dest = jnp.where(pair_index == busy_pair, busy, other_dest).astype(jnp.int32)
    coin = (jax.random.randint(done_key, (N_REP, REQS), 0, 4) > 0).astype(jnp.int32)
    done = jnp.where(pair_index == busy_pair, 1, coin).astype(jnp.int32)
    orders = jax.vmap(lambda one_key: jax.random.permutation(one_key, REQS))(jax.random.split(order_key, N_REP))
    dest = jnp.take_along_axis(dest, orders, axis=1)
    done = jnp.take_along_axis(done, orders, axis=1)
    return (dest.astype(jnp.int32), done.astype(jnp.int32))


def draw_replica_of(key, part):
    dest, done = replica_table(key)
    return dest


def draw_finished(key, part):
    dest, done = replica_table(key)
    return done


def block_scale(key, dims, shards, low, top_value):
    factor_of, own = 1.0, jax.random.fold_in(key, 6)
    for dim, blocks in shards:
        heights = jnp.exp(jax.random.uniform(jax.random.fold_in(own, dim), (blocks,), jnp.float32, low / len(shards), top_value / len(shards)))
        factor_of = factor_of * jnp.repeat(heights, dims[dim] // blocks).reshape([-1 if axis == dim else 1 for axis in range(len(dims))])
    return factor_of


def profile(count, total, bound, lean):
    loads = [(1 << 20) // math.isqrt(rank ** lean) + 1 for rank in range(2, count + 1)]
    surplus, counts = total - bound - (count - 1), [1] * (count - 1)
    while surplus > 0:
        free = [i for i in range(count - 1) if counts[i] < bound]
        whole, remaining = sum([loads[i] for i in free]), surplus
        for i in free:
            extra = min(bound - counts[i], max(1, remaining * loads[i] // whole), surplus)
            counts[i] = counts[i] + extra
            surplus = surplus - extra
    return np.array([bound] + counts)


def uneven_parts(stream_key, count, total, limit, skew):
    if count == 2:
        one = jax.random.randint(stream_key, (), max(1, total - limit), min(limit, total - 1) + 1)
        return jnp.stack([one, total - one])
    tallies = jnp.asarray(profile(count, total, limit, skew), jnp.int32)
    twos = (count - 1) // 2
    donor, receiver = tallies[1:1 + 2 * twos:2], tallies[2:2 + 2 * twos:2]
    slack = jnp.minimum(donor - 1, limit - receiver)
    shifted = jax.random.randint(jax.random.fold_in(stream_key, 1), (twos,), 0, 1 << 20) % (slack + 1)
    tallies = tallies.at[1:1 + 2 * twos:2].set(donor - shifted).at[2:2 + 2 * twos:2].set(receiver + shifted)
    return tallies[jax.random.permutation(jax.random.fold_in(stream_key, 2), count)]


def noise(key, extent, scale, most, cuts=(), kind=jnp.bfloat16):
    array = scale * jax.random.normal(key, extent, jnp.float32)
    if cuts:
        array = array * block_scale(key, extent, cuts, -0.22, 0.18)
    return jnp.clip(array, -most, most).astype(kind)


def setup_inputs(seed: int = 0) -> dict:
    seeds = jax.random.split(jax.random.key(seed), 12)
    return {
        "mixed": noise(seeds[0], (N_REP, HK, GROUP_CH, SEQ_LEN), 1.0, 6.0, ((0, 4), (3, 8))),
        "decay_in": draw_decay_in(jax.random.fold_in(seeds[11], 71), 0),
        "beta_in": noise(seeds[2], (N_REP, HK, RATIO, SEQ_LEN), 1.5, 6.0, ((0, 4), (3, 8))),
        "gate_z": noise(seeds[3], (N_REP, HK, RATIO * DV, SEQ_LEN), 1.0, 6.0, ((0, 4), (3, 8))),
        "conv_weight": noise(seeds[4], (KERNEL, HK, GROUP_CH), KERNEL ** -0.5, 3.0, ((1, 8),)),
        "a_log": draw_a_log(jax.random.fold_in(seeds[11], 71), 0),
        "dt_bias": jnp.clip(-5.5 + 2.0 * jax.random.uniform(seeds[6], (HV,), jnp.float32) ** block_scale(seeds[6], (HV,), ((0, 8),), -0.2, 0.2), -5.5, -3.5),
        "norm_gain": jnp.clip(1.0 + 0.1 * jax.random.normal(seeds[7], (DV,), jnp.float32), 0.5, 1.5),
        "req_blocks": jax.vmap(lambda own: uneven_parts(own, REQS, NBLOCKS, MOST_BLOCKS, 2))(jax.random.split(seeds[8], N_REP)).reshape((N_REP, REQS)).astype(jnp.int32),
        "replica_of": draw_replica_of(jax.random.fold_in(seeds[11], 71), 0),
        "finished": draw_finished(jax.random.fold_in(seeds[11], 71), 0),
    }


EPSILON = 1e-06

def product(spec, left, right):
    return jnp.einsum(spec, left.astype(jnp.float32), right.astype(jnp.float32), precision=lax.Precision.HIGHEST)

def request_bounds(blocks, length):
    block_ends = jnp.cumsum(blocks).astype(jnp.int32)
    block_starts = block_ends - blocks
    start_tokens = block_starts * SPAN
    position = jnp.arange(length, dtype=jnp.int32)
    begins = lax.optimization_barrier(jnp.max(jnp.where(start_tokens[None, :] <= position[:, None], start_tokens[None, :], 0), axis=1))
    first_block = jnp.any(block_starts[None, :] == jnp.arange(length // SPAN, dtype=jnp.int32)[:, None], axis=1)
    return (begins, block_ends * SPAN, first_block, block_ends - 1)

def causal_conv(pre_conv, conv_weight, begins):
    length = pre_conv.shape[-1]
    position = jnp.arange(length, dtype=jnp.int32)
    widened = pre_conv.astype(jnp.float32)
    total = jnp.zeros(pre_conv.shape, jnp.float32)
    for tap_index in range(KERNEL):
        offset_back = KERNEL - 1 - tap_index
        moved = jnp.pad(widened, ((0, 0), (0, 0), (offset_back, 0)))[:, :, :length]
        allowed = position - offset_back >= begins
        total = total + conv_weight[tap_index].astype(jnp.float32)[:, :, None] * jnp.where(allowed[None, None, :], moved, 0.0)
    return jax.nn.silu(total).astype(jnp.bfloat16)

def unit_inverse(mixing):
    minus = -mixing
    total = jnp.eye(SPAN, dtype=jnp.float32) + minus
    power = minus
    for level in range(SPAN.bit_length() - 2):
        power = jnp.matmul(power, power, precision=lax.Precision.HIGHEST)
        total = total + jnp.matmul(total, power, precision=lax.Precision.HIGHEST)
    return total

def delta_heads(convolved, decay_part, beta_part, a_log, dt_bias, first_block):
    head_count, channels, length = convolved.shape
    ratio_count = decay_part.shape[1]
    blocks_total = length // SPAN
    queries = convolved[:, :DK].reshape(head_count, DK, blocks_total, SPAN)
    key_wide = convolved[:, DK:2 * DK].astype(jnp.float32)
    keys_norm = (key_wide * lax.rsqrt(lax.optimization_barrier(jnp.sum(key_wide * key_wide, axis=1, keepdims=True)) + EPSILON)).astype(jnp.bfloat16)
    keys_norm = keys_norm.reshape(head_count, DK, blocks_total, SPAN)
    values_in = convolved[:, 2 * DK:].reshape(head_count, ratio_count, DV, blocks_total, SPAN)
    rates = jnp.exp(a_log).reshape(head_count, ratio_count, 1)
    biases = dt_bias.reshape(head_count, ratio_count, 1)
    decay = -rates * jax.nn.softplus(decay_part.astype(jnp.float32) + biases)
    strength = jax.nn.sigmoid(beta_part.astype(jnp.float32)).reshape(head_count, ratio_count, blocks_total, SPAN)
    cumulative = jnp.cumsum(decay.reshape(head_count, ratio_count, blocks_total, SPAN), axis=-1)
    later = jnp.arange(SPAN)[:, None] > jnp.arange(SPAN)[None, :]
    seen = jnp.arange(SPAN)[:, None] >= jnp.arange(SPAN)[None, :]
    spread = cumulative[..., :, None] - cumulative[..., None, :]
    gram = product('hdni,hdnj->hnij', keys_norm, keys_norm)
    mixing = jnp.where(later, strength[..., :, None] * gram[:, None] * jnp.exp(jnp.where(later, spread, 0.0)), 0.0)
    solved_system = unit_inverse(mixing).astype(jnp.bfloat16)
    lift = (strength * jnp.exp(cumulative))[:, :, None]
    scaled_keys = (lift * keys_norm[:, None].astype(jnp.float32)).astype(jnp.bfloat16)
    scaled_values = (strength[:, :, None] * values_in.astype(jnp.float32)).astype(jnp.bfloat16)
    weighted_keys = product('hrnij,hrdnj->nhrid', solved_system, scaled_keys).astype(jnp.bfloat16)
    weighted_values = product('hrnij,hrenj->nhrie', solved_system, scaled_values).astype(jnp.bfloat16)
    closing = cumulative[..., -1]
    faded = (jnp.exp(closing[..., None] - cumulative)[:, :, None] * keys_norm[:, None].astype(jnp.float32)).astype(jnp.bfloat16)
    faded = jnp.moveaxis(faded, 3, 0)
    keeping = jnp.moveaxis(jnp.exp(closing), 2, 0)

    def advance(carry, pieces):
        keys_step, step_values, faded_step, keep_step, fresh = pieces
        current = jnp.where(fresh, 0.0, carry)
        entering = current.astype(jnp.bfloat16)
        new_values = (step_values.astype(jnp.float32) - product('hrid,hrde->hrie', keys_step, entering)).astype(jnp.bfloat16)
        leaving = keep_step[:, :, None, None] * current + product('hrdi,hrie->hrde', faded_step, new_values)
        return (leaving, (leaving, new_values))
    start_state = jnp.zeros((head_count, ratio_count, DK, DV), jnp.float32)
    unused, (leaving_all, new_all) = lax.scan(advance, start_state, (weighted_keys, weighted_values, faded, keeping, first_block))
    previous = jnp.concatenate([start_state[None], leaving_all[:-1]], axis=0)
    entering_all = jnp.where(first_block[:, None, None, None, None], 0.0, previous).astype(jnp.bfloat16)
    scores = jnp.where(seen, product('hdni,hdnj->hnij', queries, keys_norm)[:, None] * jnp.exp(jnp.where(seen, spread, 0.0)), 0.0).astype(jnp.bfloat16)
    core_out = jnp.exp(cumulative)[:, :, None] * product('hdni,nhrde->hreni', queries, entering_all) + product('hrnij,nhrje->hreni', scores, new_all)
    core_out = core_out.astype(jnp.bfloat16).reshape(head_count, ratio_count * DV, length)
    return (core_out, leaving_all)

def gated_norm(core_out, gate, gain):
    shape_in = core_out.shape
    split_shape = shape_in[:-2] + (shape_in[-2] // DV, DV, shape_in[-1])
    values_wide = core_out.astype(jnp.float32).reshape(split_shape)
    inverse_rms = lax.rsqrt(lax.optimization_barrier(jnp.mean(values_wide * values_wide, axis=-2, keepdims=True)) + EPSILON)
    gate_wide = gate.astype(jnp.float32).reshape(split_shape)
    result = values_wide * inverse_rms * gain[:, None] * jax.nn.silu(gate_wide)
    return result.astype(jnp.bfloat16).reshape(shape_in)

def request_tails(pre_conv, end_tokens):
    positions = (end_tokens[:, None] - (KERNEL - 1) + jnp.arange(KERNEL - 1, dtype=jnp.int32)[None, :]).reshape(-1)
    picked = jnp.take(pre_conv, positions, axis=2)
    picked = picked.reshape(pre_conv.shape[0], pre_conv.shape[1], -1, KERNEL - 1)
    return jnp.transpose(picked, (2, 3, 0, 1))

def reference(mixed, decay_in, beta_in, gate_z, conv_weight, a_log, dt_bias, norm_gain, req_blocks, replica_of, finished):

    def one_pack(pieces):
        pre_conv, decay_part, beta_part, gate_part, blocks = pieces
        begins, end_tokens, first_block, last_block = request_bounds(blocks, pre_conv.shape[-1])
        convolved = causal_conv(pre_conv, conv_weight, begins)
        core_out, leaving_all = delta_heads(convolved, decay_part, beta_part, a_log, dt_bias, first_block)
        normed = gated_norm(core_out, gate_part, norm_gain)
        finals = jnp.take(leaving_all, last_block, axis=0)
        tail_rows = request_tails(pre_conv, end_tokens)
        return (normed, finals, tail_rows)
    mixer_out, finals, tail_rows = lax.map(one_pack, (mixed, decay_in, beta_in, gate_z, req_blocks))
    flat_dest = replica_of.reshape(-1)
    flat_done = finished.reshape(-1)
    member = ((flat_dest[:, None] == jnp.arange(N_REP, dtype=jnp.int32)[None, :]) & (flat_done[:, None] > 0)).astype(jnp.int32)
    order_rank = jnp.cumsum(member, axis=0).astype(jnp.int32) - member
    chosen = ((member[None] > 0) & (order_rank[None] == jnp.arange(SLOTS, dtype=jnp.int32)[:, None, None])).astype(jnp.float32)
    state_rows = finals.reshape(N_REP * REQS, HV, DK, DV)
    tail_flat = tail_rows.reshape(N_REP * REQS, KERNEL - 1, HK, GROUP_CH).astype(jnp.float32)
    states_out = jnp.einsum('sqd,qhab->dshab', chosen, state_rows, precision=lax.Precision.HIGHEST)
    tails_out = jnp.einsum('sqd,qkhc->dskhc', chosen, tail_flat, precision=lax.Precision.HIGHEST).astype(jnp.bfloat16)
    return (mixer_out, states_out, tails_out)
```

```python
import functools

import jax
import jax.numpy as jnp
from jax import lax
from jax.experimental import pallas as pl
from jax.experimental.pallas import tpu as pltpu
from jax.sharding import PartitionSpec as P

DK = 128
DV = 128
KERNEL = 4
SPAN = 64
CAP = 2
RATIO = 2
TILE = 2 * SPAN
KROWS = 160
STEP = 4
EPSILON = 1e-06
F32 = jnp.float32
BF16 = jnp.bfloat16
VMEM_LIMIT = 56 * 1024 * 1024


def params(**kwargs):
    return pltpu.CompilerParams(vmem_limit_bytes=VMEM_LIMIT, **kwargs)


def iota(shape, dim):
    return lax.broadcasted_iota(jnp.int32, shape, dim)


def dot(left, right):
    return jnp.dot(left, right, preferred_element_type=F32)


def split(wide):
    high = wide.astype(BF16)
    return high, (wide - high.astype(F32)).astype(BF16)


def dot3(left, right):
    lh, ll = split(left)
    rh, rl = split(right)
    both = jnp.concatenate([lh, ll], axis=1)
    top = jnp.concatenate([rh, rl], axis=1)
    low = jnp.concatenate([rh, jnp.zeros_like(rl)], axis=1)
    out = dot(both, jnp.concatenate([top, low], axis=0))
    width = right.shape[1]
    return out[:, :width] + out[:, width:]


def pack_kernel(mixed, dec, beta, cw, alog, dtb, kout, vout, hout, pout):
    row, tok = iota((32, TILE), 0), iota((32, TILE), 1)
    place = row & 15
    picks = []
    for cg in range(4):
        hit = (place < 12) & ((place & 3) == cg) & (tok == (row >> 4) * SPAN + 61 + (place >> 2))
        picks.append(jnp.where(hit, 1.0, 0.0).astype(BF16))
    for t in range(mixed.shape[0]):
        kout[t, :DK] = mixed[t, DK : 2 * DK]
        vout[t] = mixed[t, 2 * DK :]
        tails = jnp.zeros((32, TILE), F32)
        for cg in range(4):
            tails = tails + lax.dot_general(
                picks[cg],
                mixed[t, cg * 128 : (cg + 1) * 128],
                (((1,), (1,)), ((), ())),
                preferred_element_type=F32,
            )
        d, b = dec[t].astype(F32), beta[t].astype(F32)
        for r in range(RATIO):
            tails = jnp.where(row == 12 + r, d[r : r + 1], tails)
            tails = jnp.where(row == 14 + r, b[r : r + 1], tails)
        tails = tails.astype(BF16)
        kout[t, DK:] = tails
        hout[t] = tails[16:]

    @pl.when(pl.program_id(0) == 0)
    def first():
        for h in range(pout.shape[0]):
            pout[h, 16:] = jnp.zeros((8, 128), F32)
            for tap in range(KERNEL):
                for cg in range(4):
                    at = tap * 4 + cg
                    line = cw[tap, h : h + 1, cg * 128 : (cg + 1) * 128]
                    pout[h, at : at + 1] = line.astype(F32)
            for r in range(RATIO):
                v = h * RATIO + r
                pout[h, 16 + r : 17 + r] = jnp.full((1, 128), alog[v], F32)
                pout[h, 18 + r : 19 + r] = jnp.full((1, 128), dtb[v], F32)


def pack(mixed, dec, beta, cw, alog, dtb):
    heads = mixed.shape[0]
    own = cw.shape[1]
    smem = pl.BlockSpec(memory_space=pltpu.SMEM)
    return pl.pallas_call(
        pack_kernel,
        grid=(heads // STEP,),
        in_specs=[
            pl.BlockSpec((STEP, 512, TILE), lambda g: (g, 0, 0)),
            pl.BlockSpec((STEP, RATIO, TILE), lambda g: (g, 0, 0)),
            pl.BlockSpec((STEP, RATIO, TILE), lambda g: (g, 0, 0)),
            pl.BlockSpec((KERNEL, own, 512), lambda g: (0, 0, 0)),
            smem,
            smem,
        ],
        out_specs=[
            pl.BlockSpec((STEP, KROWS, TILE), lambda g: (g, 0, 0)),
            pl.BlockSpec((STEP, 256, TILE), lambda g: (g, 0, 0)),
            pl.BlockSpec((STEP, 16, TILE), lambda g: (g, 0, 0)),
            pl.BlockSpec((own, 24, 128), lambda g: (0, 0, 0)),
        ],
        out_shape=[
            jax.ShapeDtypeStruct((heads, KROWS, TILE), BF16),
            jax.ShapeDtypeStruct((heads, 256, TILE), BF16),
            jax.ShapeDtypeStruct((heads, 16, TILE), BF16),
            jax.ShapeDtypeStruct((own, 24, 128), F32),
        ],
        compiler_params=params(),
        cost_estimate=pl.CostEstimate(flops=10**8, bytes_accessed=4 << 20, transcendentals=0),
        name="pack",
    )(mixed, dec, beta, cw, alog, dtb)


def is_fresh(req, block):
    start = jnp.int32(0)
    fresh = jnp.bool_(False)
    for j in range(req.shape[1]):
        fresh = fresh | (start == block)
        start = start + req[0, j]
    return fresh


def spread_tables():
    row, col = iota((32, 7 * 128), 0), iota((32, 7 * 128), 1)
    lane, part = col & 127, col >> 7
    place = row & 15
    tables = []
    for cg in range(4):
        mine = (place & 3) == cg
        k = place >> 2
        halo = (row < 16) & (k < 3) & (part < 3) & (lane == k + part - 2)
        taps = (row >= 16) & (part == k + 3)
        tables.append(jnp.where(mine & (halo | taps), 1.0, 0.0).astype(BF16))
    return tables


def convolve(raw, rows, table, not_fresh0, masks):
    aux = lax.dot_general(rows, table, (((0,), (0,)), ((), ())), preferred_element_type=F32)
    cur = raw.astype(F32)
    total = None
    for tap in range(KERNEL):
        back = KERNEL - 1 - tap
        moved = cur
        if back:
            moved = pltpu.roll(cur, back, 1) * masks[back - 1]
            moved = moved + aux[:, (back - 1) * 128 : back * 128] * not_fresh0
        term = aux[:, (3 + tap) * 128 : (4 + tap) * 128] * moved
        total = term if total is None else total + term
    return (total / (1.0 + jnp.exp(-total))).astype(BF16)


def conv_masks(fresh1):
    lane = iota((1, TILE), 1)
    masks = []
    for back in range(1, KERNEL):
        cut = (lane >= SPAN) & (lane < SPAN + back) & fresh1
        masks.append(jnp.where((lane < back) | cut, 0.0, 1.0))
    return masks


def row_prep(dec, beta, alog, dtb):
    lane = iota(dec.shape, 1)
    x = dec + dtb
    decay = -jnp.exp(alog) * (jnp.maximum(x, 0.0) + jnp.log1p(jnp.exp(-jnp.abs(x))))
    cum = decay
    for shift in (1, 2, 4, 8, 16, 32):
        cum = cum + jnp.where((lane & (SPAN - 1)) >= shift, pltpu.roll(cum, shift, 1), 0.0)
    strength = 1.0 / (1.0 + jnp.exp(-beta))
    grown = jnp.exp(cum)
    close0, close1 = cum[:, SPAN - 1 : SPAN], cum[:, TILE - 1 :]
    fade = jnp.exp(jnp.where(lane < SPAN, close0, close1) - cum)
    keep0 = jnp.exp(jnp.broadcast_to(close0, cum.shape))
    keep1 = jnp.exp(jnp.broadcast_to(close1, cum.shape))
    return cum, strength, grown, fade, keep0, keep1


def unit_inverses(systems):
    row, col = iota((TILE, TILE), 0), iota((TILE, TILE), 1)
    near = (row >> 4) == (col >> 4)
    eye = jnp.where(row == col, 1.0, 0.0)
    power = [jnp.where(near, -a, 0.0) for a in systems]
    rest = [jnp.where(near, 0.0, a) for a in systems]
    total = [eye + p for p in power]
    power = [dot3(p, p) for p in power]
    for _ in range(2):
        both = [dot3(jnp.concatenate([t, p], axis=0), p) for t, p in zip(total, power)]
        total = [t + b[:TILE] for t, b in zip(total, both)]
        power = [b[TILE:] for b in both]
    total = [t + dot3(t, p) for t, p in zip(total, power)]
    cross = [dot3(t, r) for t, r in zip(total, rest)]
    both = [dot3(x, jnp.concatenate([x, t], axis=1)) for x, t in zip(cross, total)]
    total = [t - b[:, TILE:] for t, b in zip(total, both)]
    return [t + dot3(b[:, :TILE], t) for t, b in zip(total, both)]


def unit_keys(convolved):
    wide = convolved.astype(F32)
    return (wide * lax.rsqrt(jnp.sum(wide * wide, axis=0, keepdims=True) + EPSILON)).astype(BF16)


def solve_tiles(keys, queries, rows_out, last_is_values):
    cum, strength, grown, fade, keep0, keep1 = rows_out
    row, col = iota((TILE, TILE), 0), iota((TILE, TILE), 1)
    seen = (col >= row) & ((row >> 6) == (col >> 6))
    later = seen & (col > row)
    columns = jnp.transpose(jnp.concatenate([cum, fade], axis=0))
    count = cum.shape[0]
    systems, faded, scores = [], [], []
    for t, k in enumerate(keys):
        turned = jnp.transpose(k.astype(F32))
        if queries is None:
            gram = dot(turned.astype(BF16), k)
        else:
            prod = dot(turned.astype(BF16), jnp.concatenate([k, queries[t]], axis=1))
            gram = prod[:, :TILE]
        for r in range(RATIO):
            at = t * RATIO + r
            diff = cum[at : at + 1] - columns[:, at : at + 1]
            ratio = jnp.where(seen, jnp.exp(jnp.where(seen, diff, 0.0)), 0.0)
            systems.append(jnp.where(later, strength[at : at + 1] * gram * ratio, 0.0))
            if queries is not None:
                scores.append((prod[:, TILE:] * ratio).astype(BF16))
            faded.append((turned * columns[:, count + at : count + at + 1]).astype(BF16))
    solved = [s.astype(BF16) for s in unit_inverses(systems)]
    return solved, faded, scores


def token_prep_kernel(req, me, mixed, dec, beta, halo, par, wk, wv, sc, ft, qo, rows):
    fresh0, fresh1 = is_fresh(req, me[0] * 2), is_fresh(req, me[0] * 2 + 1)
    not_fresh0 = jnp.where(fresh0, 0.0, 1.0)
    masks = conv_masks(fresh1)
    tables = spread_tables()
    tiles = range(mixed.shape[0])

    def gather(pick):
        return jnp.concatenate([pick(t) for t in tiles], axis=0)

    prep = row_prep(
        gather(lambda t: dec[t].astype(F32)),
        gather(lambda t: beta[t].astype(F32)),
        gather(lambda t: par[t, 16:18]),
        gather(lambda t: par[t, 18:20]),
    )
    cum, strength, grown, fade, keep0, keep1 = prep
    keys, queries, values = [], [], []
    for t in tiles:
        lines = jnp.concatenate([halo[t], par[t, :16].astype(BF16)], axis=0)
        q, k, v0, v1 = [
            convolve(mixed[t, c * 128 : (c + 1) * 128], lines, tables[c], not_fresh0, masks)
            for c in range(4)
        ]
        keys.append(unit_keys(k))
        queries.append(q)
        values.append((v0, v1))
        qo[t] = q
        rows[t] = jnp.concatenate(
            [keep0[2 * t : 2 * t + 2], grown[2 * t : 2 * t + 2], keep1[2 * t : 2 * t + 2], strength[2 * t : 2 * t + 2]],
            axis=0,
        )
    solved, faded, scores = solve_tiles(keys, queries, prep, True)
    for t in tiles:
        for r in range(RATIO):
            at = t * RATIO + r
            s, lift = strength[at : at + 1], strength[at : at + 1] * grown[at : at + 1]
            stacked = jnp.concatenate(
                [
                    (lift * keys[t].astype(F32)).astype(BF16),
                    (s * values[t][r].astype(F32)).astype(BF16),
                ],
                axis=0,
            )
            out = dot(stacked, solved[at]).astype(BF16)
            wk[at] = out[:DK]
            wv[at] = out[DK:]
            sc[at] = scores[at]
            ft[at] = faded[at]


def token_prep(req, me, mixed, dec, beta, halo, par):
    heads = mixed.shape[0]
    smem = pl.BlockSpec(memory_space=pltpu.SMEM)

    def tiles(count, *rest):
        return pl.BlockSpec((count,) + rest, lambda g: (g,) + (0,) * len(rest))

    square = jax.ShapeDtypeStruct((heads * RATIO, 128, 128), BF16)
    return pl.pallas_call(
        token_prep_kernel,
        grid=(heads // STEP,),
        in_specs=[
            smem,
            smem,
            tiles(STEP, 512, TILE),
            tiles(STEP, RATIO, TILE),
            tiles(STEP, RATIO, TILE),
            tiles(STEP, 16, TILE),
            tiles(STEP, 24, 128),
        ],
        out_specs=[tiles(STEP * RATIO, 128, 128)] * 4 + [tiles(STEP, 128, 128), tiles(STEP, 8, 128)],
        out_shape=[square] * 4
        + [
            jax.ShapeDtypeStruct((heads, 128, 128), BF16),
            jax.ShapeDtypeStruct((heads, 8, 128), F32),
        ],
        compiler_params=params(),
        cost_estimate=pl.CostEstimate(flops=10**10, bytes_accessed=8 << 20, transcendentals=10**6),
        name="token_prep",
    )(req, me, mixed, dec, beta, halo, par)


def head_prep_kernel(req, kp, before, par, sol, ft, gs, rows):
    step = pl.program_id(0)
    depth, own = kp.shape[0], kp.shape[1]
    tables = spread_tables()
    order = [(d, h) for d in range(depth) for h in range(own)]

    def gather(pick):
        return jnp.concatenate([pick(d, h) for d, h in order], axis=0)

    small = [kp[d, h, DK : DK + 16].astype(F32) for d, h in order]
    prep = row_prep(
        jnp.concatenate([s[12:14] for s in small], axis=0),
        jnp.concatenate([s[14:16] for s in small], axis=0),
        gather(lambda d, h: par[h, 16:18]),
        gather(lambda d, h: par[h, 18:20]),
    )
    cum, strength, grown, fade, keep0, keep1 = prep
    keys = []
    for d in range(depth):
        block = (step * depth + d) * 2
        not_fresh0 = jnp.where(is_fresh(req, block), 0.0, 1.0)
        masks = conv_masks(is_fresh(req, block + 1))
        for h in range(own):
            halo = kp[d - 1, h, DK + 16 :] if d else before[0, h, 16:]
            lines = jnp.concatenate([halo, par[h, :16].astype(BF16)], axis=0)
            keys.append(unit_keys(convolve(kp[d, h, :DK], lines, tables[1], not_fresh0, masks)))
    solved, faded, unused = solve_tiles(keys, None, prep, False)
    lane = iota((DK, TILE), 1)
    for t, (d, h) in enumerate(order):
        rows[d, h] = jnp.concatenate(
            [keep0[2 * t : 2 * t + 2], keep1[2 * t : 2 * t + 2], strength[2 * t : 2 * t + 2], strength[2 * t : 2 * t + 2]],
            axis=0,
        )
        for r in range(RATIO):
            at = t * RATIO + r
            lift = strength[at : at + 1] * grown[at : at + 1]
            wide = dot((lift * keys[t].astype(F32)).astype(BF16), solved[at])
            halves = jnp.concatenate(
                [jnp.where(lane < SPAN, wide, 0.0), jnp.where(lane < SPAN, 0.0, wide)], axis=0
            ).astype(BF16)
            drop = dot(halves, faded[at]).astype(BF16)
            gs[d, h, r, 0] = drop[:DK]
            gs[d, h, r, 1] = drop[DK:]
            sol[d, h, r] = solved[at]
            ft[d, h, r] = faded[at]


def head_prep(req, kp, par):
    n, own = kp.shape[:2]
    depth = STEP // own
    smem = pl.BlockSpec(memory_space=pltpu.SMEM)

    def tiles(*rest):
        return pl.BlockSpec((depth, own) + rest, lambda g: (g, 0) + (0,) * len(rest))

    square = jax.ShapeDtypeStruct((n, own, RATIO, 128, 128), BF16)
    return pl.pallas_call(
        head_prep_kernel,
        grid=(n // depth,),
        in_specs=[
            smem,
            tiles(KROWS, TILE),
            pl.BlockSpec((1, own, 32, TILE), lambda g: (jnp.maximum(g * depth - 1, 0), 0, 4, 0)),
            pl.BlockSpec((own, 24, 128), lambda g: (0, 0, 0)),
        ],
        out_specs=[
            tiles(RATIO, 128, 128),
            tiles(RATIO, 128, 128),
            tiles(RATIO, 2, 128, 128),
            tiles(8, 128),
        ],
        out_shape=[
            square,
            square,
            jax.ShapeDtypeStruct((n, own, RATIO, 2, 128, 128), BF16),
            jax.ShapeDtypeStruct((n, own, 8, 128), F32),
        ],
        compiler_params=params(),
        cost_estimate=pl.CostEstimate(flops=10**10, bytes_accessed=6 << 20, transcendentals=10**6),
        name="head_prep",
    )(req, kp, kp, par)


def head_chain_kernel(
    req, rep, fin, vp, kt, before, par, sol, ft, gs, rows, sin, out, state, slots, counts
):
    step = pl.program_id(0)
    depth, own = vp.shape[0], vp.shape[1]
    n = sin.shape[0]
    replicas = counts.shape[0]
    base = own * RATIO * 128

    @pl.when(step == 0)
    def first():
        state[...] = jnp.zeros_like(state)
        out[...] = jnp.zeros_like(out)
        for i in range(2 * n):
            slots[i] = -1
        for i in range(replicas):
            counts[i] = 0
        end = jnp.int32(-1)
        for j in range(req.shape[1]):
            end = end + req[0, j]
            where = rep[0, j]
            place = counts[where]
            done = fin[0, j] > 0
            slots[end] = jnp.where(done, where * CAP + jnp.minimum(place, CAP - 1), -1)
            counts[where] = place + jnp.where(done, 1, 0)
        for i in range(replicas):
            number = jnp.full((16, 128), counts[i], jnp.int32).astype(F32).astype(BF16)
            for c in range(CAP):
                out[i * CAP + c, base + own * 16 :] = number

    tables = spread_tables()
    lane = iota((DV, TILE), 1)
    gains = {}
    for d in range(depth):
        block = (step * depth + d) * 2
        not_fresh0 = jnp.where(is_fresh(req, block), 0.0, 1.0)
        masks = conv_masks(is_fresh(req, block + 1))
        for h in range(own):
            halo = kt[d - 1, h, 16:] if d else before[0, h, 16:]
            lines = jnp.concatenate([halo, par[h, :16].astype(BF16)], axis=0)
            for r in range(RATIO):
                value = convolve(
                    vp[d, h, r * DV : (r + 1) * DV], lines, tables[2 + r], not_fresh0, masks
                )
                scaled = (rows[d, h, 4 + r : 5 + r] * value.astype(F32)).astype(BF16)
                wide = dot(scaled, sol[d, h, r])
                halves = jnp.concatenate(
                    [jnp.where(lane < SPAN, wide, 0.0), jnp.where(lane < SPAN, 0.0, wide)], axis=0
                ).astype(BF16)
                gains[d, h, r] = dot(halves, ft[d, h, r])
    current = [state[v] for v in range(own * RATIO)]
    for d in range(depth):
        tile = step * depth + d
        for half in range(2):
            block = tile * 2 + half
            stay = jnp.where(is_fresh(req, block), 0.0, 1.0)
            for h in range(own):
                for r in range(RATIO):
                    v = h * RATIO + r
                    now = current[v] * stay
                    keep = rows[d, h, 2 * half + r : 2 * half + r + 1]
                    gain = gains[d, h, r][half * DV : (half + 1) * DV]
                    current[v] = keep * now + (gain - dot(now.astype(BF16), gs[d, h, r, half]))
            slot = slots[block]

            @pl.when(slot >= 0)
            def land():
                for v in range(own * RATIO):
                    out[slot, v * 128 : (v + 1) * 128] = current[v].astype(BF16)
                for h in range(own):
                    out[slot, base + h * 16 : base + h * 16 + 16] = kt[
                        d, h, half * 16 : half * 16 + 16
                    ]

        onward = lax.rem(tile + 1, n)
        for v in range(own * RATIO):
            sin[onward, v] = current[v].astype(BF16)
    for v in range(own * RATIO):
        state[v] = current[v]


def head_chain(req, rep, fin, vp, kp, par, sol, ft, gs, rows, replicas):
    n, own = vp.shape[:2]
    depth = STEP // own
    smem = pl.BlockSpec(memory_space=pltpu.SMEM)
    lines = own * RATIO * 128 + own * 16 + 16

    def tiles(*rest):
        return pl.BlockSpec((depth, own) + rest, lambda g: (g, 0) + (0,) * len(rest))

    return pl.pallas_call(
        head_chain_kernel,
        grid=(n // depth,),
        in_specs=[
            smem,
            smem,
            smem,
            tiles(256, TILE),
            pl.BlockSpec((depth, own, 32, TILE), lambda g: (g, 0, 4, 0)),
            pl.BlockSpec((1, own, 32, TILE), lambda g: (jnp.maximum(g * depth - 1, 0), 0, 4, 0)),
            pl.BlockSpec((own, 24, 128), lambda g: (0, 0, 0)),
            tiles(RATIO, 128, 128),
            tiles(RATIO, 128, 128),
            tiles(RATIO, 2, 128, 128),
            tiles(8, 128),
        ],
        out_specs=[
            pl.BlockSpec((n, own * RATIO, 128, 128), lambda g: (0, 0, 0, 0)),
            pl.BlockSpec((replicas * CAP, lines, 128), lambda g: (0, 0, 0)),
        ],
        out_shape=[
            jax.ShapeDtypeStruct((n, own * RATIO, 128, 128), BF16),
            jax.ShapeDtypeStruct((replicas * CAP, lines, 128), BF16),
        ],
        scratch_shapes=[
            pltpu.VMEM((own * RATIO, 128, 128), F32),
            pltpu.SMEM((2 * n,), jnp.int32),
            pltpu.SMEM((replicas,), jnp.int32),
        ],
        compiler_params=params(),
        cost_estimate=pl.CostEstimate(flops=3 * 10**9, bytes_accessed=8 << 20, transcendentals=10**6),
        name="head_chain",
    )(req, rep, fin, vp, kp, kp, par, sol, ft, gs, rows)


def token_out_kernel(req, me, sin, wk, wv, sc, ft, qs, rows, gate, gain, out):
    stay0 = jnp.where(is_fresh(req, me[0] * 2), 0.0, 1.0)
    stay1 = jnp.where(is_fresh(req, me[0] * 2 + 1), 0.0, 1.0)
    lane = iota((DV, TILE), 1)
    early = lane < SPAN
    units = [(t, r) for t in range(qs.shape[0]) for r in range(RATIO)]
    both = [jnp.concatenate([wk[t * RATIO + r], qs[t]], axis=1) for t, r in units]
    enter = [sin[t * RATIO + r].astype(F32) * stay0 for t, r in units]
    first = [dot(e.astype(BF16), b) for e, b in zip(enter, both)]
    wide = [wv[t * RATIO + r].astype(F32) for t, r in units]
    new0 = [jnp.where(early, w - f[:, :TILE], 0.0) for w, f in zip(wide, first)]
    middle = [
        (rows[t, r : r + 1] * e + dot(x.astype(BF16), ft[t * RATIO + r])) * stay1
        for (t, r), e, x in zip(units, enter, new0)
    ]
    second = [dot(m.astype(BF16), b) for m, b in zip(middle, both)]
    new = [
        jnp.where(early, x, w - s[:, :TILE]).astype(BF16) for x, w, s in zip(new0, wide, second)
    ]
    for at, (t, r) in enumerate(units):
        core = rows[t, 2 + r : 3 + r] * jnp.where(early, first[at][:, TILE:], second[at][:, TILE:])
        core = (core + dot(new[at], sc[at])).astype(BF16).astype(F32)
        inverse_rms = lax.rsqrt(jnp.mean(core * core, axis=0, keepdims=True) + EPSILON)
        z = gate[t, r * DV : (r + 1) * DV].astype(F32)
        result = core * inverse_rms * gain[...] * (z / (1.0 + jnp.exp(-z)))
        out[t, r * DV : (r + 1) * DV] = result.astype(BF16)


def token_out(req, me, sin, wk, wv, sc, ft, qs, rows, gate, gain):
    heads = qs.shape[0]
    smem = pl.BlockSpec(memory_space=pltpu.SMEM)

    def tiles(count, *rest):
        return pl.BlockSpec((count,) + rest, lambda g: (g,) + (0,) * len(rest))

    return pl.pallas_call(
        token_out_kernel,
        grid=(heads // STEP,),
        in_specs=[smem, smem]
        + [tiles(STEP * RATIO, 128, 128)] * 5
        + [
            tiles(STEP, 128, 128),
            tiles(STEP, 8, 128),
            tiles(STEP, 256, TILE),
            pl.BlockSpec((128, 128), lambda g: (0, 0)),
        ],
        out_specs=tiles(STEP, 256, TILE),
        out_shape=jax.ShapeDtypeStruct((heads, 256, TILE), BF16),
        compiler_params=params(),
        cost_estimate=pl.CostEstimate(flops=10**9, bytes_accessed=8 << 20, transcendentals=10**6),
        name="token_out",
    )(req, me, sin, wk, wv, sc, ft, qs, rows, gate, gain)


def land_kernel(count, got, states, tails):
    slot = pl.program_id(0)
    heads = states.shape[1]
    start = jnp.int32(0)
    source = jnp.int32(-1)
    for p in range(got.shape[0] // CAP):
        number = count[p]
        inside = (slot >= start) & (slot < start + number)
        source = jnp.where(inside, p * CAP + (slot - start), source)
        start = start + number

    @pl.when(source >= 0)
    def take():
        for v in range(heads):
            block = got[source, v * 128 : (v + 1) * 128].astype(F32)
            states[0, v] = jnp.transpose(block)
        for h in range(tails.shape[1]):
            tails[0, h] = got[source, heads * 128 + h * 16 : heads * 128 + h * 16 + 16]

    @pl.when(source < 0)
    def clear():
        states[...] = jnp.zeros_like(states)
        tails[...] = jnp.zeros_like(tails)


def land(count, got, heads, own):
    slots, lines = got.shape[:2]
    return pl.pallas_call(
        land_kernel,
        grid=(slots,),
        in_specs=[
            pl.BlockSpec(memory_space=pltpu.SMEM),
            pl.BlockSpec((slots, lines, 128), lambda g: (0, 0, 0)),
        ],
        out_specs=[
            pl.BlockSpec((1, heads, 128, 128), lambda g: (g, 0, 0, 0)),
            pl.BlockSpec((1, own, 16, 128), lambda g: (g, 0, 0, 0)),
        ],
        out_shape=[
            jax.ShapeDtypeStruct((slots, heads, 128, 128), F32),
            jax.ShapeDtypeStruct((slots, own, 16, 128), BF16),
        ],
        compiler_params=params(),
        cost_estimate=pl.CostEstimate(flops=10**6, bytes_accessed=4 << 20, transcendentals=0),
        name="land",
    )(count, got)


def body(
    mixed,
    decay_in,
    beta_in,
    gate_z,
    conv_weight,
    a_log,
    dt_bias,
    norm_gain,
    req_blocks,
    replica_of,
    finished,
):
    n = lax.axis_size("seq")
    replicas = lax.axis_size("rep")
    heads = mixed.shape[1]
    own = heads // n
    me = lax.axis_index("seq").astype(jnp.int32).reshape(1)
    kpack, vpack, halo, par = pack(mixed[0], decay_in[0], beta_in[0], conv_weight, a_log, dt_bias)
    kp = lax.all_to_all(kpack.reshape(n, own, KROWS, TILE), "seq", 0, 0, tiled=True)
    vp = lax.all_to_all(vpack.reshape(n, own, 256, TILE), "seq", 0, 0, tiled=True)
    halo = lax.ppermute(halo, "seq", [(i, i + 1) for i in range(n - 1)])
    par_all = lax.all_gather(par, "seq", axis=0, tiled=True)
    wk, wv, sc, ft, qs, rows = token_prep(
        req_blocks, me, mixed[0], decay_in[0], beta_in[0], halo, par_all
    )
    hsol, hft, hgs, hrows = head_prep(req_blocks, kp, par)
    sin, send = head_chain(
        req_blocks, replica_of, finished, vp, kp, par, hsol, hft, hgs, hrows, replicas
    )
    lines = send.shape[1]
    sin = lax.all_to_all(sin, "seq", 0, 0, tiled=True)
    got = lax.all_to_all(send.reshape(replicas, CAP, lines, 128), "rep", 0, 0, tiled=True)
    count = got[:, 0, lines - 1, 0].astype(jnp.int32)
    states, tails = land(count, got.reshape(replicas * CAP, lines, 128), own * RATIO, own)
    tails = tails.reshape(replicas * CAP, own, 4, 512)[:, :, : KERNEL - 1].transpose(0, 2, 1, 3)
    gain = jnp.broadcast_to(norm_gain[:, None], (DV, TILE))
    out = token_out(
        req_blocks,
        me,
        sin.reshape(heads * RATIO, 128, 128),
        wk,
        wv,
        sc,
        ft,
        qs,
        rows,
        gate_z[0],
        gain,
    )
    return (out[None], states[None], tails[None])


def solution(mesh):
    placed = (
        P("rep", None, None, "seq"),
        P("rep", None, None, "seq"),
        P("rep", None, None, "seq"),
        P("rep", None, None, "seq"),
        P(None, "seq", None),
        P("seq"),
        P("seq"),
        P(),
        P("rep", None),
        P("rep", None),
        P("rep", None),
    )
    return jax.shard_map(
        body,
        mesh=mesh,
        in_specs=placed,
        out_specs=(
            P("rep", None, None, "seq"),
            P("rep", None, "seq", None, None),
            P("rep", None, None, "seq", None),
        ),
        check_vma=False,
    )
```

```python
import functools

import jax
import jax.numpy as jnp
from jax import lax
from jax.experimental import pallas as pl
from jax.experimental.pallas import tpu as pltpu
from jax.sharding import PartitionSpec as P

DK = 128
DV = 128
KERNEL = 4
SPAN = 64
CAP = 2
RATIO = 2
TILE = 2 * SPAN
KROWS = 160
STEP = 4
EPSILON = 1e-06
F32 = jnp.float32
BF16 = jnp.bfloat16
VMEM_LIMIT = 56 * 1024 * 1024


def params(**kwargs):
    return pltpu.CompilerParams(vmem_limit_bytes=VMEM_LIMIT, **kwargs)


def iota(shape, dim):
    return lax.broadcasted_iota(jnp.int32, shape, dim)


def dot(left, right):
    return jnp.dot(left, right, preferred_element_type=F32)


def split(wide):
    high = wide.astype(BF16)
    return high, (wide - high.astype(F32)).astype(BF16)


def halves(shape):
    first = iota(shape, len(shape) - 1) < SPAN
    return jnp.where(first, 1.0, 0.0).astype(BF16), jnp.where(first, 0.0, 1.0).astype(BF16)


def diagonal(packed, masks):
    return jnp.concatenate([packed * masks[0], packed * masks[1]], axis=0)


def dot3(left, right, masks):
    high = diagonal(right[0], masks)
    top = jnp.concatenate([high, diagonal(right[1], masks)], axis=1)
    low = jnp.concatenate([high, jnp.zeros_like(high)], axis=1)
    out = dot(jnp.concatenate(left, axis=1), jnp.concatenate([top, low], axis=0))
    return out[:, :TILE] + out[:, TILE:]


def pack_kernel(mixed, dec, beta, cw, alog, dtb, kout, vout, hout, pout):
    row, tok = iota((32, TILE), 0), iota((32, TILE), 1)
    place = row & 15
    picks = []
    for cg in range(4):
        hit = (place < 12) & ((place & 3) == cg) & (tok == (row >> 4) * SPAN + 61 + (place >> 2))
        picks.append(jnp.where(hit, 1.0, 0.0).astype(BF16))
    for t in range(mixed.shape[0]):
        kout[t, :DK] = mixed[t, DK : 2 * DK]
        vout[t] = mixed[t, 2 * DK :]
        tails = jnp.zeros((32, TILE), F32)
        for cg in range(4):
            tails = tails + lax.dot_general(
                picks[cg],
                mixed[t, cg * 128 : (cg + 1) * 128],
                (((1,), (1,)), ((), ())),
                preferred_element_type=F32,
            )
        d, b = dec[t].astype(F32), beta[t].astype(F32)
        for r in range(RATIO):
            tails = jnp.where(row == 12 + r, d[r : r + 1], tails)
            tails = jnp.where(row == 14 + r, b[r : r + 1], tails)
        tails = tails.astype(BF16)
        kout[t, DK:] = tails
        hout[t] = tails[16:]

    @pl.when(pl.program_id(0) == 0)
    def first():
        for h in range(pout.shape[0]):
            pout[h, 16:] = jnp.zeros((8, 128), F32)
            for tap in range(KERNEL):
                for cg in range(4):
                    at = tap * 4 + cg
                    line = cw[tap, h : h + 1, cg * 128 : (cg + 1) * 128]
                    pout[h, at : at + 1] = line.astype(F32)
            for r in range(RATIO):
                v = h * RATIO + r
                pout[h, 16 + r : 17 + r] = jnp.full((1, 128), alog[v], F32)
                pout[h, 18 + r : 19 + r] = jnp.full((1, 128), dtb[v], F32)


def pack(mixed, dec, beta, cw, alog, dtb):
    heads = mixed.shape[0]
    own = cw.shape[1]
    smem = pl.BlockSpec(memory_space=pltpu.SMEM)
    return pl.pallas_call(
        pack_kernel,
        grid=(heads // STEP,),
        in_specs=[
            pl.BlockSpec((STEP, 512, TILE), lambda g: (g, 0, 0)),
            pl.BlockSpec((STEP, RATIO, TILE), lambda g: (g, 0, 0)),
            pl.BlockSpec((STEP, RATIO, TILE), lambda g: (g, 0, 0)),
            pl.BlockSpec((KERNEL, own, 512), lambda g: (0, 0, 0)),
            smem,
            smem,
        ],
        out_specs=[
            pl.BlockSpec((STEP, KROWS, TILE), lambda g: (g, 0, 0)),
            pl.BlockSpec((STEP, 256, TILE), lambda g: (g, 0, 0)),
            pl.BlockSpec((STEP, 16, TILE), lambda g: (g, 0, 0)),
            pl.BlockSpec((own, 24, 128), lambda g: (0, 0, 0)),
        ],
        out_shape=[
            jax.ShapeDtypeStruct((heads, KROWS, TILE), BF16),
            jax.ShapeDtypeStruct((heads, 256, TILE), BF16),
            jax.ShapeDtypeStruct((heads, 16, TILE), BF16),
            jax.ShapeDtypeStruct((own, 24, 128), F32),
        ],
        compiler_params=params(),
        cost_estimate=pl.CostEstimate(flops=10**8, bytes_accessed=4 << 20, transcendentals=0),
        name="pack",
    )(mixed, dec, beta, cw, alog, dtb)


def is_fresh(req, block):
    start = jnp.int32(0)
    fresh = jnp.bool_(False)
    for j in range(req.shape[1]):
        fresh = fresh | (start == block)
        start = start + req[0, j]
    return fresh


def tap_tables():
    row, part = iota((16, 4 * 128), 0), iota((16, 4 * 128), 1) >> 7
    hits = [((row & 3) == cg) & ((row >> 2) == part) for cg in range(4)]
    return [jnp.where(hit, 1.0, 0.0).astype(BF16) for hit in hits]


def halo_tables():
    row, lane = iota((48, 128), 0), iota((48, 128), 1)
    token = (row >> 2) % 3
    hits = [((row & 3) == cg) & (row < 36) & (token == lane) for cg in range(4)]
    return [jnp.where(hit, 1.0, 0.0).astype(BF16) for hit in hits]


def turned_dot(rows, table):
    return lax.dot_general(rows, table, (((0,), (0,)), ((), ())), preferred_element_type=F32)


def spread_taps(par, table):
    both = turned_dot(par, table)
    return [both[:, tap * 128 : (tap + 1) * 128] for tap in range(KERNEL)]


def halo_terms(halo, par, not_fresh0):
    x = [halo[4 * k : 4 * k + 4].astype(F32) * not_fresh0 for k in range(3)]
    w = [par[4 * k : 4 * k + 4] for k in range(3)]
    terms = jnp.concatenate(
        [w[0] * x[0] + w[1] * x[1] + w[2] * x[2], w[0] * x[1] + w[1] * x[2], w[0] * x[2]], axis=0
    )
    high = terms.astype(BF16).astype(F32)
    middle = (terms - high).astype(BF16).astype(F32)
    parts = [high, middle, terms - high - middle, jnp.zeros((12, 128), F32)]
    return jnp.concatenate(parts, axis=0).astype(BF16)


def convolve(raw, terms, table, taps, masks):
    cur = raw.astype(F32)
    total = taps[KERNEL - 1] * cur + turned_dot(terms, table)
    for back in range(1, KERNEL):
        moved = pltpu.roll(cur, back, 1) * masks[back - 1]
        total = total + taps[KERNEL - 1 - back] * moved
    return (total / (1.0 + jnp.exp(-total))).astype(BF16)


def conv_masks(fresh1):
    lane = iota((1, TILE), 1)
    masks = []
    for back in range(1, KERNEL):
        cut = (lane >= SPAN) & (lane < SPAN + back) & fresh1
        masks.append(jnp.where((lane < back) | cut, 0.0, 1.0))
    return masks


def row_prep(dec, beta, alog, dtb):
    lane = iota(dec.shape, 1)
    x = dec + dtb
    decay = -jnp.exp(alog) * (jnp.maximum(x, 0.0) + jnp.log1p(jnp.exp(-jnp.abs(x))))
    cum = decay
    for shift in (1, 2, 4, 8, 16, 32):
        cum = cum + jnp.where((lane & (SPAN - 1)) >= shift, pltpu.roll(cum, shift, 1), 0.0)
    strength = 1.0 / (1.0 + jnp.exp(-beta))
    grown = jnp.exp(cum)
    close0, close1 = cum[:, SPAN - 1 : SPAN], cum[:, TILE - 1 :]
    fade = jnp.exp(jnp.where(lane < SPAN, close0, close1) - cum)
    keep0 = jnp.exp(jnp.broadcast_to(close0, cum.shape))
    keep1 = jnp.exp(jnp.broadcast_to(close1, cum.shape))
    return cum, strength, grown, fade, keep0, keep1


def unit_inverses(systems):
    row, col = iota((SPAN, TILE), 0), iota((SPAN, TILE), 1) & (SPAN - 1)
    near = (row >> 4) == (col >> 4)
    eye = jnp.where(row == col, 1.0, 0.0)
    masks = halves((SPAN, TILE))
    power = [jnp.where(near, -a, 0.0) for a in systems]
    rest = [split(jnp.where(near, 0.0, a)) for a in systems]
    total = [eye + p for p in power]
    parts = [split(p) for p in power]
    power = [dot3(p, p, masks) for p in parts]
    for _ in range(2):
        parts = [split(p) for p in power]
        stacks = [
            [jnp.concatenate(pair, axis=0) for pair in zip(split(t), p)]
            for t, p in zip(total, parts)
        ]
        both = [dot3(s, p, masks) for s, p in zip(stacks, parts)]
        total = [t + b[:SPAN] for t, b in zip(total, both)]
        power = [b[SPAN:] for b in both]
    total = [t + dot3(split(t), split(p), masks) for t, p in zip(total, power)]
    parts = [split(t) for t in total]
    cross = [split(dot3(t, r, masks)) for t, r in zip(parts, rest)]
    total = [t - dot3(x, p, masks) for t, x, p in zip(total, cross, parts)]
    cross = [dot3(x, x, masks) for x in cross]
    return [t + dot3(split(x), split(t), masks) for t, x in zip(total, cross)]


def unit_keys(convolved):
    wide = convolved.astype(F32)
    return (wide * lax.rsqrt(jnp.sum(wide * wide, axis=0, keepdims=True) + EPSILON)).astype(BF16)


def solve_tiles(keys, queries, prep):
    cum, strength, grown, fade, keep0, keep1 = prep
    row, lane = iota((SPAN, TILE), 0), iota((SPAN, TILE), 1)
    early = lane < SPAN
    seen = (lane & (SPAN - 1)) >= row
    later = (lane & (SPAN - 1)) > row
    columns = jnp.transpose(jnp.concatenate([cum, fade], axis=0))
    count = cum.shape[0]

    def beside(tall):
        return jnp.where(early, tall[:SPAN], tall[SPAN:])

    systems, faded, scores = [], [], []
    for t, k in enumerate(keys):
        turned = jnp.transpose(k.astype(F32))
        if queries is None:
            gram = beside(dot(turned.astype(BF16), k))
        else:
            prod = dot(turned.astype(BF16), jnp.concatenate([k, queries[t]], axis=1))
            gram, touch = beside(prod[:, :TILE]), beside(prod[:, TILE:])
        for r in range(RATIO):
            at = t * RATIO + r
            diff = cum[at : at + 1] - beside(columns[:, at : at + 1])
            ratio = jnp.where(seen, jnp.exp(jnp.where(seen, diff, 0.0)), 0.0)
            systems.append(jnp.where(later, strength[at : at + 1] * gram * ratio, 0.0))
            if queries is not None:
                scores.append((touch * ratio).astype(BF16))
            faded.append((turned * columns[:, count + at : count + at + 1]).astype(BF16))
    solved = [s.astype(BF16) for s in unit_inverses(systems)]
    return solved, faded, scores


def token_prep_kernel(req, me, mixed, dec, beta, halo, par, wk, wv, sc, ft, qo, rows):
    fresh0, fresh1 = is_fresh(req, me[0] * 2), is_fresh(req, me[0] * 2 + 1)
    not_fresh0 = jnp.where(fresh0, 0.0, 1.0)
    masks = conv_masks(fresh1)
    tap_tab, halo_tab = tap_tables(), halo_tables()
    tiles = range(mixed.shape[0])

    def gather(pick):
        return jnp.concatenate([pick(t) for t in tiles], axis=0)

    prep = row_prep(
        gather(lambda t: dec[t].astype(F32)),
        gather(lambda t: beta[t].astype(F32)),
        gather(lambda t: par[t, 16:18]),
        gather(lambda t: par[t, 18:20]),
    )
    cum, strength, grown, fade, keep0, keep1 = prep
    keys, queries, values = [], [], []
    for t in tiles:
        terms = halo_terms(halo[t], par[t], not_fresh0)
        lines = par[t, :16].astype(BF16)
        q, k, v0, v1 = [
            convolve(
                mixed[t, c * 128 : (c + 1) * 128],
                terms,
                halo_tab[c],
                spread_taps(lines, tap_tab[c]),
                masks,
            )
            for c in range(4)
        ]
        keys.append(unit_keys(k))
        queries.append(q)
        values.append((v0, v1))
        qo[t] = q
        rows[t] = jnp.concatenate(
            [keep0[2 * t : 2 * t + 2], grown[2 * t : 2 * t + 2], keep1[2 * t : 2 * t + 2], strength[2 * t : 2 * t + 2]],
            axis=0,
        )
    solved, faded, scores = solve_tiles(keys, queries, prep)
    sides = halves((SPAN, TILE))
    for t in tiles:
        for r in range(RATIO):
            at = t * RATIO + r
            s, lift = strength[at : at + 1], strength[at : at + 1] * grown[at : at + 1]
            stacked = jnp.concatenate(
                [
                    (lift * keys[t].astype(F32)).astype(BF16),
                    (s * values[t][r].astype(F32)).astype(BF16),
                ],
                axis=0,
            )
            out = dot(stacked, diagonal(solved[at], sides)).astype(BF16)
            wk[at] = out[:DK]
            wv[at] = out[DK:]
            sc[at] = scores[at]
            ft[at] = faded[at]


def token_prep(req, me, mixed, dec, beta, halo, par):
    heads = mixed.shape[0]
    smem = pl.BlockSpec(memory_space=pltpu.SMEM)

    def tiles(count, *rest):
        return pl.BlockSpec((count,) + rest, lambda g: (g,) + (0,) * len(rest))

    square = jax.ShapeDtypeStruct((heads * RATIO, 128, 128), BF16)
    return pl.pallas_call(
        token_prep_kernel,
        grid=(heads // STEP,),
        in_specs=[
            smem,
            smem,
            tiles(STEP, 512, TILE),
            tiles(STEP, RATIO, TILE),
            tiles(STEP, RATIO, TILE),
            tiles(STEP, 16, TILE),
            tiles(STEP, 24, 128),
        ],
        out_specs=[tiles(STEP * RATIO, 128, 128)] * 2
        + [tiles(STEP * RATIO, SPAN, TILE), tiles(STEP * RATIO, 128, 128)]
        + [tiles(STEP, 128, 128), tiles(STEP, 8, 128)],
        out_shape=[square] * 2
        + [
            jax.ShapeDtypeStruct((heads * RATIO, SPAN, TILE), BF16),
            square,
            jax.ShapeDtypeStruct((heads, 128, 128), BF16),
            jax.ShapeDtypeStruct((heads, 8, 128), F32),
        ],
        compiler_params=params(),
        cost_estimate=pl.CostEstimate(flops=10**10, bytes_accessed=8 << 20, transcendentals=10**6),
        name="token_prep",
    )(req, me, mixed, dec, beta, halo, par)


def head_prep_kernel(req, kp, before, par, sol, ft, gs, rows):
    step = pl.program_id(0)
    depth, own = kp.shape[0], kp.shape[1]
    tap_tab, halo_tab = tap_tables(), halo_tables()
    order = [(d, h) for d in range(depth) for h in range(own)]

    def gather(pick):
        return jnp.concatenate([pick(d, h) for d, h in order], axis=0)

    small = [kp[d, h, DK : DK + 16].astype(F32) for d, h in order]
    prep = row_prep(
        jnp.concatenate([s[12:14] for s in small], axis=0),
        jnp.concatenate([s[14:16] for s in small], axis=0),
        gather(lambda d, h: par[h, 16:18]),
        gather(lambda d, h: par[h, 18:20]),
    )
    cum, strength, grown, fade, keep0, keep1 = prep
    keys = []
    taps = [spread_taps(par[h, :16].astype(BF16), tap_tab[1]) for h in range(own)]
    for d in range(depth):
        block = (step * depth + d) * 2
        not_fresh0 = jnp.where(is_fresh(req, block), 0.0, 1.0)
        masks = conv_masks(is_fresh(req, block + 1))
        for h in range(own):
            halo = kp[d - 1, h, DK + 16 :] if d else before[0, h, 16:]
            terms = halo_terms(halo, par[h], not_fresh0)
            keys.append(unit_keys(convolve(kp[d, h, :DK], terms, halo_tab[1], taps[h], masks)))
    solved, faded, unused = solve_tiles(keys, None, prep)
    sides, wide_sides = halves((SPAN, TILE)), halves((DK, TILE))
    for t, (d, h) in enumerate(order):
        rows[d, h] = jnp.concatenate(
            [keep0[2 * t : 2 * t + 2], keep1[2 * t : 2 * t + 2], strength[2 * t : 2 * t + 2], strength[2 * t : 2 * t + 2]],
            axis=0,
        )
        for r in range(RATIO):
            at = t * RATIO + r
            lift = strength[at : at + 1] * grown[at : at + 1]
            scaled = (lift * keys[t].astype(F32)).astype(BF16)
            wide = dot(scaled, diagonal(solved[at], sides)).astype(BF16)
            drop = dot(diagonal(wide, wide_sides), faded[at]).astype(BF16)
            gs[d, h, r, 0] = drop[:DK]
            gs[d, h, r, 1] = drop[DK:]
            sol[d, h, r] = solved[at]
            ft[d, h, r] = faded[at]


def head_prep(req, kp, par):
    n, own = kp.shape[:2]
    depth = STEP // own
    smem = pl.BlockSpec(memory_space=pltpu.SMEM)

    def tiles(*rest):
        return pl.BlockSpec((depth, own) + rest, lambda g: (g, 0) + (0,) * len(rest))

    square = jax.ShapeDtypeStruct((n, own, RATIO, 128, 128), BF16)
    return pl.pallas_call(
        head_prep_kernel,
        grid=(n // depth,),
        in_specs=[
            smem,
            tiles(KROWS, TILE),
            pl.BlockSpec((1, own, 32, TILE), lambda g: (jnp.maximum(g * depth - 1, 0), 0, 4, 0)),
            pl.BlockSpec((own, 24, 128), lambda g: (0, 0, 0)),
        ],
        out_specs=[
            tiles(RATIO, SPAN, TILE),
            tiles(RATIO, 128, 128),
            tiles(RATIO, 2, 128, 128),
            tiles(8, 128),
        ],
        out_shape=[
            jax.ShapeDtypeStruct((n, own, RATIO, SPAN, TILE), BF16),
            square,
            jax.ShapeDtypeStruct((n, own, RATIO, 2, 128, 128), BF16),
            jax.ShapeDtypeStruct((n, own, 8, 128), F32),
        ],
        compiler_params=params(),
        cost_estimate=pl.CostEstimate(flops=10**10, bytes_accessed=6 << 20, transcendentals=10**6),
        name="head_prep",
    )(req, kp, kp, par)


def head_chain_kernel(req, vp, kt, before, par, sol, ft, grows, gs, rows, sin, ends, state, gains):
    step = pl.program_id(0)
    last = pl.num_programs(0) - 2
    depth, own = vp.shape[0], vp.shape[1]
    n = sin.shape[0]
    into, past = lax.rem(step, 2), lax.rem(step + 1, 2)
    group, old = jnp.minimum(step, last), jnp.maximum(step - 1, 0)

    current = [state[v] for v in range(own * RATIO)]
    for d in range(depth):
        tile = old * depth + d
        for half in range(2):
            fresh = is_fresh(req, tile * 2 + half)
            for h in range(own):
                for r in range(RATIO):
                    v = h * RATIO + r
                    now = jnp.where(fresh, 0.0, current[v])
                    keep = rows[d, h, 2 * half + r : 2 * half + r + 1]
                    gain = gains[past, (d * own + h) * RATIO + r, half]
                    current[v] = keep * now + (gain - dot(now.astype(BF16), gs[d, h, r, half]))
                    ends[d * 2 + half, v] = current[v].astype(BF16)
        onward = lax.rem(tile + 1, n)
        for v in range(own * RATIO):
            sin[onward, v] = current[v].astype(BF16)
    for v in range(own * RATIO):
        state[v] = current[v]

    tap_tab, halo_tab = tap_tables(), halo_tables()
    sides, wide_sides = halves((SPAN, TILE)), halves((DV, TILE))
    taps = {
        (h, r): spread_taps(par[h, :16].astype(BF16), tap_tab[2 + r])
        for h in range(own)
        for r in range(RATIO)
    }
    for d in range(depth):
        block = (group * depth + d) * 2
        not_fresh0 = jnp.where(is_fresh(req, block), 0.0, 1.0)
        masks = conv_masks(is_fresh(req, block + 1))
        for h in range(own):
            halo = kt[d - 1, h, 16:] if d else before[0, h, 16:]
            terms = halo_terms(halo, par[h], not_fresh0)
            for r in range(RATIO):
                raw = vp[d, h, r * DV : (r + 1) * DV]
                value = convolve(raw, terms, halo_tab[2 + r], taps[h, r], masks)
                scaled = (grows[d, h, 4 + r : 5 + r] * value.astype(F32)).astype(BF16)
                wide = dot(scaled, diagonal(sol[d, h, r], sides)).astype(BF16)
                gain = dot(diagonal(wide, wide_sides), ft[d, h, r])
                at = (d * own + h) * RATIO + r
                gains[into, at, 0] = gain[:DV]
                gains[into, at, 1] = gain[DV:]


def head_chain(req, vp, kp, par, sol, ft, gs, rows):
    n, own = vp.shape[:2]
    depth = STEP // own
    steps = n // depth
    smem = pl.BlockSpec(memory_space=pltpu.SMEM)

    def tiles(*rest):
        return pl.BlockSpec(
            (depth, own) + rest, lambda g: (jnp.minimum(g, steps - 1), 0) + (0,) * len(rest)
        )

    def old(*rest):
        return pl.BlockSpec(
            (depth, own) + rest, lambda g: (jnp.maximum(g - 1, 0), 0) + (0,) * len(rest)
        )

    def at_tails(g):
        return (jnp.minimum(g, steps - 1), 0, 4, 0)

    def at_halo(g):
        return (jnp.maximum(jnp.minimum(g, steps - 1) * depth - 1, 0), 0, 4, 0)

    return pl.pallas_call(
        head_chain_kernel,
        grid=(steps + 1,),
        in_specs=[
            smem,
            tiles(256, TILE),
            pl.BlockSpec((depth, own, 32, TILE), at_tails),
            pl.BlockSpec((1, own, 32, TILE), at_halo),
            pl.BlockSpec((own, 24, 128), lambda g: (0, 0, 0)),
            tiles(RATIO, SPAN, TILE),
            tiles(RATIO, 128, 128),
            tiles(8, 128),
            old(RATIO, 2, 128, 128),
            old(8, 128),
        ],
        out_specs=[
            pl.BlockSpec((n, own * RATIO, 128, 128), lambda g: (0, 0, 0, 0)),
            pl.BlockSpec(
                (2 * depth, own * RATIO, 128, 128), lambda g: (jnp.maximum(g - 1, 0), 0, 0, 0)
            ),
        ],
        out_shape=[
            jax.ShapeDtypeStruct((n, own * RATIO, 128, 128), BF16),
            jax.ShapeDtypeStruct((2 * n, own * RATIO, 128, 128), BF16),
        ],
        scratch_shapes=[
            pltpu.VMEM((own * RATIO, 128, 128), F32),
            pltpu.VMEM((2, STEP * RATIO, 2, 128, 128), F32),
        ],
        compiler_params=params(),
        cost_estimate=pl.CostEstimate(flops=3 * 10**9, bytes_accessed=8 << 20, transcendentals=10**6),
        name="head_chain",
    )(req, vp, kp, kp, par, sol, ft, rows, gs, rows)


def choose_kernel(req, rep, fin, ends, kt, out, counts):
    own, heads = kt.shape[1], ends.shape[1]
    base = heads * 128
    out[...] = jnp.zeros_like(out)
    for i in range(counts.shape[0]):
        counts[i] = 0
    end = jnp.int32(-1)
    for j in range(req.shape[1]):
        end = end + req[0, j]
        where = rep[0, j]
        place = counts[where]
        done = fin[0, j] > 0
        counts[where] = place + jnp.where(done, 1, 0)
        slot = where * CAP + jnp.minimum(place, CAP - 1)

        @pl.when(done)
        def take():
            for v in range(heads):
                out[slot, v * 128 : (v + 1) * 128] = ends[end, v]
            for h in range(own):
                lines = kt[end >> 1, h]
                lines = jnp.where((end & 1) > 0, lines[16:].astype(F32), lines[:16].astype(F32))
                out[slot, base + h * 16 : base + h * 16 + 16] = lines.astype(BF16)

    for i in range(counts.shape[0]):
        number = jnp.full((16, 128), counts[i], jnp.int32).astype(F32).astype(BF16)
        for c in range(CAP):
            out[i * CAP + c, base + own * 16 :] = number


def choose(req, rep, fin, ends, kp, replicas):
    n, own = kp.shape[:2]
    smem = pl.BlockSpec(memory_space=pltpu.SMEM)
    lines = own * RATIO * 128 + own * 16 + 16
    return pl.pallas_call(
        choose_kernel,
        grid=(1,),
        in_specs=[
            smem,
            smem,
            smem,
            pl.BlockSpec(ends.shape, lambda g: (0, 0, 0, 0)),
            pl.BlockSpec((n, own, 32, TILE), lambda g: (0, 0, 4, 0)),
        ],
        out_specs=pl.BlockSpec((replicas * CAP, lines, 128), lambda g: (0, 0, 0)),
        out_shape=jax.ShapeDtypeStruct((replicas * CAP, lines, 128), BF16),
        scratch_shapes=[pltpu.SMEM((replicas,), jnp.int32)],
        compiler_params=params(),
        cost_estimate=pl.CostEstimate(flops=10**6, bytes_accessed=4 << 20, transcendentals=0),
        name="choose",
    )(req, rep, fin, ends, kp)


def token_out_kernel(req, me, sin, wk, wv, sc, ft, qs, rows, gate, gain, out):
    stay0 = jnp.where(is_fresh(req, me[0] * 2), 0.0, 1.0)
    stay1 = jnp.where(is_fresh(req, me[0] * 2 + 1), 0.0, 1.0)
    lane = iota((DV, TILE), 1)
    early = lane < SPAN
    sides = halves((SPAN, TILE))
    units = [(t, r) for t in range(qs.shape[0]) for r in range(RATIO)]
    both = [jnp.concatenate([wk[t * RATIO + r], qs[t]], axis=1) for t, r in units]
    enter = [sin[t * RATIO + r].astype(F32) * stay0 for t, r in units]
    first = [dot(e.astype(BF16), b) for e, b in zip(enter, both)]
    wide = [wv[t * RATIO + r].astype(F32) for t, r in units]
    new0 = [jnp.where(early, w - f[:, :TILE], 0.0) for w, f in zip(wide, first)]
    middle = [
        (rows[t, r : r + 1] * e + dot(x.astype(BF16), ft[t * RATIO + r])) * stay1
        for (t, r), e, x in zip(units, enter, new0)
    ]
    second = [dot(m.astype(BF16), b) for m, b in zip(middle, both)]
    new = [
        jnp.where(early, x, w - s[:, :TILE]).astype(BF16) for x, w, s in zip(new0, wide, second)
    ]
    for at, (t, r) in enumerate(units):
        core = rows[t, 2 + r : 3 + r] * jnp.where(early, first[at][:, TILE:], second[at][:, TILE:])
        core = (core + dot(new[at], diagonal(sc[at], sides))).astype(BF16).astype(F32)
        inverse_rms = lax.rsqrt(jnp.mean(core * core, axis=0, keepdims=True) + EPSILON)
        z = gate[t, r * DV : (r + 1) * DV].astype(F32)
        result = core * inverse_rms * gain[...] * (z / (1.0 + jnp.exp(-z)))
        out[t, r * DV : (r + 1) * DV] = result.astype(BF16)


def token_out(req, me, sin, wk, wv, sc, ft, qs, rows, gate, gain):
    heads = qs.shape[0]
    smem = pl.BlockSpec(memory_space=pltpu.SMEM)

    def tiles(count, *rest):
        return pl.BlockSpec((count,) + rest, lambda g: (g,) + (0,) * len(rest))

    return pl.pallas_call(
        token_out_kernel,
        grid=(heads // STEP,),
        in_specs=[smem, smem]
        + [tiles(STEP * RATIO, 128, 128)] * 3
        + [tiles(STEP * RATIO, SPAN, TILE), tiles(STEP * RATIO, 128, 128)]
        + [
            tiles(STEP, 128, 128),
            tiles(STEP, 8, 128),
            tiles(STEP, 256, TILE),
            pl.BlockSpec((128, 128), lambda g: (0, 0)),
        ],
        out_specs=tiles(STEP, 256, TILE),
        out_shape=jax.ShapeDtypeStruct((heads, 256, TILE), BF16),
        compiler_params=params(),
        cost_estimate=pl.CostEstimate(flops=10**9, bytes_accessed=8 << 20, transcendentals=10**6),
        name="token_out",
    )(req, me, sin, wk, wv, sc, ft, qs, rows, gate, gain)


def land_kernel(count, got, states, tails):
    slot = pl.program_id(0)
    heads = states.shape[1]
    start = jnp.int32(0)
    source = jnp.int32(-1)
    for p in range(got.shape[0] // CAP):
        number = count[p]
        inside = (slot >= start) & (slot < start + number)
        source = jnp.where(inside, p * CAP + (slot - start), source)
        start = start + number

    @pl.when(source >= 0)
    def take():
        for v in range(heads):
            block = got[source, v * 128 : (v + 1) * 128].astype(F32)
            states[0, v] = jnp.transpose(block)
        for h in range(tails.shape[1]):
            tails[0, h] = got[source, heads * 128 + h * 16 : heads * 128 + h * 16 + 16]

    @pl.when(source < 0)
    def clear():
        states[...] = jnp.zeros_like(states)
        tails[...] = jnp.zeros_like(tails)


def land(count, got, heads, own):
    slots, lines = got.shape[:2]
    return pl.pallas_call(
        land_kernel,
        grid=(slots,),
        in_specs=[
            pl.BlockSpec(memory_space=pltpu.SMEM),
            pl.BlockSpec((slots, lines, 128), lambda g: (0, 0, 0)),
        ],
        out_specs=[
            pl.BlockSpec((1, heads, 128, 128), lambda g: (g, 0, 0, 0)),
            pl.BlockSpec((1, own, 16, 128), lambda g: (g, 0, 0, 0)),
        ],
        out_shape=[
            jax.ShapeDtypeStruct((slots, heads, 128, 128), F32),
            jax.ShapeDtypeStruct((slots, own, 16, 128), BF16),
        ],
        compiler_params=params(),
        cost_estimate=pl.CostEstimate(flops=10**6, bytes_accessed=4 << 20, transcendentals=0),
        name="land",
    )(count, got)


def body(
    mixed,
    decay_in,
    beta_in,
    gate_z,
    conv_weight,
    a_log,
    dt_bias,
    norm_gain,
    req_blocks,
    replica_of,
    finished,
):
    n = lax.axis_size("seq")
    replicas = lax.axis_size("rep")
    heads = mixed.shape[1]
    own = heads // n
    me = lax.axis_index("seq").astype(jnp.int32).reshape(1)
    kpack, vpack, halo, par = pack(mixed[0], decay_in[0], beta_in[0], conv_weight, a_log, dt_bias)
    halo = lax.ppermute(halo, "seq", [(i, i + 1) for i in range(n - 1)])
    par_all = lax.all_gather(par, "seq", axis=0, tiled=True)
    kpack, vpack, par_all = lax.optimization_barrier((kpack, vpack, par_all))
    kp = lax.all_to_all(kpack.reshape(n, own, KROWS, TILE), "seq", 0, 0, tiled=True)
    vp = lax.all_to_all(vpack.reshape(n, own, 256, TILE), "seq", 0, 0, tiled=True)
    wk, wv, sc, ft, qs, rows = token_prep(
        req_blocks, me, mixed[0], decay_in[0], beta_in[0], halo, par_all
    )
    kp, rows = lax.optimization_barrier((kp, rows))
    hsol, hft, hgs, hrows = head_prep(req_blocks, kp, par)
    sin, ends = head_chain(req_blocks, vp, kp, par, hsol, hft, hgs, hrows)
    sin = lax.all_to_all(sin, "seq", 0, 0, tiled=True)
    send = choose(req_blocks, replica_of, finished, ends, kp, replicas)
    lines = send.shape[1]
    got = lax.all_to_all(send.reshape(replicas, CAP, lines, 128), "rep", 0, 0, tiled=True)
    count = got[:, 0, lines - 1, 0].astype(jnp.int32)
    states, tails = land(count, got.reshape(replicas * CAP, lines, 128), own * RATIO, own)
    tails = tails.reshape(replicas * CAP, own, 4, 512)[:, :, : KERNEL - 1].transpose(0, 2, 1, 3)
    gain = jnp.broadcast_to(norm_gain[:, None], (DV, TILE))
    out = token_out(
        req_blocks,
        me,
        sin.reshape(heads * RATIO, 128, 128),
        wk,
        wv,
        sc,
        ft,
        qs,
        rows,
        gate_z[0],
        gain,
    )
    return (out[None], states[None], tails[None])


def solution(mesh):
    placed = (
        P("rep", None, None, "seq"),
        P("rep", None, None, "seq"),
        P("rep", None, None, "seq"),
        P("rep", None, None, "seq"),
        P(None, "seq", None),
        P("seq"),
        P("seq"),
        P(),
        P("rep", None),
        P("rep", None),
        P("rep", None),
    )
    return jax.shard_map(
        body,
        mesh=mesh,
        in_specs=placed,
        out_specs=(
            P("rep", None, None, "seq"),
            P("rep", None, "seq", None, None),
            P("rep", None, None, "seq", None),
        ),
        check_vma=False,
    )
```

```python
import jax
import jax.numpy as jnp
from jax import lax
from jax.experimental import pallas as pl
from jax.experimental.pallas import tpu as pltpu
from jax.sharding import PartitionSpec as P

DK = 128
DV = 128
KERNEL = 4
SPAN = 64
CAP = 2
RATIO = 2
TILE = 2 * SPAN
KROWS = 192
STEP = 4
WIDE = 8
EPSILON = 1e-06
F32 = jnp.float32
BF16 = jnp.bfloat16
VMEM_LIMIT = 56 * 1024 * 1024


def params(**kwargs):
    return pltpu.CompilerParams(vmem_limit_bytes=VMEM_LIMIT, **kwargs)


def iota(shape, dim):
    return lax.broadcasted_iota(jnp.int32, shape, dim)


def dot(left, right):
    return jnp.dot(left, right, preferred_element_type=F32)


def split(wide):
    high = wide.astype(BF16)
    return high, (wide - high.astype(F32)).astype(BF16)


def halves(shape):
    first = iota(shape, len(shape) - 1) < SPAN
    return jnp.where(first, 1.0, 0.0).astype(BF16), jnp.where(first, 0.0, 1.0).astype(BF16)


def diagonal(packed, masks):
    return jnp.concatenate([packed * masks[0], packed * masks[1]], axis=0)


def dot3(left, right, masks):
    high = diagonal(right[0], masks)
    top = jnp.concatenate([high, diagonal(right[1], masks)], axis=1)
    low = jnp.concatenate([high, jnp.zeros_like(high)], axis=1)
    out = dot(jnp.concatenate(left, axis=1), jnp.concatenate([top, low], axis=0))
    return out[:, :TILE] + out[:, TILE:]


def parameter_lines(h, cw, alog, dtb):
    taps = cw[:, h].astype(F32)
    rows = [taps[tap : tap + 1, cg * 128 : (cg + 1) * 128] for tap in range(KERNEL) for cg in range(4)]
    rest = jnp.concatenate(
        [jnp.full((1, 128), ref[h * RATIO + r], F32) for ref in (alog, dtb) for r in range(RATIO)], axis=0
    )
    parts = []
    for _ in range(3):
        part = rest.astype(BF16).astype(F32)
        rest = rest - part
        parts.append(part)
    return jnp.concatenate(rows + parts + [jnp.zeros((4, 128), F32)], axis=0).astype(BF16)


def parameters(lines):
    wide = lines.astype(F32)
    rest = wide[16:20] + wide[20:24] + wide[24:28]
    return wide[:16], rest[:RATIO], rest[RATIO:]


def pack_kernel(mixed, dec, beta, cw, alog, dtb, kout, vout, hout, pout):
    row, tok = iota((32, TILE), 0), iota((32, TILE), 1)
    place = row & 15
    picks = []
    for cg in range(4):
        hit = (place < 12) & ((place & 3) == cg) & (tok == (row >> 4) * SPAN + 61 + (place >> 2))
        picks.append(jnp.where(hit, 1.0, 0.0).astype(BF16))
    own = pout.shape[0]
    lines = [parameter_lines(h, cw, alog, dtb) for h in range(own)]
    for t in range(mixed.shape[0]):
        kout[t, :DK] = mixed[t, DK : 2 * DK]
        vout[t] = mixed[t, 2 * DK :]
        tails = jnp.zeros((32, TILE), F32)
        for cg in range(4):
            tails = tails + lax.dot_general(
                picks[cg],
                mixed[t, cg * 128 : (cg + 1) * 128],
                (((1,), (1,)), ((), ())),
                preferred_element_type=F32,
            )
        d, b = dec[t].astype(F32), beta[t].astype(F32)
        for r in range(RATIO):
            tails = jnp.where(row == 12 + r, d[r : r + 1], tails)
            tails = jnp.where(row == 14 + r, b[r : r + 1], tails)
        tails = tails.astype(BF16)
        kout[t, DK : DK + 32] = tails
        hout[t] = tails[16:]
        kout[t, DK + 32 :] = lines[t % own]

    @pl.when(pl.program_id(0) == 0)
    def first():
        for h in range(own):
            pout[h] = lines[h]


def pack(mixed, dec, beta, cw, alog, dtb):
    heads = mixed.shape[0]
    own = cw.shape[1]
    smem = pl.BlockSpec(memory_space=pltpu.SMEM)
    return pl.pallas_call(
        pack_kernel,
        grid=(heads // STEP,),
        in_specs=[
            pl.BlockSpec((STEP, 512, TILE), lambda g: (g, 0, 0)),
            pl.BlockSpec((STEP, RATIO, TILE), lambda g: (g, 0, 0)),
            pl.BlockSpec((STEP, RATIO, TILE), lambda g: (g, 0, 0)),
            pl.BlockSpec((KERNEL, own, 512), lambda g: (0, 0, 0)),
            smem,
            smem,
        ],
        out_specs=[
            pl.BlockSpec((STEP, KROWS, TILE), lambda g: (g, 0, 0)),
            pl.BlockSpec((STEP, 256, TILE), lambda g: (g, 0, 0)),
            pl.BlockSpec((STEP, 16, TILE), lambda g: (g, 0, 0)),
            pl.BlockSpec((own, 32, 128), lambda g: (0, 0, 0)),
        ],
        out_shape=[
            jax.ShapeDtypeStruct((heads, KROWS, TILE), BF16),
            jax.ShapeDtypeStruct((heads, 256, TILE), BF16),
            jax.ShapeDtypeStruct((heads, 16, TILE), BF16),
            jax.ShapeDtypeStruct((own, 32, 128), BF16),
        ],
        compiler_params=params(),
        cost_estimate=pl.CostEstimate(flops=10**8, bytes_accessed=4 << 20, transcendentals=0),
        name="pack",
    )(mixed, dec, beta, cw, alog, dtb)


def is_fresh(req, block):
    start = jnp.int32(0)
    fresh = jnp.bool_(False)
    for j in range(req.shape[1]):
        fresh = fresh | (start == block)
        start = start + req[0, j]
    return fresh


def tap_tables():
    row, part = iota((16, 4 * 128), 0), iota((16, 4 * 128), 1) >> 7
    hits = [((row & 3) == cg) & ((row >> 2) == part) for cg in range(4)]
    return [jnp.where(hit, 1.0, 0.0).astype(BF16) for hit in hits]


def halo_tables():
    row, lane = iota((48, 128), 0), iota((48, 128), 1)
    token = (row >> 2) % 3
    hits = [((row & 3) == cg) & (row < 36) & (token == lane) for cg in range(4)]
    return [jnp.where(hit, 1.0, 0.0).astype(BF16) for hit in hits]


def turned_dot(rows, table):
    return lax.dot_general(rows, table, (((0,), (0,)), ((), ())), preferred_element_type=F32)


def spread_taps(par, table):
    both = turned_dot(par, table)
    return [both[:, tap * 128 : (tap + 1) * 128] for tap in range(KERNEL)]


def halo_terms(halo, par, not_fresh0):
    x = [halo[4 * k : 4 * k + 4].astype(F32) * not_fresh0 for k in range(3)]
    w = [par[4 * k : 4 * k + 4] for k in range(3)]
    terms = jnp.concatenate(
        [w[0] * x[0] + w[1] * x[1] + w[2] * x[2], w[0] * x[1] + w[1] * x[2], w[0] * x[2]], axis=0
    )
    high = terms.astype(BF16).astype(F32)
    middle = (terms - high).astype(BF16).astype(F32)
    parts = [high, middle, terms - high - middle, jnp.zeros((12, 128), F32)]
    return jnp.concatenate(parts, axis=0).astype(BF16)


def convolve(raw, terms, table, taps, masks):
    cur = raw.astype(F32)
    total = taps[KERNEL - 1] * cur + turned_dot(terms, table)
    for back in range(1, KERNEL):
        moved = pltpu.roll(cur, back, 1) * masks[back - 1]
        total = total + taps[KERNEL - 1 - back] * moved
    return (total / (1.0 + jnp.exp(-total))).astype(BF16)


def conv_masks(fresh1):
    lane = iota((1, TILE), 1)
    masks = []
    for back in range(1, KERNEL):
        cut = (lane >= SPAN) & (lane < SPAN + back) & fresh1
        masks.append(jnp.where((lane < back) | cut, 0.0, 1.0))
    return masks


def row_prep(dec, beta, alog, dtb):
    lane = iota(dec.shape, 1)
    x = dec + dtb
    decay = -jnp.exp(alog) * (jnp.maximum(x, 0.0) + jnp.log1p(jnp.exp(-jnp.abs(x))))
    cum = decay
    for shift in (1, 2, 4, 8, 16, 32):
        cum = cum + jnp.where((lane & (SPAN - 1)) >= shift, pltpu.roll(cum, shift, 1), 0.0)
    strength = 1.0 / (1.0 + jnp.exp(-beta))
    grown = jnp.exp(cum)
    close0, close1 = cum[:, SPAN - 1 : SPAN], cum[:, TILE - 1 :]
    fade = jnp.exp(jnp.where(lane < SPAN, close0, close1) - cum)
    keep0 = jnp.exp(jnp.broadcast_to(close0, cum.shape))
    keep1 = jnp.exp(jnp.broadcast_to(close1, cum.shape))
    return cum, strength, grown, fade, keep0, keep1


def unit_inverses(systems):
    row, col = iota((SPAN, TILE), 0), iota((SPAN, TILE), 1) & (SPAN - 1)
    near = (row >> 4) == (col >> 4)
    eye = jnp.where(row == col, 1.0, 0.0)
    masks = halves((SPAN, TILE))
    power = [jnp.where(near, -a, 0.0) for a in systems]
    rest = [split(jnp.where(near, 0.0, a)) for a in systems]
    total = [eye + p for p in power]
    parts = [split(p) for p in power]
    power = [dot3(p, p, masks) for p in parts]
    for _ in range(2):
        parts = [split(p) for p in power]
        stacks = [
            [jnp.concatenate(pair, axis=0) for pair in zip(split(t), p)]
            for t, p in zip(total, parts)
        ]
        both = [dot3(s, p, masks) for s, p in zip(stacks, parts)]
        total = [t + b[:SPAN] for t, b in zip(total, both)]
        power = [b[SPAN:] for b in both]
    total = [t + dot3(split(t), split(p), masks) for t, p in zip(total, power)]
    parts = [split(t) for t in total]
    cross = [split(dot3(t, r, masks)) for t, r in zip(parts, rest)]
    total = [t - dot3(x, p, masks) for t, x, p in zip(total, cross, parts)]
    cross = [dot3(x, x, masks) for x in cross]
    return [t + dot3(split(x), split(t), masks) for t, x in zip(total, cross)]


def unit_keys(convolved):
    wide = convolved.astype(F32)
    return (wide * lax.rsqrt(jnp.sum(wide * wide, axis=0, keepdims=True) + EPSILON)).astype(BF16)


def solve_tiles(keys, queries, prep):
    cum, strength, grown, fade, keep0, keep1 = prep
    row, lane = iota((SPAN, TILE), 0), iota((SPAN, TILE), 1)
    early = lane < SPAN
    seen = (lane & (SPAN - 1)) >= row
    later = (lane & (SPAN - 1)) > row
    columns = jnp.transpose(jnp.concatenate([cum, fade], axis=0))
    count = cum.shape[0]

    def beside(tall):
        return jnp.where(early, tall[:SPAN], tall[SPAN:])

    systems, faded, scores = [], [], []
    for t, k in enumerate(keys):
        turned = jnp.transpose(k.astype(F32))
        if queries is None:
            gram = beside(dot(turned.astype(BF16), k))
        else:
            prod = dot(turned.astype(BF16), jnp.concatenate([k, queries[t]], axis=1))
            gram, touch = beside(prod[:, :TILE]), beside(prod[:, TILE:])
        for r in range(RATIO):
            at = t * RATIO + r
            diff = cum[at : at + 1] - beside(columns[:, at : at + 1])
            ratio = jnp.where(seen, jnp.exp(jnp.where(seen, diff, 0.0)), 0.0)
            systems.append(jnp.where(later, strength[at : at + 1] * gram * ratio, 0.0))
            if queries is not None:
                scores.append((touch * ratio).astype(BF16))
            faded.append((turned * columns[:, count + at : count + at + 1]).astype(BF16))
    solved = [s.astype(BF16) for s in unit_inverses(systems)]
    return solved, faded, scores


def token_prep_kernel(req, me, mixed, dec, beta, halo, par_lines, wk, wv, sc, ft, qo, rows):
    fresh0, fresh1 = is_fresh(req, me[0] * 2), is_fresh(req, me[0] * 2 + 1)
    not_fresh0 = jnp.where(fresh0, 0.0, 1.0)
    masks = conv_masks(fresh1)
    tap_tab, halo_tab = tap_tables(), halo_tables()
    tiles = range(mixed.shape[0])
    par = [parameters(par_lines[t]) for t in tiles]

    def gather(pick):
        return jnp.concatenate([pick(t) for t in tiles], axis=0)

    prep = row_prep(
        gather(lambda t: dec[t].astype(F32)),
        gather(lambda t: beta[t].astype(F32)),
        jnp.concatenate([p[1] for p in par], axis=0),
        jnp.concatenate([p[2] for p in par], axis=0),
    )
    cum, strength, grown, fade, keep0, keep1 = prep
    keys, queries, values = [], [], []
    for t in tiles:
        terms = halo_terms(halo[t], par[t][0], not_fresh0)
        lines = par_lines[t, :16]
        q, k, v0, v1 = [
            convolve(
                mixed[t, c * 128 : (c + 1) * 128],
                terms,
                halo_tab[c],
                spread_taps(lines, tap_tab[c]),
                masks,
            )
            for c in range(4)
        ]
        keys.append(unit_keys(k))
        queries.append(q)
        values.append((v0, v1))
        qo[t] = q
        rows[t] = jnp.concatenate(
            [keep0[2 * t : 2 * t + 2], grown[2 * t : 2 * t + 2], keep1[2 * t : 2 * t + 2], strength[2 * t : 2 * t + 2]],
            axis=0,
        )
    solved, faded, scores = solve_tiles(keys, queries, prep)
    sides = halves((SPAN, TILE))
    for t in tiles:
        for r in range(RATIO):
            at = t * RATIO + r
            s, lift = strength[at : at + 1], strength[at : at + 1] * grown[at : at + 1]
            stacked = jnp.concatenate(
                [
                    (lift * keys[t].astype(F32)).astype(BF16),
                    (s * values[t][r].astype(F32)).astype(BF16),
                ],
                axis=0,
            )
            out = dot(stacked, diagonal(solved[at], sides)).astype(BF16)
            wk[at] = out[:DK]
            wv[at] = out[DK:]
            sc[at] = scores[at]
            ft[at] = faded[at]


def token_prep(req, me, mixed, dec, beta, halo, par):
    heads = mixed.shape[0]
    smem = pl.BlockSpec(memory_space=pltpu.SMEM)

    def tiles(count, *rest):
        return pl.BlockSpec((count,) + rest, lambda g: (g,) + (0,) * len(rest))

    square = jax.ShapeDtypeStruct((heads * RATIO, 128, 128), BF16)
    return pl.pallas_call(
        token_prep_kernel,
        grid=(heads // WIDE,),
        in_specs=[
            smem,
            smem,
            tiles(WIDE, 512, TILE),
            tiles(WIDE, RATIO, TILE),
            tiles(WIDE, RATIO, TILE),
            tiles(WIDE, 16, TILE),
            pl.BlockSpec((WIDE, 32, 128), lambda g: (g, 5, 0)),
        ],
        out_specs=[tiles(WIDE * RATIO, 128, 128)] * 2
        + [tiles(WIDE * RATIO, SPAN, TILE), tiles(WIDE * RATIO, 128, 128)]
        + [tiles(WIDE, 128, 128), tiles(WIDE, 8, 128)],
        out_shape=[square] * 2
        + [
            jax.ShapeDtypeStruct((heads * RATIO, SPAN, TILE), BF16),
            square,
            jax.ShapeDtypeStruct((heads, 128, 128), BF16),
            jax.ShapeDtypeStruct((heads, 8, 128), F32),
        ],
        compiler_params=params(),
        cost_estimate=pl.CostEstimate(flops=10**10, bytes_accessed=8 << 20, transcendentals=10**6),
        name="token_prep",
    )(req, me, mixed, dec, beta, halo, par)


def head_prep_kernel(req, kp, before, par_lines, sol, ft, gs, rows):
    step = pl.program_id(0)
    depth, own = kp.shape[0], kp.shape[1]
    tap_tab, halo_tab = tap_tables(), halo_tables()
    order = [(d, h) for d in range(depth) for h in range(own)]
    par = [parameters(par_lines[h]) for h in range(own)]

    small = [kp[d, h, DK : DK + 16].astype(F32) for d, h in order]
    prep = row_prep(
        jnp.concatenate([s[12:14] for s in small], axis=0),
        jnp.concatenate([s[14:16] for s in small], axis=0),
        jnp.concatenate([par[h][1] for d, h in order], axis=0),
        jnp.concatenate([par[h][2] for d, h in order], axis=0),
    )
    cum, strength, grown, fade, keep0, keep1 = prep
    keys = []
    taps = [spread_taps(par_lines[h, :16], tap_tab[1]) for h in range(own)]
    for d in range(depth):
        block = (step * depth + d) * 2
        not_fresh0 = jnp.where(is_fresh(req, block), 0.0, 1.0)
        masks = conv_masks(is_fresh(req, block + 1))
        for h in range(own):
            halo = kp[d - 1, h, DK + 16 : DK + 32] if d else before[0, h, 16:]
            terms = halo_terms(halo, par[h][0], not_fresh0)
            keys.append(unit_keys(convolve(kp[d, h, :DK], terms, halo_tab[1], taps[h], masks)))
    solved, faded, unused = solve_tiles(keys, None, prep)
    sides, wide_sides = halves((SPAN, TILE)), halves((DK, TILE))
    for t, (d, h) in enumerate(order):
        rows[d, h] = jnp.concatenate(
            [keep0[2 * t : 2 * t + 2], keep1[2 * t : 2 * t + 2], strength[2 * t : 2 * t + 2], strength[2 * t : 2 * t + 2]],
            axis=0,
        )
        for r in range(RATIO):
            at = t * RATIO + r
            lift = strength[at : at + 1] * grown[at : at + 1]
            scaled = (lift * keys[t].astype(F32)).astype(BF16)
            wide = dot(scaled, diagonal(solved[at], sides)).astype(BF16)
            drop = dot(diagonal(wide, wide_sides), faded[at]).astype(BF16)
            gs[d, h, r, 0] = drop[:DK]
            gs[d, h, r, 1] = drop[DK:]
            sol[d, h, r] = solved[at]
            ft[d, h, r] = faded[at]


def head_prep(req, kp, par):
    n, own = kp.shape[:2]
    depth = WIDE // own
    smem = pl.BlockSpec(memory_space=pltpu.SMEM)

    def tiles(*rest):
        return pl.BlockSpec((depth, own) + rest, lambda g: (g, 0) + (0,) * len(rest))

    square = jax.ShapeDtypeStruct((n, own, RATIO, 128, 128), BF16)
    return pl.pallas_call(
        head_prep_kernel,
        grid=(n // depth,),
        in_specs=[
            smem,
            tiles(KROWS, TILE),
            pl.BlockSpec((1, own, 32, TILE), lambda g: (jnp.maximum(g * depth - 1, 0), 0, 4, 0)),
            pl.BlockSpec((own, 32, 128), lambda g: (0, 0, 0)),
        ],
        out_specs=[
            tiles(RATIO, SPAN, TILE),
            tiles(RATIO, 128, 128),
            tiles(RATIO, 2, 128, 128),
            tiles(8, 128),
        ],
        out_shape=[
            jax.ShapeDtypeStruct((n, own, RATIO, SPAN, TILE), BF16),
            square,
            jax.ShapeDtypeStruct((n, own, RATIO, 2, 128, 128), BF16),
            jax.ShapeDtypeStruct((n, own, 8, 128), F32),
        ],
        compiler_params=params(),
        cost_estimate=pl.CostEstimate(flops=10**10, bytes_accessed=6 << 20, transcendentals=10**6),
        name="head_prep",
    )(req, kp, kp, par)


def head_chain_kernel(req, vp, kt, before, par_lines, sol, ft, gs, rows, sin, ends, state):
    step = pl.program_id(0)
    depth, own = vp.shape[0], vp.shape[1]
    n = sin.shape[0]
    par = [parameters(par_lines[h])[0] for h in range(own)]
    tap_tab, halo_tab = tap_tables(), halo_tables()
    sides, wide_sides = halves((SPAN, TILE)), halves((DV, TILE))
    heads = [(h, r) for h in range(own) for r in range(RATIO)]
    taps = [spread_taps(par_lines[h, :16], tap_tab[2 + r]) for h, r in heads]
    current = [state[v] for v in range(len(heads))]
    for d in range(depth):
        tile = step * depth + d
        fresh = [is_fresh(req, tile * 2), is_fresh(req, tile * 2 + 1)]
        not_fresh0 = jnp.where(fresh[0], 0.0, 1.0)
        masks = conv_masks(fresh[1])
        halos = [kt[d - 1, h, 16:] if d else before[0, h, 16:] for h in range(own)]
        terms = [halo_terms(halos[h], par[h], not_fresh0) for h in range(own)]
        gains = []
        for v, (h, r) in enumerate(heads):
            raw = vp[d, h, r * DV : (r + 1) * DV]
            value = convolve(raw, terms[h], halo_tab[2 + r], taps[v], masks)
            scaled = (rows[d, h, 4 + r : 5 + r] * value.astype(F32)).astype(BF16)
            wide = dot(scaled, diagonal(sol[d, h, r], sides)).astype(BF16)
            gains.append(dot(diagonal(wide, wide_sides), ft[d, h, r]))
        for half in range(2):
            for v, (h, r) in enumerate(heads):
                now = jnp.where(fresh[half], 0.0, current[v])
                keep = rows[d, h, 2 * half + r : 2 * half + r + 1]
                gain = gains[v][half * DV : (half + 1) * DV]
                current[v] = keep * now + (gain - dot(now.astype(BF16), gs[d, h, r, half]))
                ends[d * 2 + half, v] = current[v].astype(BF16)
        onward = lax.rem(tile + 1, n)
        for v in range(len(heads)):
            sin[onward, v] = current[v].astype(BF16)
    for v in range(len(heads)):
        state[v] = current[v]


def head_chain(req, vp, kp, par, sol, ft, gs, rows):
    n, own = vp.shape[:2]
    depth = WIDE // own
    smem = pl.BlockSpec(memory_space=pltpu.SMEM)

    def tiles(*rest):
        return pl.BlockSpec((depth, own) + rest, lambda g: (g, 0) + (0,) * len(rest))

    return pl.pallas_call(
        head_chain_kernel,
        grid=(n // depth,),
        in_specs=[
            smem,
            tiles(256, TILE),
            pl.BlockSpec((depth, own, 32, TILE), lambda g: (g, 0, 4, 0)),
            pl.BlockSpec((1, own, 32, TILE), lambda g: (jnp.maximum(g * depth - 1, 0), 0, 4, 0)),
            pl.BlockSpec((own, 32, 128), lambda g: (0, 0, 0)),
            tiles(RATIO, SPAN, TILE),
            tiles(RATIO, 128, 128),
            tiles(RATIO, 2, 128, 128),
            tiles(8, 128),
        ],
        out_specs=[
            pl.BlockSpec((n, own * RATIO, 128, 128), lambda g: (0, 0, 0, 0)),
            pl.BlockSpec((2 * depth, own * RATIO, 128, 128), lambda g: (g, 0, 0, 0)),
        ],
        out_shape=[
            jax.ShapeDtypeStruct((n, own * RATIO, 128, 128), BF16),
            jax.ShapeDtypeStruct((2 * n, own * RATIO, 128, 128), BF16),
        ],
        scratch_shapes=[pltpu.VMEM((own * RATIO, 128, 128), F32)],
        compiler_params=params(),
        cost_estimate=pl.CostEstimate(flops=3 * 10**9, bytes_accessed=8 << 20, transcendentals=10**6),
        name="head_chain",
    )(req, vp, kp, kp, par, sol, ft, gs, rows)


def choose_kernel(req, rep, fin, me, ends, kt, *refs):
    outs, counts = refs[:-1], refs[-1]
    own, heads = kt.shape[1], ends.shape[1]
    base = heads * 128
    for i, out in enumerate(outs):
        out[...] = jnp.zeros_like(out)
        counts[i] = 0
    end = jnp.int32(-1)
    for j in range(req.shape[1]):
        end = end + req[0, j]
        where = rep[0, j] ^ me[0]
        place = jnp.minimum(counts[where], CAP - 1)
        done = fin[0, j] > 0
        counts[where] = counts[where] + jnp.where(done, 1, 0)
        for i, out in enumerate(outs):

            @pl.when(done & (where == i))
            def take():
                for v in range(heads):
                    out[place, v * 128 : (v + 1) * 128] = ends[end, v]
                for h in range(own):
                    lines = kt[end >> 1, h].astype(F32)
                    lines = jnp.where((end & 1) > 0, lines[16:], lines[:16]).astype(BF16)
                    out[place, base + h * 16 : base + h * 16 + 16] = lines

    for i, out in enumerate(outs):
        number = jnp.full((16, 128), counts[i], jnp.int32).astype(F32).astype(BF16)
        for c in range(CAP):
            out[c, base + own * 16 :] = number


def choose(req, rep, fin, me, ends, kp, replicas):
    n, own = kp.shape[:2]
    smem = pl.BlockSpec(memory_space=pltpu.SMEM)
    lines = own * RATIO * 128 + own * 16 + 16
    return pl.pallas_call(
        choose_kernel,
        grid=(1,),
        in_specs=[
            smem,
            smem,
            smem,
            smem,
            pl.BlockSpec(ends.shape, lambda g: (0, 0, 0, 0)),
            pl.BlockSpec((n, own, 32, TILE), lambda g: (0, 0, 4, 0)),
        ],
        out_specs=[pl.BlockSpec((CAP, lines, 128), lambda g: (0, 0, 0))] * replicas,
        out_shape=[jax.ShapeDtypeStruct((CAP, lines, 128), BF16)] * replicas,
        scratch_shapes=[pltpu.SMEM((replicas,), jnp.int32)],
        compiler_params=params(),
        cost_estimate=pl.CostEstimate(flops=10**6, bytes_accessed=4 << 20, transcendentals=0),
        name="choose",
    )(req, rep, fin, me, ends, kp)


def token_out_kernel(req, me, sin, wk, wv, sc, ft, qs, rows, gate, gain, out):
    stay0 = jnp.where(is_fresh(req, me[0] * 2), 0.0, 1.0)
    stay1 = jnp.where(is_fresh(req, me[0] * 2 + 1), 0.0, 1.0)
    lane = iota((DV, TILE), 1)
    early = lane < SPAN
    sides = halves((SPAN, TILE))
    units = [(t, r) for t in range(qs.shape[0]) for r in range(RATIO)]
    both = [jnp.concatenate([wk[t * RATIO + r], qs[t]], axis=1) for t, r in units]
    enter = [sin[t * RATIO + r].astype(F32) * stay0 for t, r in units]
    first = [dot(e.astype(BF16), b) for e, b in zip(enter, both)]
    wide = [wv[t * RATIO + r].astype(F32) for t, r in units]
    new0 = [jnp.where(early, w - f[:, :TILE], 0.0) for w, f in zip(wide, first)]
    middle = [
        (rows[t, r : r + 1] * e + dot(x.astype(BF16), ft[t * RATIO + r])) * stay1
        for (t, r), e, x in zip(units, enter, new0)
    ]
    second = [dot(m.astype(BF16), b) for m, b in zip(middle, both)]
    new = [
        jnp.where(early, x, w - s[:, :TILE]).astype(BF16) for x, w, s in zip(new0, wide, second)
    ]
    for at, (t, r) in enumerate(units):
        core = rows[t, 2 + r : 3 + r] * jnp.where(early, first[at][:, TILE:], second[at][:, TILE:])
        core = (core + dot(new[at], diagonal(sc[at], sides))).astype(BF16).astype(F32)
        inverse_rms = lax.rsqrt(jnp.mean(core * core, axis=0, keepdims=True) + EPSILON)
        z = gate[t, r * DV : (r + 1) * DV].astype(F32)
        result = core * inverse_rms * gain[...] * (z / (1.0 + jnp.exp(-z)))
        out[t, r * DV : (r + 1) * DV] = result.astype(BF16)


def token_out(req, me, sin, wk, wv, sc, ft, qs, rows, gate, gain):
    heads = qs.shape[0]
    smem = pl.BlockSpec(memory_space=pltpu.SMEM)

    def tiles(count, *rest):
        return pl.BlockSpec((count,) + rest, lambda g: (g,) + (0,) * len(rest))

    return pl.pallas_call(
        token_out_kernel,
        grid=(heads // STEP,),
        in_specs=[smem, smem]
        + [tiles(STEP * RATIO, 128, 128)] * 3
        + [tiles(STEP * RATIO, SPAN, TILE), tiles(STEP * RATIO, 128, 128)]
        + [
            tiles(STEP, 128, 128),
            tiles(STEP, 8, 128),
            tiles(STEP, 256, TILE),
            pl.BlockSpec((128, 128), lambda g: (0, 0)),
        ],
        out_specs=tiles(STEP, 256, TILE),
        out_shape=jax.ShapeDtypeStruct((heads, 256, TILE), BF16),
        compiler_params=params(),
        cost_estimate=pl.CostEstimate(flops=10**9, bytes_accessed=8 << 20, transcendentals=10**6),
        name="token_out",
    )(req, me, sin, wk, wv, sc, ft, qs, rows, gate, gain)


def land_kernel(me, *refs):
    got, (states, tails, counts) = refs[:-3], refs[-3:]
    slot = pl.program_id(0)
    heads, own = states.shape[1], tails.shape[1]
    base = heads * 128

    @pl.when(slot == 0)
    def first():
        for i, one in enumerate(got):
            number = jnp.max(one[0, base + own * 16 :].astype(F32))
            counts[i] = number.astype(jnp.int32)

    start = jnp.int32(0)
    source, place = jnp.int32(-1), jnp.int32(0)
    for p in range(len(got)):
        away = me[0] ^ p
        number = counts[away]
        inside = (slot >= start) & (slot < start + number)
        source = jnp.where(inside, away, source)
        place = jnp.where(inside, slot - start, place)
        start = start + number
    place = jnp.clip(place, 0, CAP - 1)
    for i, one in enumerate(got):

        @pl.when(source == i)
        def take():
            for v in range(heads):
                block = one[place, v * 128 : (v + 1) * 128].astype(F32)
                states[0, v] = jnp.transpose(block)
            for h in range(own):
                tails[0, h] = one[place, base + h * 16 : base + h * 16 + 16]

    @pl.when(source < 0)
    def clear():
        states[...] = jnp.zeros_like(states)
        tails[...] = jnp.zeros_like(tails)


def land(me, got, heads, own):
    lines = got[0].shape[1]
    slots = len(got) * CAP
    smem = pl.BlockSpec(memory_space=pltpu.SMEM)
    return pl.pallas_call(
        land_kernel,
        grid=(slots,),
        in_specs=[smem] + [pl.BlockSpec((CAP, lines, 128), lambda g: (0, 0, 0))] * len(got),
        out_specs=[
            pl.BlockSpec((1, heads, 128, 128), lambda g: (g, 0, 0, 0)),
            pl.BlockSpec((1, own, 16, 128), lambda g: (g, 0, 0, 0)),
        ],
        out_shape=[
            jax.ShapeDtypeStruct((slots, heads, 128, 128), F32),
            jax.ShapeDtypeStruct((slots, own, 16, 128), BF16),
        ],
        scratch_shapes=[pltpu.SMEM((len(got),), jnp.int32)],
        compiler_params=params(),
        cost_estimate=pl.CostEstimate(flops=10**6, bytes_accessed=4 << 20, transcendentals=0),
        name="land",
    )(me, *got)


def body(
    mixed,
    decay_in,
    beta_in,
    gate_z,
    conv_weight,
    a_log,
    dt_bias,
    norm_gain,
    req_blocks,
    replica_of,
    finished,
):
    n = lax.axis_size("seq")
    replicas = lax.axis_size("rep")
    heads = mixed.shape[1]
    own = heads // n
    me = lax.axis_index("seq").astype(jnp.int32).reshape(1)
    kpack, vpack, halo, par = pack(mixed[0], decay_in[0], beta_in[0], conv_weight, a_log, dt_bias)
    halo = lax.ppermute(halo, "seq", [(i, i + 1) for i in range(n - 1)])
    kp = lax.all_to_all(kpack.reshape(n, own, KROWS, TILE), "seq", 0, 0, tiled=True)
    vp = lax.all_to_all(vpack.reshape(n, own, 256, TILE), "seq", 0, 0, tiled=True)
    wk, wv, sc, ft, qs, rows = token_prep(
        req_blocks, me, mixed[0], decay_in[0], beta_in[0], halo, kp.reshape(heads, KROWS, TILE)
    )
    hsol, hft, hgs, hrows = head_prep(req_blocks, kp, par)
    hrows, rows = lax.optimization_barrier((hrows, rows))
    sin, ends = head_chain(req_blocks, vp, kp, par, hsol, hft, hgs, hrows)
    sin = lax.all_to_all(sin, "seq", 0, 0, tiled=True)
    my_rep = lax.axis_index("rep").astype(jnp.int32).reshape(1)
    send = choose(req_blocks, replica_of, finished, my_rep, ends, kp, replicas)
    got = [send[0]] + [
        lax.ppermute(send[k], "rep", [(i, i ^ k) for i in range(replicas)])
        for k in range(1, replicas)
    ]
    states, tails = land(my_rep, got, own * RATIO, own)
    tails = tails.reshape(replicas * CAP, own, 4, 512)[:, :, : KERNEL - 1].transpose(0, 2, 1, 3)
    gain = jnp.broadcast_to(norm_gain[:, None], (DV, TILE))
    out = token_out(
        req_blocks,
        me,
        sin.reshape(heads * RATIO, 128, 128),
        wk,
        wv,
        sc,
        ft,
        qs,
        rows,
        gate_z[0],
        gain,
    )
    return (out[None], states[None], tails[None])


def solution(mesh):
    placed = (
        P("rep", None, None, "seq"),
        P("rep", None, None, "seq"),
        P("rep", None, None, "seq"),
        P("rep", None, None, "seq"),
        P(None, "seq", None),
        P("seq"),
        P("seq"),
        P(),
        P("rep", None),
        P("rep", None),
        P("rep", None),
    )
    return jax.shard_map(
        body,
        mesh=mesh,
        in_specs=placed,
        out_specs=(
            P("rep", None, None, "seq"),
            P("rep", None, "seq", None, None),
            P("rep", None, None, "seq", None),
        ),
        check_vma=False,
    )
```

```python
import jax
import jax.numpy as jnp
from jax import lax
from jax.experimental import pallas as pl
from jax.experimental.pallas import tpu as pltpu
from jax.sharding import PartitionSpec as P

DK = 128
DV = 128
KERNEL = 4
SPAN = 64
CAP = 2
RATIO = 2
TILE = 2 * SPAN
KROWS = 160
VROWS = 288
STEP = 4
WIDE = 8
EPSILON = 1e-06
F32 = jnp.float32
BF16 = jnp.bfloat16
VMEM_LIMIT = 56 * 1024 * 1024


def params(**kwargs):
    return pltpu.CompilerParams(vmem_limit_bytes=VMEM_LIMIT, **kwargs)


def iota(shape, dim):
    return lax.broadcasted_iota(jnp.int32, shape, dim)


def dot(left, right):
    return jnp.dot(left, right, preferred_element_type=F32)


def split(wide):
    high = wide.astype(BF16)
    return high, (wide - high.astype(F32)).astype(BF16)


def halves(shape):
    first = iota(shape, len(shape) - 1) < SPAN
    return jnp.where(first, 1.0, 0.0).astype(BF16), jnp.where(first, 0.0, 1.0).astype(BF16)


def diagonal(packed, masks):
    return jnp.concatenate([packed * masks[0], packed * masks[1]], axis=0)


def block_dot(left, right, masks):
    return dot(left, diagonal(right, masks))


def parameter_lines(h, cw, alog, dtb):
    taps = cw[:, h].astype(F32)
    rows = [taps[tap : tap + 1, cg * 128 : (cg + 1) * 128] for tap in range(KERNEL) for cg in range(4)]
    rest = jnp.concatenate(
        [jnp.full((1, 128), ref[h * RATIO + r], F32) for ref in (alog, dtb) for r in range(RATIO)], axis=0
    )
    parts = []
    for _ in range(3):
        part = rest.astype(BF16).astype(F32)
        rest = rest - part
        parts.append(part)
    return jnp.concatenate(rows + parts + [jnp.zeros((4, 128), F32)], axis=0)


def parameters(lines):
    wide = lines.astype(F32)
    rest = wide[16:20] + wide[20:24] + wide[24:28]
    return wide[:16], rest[:RATIO], rest[RATIO:]


def pack_keys_kernel(mixed, dec, beta, cw, alog, dtb, kout, pout):
    row = iota((32, TILE), 0)
    own = pout.shape[0]
    lines = [parameter_lines(h, cw, alog, dtb) for h in range(own)]
    for t in range(mixed.shape[0]):
        kout[t, :DK] = mixed[t]
        rest = lines[t % own]
        d, b = dec[t].astype(F32), beta[t].astype(F32)
        for r in range(RATIO):
            rest = jnp.where(row == 28 + r, d[r : r + 1], rest)
            rest = jnp.where(row == 30 + r, b[r : r + 1], rest)
        kout[t, DK:] = rest.astype(BF16)

    @pl.when(pl.program_id(0) == 0)
    def first():
        for h in range(own):
            pout[h] = lines[h].astype(BF16)


def pack_keys(mixed, dec, beta, cw, alog, dtb):
    heads = mixed.shape[0]
    own = cw.shape[1]
    step = heads // 2
    smem = pl.BlockSpec(memory_space=pltpu.SMEM)
    return pl.pallas_call(
        pack_keys_kernel,
        grid=(heads // step,),
        in_specs=[
            pl.BlockSpec((step, DK, TILE), lambda g: (g, 1, 0)),
            pl.BlockSpec((step, RATIO, TILE), lambda g: (g, 0, 0)),
            pl.BlockSpec((step, RATIO, TILE), lambda g: (g, 0, 0)),
            pl.BlockSpec((KERNEL, own, 512), lambda g: (0, 0, 0)),
            smem,
            smem,
        ],
        out_specs=[
            pl.BlockSpec((step, KROWS, TILE), lambda g: (g, 0, 0)),
            pl.BlockSpec((own, 32, 128), lambda g: (0, 0, 0)),
        ],
        out_shape=[
            jax.ShapeDtypeStruct((heads, KROWS, TILE), BF16),
            jax.ShapeDtypeStruct((own, 32, 128), BF16),
        ],
        compiler_params=params(),
        cost_estimate=pl.CostEstimate(flops=10**6, bytes_accessed=2 << 20, transcendentals=0),
        name="pack_keys",
    )(mixed, dec, beta, cw, alog, dtb)


def pack_values_kernel(me, mixed, hout, *outs):
    step = pl.program_id(0)
    row, tok = iota((32, TILE), 0), iota((32, TILE), 1)
    place = row & 15
    picks = []
    for cg in range(4):
        hit = (place < 12) & ((place & 3) == cg) & (tok == (row >> 4) * SPAN + 61 + (place >> 2))
        picks.append(jnp.where(hit, 1.0, 0.0).astype(BF16))
    all_tails = []
    for h in range(mixed.shape[0]):
        tails = jnp.zeros((32, TILE), F32)
        for cg in range(4):
            tails = tails + lax.dot_general(
                picks[cg],
                mixed[h, cg * 128 : (cg + 1) * 128],
                (((1,), (1,)), ((), ())),
                preferred_element_type=F32,
            )
        all_tails.append(tails.astype(BF16))
        hout[h] = all_tails[h][16:]
    for i, out in enumerate(outs):

        @pl.when(step == i)
        def put():
            for h in range(mixed.shape[0]):
                out[h, :256] = mixed[h, 2 * DK :]
                out[h, 256:] = all_tails[h]


def pack_values(me, mixed, n):
    heads = mixed.shape[0]
    own = heads // n
    return pl.pallas_call(
        pack_values_kernel,
        grid_spec=pltpu.PrefetchScalarGridSpec(
            num_scalar_prefetch=1,
            grid=(n,),
            in_specs=[pl.BlockSpec((own, 512, TILE), lambda g, me: (me[0] ^ g, 0, 0))],
            out_specs=[pl.BlockSpec((own, 16, TILE), lambda g, me: (me[0] ^ g, 0, 0))]
            + [pl.BlockSpec((own, VROWS, TILE), lambda g, me: (0, 0, 0))] * n,
        ),
        out_shape=[jax.ShapeDtypeStruct((heads, 16, TILE), BF16)]
        + [jax.ShapeDtypeStruct((own, VROWS, TILE), BF16)] * n,
        compiler_params=params(),
        cost_estimate=pl.CostEstimate(flops=10**8, bytes_accessed=4 << 20, transcendentals=0),
        name="pack_values",
    )(me, mixed)


def is_fresh(req, block):
    start = jnp.int32(0)
    fresh = jnp.bool_(False)
    for j in range(req.shape[1]):
        fresh = fresh | (start == block)
        start = start + req[0, j]
    return fresh


def tap_tables():
    row, part = iota((16, 4 * 128), 0), iota((16, 4 * 128), 1) >> 7
    hits = [((row & 3) == cg) & ((row >> 2) == part) for cg in range(4)]
    return [jnp.where(hit, 1.0, 0.0).astype(BF16) for hit in hits]


def halo_tables():
    row, lane = iota((48, 128), 0), iota((48, 128), 1)
    token = (row >> 2) % 3
    hits = [((row & 3) == cg) & (row < 36) & (token == lane) for cg in range(4)]
    return [jnp.where(hit, 1.0, 0.0).astype(BF16) for hit in hits]


def turned_dot(rows, table):
    return lax.dot_general(rows, table, (((0,), (0,)), ((), ())), preferred_element_type=F32)


def spread_taps(par, table):
    both = turned_dot(par, table)
    return [both[:, tap * 128 : (tap + 1) * 128] for tap in range(KERNEL)]


def halo_terms(halo, par, not_fresh0):
    x = [halo[4 * k : 4 * k + 4].astype(F32) * not_fresh0 for k in range(3)]
    w = [par[4 * k : 4 * k + 4] for k in range(3)]
    terms = jnp.concatenate(
        [w[0] * x[0] + w[1] * x[1] + w[2] * x[2], w[0] * x[1] + w[1] * x[2], w[0] * x[2]], axis=0
    )
    high = terms.astype(BF16).astype(F32)
    middle = (terms - high).astype(BF16).astype(F32)
    parts = [high, middle, terms - high - middle, jnp.zeros((12, 128), F32)]
    return jnp.concatenate(parts, axis=0).astype(BF16)


def convolve(raw, before, terms, taps, masks):
    lane = iota((1, TILE), 1)
    cur = raw.astype(F32)
    total = taps[KERNEL - 1] * cur
    if terms is not None:
        total = total + terms
    for back in range(1, KERNEL):
        moved = cur if before is None else jnp.where(lane >= TILE - back, before, cur)
        total = total + taps[KERNEL - 1 - back] * (pltpu.roll(moved, back, 1) * masks[back - 1])
    return (total / (1.0 + jnp.exp(-total))).astype(BF16)


def conv_masks(cut0, cut1):
    lane = iota((1, TILE), 1)
    masks = []
    for back in range(1, KERNEL):
        gone = ((lane < back) & cut0) | ((lane >= SPAN) & (lane < SPAN + back) & cut1)
        masks.append(jnp.where(gone, 0.0, 1.0))
    return masks


def row_prep(dec, beta, alog, dtb):
    lane = iota(dec.shape, 1)
    x = dec + dtb
    decay = -jnp.exp(alog) * (jnp.maximum(x, 0.0) + jnp.log1p(jnp.exp(-jnp.abs(x))))
    cum = decay
    for shift in (1, 2, 4, 8, 16, 32):
        cum = cum + jnp.where((lane & (SPAN - 1)) >= shift, pltpu.roll(cum, shift, 1), 0.0)
    strength = 1.0 / (1.0 + jnp.exp(-beta))
    grown = jnp.exp(cum)
    close0, close1 = cum[:, SPAN - 1 : SPAN], cum[:, TILE - 1 :]
    fade = jnp.exp(jnp.where(lane < SPAN, close0, close1) - cum)
    keep0 = jnp.exp(jnp.broadcast_to(close0, cum.shape))
    keep1 = jnp.exp(jnp.broadcast_to(close1, cum.shape))
    return cum, strength, grown, fade, keep0, keep1


def unit_inverses(systems):
    row, col = iota((SPAN, TILE), 0), iota((SPAN, TILE), 1) & (SPAN - 1)
    near = (row >> 4) == (col >> 4)
    eye = jnp.where(row == col, 1.0, 0.0)
    masks = halves((SPAN, TILE))

    def low(arrays):
        return [a.astype(BF16) for a in arrays]

    total = [jnp.where(near, eye - a, 0.0) for a in systems]
    power = low([jnp.where(near, -a, 0.0) for a in systems])
    power = low([block_dot(p, p, masks) for p in power])
    for _ in range(2):
        stacks = [jnp.concatenate(pair, axis=0) for pair in zip(low(total), power)]
        both = [block_dot(s, p, masks) for s, p in zip(stacks, power)]
        total = [t + b[:SPAN] for t, b in zip(total, both)]
        power = low([b[SPAN:] for b in both])
    total = [t + block_dot(l, p, masks) for t, l, p in zip(total, low(total), power)]
    small = low(total)
    rest = low([jnp.where(near, 0.0, a) for a in systems])
    cross = low([block_dot(t, r, masks) for t, r in zip(small, rest)])
    total = [t - block_dot(x, l, masks) for t, x, l in zip(total, cross, small)]
    cross = low([block_dot(x, x, masks) for x in cross])
    small = low([t + block_dot(x, l, masks) for t, x, l in zip(total, cross, low(total))])
    solved = []
    for a, x in zip(systems, small):
        block = diagonal(x, masks)
        parts = jnp.concatenate(split(a), axis=1)
        wide = x.astype(F32)
        miss = eye - wide - dot(parts, jnp.concatenate([block, block], axis=0))
        solved.append(wide + block_dot(x, miss.astype(BF16), masks))
    return solved


def both_blocks(square):
    none = jnp.zeros((SPAN, square.shape[1]), square.dtype)
    first = jnp.concatenate([square[:SPAN], none], axis=0)
    return jnp.concatenate([first, jnp.concatenate([none, square[SPAN:]], axis=0)], axis=1)


def unit_keys(convolved):
    wide = convolved.astype(F32)
    return (wide * lax.rsqrt(jnp.sum(wide * wide, axis=0, keepdims=True) + EPSILON)).astype(BF16)


def solve_tiles(keys, queries, prep):
    cum, strength, grown, fade, keep0, keep1 = prep
    row, lane = iota((SPAN, TILE), 0), iota((SPAN, TILE), 1)
    early = lane < SPAN
    seen = (lane & (SPAN - 1)) >= row
    later = (lane & (SPAN - 1)) > row
    columns = jnp.transpose(jnp.concatenate([cum, fade], axis=0))
    count = cum.shape[0]

    def beside(tall):
        return jnp.where(early, tall[:SPAN], tall[SPAN:])

    systems, faded, scores = [], [], []
    for t, k in enumerate(keys):
        turned = jnp.transpose(k.astype(F32))
        if queries is None:
            gram = beside(dot(turned.astype(BF16), k))
        else:
            prod = dot(turned.astype(BF16), jnp.concatenate([k, queries[t]], axis=1))
            gram, touch = beside(prod[:, :TILE]), beside(prod[:, TILE:])
        for r in range(RATIO):
            at = t * RATIO + r
            diff = cum[at : at + 1] - beside(columns[:, at : at + 1])
            ratio = jnp.where(seen, jnp.exp(jnp.where(seen, diff, 0.0)), 0.0)
            systems.append(jnp.where(later, strength[at : at + 1] * gram * ratio, 0.0))
            if queries is not None:
                scores.append((touch * ratio).astype(BF16))
            faded.append((turned * columns[:, count + at : count + at + 1]).astype(BF16))
    solved = [s.astype(BF16) for s in unit_inverses(systems)]
    return solved, faded, scores


def token_prep_kernel(req, me, mixed, dec, beta, halo, par_lines, wk, wv, sc, ft, qo, rows):
    fresh0, fresh1 = is_fresh(req, me[0] * 2), is_fresh(req, me[0] * 2 + 1)
    not_fresh0 = jnp.where(fresh0, 0.0, 1.0)
    masks = conv_masks(True, fresh1)
    tap_tab, halo_tab = tap_tables(), halo_tables()
    tiles = range(mixed.shape[0])
    par = [parameters(par_lines[t]) for t in tiles]

    def gather(pick):
        return jnp.concatenate([pick(t) for t in tiles], axis=0)

    prep = row_prep(
        gather(lambda t: dec[t].astype(F32)),
        gather(lambda t: beta[t].astype(F32)),
        jnp.concatenate([p[1] for p in par], axis=0),
        jnp.concatenate([p[2] for p in par], axis=0),
    )
    cum, strength, grown, fade, keep0, keep1 = prep
    keys, queries, values = [], [], []
    for t in tiles:
        terms = halo_terms(halo[t], par[t][0], not_fresh0)
        lines = par_lines[t, :16]
        q, k, v0, v1 = [
            convolve(
                mixed[t, c * 128 : (c + 1) * 128],
                None,
                turned_dot(terms, halo_tab[c]),
                spread_taps(lines, tap_tab[c]),
                masks,
            )
            for c in range(4)
        ]
        keys.append(unit_keys(k))
        queries.append(q)
        values.append((v0, v1))
        qo[t] = q
        rows[t] = jnp.concatenate(
            [keep0[2 * t : 2 * t + 2], grown[2 * t : 2 * t + 2], keep1[2 * t : 2 * t + 2], strength[2 * t : 2 * t + 2]],
            axis=0,
        )
    solved, faded, scores = solve_tiles(keys, queries, prep)
    sides = halves((SPAN, TILE))
    for t in tiles:
        for r in range(RATIO):
            at = t * RATIO + r
            s, lift = strength[at : at + 1], strength[at : at + 1] * grown[at : at + 1]
            stacked = jnp.concatenate(
                [
                    (lift * keys[t].astype(F32)).astype(BF16),
                    (s * values[t][r].astype(F32)).astype(BF16),
                ],
                axis=0,
            )
            out = dot(stacked, diagonal(solved[at], sides)).astype(BF16)
            wk[at] = out[:DK]
            wv[at] = out[DK:]
            sc[at] = scores[at]
            ft[at] = faded[at]


def token_prep(req, me, mixed, dec, beta, halo, par):
    heads = mixed.shape[0]
    smem = pl.BlockSpec(memory_space=pltpu.SMEM)

    def tiles(count, *rest):
        return pl.BlockSpec((count,) + rest, lambda g: (g,) + (0,) * len(rest))

    square = jax.ShapeDtypeStruct((heads * RATIO, 128, 128), BF16)
    return pl.pallas_call(
        token_prep_kernel,
        grid=(heads // WIDE,),
        in_specs=[
            smem,
            smem,
            tiles(WIDE, 512, TILE),
            tiles(WIDE, RATIO, TILE),
            tiles(WIDE, RATIO, TILE),
            tiles(WIDE, 16, TILE),
            pl.BlockSpec((WIDE, 32, 128), lambda g: (g, 4, 0)),
        ],
        out_specs=[tiles(WIDE * RATIO, 128, 128)] * 2
        + [tiles(WIDE * RATIO, SPAN, TILE), tiles(WIDE * RATIO, 128, 128)]
        + [tiles(WIDE, 128, 128), tiles(WIDE, 8, 128)],
        out_shape=[square] * 2
        + [
            jax.ShapeDtypeStruct((heads * RATIO, SPAN, TILE), BF16),
            square,
            jax.ShapeDtypeStruct((heads, 128, 128), BF16),
            jax.ShapeDtypeStruct((heads, 8, 128), F32),
        ],
        compiler_params=params(),
        cost_estimate=pl.CostEstimate(flops=10**10, bytes_accessed=8 << 20, transcendentals=10**6),
        name="token_prep",
    )(req, me, mixed, dec, beta, halo, par)


def head_prep_kernel(req, kp, previous, par_lines, sol, ft, gs, rows):
    step = pl.program_id(0)
    depth, own = kp.shape[0], kp.shape[1]
    tap_tab = tap_tables()
    order = [(d, h) for d in range(depth) for h in range(own)]
    par = [parameters(par_lines[h]) for h in range(own)]

    small = [kp[d, h, DK:].astype(F32) for d, h in order]
    prep = row_prep(
        jnp.concatenate([s[28:30] for s in small], axis=0),
        jnp.concatenate([s[30:32] for s in small], axis=0),
        jnp.concatenate([par[h][1] for d, h in order], axis=0),
        jnp.concatenate([par[h][2] for d, h in order], axis=0),
    )
    cum, strength, grown, fade, keep0, keep1 = prep
    keys = []
    taps = [spread_taps(par_lines[h, :16], tap_tab[1]) for h in range(own)]
    for d in range(depth):
        block = (step * depth + d) * 2
        masks = conv_masks(is_fresh(req, block), is_fresh(req, block + 1))
        for h in range(own):
            before = (kp[d - 1, h, :DK] if d else previous[0, h]).astype(F32)
            keys.append(unit_keys(convolve(kp[d, h, :DK], before, None, taps[h], masks)))
    solved, faded, unused = solve_tiles(keys, None, prep)
    sides = halves((SPAN, TILE))
    for t, (d, h) in enumerate(order):
        rows[d, h] = jnp.concatenate(
            [keep0[2 * t : 2 * t + 2], keep1[2 * t : 2 * t + 2], strength[2 * t : 2 * t + 2], strength[2 * t : 2 * t + 2]],
            axis=0,
        )
        for r in range(RATIO):
            at = t * RATIO + r
            lift = strength[at : at + 1] * grown[at : at + 1]
            scaled = (lift * keys[t].astype(F32)).astype(BF16)
            wide = dot(scaled, diagonal(solved[at], sides)).astype(BF16)
            drop = dot(wide, both_blocks(faded[at])).astype(BF16)
            gs[d, h, r, 0] = drop[:, :DK]
            gs[d, h, r, 1] = drop[:, DK:]
            sol[d, h, r] = solved[at]
            ft[d, h, r] = faded[at]


def head_prep(req, kp, par):
    n, own = kp.shape[:2]
    depth = WIDE // own
    smem = pl.BlockSpec(memory_space=pltpu.SMEM)

    def tiles(*rest):
        return pl.BlockSpec((depth, own) + rest, lambda g: (g, 0) + (0,) * len(rest))

    square = jax.ShapeDtypeStruct((n, own, RATIO, 128, 128), BF16)
    return pl.pallas_call(
        head_prep_kernel,
        grid=(n // depth,),
        in_specs=[
            smem,
            tiles(KROWS, TILE),
            pl.BlockSpec((1, own, DK, TILE), lambda g: (jnp.maximum(g * depth - 1, 0), 0, 0, 0)),
            pl.BlockSpec((own, 32, 128), lambda g: (0, 0, 0)),
        ],
        out_specs=[
            tiles(RATIO, SPAN, TILE),
            tiles(RATIO, 128, 128),
            tiles(RATIO, 2, 128, 128),
            tiles(8, 128),
        ],
        out_shape=[
            jax.ShapeDtypeStruct((n, own, RATIO, SPAN, TILE), BF16),
            square,
            jax.ShapeDtypeStruct((n, own, RATIO, 2, 128, 128), BF16),
            jax.ShapeDtypeStruct((n, own, 8, 128), F32),
        ],
        compiler_params=params(),
        cost_estimate=pl.CostEstimate(flops=10**10, bytes_accessed=6 << 20, transcendentals=10**6),
        name="head_prep",
    )(req, kp, kp, par)


def head_chain_kernel(req, me, par_lines, sol, ft, gs, rows, *refs):
    n = refs[-5].shape[0]
    arrived, (sin, ends, tails, state, vp) = refs[:n], refs[n:]
    step = pl.program_id(0)
    depth, own = sol.shape[0], sol.shape[1]

    @pl.when(step == 0)
    def first():
        for k, one in enumerate(arrived):
            vp[me[0] ^ k] = one[...]
            tails[me[0] ^ k] = one[:, 256:]

    tap_tab = tap_tables()
    sides = halves((SPAN, TILE))
    heads = [(h, r) for h in range(own) for r in range(RATIO)]
    taps = [spread_taps(par_lines[h, :16], tap_tab[2 + r]) for h, r in heads]
    current = [state[v] for v in range(len(heads))]
    for d in range(depth):
        tile = step * depth + d
        past = jnp.maximum(tile - 1, 0)
        fresh = [is_fresh(req, tile * 2), is_fresh(req, tile * 2 + 1)]
        masks = conv_masks(fresh[0], fresh[1])
        gains = []
        for v, (h, r) in enumerate(heads):
            raw = vp[tile, h, r * DV : (r + 1) * DV]
            before = vp[past, h, r * DV : (r + 1) * DV].astype(F32)
            value = convolve(raw, before, None, taps[v], masks)
            scaled = (rows[d, h, 4 + r : 5 + r] * value.astype(F32)).astype(BF16)
            wide = block_dot(scaled, sol[d, h, r], sides).astype(BF16)
            gains.append(dot(wide, both_blocks(ft[d, h, r])))
        for half in range(2):
            for v, (h, r) in enumerate(heads):
                now = jnp.where(fresh[half], 0.0, current[v])
                keep = rows[d, h, 2 * half + r : 2 * half + r + 1]
                gain = gains[v][:, half * DV : (half + 1) * DV]
                current[v] = keep * now + (gain - dot(now.astype(BF16), gs[d, h, r, half]))
                ends[d * 2 + half, v] = current[v].astype(BF16)
        onward = lax.rem(tile + 1, n)
        for v in range(len(heads)):
            sin[onward, v] = current[v].astype(BF16)
    for v in range(len(heads)):
        state[v] = current[v]


def head_chain(req, me, par, sol, ft, gs, rows, arrived):
    n, own = sol.shape[:2]
    depth = WIDE // own
    smem = pl.BlockSpec(memory_space=pltpu.SMEM)

    def tiles(*rest):
        return pl.BlockSpec((depth, own) + rest, lambda g: (g, 0) + (0,) * len(rest))

    return pl.pallas_call(
        head_chain_kernel,
        grid=(n // depth,),
        in_specs=[
            smem,
            smem,
            pl.BlockSpec((own, 32, 128), lambda g: (0, 0, 0)),
            tiles(RATIO, SPAN, TILE),
            tiles(RATIO, 128, 128),
            tiles(RATIO, 2, 128, 128),
            tiles(8, 128),
        ]
        + [pl.BlockSpec((own, VROWS, TILE), lambda g: (0, 0, 0))] * n,
        out_specs=[
            pl.BlockSpec((n, own * RATIO, 128, 128), lambda g: (0, 0, 0, 0)),
            pl.BlockSpec((2 * depth, own * RATIO, 128, 128), lambda g: (g, 0, 0, 0)),
            pl.BlockSpec((n, own, 32, TILE), lambda g: (0, 0, 0, 0)),
        ],
        out_shape=[
            jax.ShapeDtypeStruct((n, own * RATIO, 128, 128), BF16),
            jax.ShapeDtypeStruct((2 * n, own * RATIO, 128, 128), BF16),
            jax.ShapeDtypeStruct((n, own, 32, TILE), BF16),
        ],
        scratch_shapes=[
            pltpu.VMEM((own * RATIO, 128, 128), F32),
            pltpu.VMEM((n, own, VROWS, TILE), BF16),
        ],
        compiler_params=params(),
        cost_estimate=pl.CostEstimate(flops=3 * 10**9, bytes_accessed=8 << 20, transcendentals=10**6),
        name="head_chain",
    )(req, me, par, sol, ft, gs, rows, *arrived)


def choose_kernel(req, rep, fin, me, ends, kt, *refs):
    outs, counts = refs[:-1], refs[-1]
    own, heads = kt.shape[1], ends.shape[1]
    base = heads * 128
    for i, out in enumerate(outs):
        out[...] = jnp.zeros_like(out)
        counts[i] = 0
    end = jnp.int32(-1)
    for j in range(req.shape[1]):
        end = end + req[0, j]
        where = rep[0, j] ^ me[0]
        place = jnp.minimum(counts[where], CAP - 1)
        done = fin[0, j] > 0
        counts[where] = counts[where] + jnp.where(done, 1, 0)
        for i, out in enumerate(outs):

            @pl.when(done & (where == i))
            def take():
                for v in range(heads):
                    out[place, v * 128 : (v + 1) * 128] = ends[end, v]
                for h in range(own):
                    lines = kt[end >> 1, h].astype(F32)
                    lines = jnp.where((end & 1) > 0, lines[16:], lines[:16]).astype(BF16)
                    out[place, base + h * 16 : base + h * 16 + 16] = lines

    for i, out in enumerate(outs):
        number = jnp.full((16, 128), counts[i], jnp.int32).astype(F32).astype(BF16)
        for c in range(CAP):
            out[c, base + own * 16 :] = number


def choose(req, rep, fin, me, ends, tails, replicas):
    own = tails.shape[1]
    smem = pl.BlockSpec(memory_space=pltpu.SMEM)
    lines = own * RATIO * 128 + own * 16 + 16
    return pl.pallas_call(
        choose_kernel,
        grid=(1,),
        in_specs=[
            smem,
            smem,
            smem,
            smem,
            pl.BlockSpec(ends.shape, lambda g: (0, 0, 0, 0)),
            pl.BlockSpec(tails.shape, lambda g: (0, 0, 0, 0)),
        ],
        out_specs=[pl.BlockSpec((CAP, lines, 128), lambda g: (0, 0, 0))] * replicas,
        out_shape=[jax.ShapeDtypeStruct((CAP, lines, 128), BF16)] * replicas,
        scratch_shapes=[pltpu.SMEM((replicas,), jnp.int32)],
        compiler_params=params(),
        cost_estimate=pl.CostEstimate(flops=10**6, bytes_accessed=4 << 20, transcendentals=0),
        name="choose",
    )(req, rep, fin, me, ends, tails)


def token_out_kernel(req, me, sin, wk, wv, sc, ft, qs, rows, gate, gain, out):
    stay0 = jnp.where(is_fresh(req, me[0] * 2), 0.0, 1.0)
    stay1 = jnp.where(is_fresh(req, me[0] * 2 + 1), 0.0, 1.0)
    lane = iota((DV, TILE), 1)
    early = lane < SPAN
    sides = halves((SPAN, TILE))
    units = [(t, r) for t in range(qs.shape[0]) for r in range(RATIO)]
    both = [jnp.concatenate([wk[t * RATIO + r], qs[t]], axis=1) for t, r in units]
    enter = [sin[t * RATIO + r].astype(F32) * stay0 for t, r in units]
    first = [dot(e.astype(BF16), b) for e, b in zip(enter, both)]
    wide = [wv[t * RATIO + r].astype(F32) for t, r in units]
    new0 = [jnp.where(early, w - f[:, :TILE], 0.0) for w, f in zip(wide, first)]
    middle = [
        (rows[t, r : r + 1] * e + dot(x.astype(BF16), ft[t * RATIO + r])) * stay1
        for (t, r), e, x in zip(units, enter, new0)
    ]
    second = [dot(m.astype(BF16), b) for m, b in zip(middle, both)]
    new = [
        jnp.where(early, x, w - s[:, :TILE]).astype(BF16) for x, w, s in zip(new0, wide, second)
    ]
    for at, (t, r) in enumerate(units):
        core = rows[t, 2 + r : 3 + r] * jnp.where(early, first[at][:, TILE:], second[at][:, TILE:])
        core = (core + dot(new[at], diagonal(sc[at], sides))).astype(BF16).astype(F32)
        inverse_rms = lax.rsqrt(jnp.mean(core * core, axis=0, keepdims=True) + EPSILON)
        z = gate[t, r * DV : (r + 1) * DV].astype(F32)
        result = core * inverse_rms * gain[...] * (z / (1.0 + jnp.exp(-z)))
        out[t, r * DV : (r + 1) * DV] = result.astype(BF16)


def token_out(req, me, sin, wk, wv, sc, ft, qs, rows, gate, gain):
    heads = qs.shape[0]
    smem = pl.BlockSpec(memory_space=pltpu.SMEM)

    def tiles(count, *rest):
        return pl.BlockSpec((count,) + rest, lambda g: (g,) + (0,) * len(rest))

    return pl.pallas_call(
        token_out_kernel,
        grid=(heads // STEP,),
        in_specs=[smem, smem]
        + [tiles(STEP * RATIO, 128, 128)] * 3
        + [tiles(STEP * RATIO, SPAN, TILE), tiles(STEP * RATIO, 128, 128)]
        + [
            tiles(STEP, 128, 128),
            tiles(STEP, 8, 128),
            tiles(STEP, 256, TILE),
            pl.BlockSpec((128, 128), lambda g: (0, 0)),
        ],
        out_specs=tiles(STEP, 256, TILE),
        out_shape=jax.ShapeDtypeStruct((heads, 256, TILE), BF16),
        compiler_params=params(),
        cost_estimate=pl.CostEstimate(flops=10**9, bytes_accessed=8 << 20, transcendentals=10**6),
        name="token_out",
    )(req, me, sin, wk, wv, sc, ft, qs, rows, gate, gain)


def land_kernel(me, *refs):
    got, (states, tails, counts) = refs[:-3], refs[-3:]
    slot = pl.program_id(0)
    heads, own = states.shape[1], tails.shape[1]
    base = heads * 128

    @pl.when(slot == 0)
    def first():
        for i, one in enumerate(got):
            number = jnp.max(one[0, base + own * 16 :].astype(F32))
            counts[i] = number.astype(jnp.int32)

    start = jnp.int32(0)
    source, place = jnp.int32(-1), jnp.int32(0)
    for p in range(len(got)):
        away = me[0] ^ p
        number = counts[away]
        inside = (slot >= start) & (slot < start + number)
        source = jnp.where(inside, away, source)
        place = jnp.where(inside, slot - start, place)
        start = start + number
    place = jnp.clip(place, 0, CAP - 1)
    for i, one in enumerate(got):

        @pl.when(source == i)
        def take():
            for v in range(heads):
                block = one[place, v * 128 : (v + 1) * 128].astype(F32)
                states[0, v] = jnp.transpose(block)
            for h in range(own):
                tails[0, h] = one[place, base + h * 16 : base + h * 16 + 16]

    @pl.when(source < 0)
    def clear():
        states[...] = jnp.zeros_like(states)
        tails[...] = jnp.zeros_like(tails)


def land(me, got, heads, own):
    lines = got[0].shape[1]
    slots = len(got) * CAP
    smem = pl.BlockSpec(memory_space=pltpu.SMEM)
    return pl.pallas_call(
        land_kernel,
        grid=(slots,),
        in_specs=[smem] + [pl.BlockSpec((CAP, lines, 128), lambda g: (0, 0, 0))] * len(got),
        out_specs=[
            pl.BlockSpec((1, heads, 128, 128), lambda g: (g, 0, 0, 0)),
            pl.BlockSpec((1, own, 16, 128), lambda g: (g, 0, 0, 0)),
        ],
        out_shape=[
            jax.ShapeDtypeStruct((slots, heads, 128, 128), F32),
            jax.ShapeDtypeStruct((slots, own, 16, 128), BF16),
        ],
        scratch_shapes=[pltpu.SMEM((len(got),), jnp.int32)],
        compiler_params=params(),
        cost_estimate=pl.CostEstimate(flops=10**6, bytes_accessed=4 << 20, transcendentals=0),
        name="land",
    )(me, *got)


def body(
    mixed,
    decay_in,
    beta_in,
    gate_z,
    conv_weight,
    a_log,
    dt_bias,
    norm_gain,
    req_blocks,
    replica_of,
    finished,
):
    n = lax.axis_size("seq")
    replicas = lax.axis_size("rep")
    heads = mixed.shape[1]
    own = heads // n
    me = lax.axis_index("seq").astype(jnp.int32).reshape(1)
    kpack, par = pack_keys(mixed[0], decay_in[0], beta_in[0], conv_weight, a_log, dt_bias)
    halo, *vpack = pack_values(me, mixed[0], n)
    kp = lax.all_to_all(kpack.reshape(n, own, KROWS, TILE), "seq", 0, 0, tiled=True)
    vp = [vpack[0]] + [
        lax.ppermute(vpack[k], "seq", [(i, i ^ k) for i in range(n)]) for k in range(1, n)
    ]
    halo = lax.ppermute(halo, "seq", [(i, i + 1) for i in range(n - 1)])
    wk, wv, sc, ft, qs, rows = token_prep(
        req_blocks, me, mixed[0], decay_in[0], beta_in[0], halo, kp.reshape(heads, KROWS, TILE)
    )
    hsol, hft, hgs, hrows = head_prep(req_blocks, kp, par)
    hrows, rows = lax.optimization_barrier((hrows, rows))
    sin, ends, ktails = head_chain(req_blocks, me, par, hsol, hft, hgs, hrows, vp)
    sin = lax.all_to_all(sin, "seq", 0, 0, tiled=True)
    my_rep = lax.axis_index("rep").astype(jnp.int32).reshape(1)
    send = choose(req_blocks, replica_of, finished, my_rep, ends, ktails, replicas)
    got = [send[0]] + [
        lax.ppermute(send[k], "rep", [(i, i ^ k) for i in range(replicas)])
        for k in range(1, replicas)
    ]
    states, tails = land(my_rep, got, own * RATIO, own)
    tails = tails.reshape(replicas * CAP, own, 4, 512)[:, :, : KERNEL - 1].transpose(0, 2, 1, 3)
    gain = jnp.broadcast_to(norm_gain[:, None], (DV, TILE))
    out = token_out(
        req_blocks,
        me,
        sin.reshape(heads * RATIO, 128, 128),
        wk,
        wv,
        sc,
        ft,
        qs,
        rows,
        gate_z[0],
        gain,
    )
    return (out[None], states[None], tails[None])


def solution(mesh):
    placed = (
        P("rep", None, None, "seq"),
        P("rep", None, None, "seq"),
        P("rep", None, None, "seq"),
        P("rep", None, None, "seq"),
        P(None, "seq", None),
        P("seq"),
        P("seq"),
        P(),
        P("rep", None),
        P("rep", None),
        P("rep", None),
    )
    return jax.shard_map(
        body,
        mesh=mesh,
        in_specs=placed,
        out_specs=(
            P("rep", None, None, "seq"),
            P("rep", None, "seq", None, None),
            P("rep", None, None, "seq", None),
        ),
        check_vma=False,
    )
```

```python
import jax
import jax.numpy as jnp
from jax import lax
from jax.experimental import pallas as pl
from jax.experimental.pallas import tpu as pltpu
from jax.sharding import PartitionSpec as P

DK = 128
DV = 128
KERNEL = 4
SPAN = 64
CAP = 2
RATIO = 2
TILE = 2 * SPAN
KROWS = 160
VROWS = 288
STEP = 4
WIDE = 8
EPSILON = 1e-06
F32 = jnp.float32
BF16 = jnp.bfloat16
VMEM_LIMIT = 56 * 1024 * 1024


def params(**kwargs):
    return pltpu.CompilerParams(vmem_limit_bytes=VMEM_LIMIT, **kwargs)


def iota(shape, dim):
    return lax.broadcasted_iota(jnp.int32, shape, dim)


def dot(left, right):
    return jnp.dot(left, right, preferred_element_type=F32)


def split(wide):
    high = wide.astype(BF16)
    return high, (wide - high.astype(F32)).astype(BF16)


def halves(shape):
    first = iota(shape, len(shape) - 1) < SPAN
    return jnp.where(first, 1.0, 0.0).astype(BF16), jnp.where(first, 0.0, 1.0).astype(BF16)


def corner(first, second):
    none = jnp.zeros_like(first)
    top = jnp.concatenate([first, none], axis=1)
    return jnp.concatenate([top, jnp.concatenate([none, second], axis=1)], axis=0)


def diagonal(packed, masks):
    squares = []
    for r in range(RATIO):
        one = packed[:, r * TILE : (r + 1) * TILE]
        squares.append(jnp.concatenate([one * masks[0], one * masks[1]], axis=0))
    return corner(*squares)


def block_dot(left, right, masks):
    return dot(left, diagonal(right, masks))


def parameter_lines(h, cw, alog, dtb):
    taps = cw[:, h].astype(F32)
    rows = [taps[tap : tap + 1, cg * 128 : (cg + 1) * 128] for tap in range(KERNEL) for cg in range(4)]
    rest = jnp.concatenate(
        [jnp.full((1, 128), ref[h * RATIO + r], F32) for ref in (alog, dtb) for r in range(RATIO)], axis=0
    )
    parts = []
    for _ in range(3):
        part = rest.astype(BF16).astype(F32)
        rest = rest - part
        parts.append(part)
    return jnp.concatenate(rows + parts + [jnp.zeros((4, 128), F32)], axis=0)


def parameters(lines):
    wide = lines.astype(F32)
    rest = wide[16:20] + wide[20:24] + wide[24:28]
    return wide[:16], rest[:RATIO], rest[RATIO:]


def pack_keys_kernel(mixed, dec, beta, cw, alog, dtb, kout, pout):
    row = iota((32, TILE), 0)
    own = pout.shape[0]
    lines = [parameter_lines(h, cw, alog, dtb) for h in range(own)]
    for t in range(mixed.shape[0]):
        kout[t, :DK] = mixed[t]
        rest = lines[t % own]
        d, b = dec[t].astype(F32), beta[t].astype(F32)
        for r in range(RATIO):
            rest = jnp.where(row == 28 + r, d[r : r + 1], rest)
            rest = jnp.where(row == 30 + r, b[r : r + 1], rest)
        kout[t, DK:] = rest.astype(BF16)

    @pl.when(pl.program_id(0) == 0)
    def first():
        for h in range(own):
            pout[h] = lines[h].astype(BF16)


def pack_keys(mixed, dec, beta, cw, alog, dtb):
    heads = mixed.shape[0]
    own = cw.shape[1]
    step = heads // 2
    smem = pl.BlockSpec(memory_space=pltpu.SMEM)
    return pl.pallas_call(
        pack_keys_kernel,
        grid=(heads // step,),
        in_specs=[
            pl.BlockSpec((step, DK, TILE), lambda g: (g, 1, 0)),
            pl.BlockSpec((step, RATIO, TILE), lambda g: (g, 0, 0)),
            pl.BlockSpec((step, RATIO, TILE), lambda g: (g, 0, 0)),
            pl.BlockSpec((KERNEL, own, 512), lambda g: (0, 0, 0)),
            smem,
            smem,
        ],
        out_specs=[
            pl.BlockSpec((step, KROWS, TILE), lambda g: (g, 0, 0)),
            pl.BlockSpec((own, 32, 128), lambda g: (0, 0, 0)),
        ],
        out_shape=[
            jax.ShapeDtypeStruct((heads, KROWS, TILE), BF16),
            jax.ShapeDtypeStruct((own, 32, 128), BF16),
        ],
        compiler_params=params(),
        cost_estimate=pl.CostEstimate(flops=10**6, bytes_accessed=2 << 20, transcendentals=0),
        name="pack_keys",
    )(mixed, dec, beta, cw, alog, dtb)


def pack_values_kernel(me, mixed, hout, *outs):
    step = pl.program_id(0)
    own = outs[0].shape[0]
    row, tok = iota((TILE, 128), 1), iota((TILE, 128), 0)
    place = row & 15
    picks = []
    for cg in range(4):
        hit = (row < 32) & (place < 12) & ((place & 3) == cg)
        hit = hit & (tok == (row >> 4) * SPAN + 61 + (place >> 2))
        picks.append(jnp.where(hit, 1.0, 0.0).astype(BF16))
    all_tails = []
    for h in range(mixed.shape[0]):
        tails = dot(mixed[h, :128], picks[0])
        for cg in range(1, 4):
            tails = tails + dot(mixed[h, cg * 128 : (cg + 1) * 128], picks[cg])
        all_tails.append(jnp.transpose(tails)[:32].astype(BF16))
        hout[h] = all_tails[h][16:]
    for i, out in enumerate(outs):

        @pl.when((step == i // 4) & ((me[0] & 3) == 0))
        def put0():
            put(mixed, all_tails, out, (i & 3) ^ 0, own)

        @pl.when((step == i // 4) & ((me[0] & 3) == 1))
        def put1():
            put(mixed, all_tails, out, (i & 3) ^ 1, own)

        @pl.when((step == i // 4) & ((me[0] & 3) == 2))
        def put2():
            put(mixed, all_tails, out, (i & 3) ^ 2, own)

        @pl.when((step == i // 4) & ((me[0] & 3) == 3))
        def put3():
            put(mixed, all_tails, out, (i & 3) ^ 3, own)


def put(mixed, all_tails, out, place, own):
    for h in range(own):
        out[h, :256] = mixed[place * own + h, 2 * DK :]
        out[h, 256:] = all_tails[place * own + h]


def pack_values(me, mixed, n):
    heads = mixed.shape[0]
    own = heads // n
    return pl.pallas_call(
        pack_values_kernel,
        grid_spec=pltpu.PrefetchScalarGridSpec(
            num_scalar_prefetch=1,
            grid=(n // 4,),
            in_specs=[pl.BlockSpec((4 * own, 512, TILE), lambda g, me: ((me[0] >> 2) ^ g, 0, 0))],
            out_specs=[pl.BlockSpec((4 * own, 16, TILE), lambda g, me: ((me[0] >> 2) ^ g, 0, 0))]
            + [pl.BlockSpec((own, VROWS, TILE), lambda g, me: (0, 0, 0))] * n,
        ),
        out_shape=[jax.ShapeDtypeStruct((heads, 16, TILE), BF16)]
        + [jax.ShapeDtypeStruct((own, VROWS, TILE), BF16)] * n,
        compiler_params=params(),
        cost_estimate=pl.CostEstimate(flops=10**8, bytes_accessed=4 << 20, transcendentals=0),
        name="pack_values",
    )(me, mixed)


def is_fresh(req, block):
    start = jnp.int32(0)
    fresh = jnp.bool_(False)
    for j in range(req.shape[1]):
        fresh = fresh | (start == block)
        start = start + req[0, j]
    return fresh


def tap_tables():
    row, part = iota((16, 4 * 128), 0), iota((16, 4 * 128), 1) >> 7
    hits = [((row & 3) == cg) & ((row >> 2) == part) for cg in range(4)]
    return [jnp.where(hit, 1.0, 0.0).astype(BF16) for hit in hits]


def halo_tables():
    row, lane = iota((48, 128), 0), iota((48, 128), 1)
    token = (row >> 2) % 3
    hits = [((row & 3) == cg) & (row < 36) & (token == lane) for cg in range(4)]
    return [jnp.where(hit, 1.0, 0.0).astype(BF16) for hit in hits]


def turned_dot(rows, table):
    return lax.dot_general(rows, table, (((0,), (0,)), ((), ())), preferred_element_type=F32)


def spread_taps(par, table):
    both = turned_dot(par, table)
    return [both[:, tap * 128 : (tap + 1) * 128] for tap in range(KERNEL)]


def halo_terms(halo, par, not_fresh0):
    x = [halo[4 * k : 4 * k + 4].astype(F32) * not_fresh0 for k in range(3)]
    w = [par[4 * k : 4 * k + 4] for k in range(3)]
    terms = jnp.concatenate(
        [w[0] * x[0] + w[1] * x[1] + w[2] * x[2], w[0] * x[1] + w[1] * x[2], w[0] * x[2]], axis=0
    )
    high = terms.astype(BF16).astype(F32)
    middle = (terms - high).astype(BF16).astype(F32)
    parts = [high, middle, terms - high - middle, jnp.zeros((12, 128), F32)]
    return jnp.concatenate(parts, axis=0).astype(BF16)


def convolve(raw, before, terms, taps, masks):
    lane = iota((1, TILE), 1)
    cur = raw.astype(F32)
    total = taps[KERNEL - 1] * cur
    if terms is not None:
        total = total + terms
    for back in range(1, KERNEL):
        moved = cur if before is None else jnp.where(lane >= TILE - back, before, cur)
        total = total + taps[KERNEL - 1 - back] * (pltpu.roll(moved, back, 1) * masks[back - 1])
    return (total / (1.0 + jnp.exp(-total))).astype(BF16)


def conv_masks(cut0, cut1):
    lane = iota((1, TILE), 1)
    masks = []
    for back in range(1, KERNEL):
        gone = ((lane < back) & cut0) | ((lane >= SPAN) & (lane < SPAN + back) & cut1)
        masks.append(jnp.where(gone, 0.0, 1.0))
    return masks


def row_prep(dec, beta, alog, dtb):
    lane = iota(dec.shape, 1)
    x = dec + dtb
    decay = -jnp.exp(alog) * (jnp.maximum(x, 0.0) + jnp.log1p(jnp.exp(-jnp.abs(x))))
    cum = decay
    for shift in (1, 2, 4, 8, 16, 32):
        cum = cum + jnp.where((lane & (SPAN - 1)) >= shift, pltpu.roll(cum, shift, 1), 0.0)
    strength = 1.0 / (1.0 + jnp.exp(-beta))
    grown = jnp.exp(cum)
    close0, close1 = cum[:, SPAN - 1 : SPAN], cum[:, TILE - 1 :]
    fade = jnp.exp(jnp.where(lane < SPAN, close0, close1) - cum)
    keep0 = jnp.exp(jnp.broadcast_to(close0, cum.shape))
    keep1 = jnp.exp(jnp.broadcast_to(close1, cum.shape))
    return cum, strength, grown, fade, keep0, keep1


def unit_inverses(systems):
    shape = (SPAN, RATIO * TILE)
    row, col = iota(shape, 0), iota(shape, 1) & (SPAN - 1)
    near = (row >> 4) == (col >> 4)
    eye = jnp.where(row == col, 1.0, 0.0)
    masks = halves((SPAN, TILE))

    def low(arrays):
        return [a.astype(BF16) for a in arrays]

    def stack(pair):
        return jnp.concatenate(pair, axis=0)

    total = [jnp.where(near, eye - a, 0.0) for a in systems]
    power = low([jnp.where(near, -a, 0.0) for a in systems])
    power = low([block_dot(p, p, masks) for p in power])
    for _ in range(2):
        both = [block_dot(stack([t, p]), p, masks) for t, p in zip(low(total), power)]
        total = [t + b[:SPAN] for t, b in zip(total, both)]
        power = low([b[SPAN:] for b in both])
    total = [t + block_dot(l, p, masks) for t, l, p in zip(total, low(total), power)]
    small = low(total)
    rest = low([jnp.where(near, 0.0, a) for a in systems])
    cross = low([block_dot(t, r, masks) for t, r in zip(small, rest)])
    total = [t - block_dot(x, l, masks) for t, x, l in zip(total, cross, small)]
    cross = low([block_dot(x, x, masks) for x in cross])
    small = low([t + block_dot(x, l, masks) for t, x, l in zip(total, cross, low(total))])
    solved = []
    for a, x in zip(systems, small):
        wide = x.astype(F32)
        parts = block_dot(stack(split(a)), x, masks)
        miss = eye - wide - (parts[:SPAN] + parts[SPAN:])
        solved.append((wide + block_dot(x, miss.astype(BF16), masks)).astype(BF16))
    return solved


def both_blocks(square):
    none = jnp.zeros((SPAN, square.shape[1]), square.dtype)
    first = jnp.concatenate([square[:SPAN], none], axis=0)
    return jnp.concatenate([first, jnp.concatenate([none, square[SPAN:]], axis=0)], axis=1)


def unit_keys(convolved):
    wide = convolved.astype(F32)
    return (wide * lax.rsqrt(jnp.sum(wide * wide, axis=0, keepdims=True) + EPSILON)).astype(BF16)


def solve_tiles(keys, queries, prep):
    cum, strength, grown, fade, keep0, keep1 = prep
    row, lane = iota((SPAN, TILE), 0), iota((SPAN, TILE), 1)
    early = lane < SPAN
    seen = (lane & (SPAN - 1)) >= row
    later = (lane & (SPAN - 1)) > row
    columns = jnp.transpose(jnp.concatenate([cum, fade], axis=0))
    count = cum.shape[0]

    def beside(tall):
        return jnp.where(early, tall[:SPAN], tall[SPAN:])

    systems, faded, scores = [], [], []
    for t, k in enumerate(keys):
        turned = jnp.transpose(k.astype(F32))
        if queries is None:
            gram = beside(dot(turned.astype(BF16), k))
        else:
            prod = dot(turned.astype(BF16), jnp.concatenate([k, queries[t]], axis=1))
            gram, touch = beside(prod[:, :TILE]), beside(prod[:, TILE:])
        pair = []
        for r in range(RATIO):
            at = t * RATIO + r
            diff = cum[at : at + 1] - beside(columns[:, at : at + 1])
            ratio = jnp.where(seen, jnp.exp(jnp.where(seen, diff, 0.0)), 0.0)
            pair.append(jnp.where(later, strength[at : at + 1] * gram * ratio, 0.0))
            if queries is not None:
                scores.append((touch * ratio).astype(BF16))
            faded.append((turned * columns[:, count + at : count + at + 1]).astype(BF16))
        systems.append(jnp.concatenate(pair, axis=1))
    return unit_inverses(systems), faded, scores


def token_prep_kernel(req, me, mixed, dec, beta, halo, par_lines, wk, wv, sc, ft, qo, rows):
    fresh0, fresh1 = is_fresh(req, me[0] * 2), is_fresh(req, me[0] * 2 + 1)
    not_fresh0 = jnp.where(fresh0, 0.0, 1.0)
    masks = conv_masks(True, fresh1)
    tap_tab, halo_tab = tap_tables(), halo_tables()
    tiles = range(mixed.shape[0])
    par = [parameters(par_lines[t]) for t in tiles]

    def gather(pick):
        return jnp.concatenate([pick(t) for t in tiles], axis=0)

    prep = row_prep(
        gather(lambda t: dec[t].astype(F32)),
        gather(lambda t: beta[t].astype(F32)),
        jnp.concatenate([p[1] for p in par], axis=0),
        jnp.concatenate([p[2] for p in par], axis=0),
    )
    cum, strength, grown, fade, keep0, keep1 = prep
    keys, queries, values = [], [], []
    for t in tiles:
        terms = halo_terms(halo[t], par[t][0], not_fresh0)
        lines = par_lines[t, :16]
        q, k, v0, v1 = [
            convolve(
                mixed[t, c * 128 : (c + 1) * 128],
                None,
                turned_dot(terms, halo_tab[c]),
                spread_taps(lines, tap_tab[c]),
                masks,
            )
            for c in range(4)
        ]
        keys.append(unit_keys(k))
        queries.append(q)
        values.append((v0, v1))
        qo[t] = q
        rows[t] = jnp.concatenate(
            [keep0[2 * t : 2 * t + 2], grown[2 * t : 2 * t + 2], keep1[2 * t : 2 * t + 2], strength[2 * t : 2 * t + 2]],
            axis=0,
        )
    solved, faded, scores = solve_tiles(keys, queries, prep)
    sides = halves((SPAN, TILE))
    for t in tiles:
        stacks = []
        for r in range(RATIO):
            at = t * RATIO + r
            s, lift = strength[at : at + 1], strength[at : at + 1] * grown[at : at + 1]
            stacked = jnp.concatenate(
                [lift * keys[t].astype(F32), s * values[t][r].astype(F32)], axis=0
            )
            stacks.append(stacked.astype(BF16))
            sc[t, :, r * TILE : (r + 1) * TILE] = scores[at]
            ft[at] = faded[at]
        out = block_dot(jnp.concatenate(stacks, axis=1), solved[t], sides).astype(BF16)
        for r in range(RATIO):
            wk[t * RATIO + r] = out[:DK, r * TILE : (r + 1) * TILE]
            wv[t * RATIO + r] = out[DK:, r * TILE : (r + 1) * TILE]


def token_prep(req, me, mixed, dec, beta, halo, par):
    heads = mixed.shape[0]
    smem = pl.BlockSpec(memory_space=pltpu.SMEM)

    def tiles(count, *rest):
        return pl.BlockSpec((count,) + rest, lambda g: (g,) + (0,) * len(rest))

    square = jax.ShapeDtypeStruct((heads * RATIO, 128, 128), BF16)
    return pl.pallas_call(
        token_prep_kernel,
        grid=(heads // WIDE,),
        in_specs=[
            smem,
            smem,
            tiles(WIDE, 512, TILE),
            tiles(WIDE, RATIO, TILE),
            tiles(WIDE, RATIO, TILE),
            tiles(WIDE, 16, TILE),
            pl.BlockSpec((WIDE, 32, 128), lambda g: (g, 4, 0)),
        ],
        out_specs=[tiles(WIDE * RATIO, 128, 128)] * 2
        + [tiles(WIDE, SPAN, RATIO * TILE), tiles(WIDE * RATIO, 128, 128)]
        + [tiles(WIDE, 128, 128), tiles(WIDE, 8, 128)],
        out_shape=[square] * 2
        + [
            jax.ShapeDtypeStruct((heads, SPAN, RATIO * TILE), BF16),
            square,
            jax.ShapeDtypeStruct((heads, 128, 128), BF16),
            jax.ShapeDtypeStruct((heads, 8, 128), F32),
        ],
        compiler_params=params(),
        cost_estimate=pl.CostEstimate(flops=10**10, bytes_accessed=8 << 20, transcendentals=10**6),
        name="token_prep",
    )(req, me, mixed, dec, beta, halo, par)


def head_prep_kernel(req, kp, previous, par_lines, sol, ft, gs, rows):
    step = pl.program_id(0)
    depth, own = kp.shape[0], kp.shape[1]
    tap_tab = tap_tables()
    order = [(d, h) for d in range(depth) for h in range(own)]
    par = [parameters(par_lines[h]) for h in range(own)]

    small = [kp[d, h, DK:].astype(F32) for d, h in order]
    prep = row_prep(
        jnp.concatenate([s[28:30] for s in small], axis=0),
        jnp.concatenate([s[30:32] for s in small], axis=0),
        jnp.concatenate([par[h][1] for d, h in order], axis=0),
        jnp.concatenate([par[h][2] for d, h in order], axis=0),
    )
    cum, strength, grown, fade, keep0, keep1 = prep
    keys = []
    taps = [spread_taps(par_lines[h, :16], tap_tab[1]) for h in range(own)]
    for d in range(depth):
        block = (step * depth + d) * 2
        masks = conv_masks(is_fresh(req, block), is_fresh(req, block + 1))
        for h in range(own):
            before = (kp[d - 1, h, :DK] if d else previous[0, h]).astype(F32)
            keys.append(unit_keys(convolve(kp[d, h, :DK], before, None, taps[h], masks)))
    solved, faded, unused = solve_tiles(keys, None, prep)
    sides = halves((SPAN, TILE))
    for t, (d, h) in enumerate(order):
        rows[d, h] = jnp.concatenate(
            [keep0[2 * t : 2 * t + 2], keep1[2 * t : 2 * t + 2], strength[2 * t : 2 * t + 2], strength[2 * t : 2 * t + 2]],
            axis=0,
        )
        scaled = []
        for r in range(RATIO):
            at = t * RATIO + r
            lift = strength[at : at + 1] * grown[at : at + 1]
            scaled.append((lift * keys[t].astype(F32)).astype(BF16))
        wide = block_dot(jnp.concatenate(scaled, axis=1), solved[t], sides).astype(BF16)
        sol[d, h] = solved[t]
        for r in range(RATIO):
            at = t * RATIO + r
            drop = dot(wide[:, r * TILE : (r + 1) * TILE], both_blocks(faded[at])).astype(BF16)
            gs[d, h, r, 0] = drop[:, :DK]
            gs[d, h, r, 1] = drop[:, DK:]
            ft[d, h, r] = faded[at]


def head_prep(req, kp, par):
    n, own = kp.shape[:2]
    depth = WIDE // own
    smem = pl.BlockSpec(memory_space=pltpu.SMEM)

    def tiles(*rest):
        return pl.BlockSpec((depth, own) + rest, lambda g: (g, 0) + (0,) * len(rest))

    square = jax.ShapeDtypeStruct((n, own, RATIO, 128, 128), BF16)
    return pl.pallas_call(
        head_prep_kernel,
        grid=(n // depth,),
        in_specs=[
            smem,
            tiles(KROWS, TILE),
            pl.BlockSpec((1, own, DK, TILE), lambda g: (jnp.maximum(g * depth - 1, 0), 0, 0, 0)),
            pl.BlockSpec((own, 32, 128), lambda g: (0, 0, 0)),
        ],
        out_specs=[
            tiles(SPAN, RATIO * TILE),
            tiles(RATIO, 128, 128),
            tiles(RATIO, 2, 128, 128),
            tiles(8, 128),
        ],
        out_shape=[
            jax.ShapeDtypeStruct((n, own, SPAN, RATIO * TILE), BF16),
            square,
            jax.ShapeDtypeStruct((n, own, RATIO, 2, 128, 128), BF16),
            jax.ShapeDtypeStruct((n, own, 8, 128), F32),
        ],
        compiler_params=params(),
        cost_estimate=pl.CostEstimate(flops=10**10, bytes_accessed=6 << 20, transcendentals=10**6),
        name="head_prep",
    )(req, kp, kp, par)


def head_chain_kernel(req, me, par_lines, sol, ft, gs, rows, *refs):
    n = refs[-5].shape[0]
    arrived, (sin, ends, tails, state, vp) = refs[:n], refs[n:]
    step = pl.program_id(0)
    depth, own = sol.shape[0], sol.shape[1]

    @pl.when(step == 0)
    def first():
        for k, one in enumerate(arrived):
            vp[me[0] ^ k] = one[...]
            tails[me[0] ^ k] = one[:, 256:]

    tap_tab = tap_tables()
    sides = halves((SPAN, TILE))
    heads = [(h, r) for h in range(own) for r in range(RATIO)]
    taps = [spread_taps(par_lines[h, :16], tap_tab[2 + r]) for h, r in heads]
    current = [state[v] for v in range(len(heads))]
    for d in range(depth):
        tile = step * depth + d
        past = jnp.maximum(tile - 1, 0)
        fresh = [is_fresh(req, tile * 2), is_fresh(req, tile * 2 + 1)]
        masks = conv_masks(fresh[0], fresh[1])
        gains = []
        for h in range(own):
            scaled = []
            for r in range(RATIO):
                raw = vp[tile, h, r * DV : (r + 1) * DV]
                before = vp[past, h, r * DV : (r + 1) * DV].astype(F32)
                value = convolve(raw, before, None, taps[h * RATIO + r], masks)
                scaled.append((rows[d, h, 4 + r : 5 + r] * value.astype(F32)).astype(BF16))
            wide = block_dot(jnp.concatenate(scaled, axis=1), sol[d, h], sides).astype(BF16)
            for r in range(RATIO):
                gains.append(dot(wide[:, r * TILE : (r + 1) * TILE], both_blocks(ft[d, h, r])))
        for half in range(2):
            for h in range(own):
                now = [jnp.where(fresh[half], 0.0, current[h * RATIO + r]) for r in range(RATIO)]
                lost = dot(
                    jnp.concatenate([x.astype(BF16) for x in now], axis=1),
                    corner(gs[d, h, 0, half], gs[d, h, 1, half]),
                )
                for r in range(RATIO):
                    v = h * RATIO + r
                    keep = rows[d, h, 2 * half + r : 2 * half + r + 1]
                    gain = gains[v][:, half * DV : (half + 1) * DV]
                    current[v] = keep * now[r] + (gain - lost[:, r * TILE : (r + 1) * TILE])
                    ends[d * 2 + half, v] = current[v].astype(BF16)
        onward = lax.rem(tile + 1, n)
        for v in range(len(heads)):
            sin[onward, v] = current[v].astype(BF16)
    for v in range(len(heads)):
        state[v] = current[v]


def head_chain(req, me, par, sol, ft, gs, rows, arrived):
    n, own = sol.shape[:2]
    depth = WIDE // own
    smem = pl.BlockSpec(memory_space=pltpu.SMEM)

    def tiles(*rest):
        return pl.BlockSpec((depth, own) + rest, lambda g: (g, 0) + (0,) * len(rest))

    return pl.pallas_call(
        head_chain_kernel,
        grid=(n // depth,),
        in_specs=[
            smem,
            smem,
            pl.BlockSpec((own, 32, 128), lambda g: (0, 0, 0)),
            tiles(SPAN, RATIO * TILE),
            tiles(RATIO, 128, 128),
            tiles(RATIO, 2, 128, 128),
            tiles(8, 128),
        ]
        + [pl.BlockSpec((own, VROWS, TILE), lambda g: (0, 0, 0))] * n,
        out_specs=[
            pl.BlockSpec((n, own * RATIO, 128, 128), lambda g: (0, 0, 0, 0)),
            pl.BlockSpec((2 * depth, own * RATIO, 128, 128), lambda g: (g, 0, 0, 0)),
            pl.BlockSpec((n, own, 32, TILE), lambda g: (0, 0, 0, 0)),
        ],
        out_shape=[
            jax.ShapeDtypeStruct((n, own * RATIO, 128, 128), BF16),
            jax.ShapeDtypeStruct((2 * n, own * RATIO, 128, 128), BF16),
            jax.ShapeDtypeStruct((n, own, 32, TILE), BF16),
        ],
        scratch_shapes=[
            pltpu.VMEM((own * RATIO, 128, 128), F32),
            pltpu.VMEM((n, own, VROWS, TILE), BF16),
        ],
        compiler_params=params(),
        cost_estimate=pl.CostEstimate(flops=3 * 10**9, bytes_accessed=8 << 20, transcendentals=10**6),
        name="head_chain",
    )(req, me, par, sol, ft, gs, rows, *arrived)


def choose_kernel(req, rep, fin, me, ends, kt, *refs):
    outs, counts = refs[:-1], refs[-1]
    own, heads = kt.shape[1], ends.shape[1]
    base = heads * 128
    for i, out in enumerate(outs):
        out[...] = jnp.zeros_like(out)
        counts[i] = 0
    end = jnp.int32(-1)
    for j in range(req.shape[1]):
        end = end + req[0, j]
        where = rep[0, j] ^ me[0]
        place = jnp.minimum(counts[where], CAP - 1)
        done = fin[0, j] > 0
        counts[where] = counts[where] + jnp.where(done, 1, 0)
        for i, out in enumerate(outs):

            @pl.when(done & (where == i))
            def take():
                for v in range(heads):
                    out[place, v * 128 : (v + 1) * 128] = ends[end, v]
                for h in range(own):
                    lines = kt[end >> 1, h].astype(F32)
                    lines = jnp.where((end & 1) > 0, lines[16:], lines[:16]).astype(BF16)
                    out[place, base + h * 16 : base + h * 16 + 16] = lines

    for i, out in enumerate(outs):
        number = jnp.full((16, 128), counts[i], jnp.int32).astype(F32).astype(BF16)
        for c in range(CAP):
            out[c, base + own * 16 :] = number


def choose(req, rep, fin, me, ends, tails, replicas):
    own = tails.shape[1]
    smem = pl.BlockSpec(memory_space=pltpu.SMEM)
    lines = own * RATIO * 128 + own * 16 + 16
    return pl.pallas_call(
        choose_kernel,
        grid=(1,),
        in_specs=[
            smem,
            smem,
            smem,
            smem,
            pl.BlockSpec(ends.shape, lambda g: (0, 0, 0, 0)),
            pl.BlockSpec(tails.shape, lambda g: (0, 0, 0, 0)),
        ],
        out_specs=[pl.BlockSpec((CAP, lines, 128), lambda g: (0, 0, 0))] * replicas,
        out_shape=[jax.ShapeDtypeStruct((CAP, lines, 128), BF16)] * replicas,
        scratch_shapes=[pltpu.SMEM((replicas,), jnp.int32)],
        compiler_params=params(),
        cost_estimate=pl.CostEstimate(flops=10**6, bytes_accessed=4 << 20, transcendentals=0),
        name="choose",
    )(req, rep, fin, me, ends, tails)


def token_out_kernel(req, me, sin, wk, wv, sc, ft, qs, rows, gate, gain, out):
    stay0 = jnp.where(is_fresh(req, me[0] * 2), 0.0, 1.0)
    stay1 = jnp.where(is_fresh(req, me[0] * 2 + 1), 0.0, 1.0)
    lane = iota((DV, TILE), 1)
    early = lane < SPAN
    sides = halves((SPAN, TILE))
    units = [(t, r) for t in range(qs.shape[0]) for r in range(RATIO)]
    both = [jnp.concatenate([wk[t * RATIO + r], qs[t]], axis=1) for t, r in units]
    enter = [sin[t * RATIO + r].astype(F32) * stay0 for t, r in units]
    first = [dot(e.astype(BF16), b) for e, b in zip(enter, both)]
    wide = [wv[t * RATIO + r].astype(F32) for t, r in units]
    new0 = [jnp.where(early, w - f[:, :TILE], 0.0) for w, f in zip(wide, first)]
    tiles = range(qs.shape[0])
    pairs = [
        dot(
            jnp.concatenate([new0[2 * t].astype(BF16), new0[2 * t + 1].astype(BF16)], axis=1),
            corner(ft[2 * t], ft[2 * t + 1]),
        )
        for t in tiles
    ]
    middle = [
        (rows[t, r : r + 1] * e + pairs[t][:, r * TILE : (r + 1) * TILE]) * stay1
        for (t, r), e in zip(units, enter)
    ]
    second = [dot(m.astype(BF16), b) for m, b in zip(middle, both)]
    new = [
        jnp.where(early, x, w - s[:, :TILE]).astype(BF16) for x, w, s in zip(new0, wide, second)
    ]
    near = [
        block_dot(jnp.concatenate([new[2 * t], new[2 * t + 1]], axis=1), sc[t], sides) for t in tiles
    ]
    for at, (t, r) in enumerate(units):
        core = rows[t, 2 + r : 3 + r] * jnp.where(early, first[at][:, TILE:], second[at][:, TILE:])
        core = (core + near[t][:, r * TILE : (r + 1) * TILE]).astype(BF16).astype(F32)
        inverse_rms = lax.rsqrt(jnp.mean(core * core, axis=0, keepdims=True) + EPSILON)
        z = gate[t, r * DV : (r + 1) * DV].astype(F32)
        result = core * inverse_rms * gain[...] * (z / (1.0 + jnp.exp(-z)))
        out[t, r * DV : (r + 1) * DV] = result.astype(BF16)


def token_out(req, me, sin, wk, wv, sc, ft, qs, rows, gate, gain):
    heads = qs.shape[0]
    smem = pl.BlockSpec(memory_space=pltpu.SMEM)

    def tiles(count, *rest):
        return pl.BlockSpec((count,) + rest, lambda g: (g,) + (0,) * len(rest))

    return pl.pallas_call(
        token_out_kernel,
        grid=(heads // STEP,),
        in_specs=[smem, smem]
        + [tiles(STEP * RATIO, 128, 128)] * 3
        + [tiles(STEP, SPAN, RATIO * TILE), tiles(STEP * RATIO, 128, 128)]
        + [
            tiles(STEP, 128, 128),
            tiles(STEP, 8, 128),
            tiles(STEP, 256, TILE),
            pl.BlockSpec((128, 128), lambda g: (0, 0)),
        ],
        out_specs=tiles(STEP, 256, TILE),
        out_shape=jax.ShapeDtypeStruct((heads, 256, TILE), BF16),
        compiler_params=params(),
        cost_estimate=pl.CostEstimate(flops=10**9, bytes_accessed=8 << 20, transcendentals=10**6),
        name="token_out",
    )(req, me, sin, wk, wv, sc, ft, qs, rows, gate, gain)


def land_kernel(me, *refs):
    got, (states, tails, counts) = refs[:-3], refs[-3:]
    slot = pl.program_id(0)
    heads, own = states.shape[1], tails.shape[1]
    base = heads * 128

    @pl.when(slot == 0)
    def first():
        for i, one in enumerate(got):
            number = jnp.max(one[0, base + own * 16 :].astype(F32))
            counts[i] = number.astype(jnp.int32)

    start = jnp.int32(0)
    source, place = jnp.int32(-1), jnp.int32(0)
    for p in range(len(got)):
        away = me[0] ^ p
        number = counts[away]
        inside = (slot >= start) & (slot < start + number)
        source = jnp.where(inside, away, source)
        place = jnp.where(inside, slot - start, place)
        start = start + number
    place = jnp.clip(place, 0, CAP - 1)
    for i, one in enumerate(got):

        @pl.when(source == i)
        def take():
            for v in range(heads):
                block = one[place, v * 128 : (v + 1) * 128].astype(F32)
                states[0, v] = jnp.transpose(block)
            for h in range(own):
                tails[0, h] = one[place, base + h * 16 : base + h * 16 + 16]

    @pl.when(source < 0)
    def clear():
        states[...] = jnp.zeros_like(states)
        tails[...] = jnp.zeros_like(tails)


def land(me, got, heads, own):
    lines = got[0].shape[1]
    slots = len(got) * CAP
    smem = pl.BlockSpec(memory_space=pltpu.SMEM)
    return pl.pallas_call(
        land_kernel,
        grid=(slots,),
        in_specs=[smem] + [pl.BlockSpec((CAP, lines, 128), lambda g: (0, 0, 0))] * len(got),
        out_specs=[
            pl.BlockSpec((1, heads, 128, 128), lambda g: (g, 0, 0, 0)),
            pl.BlockSpec((1, own, 16, 128), lambda g: (g, 0, 0, 0)),
        ],
        out_shape=[
            jax.ShapeDtypeStruct((slots, heads, 128, 128), F32),
            jax.ShapeDtypeStruct((slots, own, 16, 128), BF16),
        ],
        scratch_shapes=[pltpu.SMEM((len(got),), jnp.int32)],
        compiler_params=params(),
        cost_estimate=pl.CostEstimate(flops=10**6, bytes_accessed=4 << 20, transcendentals=0),
        name="land",
    )(me, *got)


def body(
    mixed,
    decay_in,
    beta_in,
    gate_z,
    conv_weight,
    a_log,
    dt_bias,
    norm_gain,
    req_blocks,
    replica_of,
    finished,
):
    n = lax.axis_size("seq")
    replicas = lax.axis_size("rep")
    heads = mixed.shape[1]
    own = heads // n
    me = lax.axis_index("seq").astype(jnp.int32).reshape(1)
    kpack, par = pack_keys(mixed[0], decay_in[0], beta_in[0], conv_weight, a_log, dt_bias)
    halo, *vpack = pack_values(me, mixed[0], n)
    kp = lax.all_to_all(kpack.reshape(n, own, KROWS, TILE), "seq", 0, 0, tiled=True)
    vp = [vpack[0]] + [
        lax.ppermute(vpack[k], "seq", [(i, i ^ k) for i in range(n)]) for k in range(1, n)
    ]
    halo = lax.ppermute(halo, "seq", [(i, i + 1) for i in range(n - 1)])
    wk, wv, sc, ft, qs, rows = token_prep(
        req_blocks, me, mixed[0], decay_in[0], beta_in[0], halo, kp.reshape(heads, KROWS, TILE)
    )
    hsol, hft, hgs, hrows = head_prep(req_blocks, kp, par)
    sin, ends, ktails = head_chain(req_blocks, me, par, hsol, hft, hgs, hrows, vp)
    sin = lax.all_to_all(sin, "seq", 0, 0, tiled=True)
    my_rep = lax.axis_index("rep").astype(jnp.int32).reshape(1)
    send = choose(req_blocks, replica_of, finished, my_rep, ends, ktails, replicas)
    got = [send[0]] + [
        lax.ppermute(send[k], "rep", [(i, i ^ k) for i in range(replicas)])
        for k in range(1, replicas)
    ]
    states, tails = land(my_rep, got, own * RATIO, own)
    tails = tails.reshape(replicas * CAP, own, 4, 512)[:, :, : KERNEL - 1].transpose(0, 2, 1, 3)
    gain = jnp.broadcast_to(norm_gain[:, None], (DV, TILE))
    out = token_out(
        req_blocks,
        me,
        sin.reshape(heads * RATIO, 128, 128),
        wk,
        wv,
        sc,
        ft,
        qs,
        rows,
        gate_z[0],
        gain,
    )
    return (out[None], states[None], tails[None])


def solution(mesh):
    placed = (
        P("rep", None, None, "seq"),
        P("rep", None, None, "seq"),
        P("rep", None, None, "seq"),
        P("rep", None, None, "seq"),
        P(None, "seq", None),
        P("seq"),
        P("seq"),
        P(),
        P("rep", None),
        P("rep", None),
        P("rep", None),
    )
    return jax.shard_map(
        body,
        mesh=mesh,
        in_specs=placed,
        out_specs=(
            P("rep", None, None, "seq"),
            P("rep", None, "seq", None, None),
            P("rep", None, None, "seq", None),
        ),
        check_vma=False,
    )
```

```python
import jax
import jax.numpy as jnp
from jax import lax
from jax.experimental import pallas as pl
from jax.experimental.pallas import tpu as pltpu
from jax.sharding import PartitionSpec as P

DK = 128
DV = 128
KERNEL = 4
SPAN = 64
CAP = 2
RATIO = 2
TILE = 2 * SPAN
KROWS = 160
VROWS = 288
STEP = 4
WIDE = 8
EPSILON = 1e-06
F32 = jnp.float32
BF16 = jnp.bfloat16
VMEM_LIMIT = 56 * 1024 * 1024


def params(**kwargs):
    return pltpu.CompilerParams(vmem_limit_bytes=VMEM_LIMIT, **kwargs)


def iota(shape, dim):
    return lax.broadcasted_iota(jnp.int32, shape, dim)


def dot(left, right):
    return jnp.dot(left, right, preferred_element_type=F32)


def split(wide):
    high = wide.astype(BF16)
    return high, (wide - high.astype(F32)).astype(BF16)


def halves(shape):
    first = iota(shape, len(shape) - 1) < SPAN
    return jnp.where(first, 1.0, 0.0).astype(BF16), jnp.where(first, 0.0, 1.0).astype(BF16)


def corner(first, second):
    none = jnp.zeros_like(first)
    top = jnp.concatenate([first, none], axis=1)
    return jnp.concatenate([top, jnp.concatenate([none, second], axis=1)], axis=0)


def diagonal(packed, masks):
    squares = []
    for r in range(RATIO):
        one = packed[:, r * TILE : (r + 1) * TILE]
        squares.append(jnp.concatenate([one * masks[0], one * masks[1]], axis=0))
    return corner(*squares)


def block_dot(left, right, masks):
    return dot(left, diagonal(right, masks))


def parameter_lines(h, cw, alog, dtb):
    taps = cw[:, h].astype(F32)
    rows = [taps[tap : tap + 1, cg * 128 : (cg + 1) * 128] for tap in range(KERNEL) for cg in range(4)]
    rest = jnp.concatenate(
        [jnp.full((1, 128), ref[h * RATIO + r], F32) for ref in (alog, dtb) for r in range(RATIO)], axis=0
    )
    parts = []
    for _ in range(3):
        part = rest.astype(BF16).astype(F32)
        rest = rest - part
        parts.append(part)
    return jnp.concatenate(rows + parts + [jnp.zeros((4, 128), F32)], axis=0)


def parameters(lines):
    wide = lines.astype(F32)
    rest = wide[16:20] + wide[20:24] + wide[24:28]
    return wide[:16], rest[:RATIO], rest[RATIO:]


def pack_keys_kernel(mixed, dec, beta, cw, alog, dtb, kout, pout):
    row = iota((32, TILE), 0)
    own = pout.shape[0]
    lines = [parameter_lines(h, cw, alog, dtb) for h in range(own)]
    for t in range(mixed.shape[0]):
        kout[t, :DK] = mixed[t]
        rest = lines[t % own]
        d, b = dec[t].astype(F32), beta[t].astype(F32)
        for r in range(RATIO):
            rest = jnp.where(row == 28 + r, d[r : r + 1], rest)
            rest = jnp.where(row == 30 + r, b[r : r + 1], rest)
        kout[t, DK:] = rest.astype(BF16)

    @pl.when(pl.program_id(0) == 0)
    def first():
        for h in range(own):
            pout[h] = lines[h].astype(BF16)


def pack_keys(mixed, dec, beta, cw, alog, dtb):
    heads = mixed.shape[0]
    own = cw.shape[1]
    step = heads // 2
    smem = pl.BlockSpec(memory_space=pltpu.SMEM)
    return pl.pallas_call(
        pack_keys_kernel,
        grid=(heads // step,),
        in_specs=[
            pl.BlockSpec((step, DK, TILE), lambda g: (g, 1, 0)),
            pl.BlockSpec((step, RATIO, TILE), lambda g: (g, 0, 0)),
            pl.BlockSpec((step, RATIO, TILE), lambda g: (g, 0, 0)),
            pl.BlockSpec((KERNEL, own, 512), lambda g: (0, 0, 0)),
            smem,
            smem,
        ],
        out_specs=[
            pl.BlockSpec((step, KROWS, TILE), lambda g: (g, 0, 0)),
            pl.BlockSpec((own, 32, 128), lambda g: (0, 0, 0)),
        ],
        out_shape=[
            jax.ShapeDtypeStruct((heads, KROWS, TILE), BF16),
            jax.ShapeDtypeStruct((own, 32, 128), BF16),
        ],
        compiler_params=params(),
        cost_estimate=pl.CostEstimate(flops=10**6, bytes_accessed=2 << 20, transcendentals=0),
        name="pack_keys",
    )(mixed, dec, beta, cw, alog, dtb)


def pack_values_kernel(me, mixed, hout, *outs):
    step = pl.program_id(0)
    own = outs[0].shape[0]
    row, tok = iota((TILE, 128), 1), iota((TILE, 128), 0)
    place = row & 15
    picks = []
    for cg in range(4):
        hit = (row < 32) & (place < 12) & ((place & 3) == cg)
        hit = hit & (tok == (row >> 4) * SPAN + 61 + (place >> 2))
        picks.append(jnp.where(hit, 1.0, 0.0).astype(BF16))
    all_tails = []
    for h in range(mixed.shape[0]):
        tails = dot(mixed[h, :128], picks[0])
        for cg in range(1, 4):
            tails = tails + dot(mixed[h, cg * 128 : (cg + 1) * 128], picks[cg])
        all_tails.append(jnp.transpose(tails)[:32].astype(BF16))
        hout[h] = all_tails[h][16:]
    for i, out in enumerate(outs):

        @pl.when((step == i // 4) & ((me[0] & 3) == 0))
        def put0():
            put(mixed, all_tails, out, (i & 3) ^ 0, own)

        @pl.when((step == i // 4) & ((me[0] & 3) == 1))
        def put1():
            put(mixed, all_tails, out, (i & 3) ^ 1, own)

        @pl.when((step == i // 4) & ((me[0] & 3) == 2))
        def put2():
            put(mixed, all_tails, out, (i & 3) ^ 2, own)

        @pl.when((step == i // 4) & ((me[0] & 3) == 3))
        def put3():
            put(mixed, all_tails, out, (i & 3) ^ 3, own)


def put(mixed, all_tails, out, place, own):
    for h in range(own):
        out[h, :256] = mixed[place * own + h, 2 * DK :]
        out[h, 256:] = all_tails[place * own + h]


def pack_values(me, mixed, n):
    heads = mixed.shape[0]
    own = heads // n
    return pl.pallas_call(
        pack_values_kernel,
        grid_spec=pltpu.PrefetchScalarGridSpec(
            num_scalar_prefetch=1,
            grid=(n // 4,),
            in_specs=[pl.BlockSpec((4 * own, 512, TILE), lambda g, me: ((me[0] >> 2) ^ g, 0, 0))],
            out_specs=[pl.BlockSpec((4 * own, 16, TILE), lambda g, me: ((me[0] >> 2) ^ g, 0, 0))]
            + [pl.BlockSpec((own, VROWS, TILE), lambda g, me: (0, 0, 0))] * n,
        ),
        out_shape=[jax.ShapeDtypeStruct((heads, 16, TILE), BF16)]
        + [jax.ShapeDtypeStruct((own, VROWS, TILE), BF16)] * n,
        compiler_params=params(),
        cost_estimate=pl.CostEstimate(flops=10**8, bytes_accessed=4 << 20, transcendentals=0),
        name="pack_values",
    )(me, mixed)


def is_fresh(req, block):
    start = jnp.int32(0)
    fresh = jnp.bool_(False)
    for j in range(req.shape[1]):
        fresh = fresh | (start == block)
        start = start + req[0, j]
    return fresh


def tap_tables():
    row, part = iota((16, 4 * 128), 0), iota((16, 4 * 128), 1) >> 7
    hits = [((row & 3) == cg) & ((row >> 2) == part) for cg in range(4)]
    return [jnp.where(hit, 1.0, 0.0).astype(BF16) for hit in hits]


def turned_dot(rows, table):
    return lax.dot_general(rows, table, (((0,), (0,)), ((), ())), preferred_element_type=F32)


def spread_taps(par, table):
    both = turned_dot(par, table)
    return [both[:, tap * 128 : (tap + 1) * 128] for tap in range(KERNEL)]


def halo_terms(halo, par, not_fresh0):
    x = [halo[4 * k : 4 * k + 4].astype(F32) * not_fresh0 for k in range(3)]
    w = [par[4 * k : 4 * k + 4] for k in range(3)]
    terms = [w[0] * x[0] + w[1] * x[1] + w[2] * x[2], w[0] * x[1] + w[1] * x[2], w[0] * x[2]]
    none = jnp.zeros((1, 128), F32)
    rows = [r for cg in range(4) for r in [t[cg : cg + 1] for t in terms] + [none]]
    return jnp.transpose(jnp.concatenate(rows + [jnp.zeros((112, 128), F32)], axis=0))


def convolve(raw, before, terms, taps, masks):
    lane = iota((1, TILE), 1)
    cur = raw.astype(F32)
    total = taps[KERNEL - 1] * cur
    if terms is not None:
        total = total + terms
    for back in range(1, KERNEL):
        moved = cur if before is None else jnp.where(lane >= TILE - back, before, cur)
        total = total + taps[KERNEL - 1 - back] * (pltpu.roll(moved, back, 1) * masks[back - 1])
    return (total / (1.0 + jnp.exp(-total))).astype(BF16)


def conv_masks(cut0, cut1):
    lane = iota((1, TILE), 1)
    masks = []
    for back in range(1, KERNEL):
        gone = ((lane < back) & cut0) | ((lane >= SPAN) & (lane < SPAN + back) & cut1)
        masks.append(jnp.where(gone, 0.0, 1.0))
    return masks


def row_prep(dec, beta, alog, dtb):
    lane = iota(dec.shape, 1)
    x = dec + dtb
    decay = -jnp.exp(alog) * (jnp.maximum(x, 0.0) + jnp.log1p(jnp.exp(-jnp.abs(x))))
    cum = decay
    for shift in (1, 2, 4, 8, 16, 32):
        cum = cum + jnp.where((lane & (SPAN - 1)) >= shift, pltpu.roll(cum, shift, 1), 0.0)
    strength = 1.0 / (1.0 + jnp.exp(-beta))
    grown = jnp.exp(cum)
    close0, close1 = cum[:, SPAN - 1 : SPAN], cum[:, TILE - 1 :]
    fade = jnp.exp(jnp.where(lane < SPAN, close0, close1) - cum)
    keep0 = jnp.exp(jnp.broadcast_to(close0, cum.shape))
    keep1 = jnp.exp(jnp.broadcast_to(close1, cum.shape))
    return cum, strength, grown, fade, keep0, keep1


def unit_inverses(systems):
    shape = (SPAN, RATIO * TILE)
    row, col = iota(shape, 0), iota(shape, 1) & (SPAN - 1)
    near = (row >> 4) == (col >> 4)
    eye = jnp.where(row == col, 1.0, 0.0)
    masks = halves((SPAN, TILE))

    def low(arrays):
        return [a.astype(BF16) for a in arrays]

    def stack(pair):
        return jnp.concatenate(pair, axis=0)

    total = [jnp.where(near, eye - a, 0.0) for a in systems]
    power = low([jnp.where(near, -a, 0.0) for a in systems])
    power = low([block_dot(p, p, masks) for p in power])
    for _ in range(2):
        both = [block_dot(stack([t, p]), p, masks) for t, p in zip(low(total), power)]
        total = [t + b[:SPAN] for t, b in zip(total, both)]
        power = low([b[SPAN:] for b in both])
    total = [t + block_dot(l, p, masks) for t, l, p in zip(total, low(total), power)]
    small = low(total)
    rest = low([jnp.where(near, 0.0, a) for a in systems])
    cross = low([block_dot(t, r, masks) for t, r in zip(small, rest)])
    total = [t - block_dot(x, l, masks) for t, x, l in zip(total, cross, small)]
    cross = low([block_dot(x, x, masks) for x in cross])
    small = low([t + block_dot(x, l, masks) for t, x, l in zip(total, cross, low(total))])
    solved = []
    for a, x in zip(systems, small):
        wide = x.astype(F32)
        parts = block_dot(stack(split(a)), x, masks)
        miss = eye - wide - (parts[:SPAN] + parts[SPAN:])
        solved.append((wide + block_dot(x, miss.astype(BF16), masks)).astype(BF16))
    return solved


def both_blocks(square):
    none = jnp.zeros((SPAN, square.shape[1]), square.dtype)
    first = jnp.concatenate([square[:SPAN], none], axis=0)
    return jnp.concatenate([first, jnp.concatenate([none, square[SPAN:]], axis=0)], axis=1)


def unit_keys(convolved):
    wide = convolved.astype(F32)
    return (wide * lax.rsqrt(jnp.sum(wide * wide, axis=0, keepdims=True) + EPSILON)).astype(BF16)


def solve_tiles(keys, queries, prep):
    cum, strength, grown, fade, keep0, keep1 = prep
    row, lane = iota((SPAN, TILE), 0), iota((SPAN, TILE), 1)
    early = lane < SPAN
    seen = (lane & (SPAN - 1)) >= row
    later = (lane & (SPAN - 1)) > row
    columns = jnp.transpose(jnp.concatenate([cum, fade], axis=0))
    count = cum.shape[0]

    def beside(tall):
        return jnp.where(early, tall[:SPAN], tall[SPAN:])

    systems, faded, scores = [], [], []
    for t, k in enumerate(keys):
        turned = jnp.transpose(k.astype(F32))
        if queries is None:
            gram = beside(dot(turned.astype(BF16), k))
        else:
            prod = dot(turned.astype(BF16), jnp.concatenate([k, queries[t]], axis=1))
            gram, touch = beside(prod[:, :TILE]), beside(prod[:, TILE:])
        pair = []
        for r in range(RATIO):
            at = t * RATIO + r
            diff = cum[at : at + 1] - beside(columns[:, at : at + 1])
            ratio = jnp.where(seen, jnp.exp(jnp.where(seen, diff, 0.0)), 0.0)
            pair.append(jnp.where(later, strength[at : at + 1] * gram * ratio, 0.0))
            if queries is not None:
                scores.append((touch * ratio).astype(BF16))
            faded.append((turned * columns[:, count + at : count + at + 1]).astype(BF16))
        systems.append(jnp.concatenate(pair, axis=1))
    return unit_inverses(systems), faded, scores


def token_prep_kernel(req, me, mixed, dec, beta, halo, par_lines, wk, wv, sc, ft, qo, rows):
    fresh0, fresh1 = is_fresh(req, me[0] * 2), is_fresh(req, me[0] * 2 + 1)
    not_fresh0 = jnp.where(fresh0, 0.0, 1.0)
    masks = conv_masks(True, fresh1)
    tap_tab = tap_tables()
    front = iota((128, TILE), 1) < 3
    tiles = range(mixed.shape[0])
    par = [parameters(par_lines[t]) for t in tiles]

    def gather(pick):
        return jnp.concatenate([pick(t) for t in tiles], axis=0)

    prep = row_prep(
        gather(lambda t: dec[t].astype(F32)),
        gather(lambda t: beta[t].astype(F32)),
        jnp.concatenate([p[1] for p in par], axis=0),
        jnp.concatenate([p[2] for p in par], axis=0),
    )
    cum, strength, grown, fade, keep0, keep1 = prep
    keys, queries, values = [], [], []
    for t in tiles:
        terms = halo_terms(halo[t], par[t][0], not_fresh0)
        lines = par_lines[t, :16]
        q, k, v0, v1 = [
            convolve(
                mixed[t, c * 128 : (c + 1) * 128],
                None,
                jnp.where(front, pltpu.roll(terms, TILE - 4 * c, 1) if c else terms, 0.0),
                spread_taps(lines, tap_tab[c]),
                masks,
            )
            for c in range(4)
        ]
        keys.append(unit_keys(k))
        queries.append(q)
        values.append((v0, v1))
        qo[t] = q
        rows[t] = jnp.concatenate(
            [keep0[2 * t : 2 * t + 2], grown[2 * t : 2 * t + 2], keep1[2 * t : 2 * t + 2], strength[2 * t : 2 * t + 2]],
            axis=0,
        )
    solved, faded, scores = solve_tiles(keys, queries, prep)
    sides = halves((SPAN, TILE))
    for t in tiles:
        stacks = []
        for r in range(RATIO):
            at = t * RATIO + r
            s, lift = strength[at : at + 1], strength[at : at + 1] * grown[at : at + 1]
            stacked = jnp.concatenate(
                [lift * keys[t].astype(F32), s * values[t][r].astype(F32)], axis=0
            )
            stacks.append(stacked.astype(BF16))
            sc[t, :, r * TILE : (r + 1) * TILE] = scores[at]
            ft[at] = faded[at]
        out = block_dot(jnp.concatenate(stacks, axis=1), solved[t], sides).astype(BF16)
        for r in range(RATIO):
            wk[t * RATIO + r] = out[:DK, r * TILE : (r + 1) * TILE]
            wv[t * RATIO + r] = out[DK:, r * TILE : (r + 1) * TILE]


def token_prep(req, me, mixed, dec, beta, halo, par):
    heads = mixed.shape[0]
    smem = pl.BlockSpec(memory_space=pltpu.SMEM)

    def tiles(count, *rest):
        return pl.BlockSpec((count,) + rest, lambda g: (g,) + (0,) * len(rest))

    square = jax.ShapeDtypeStruct((heads * RATIO, 128, 128), BF16)
    return pl.pallas_call(
        token_prep_kernel,
        grid=(heads // WIDE,),
        in_specs=[
            smem,
            smem,
            tiles(WIDE, 512, TILE),
            tiles(WIDE, RATIO, TILE),
            tiles(WIDE, RATIO, TILE),
            tiles(WIDE, 16, TILE),
            pl.BlockSpec((WIDE, 32, 128), lambda g: (g, 4, 0)),
        ],
        out_specs=[tiles(WIDE * RATIO, 128, 128)] * 2
        + [tiles(WIDE, SPAN, RATIO * TILE), tiles(WIDE * RATIO, 128, 128)]
        + [tiles(WIDE, 128, 128), tiles(WIDE, 8, 128)],
        out_shape=[square] * 2
        + [
            jax.ShapeDtypeStruct((heads, SPAN, RATIO * TILE), BF16),
            square,
            jax.ShapeDtypeStruct((heads, 128, 128), BF16),
            jax.ShapeDtypeStruct((heads, 8, 128), F32),
        ],
        compiler_params=params(),
        cost_estimate=pl.CostEstimate(flops=10**10, bytes_accessed=8 << 20, transcendentals=10**6),
        name="token_prep",
    )(req, me, mixed, dec, beta, halo, par)


def head_prep_kernel(req, kp, previous, par_lines, sol, ft, gs, rows):
    step = pl.program_id(0)
    depth, own = kp.shape[0], kp.shape[1]
    tap_tab = tap_tables()
    order = [(d, h) for d in range(depth) for h in range(own)]
    par = [parameters(par_lines[h]) for h in range(own)]

    small = [kp[d, h, DK:].astype(F32) for d, h in order]
    prep = row_prep(
        jnp.concatenate([s[28:30] for s in small], axis=0),
        jnp.concatenate([s[30:32] for s in small], axis=0),
        jnp.concatenate([par[h][1] for d, h in order], axis=0),
        jnp.concatenate([par[h][2] for d, h in order], axis=0),
    )
    cum, strength, grown, fade, keep0, keep1 = prep
    keys = []
    taps = [spread_taps(par_lines[h, :16], tap_tab[1]) for h in range(own)]
    for d in range(depth):
        block = (step * depth + d) * 2
        masks = conv_masks(is_fresh(req, block), is_fresh(req, block + 1))
        for h in range(own):
            before = (kp[d - 1, h, :DK] if d else previous[0, h]).astype(F32)
            keys.append(unit_keys(convolve(kp[d, h, :DK], before, None, taps[h], masks)))
    solved, faded, unused = solve_tiles(keys, None, prep)
    sides = halves((SPAN, TILE))
    for t, (d, h) in enumerate(order):
        rows[d, h] = jnp.concatenate(
            [keep0[2 * t : 2 * t + 2], keep1[2 * t : 2 * t + 2], strength[2 * t : 2 * t + 2], strength[2 * t : 2 * t + 2]],
            axis=0,
        )
        scaled = []
        for r in range(RATIO):
            at = t * RATIO + r
            lift = strength[at : at + 1] * grown[at : at + 1]
            scaled.append((lift * keys[t].astype(F32)).astype(BF16))
        wide = block_dot(jnp.concatenate(scaled, axis=1), solved[t], sides).astype(BF16)
        sol[d, h] = solved[t]
        for r in range(RATIO):
            at = t * RATIO + r
            drop = dot(wide[:, r * TILE : (r + 1) * TILE], both_blocks(faded[at])).astype(BF16)
            gs[d, h, r, 0] = drop[:, :DK]
            gs[d, h, r, 1] = drop[:, DK:]
            ft[d, h, r] = faded[at]


def head_prep(req, kp, par):
    n, own = kp.shape[:2]
    depth = WIDE // own
    smem = pl.BlockSpec(memory_space=pltpu.SMEM)

    def tiles(*rest):
        return pl.BlockSpec((depth, own) + rest, lambda g: (g, 0) + (0,) * len(rest))

    square = jax.ShapeDtypeStruct((n, own, RATIO, 128, 128), BF16)
    return pl.pallas_call(
        head_prep_kernel,
        grid=(n // depth,),
        in_specs=[
            smem,
            tiles(KROWS, TILE),
            pl.BlockSpec((1, own, DK, TILE), lambda g: (jnp.maximum(g * depth - 1, 0), 0, 0, 0)),
            pl.BlockSpec((own, 32, 128), lambda g: (0, 0, 0)),
        ],
        out_specs=[
            tiles(SPAN, RATIO * TILE),
            tiles(RATIO, 128, 128),
            tiles(RATIO, 2, 128, 128),
            tiles(8, 128),
        ],
        out_shape=[
            jax.ShapeDtypeStruct((n, own, SPAN, RATIO * TILE), BF16),
            square,
            jax.ShapeDtypeStruct((n, own, RATIO, 2, 128, 128), BF16),
            jax.ShapeDtypeStruct((n, own, 8, 128), F32),
        ],
        compiler_params=params(),
        cost_estimate=pl.CostEstimate(flops=10**10, bytes_accessed=6 << 20, transcendentals=10**6),
        name="head_prep",
    )(req, kp, kp, par)


def head_chain_kernel(req, me, par_lines, sol, ft, gs, rows, *refs):
    n = len(refs) // 2 - 2
    arrived, outs, (ends, tails, state, vp, sin) = refs[:n], refs[n : 2 * n], refs[2 * n :]
    step = pl.program_id(0)
    depth, own = sol.shape[0], sol.shape[1]

    @pl.when(step == 0)
    def first():
        for k, one in enumerate(arrived):
            vp[me[0] ^ k] = one[...]
            tails[me[0] ^ k] = one[:, 256:]

    tap_tab = tap_tables()
    sides = halves((SPAN, TILE))
    heads = [(h, r) for h in range(own) for r in range(RATIO)]
    taps = [spread_taps(par_lines[h, :16], tap_tab[2 + r]) for h, r in heads]
    current = [state[v] for v in range(len(heads))]
    for d in range(depth):
        tile = step * depth + d
        past = jnp.maximum(tile - 1, 0)
        fresh = [is_fresh(req, tile * 2), is_fresh(req, tile * 2 + 1)]
        masks = conv_masks(fresh[0], fresh[1])
        gains = []
        for h in range(own):
            scaled = []
            for r in range(RATIO):
                raw = vp[tile, h, r * DV : (r + 1) * DV]
                before = vp[past, h, r * DV : (r + 1) * DV].astype(F32)
                value = convolve(raw, before, None, taps[h * RATIO + r], masks)
                scaled.append((rows[d, h, 4 + r : 5 + r] * value.astype(F32)).astype(BF16))
            wide = block_dot(jnp.concatenate(scaled, axis=1), sol[d, h], sides).astype(BF16)
            for r in range(RATIO):
                gains.append(dot(wide[:, r * TILE : (r + 1) * TILE], both_blocks(ft[d, h, r])))
        for half in range(2):
            for h in range(own):
                now = [jnp.where(fresh[half], 0.0, current[h * RATIO + r]) for r in range(RATIO)]
                lost = dot(
                    jnp.concatenate([x.astype(BF16) for x in now], axis=1),
                    corner(gs[d, h, 0, half], gs[d, h, 1, half]),
                )
                for r in range(RATIO):
                    v = h * RATIO + r
                    keep = rows[d, h, 2 * half + r : 2 * half + r + 1]
                    gain = gains[v][:, half * DV : (half + 1) * DV]
                    current[v] = keep * now[r] + (gain - lost[:, r * TILE : (r + 1) * TILE])
                    ends[d * 2 + half, v * 128 : (v + 1) * 128] = current[v].astype(BF16)
        onward = lax.rem(tile + 1, n)
        for v in range(len(heads)):
            sin[onward, v] = current[v].astype(BF16)
    for v in range(len(heads)):
        state[v] = current[v]

    @pl.when(step == pl.num_programs(0) - 1)
    def last():
        for k, one in enumerate(outs):
            one[...] = sin[me[0] ^ k]


def head_chain(req, me, par, sol, ft, gs, rows, arrived):
    n, own = sol.shape[:2]
    depth = WIDE // own
    smem = pl.BlockSpec(memory_space=pltpu.SMEM)

    def tiles(*rest):
        return pl.BlockSpec((depth, own) + rest, lambda g: (g, 0) + (0,) * len(rest))

    return pl.pallas_call(
        head_chain_kernel,
        grid=(n // depth,),
        in_specs=[
            smem,
            smem,
            pl.BlockSpec((own, 32, 128), lambda g: (0, 0, 0)),
            tiles(SPAN, RATIO * TILE),
            tiles(RATIO, 128, 128),
            tiles(RATIO, 2, 128, 128),
            tiles(8, 128),
        ]
        + [pl.BlockSpec((own, VROWS, TILE), lambda g: (0, 0, 0))] * n,
        out_specs=[pl.BlockSpec((own * RATIO, 128, 128), lambda g: (0, 0, 0))] * n
        + [
            pl.BlockSpec((2 * depth, own * RATIO * 128, 128), lambda g: (g, 0, 0)),
            pl.BlockSpec((n, own, 32, TILE), lambda g: (0, 0, 0, 0)),
        ],
        out_shape=[jax.ShapeDtypeStruct((own * RATIO, 128, 128), BF16)] * n
        + [
            jax.ShapeDtypeStruct((2 * n, own * RATIO * 128, 128), BF16),
            jax.ShapeDtypeStruct((n, own, 32, TILE), BF16),
        ],
        scratch_shapes=[
            pltpu.VMEM((own * RATIO, 128, 128), F32),
            pltpu.VMEM((n, own, VROWS, TILE), BF16),
            pltpu.VMEM((n, own * RATIO, 128, 128), BF16),
        ],
        compiler_params=params(),
        cost_estimate=pl.CostEstimate(flops=3 * 10**9, bytes_accessed=8 << 20, transcendentals=10**6),
        name="head_chain",
    )(req, me, par, sol, ft, gs, rows, *arrived)


def choose_kernel(req, rep, fin, me, ends, kt, *refs):
    outs, (counts, places, number, sems) = refs[:-4], refs[-4:]
    own, base = kt.shape[1], ends.shape[1]
    total = req.shape[1]
    for i in range(len(outs)):
        counts[i] = 0
    end = jnp.int32(-1)
    for j in range(total):
        end = end + req[0, j]
        where = rep[0, j] ^ me[0]
        place = jnp.minimum(counts[where], CAP - 1)
        done = fin[0, j] > 0
        counts[where] = counts[where] + jnp.where(done, 1, 0)
        places[0, j] = jnp.where(done, where, -1)
        places[1, j] = place
        places[2, j] = end
    for i in range(len(outs)):
        number[i] = jnp.full((16, 128), counts[i], jnp.int32).astype(F32).astype(BF16)

    def copies(i, j):
        place, last = places[1, j], places[2, j]
        rows = pl.ds(pl.multiple_of((last & 1) * 16, 16), 16)
        yield ends.at[last], outs[i].at[place, pl.ds(0, base)], sems.at[j, 0]
        for h in range(own):
            to = outs[i].at[place, pl.ds(base + h * 16, 16)]
            yield kt.at[last >> 1, h, rows], to, sems.at[j, 1 + h]

    def flags(i, c):
        to = outs[i].at[c, pl.ds(base + own * 16, 16)]
        return pltpu.make_async_copy(number.at[i], to, sems.at[total + i, c])

    for wait in (False, True):
        for i in range(len(outs)):
            for c in range(CAP):
                flags(i, c).wait() if wait else flags(i, c).start()
            for j in range(total):

                @pl.when(places[0, j] == i)
                def move():
                    for source, to, sem in copies(i, j):
                        copy = pltpu.make_async_copy(source, to, sem)
                        copy.wait() if wait else copy.start()


def choose(req, rep, fin, me, ends, tails, replicas):
    own, total = tails.shape[1], req.shape[1]
    smem = pl.BlockSpec(memory_space=pltpu.SMEM)
    far = pl.BlockSpec(memory_space=pl.ANY)
    lines = ends.shape[1] + own * 16 + 16
    return pl.pallas_call(
        choose_kernel,
        in_specs=[smem, smem, smem, smem, far, far],
        out_specs=[far] * replicas,
        out_shape=[jax.ShapeDtypeStruct((CAP, lines, 128), BF16)] * replicas,
        scratch_shapes=[
            pltpu.SMEM((replicas,), jnp.int32),
            pltpu.SMEM((3, total), jnp.int32),
            pltpu.VMEM((replicas, 16, 128), BF16),
            pltpu.SemaphoreType.DMA((total + replicas, max(CAP, 1 + own))),
        ],
        compiler_params=params(),
        cost_estimate=pl.CostEstimate(flops=10**6, bytes_accessed=2 << 20, transcendentals=0),
        name="choose",
    )(req, rep, fin, me, ends, tails)


def token_out_kernel(me, req, wk, wv, sc, ft, qs, rows, gate, norm_gain, *refs):
    arrived, (out, sin) = refs[:-2], refs[-2:]
    arrived = arrived[: len(arrived) // sin.shape[0] * sin.shape[0]]
    share = sin.shape[0]
    for i, one in enumerate(arrived):

        @pl.when(pl.program_id(0) == i // share)
        def take():
            sin[(me[0] & (share - 1)) ^ (i % share)] = one[...]

    each = arrived[0].shape[0]
    gain = jnp.transpose(jnp.broadcast_to(norm_gain[...], (TILE, DV)))
    stay0 = jnp.where(is_fresh(req, me[0] * 2), 0.0, 1.0)
    stay1 = jnp.where(is_fresh(req, me[0] * 2 + 1), 0.0, 1.0)
    lane = iota((DV, TILE), 1)
    early = lane < SPAN
    sides = halves((SPAN, TILE))
    units = [(t, r) for t in range(qs.shape[0]) for r in range(RATIO)]
    both = [jnp.concatenate([wk[t * RATIO + r], qs[t]], axis=1) for t, r in units]
    enter = [sin[at // each, at % each].astype(F32) * stay0 for at in range(len(units))]
    first = [dot(e.astype(BF16), b) for e, b in zip(enter, both)]
    wide = [wv[t * RATIO + r].astype(F32) for t, r in units]
    new0 = [jnp.where(early, w - f[:, :TILE], 0.0) for w, f in zip(wide, first)]
    tiles = range(qs.shape[0])
    pairs = [
        dot(
            jnp.concatenate([new0[2 * t].astype(BF16), new0[2 * t + 1].astype(BF16)], axis=1),
            corner(ft[2 * t], ft[2 * t + 1]),
        )
        for t in tiles
    ]
    middle = [
        (rows[t, r : r + 1] * e + pairs[t][:, r * TILE : (r + 1) * TILE]) * stay1
        for (t, r), e in zip(units, enter)
    ]
    second = [dot(m.astype(BF16), b) for m, b in zip(middle, both)]
    new = [
        jnp.where(early, x, w - s[:, :TILE]).astype(BF16) for x, w, s in zip(new0, wide, second)
    ]
    near = [
        block_dot(jnp.concatenate([new[2 * t], new[2 * t + 1]], axis=1), sc[t], sides) for t in tiles
    ]
    for at, (t, r) in enumerate(units):
        core = rows[t, 2 + r : 3 + r] * jnp.where(early, first[at][:, TILE:], second[at][:, TILE:])
        core = (core + near[t][:, r * TILE : (r + 1) * TILE]).astype(BF16).astype(F32)
        inverse_rms = lax.rsqrt(jnp.mean(core * core, axis=0, keepdims=True) + EPSILON)
        z = gate[t, r * DV : (r + 1) * DV].astype(F32)
        result = core * inverse_rms * gain * (z / (1.0 + jnp.exp(-z)))
        out[t, r * DV : (r + 1) * DV] = result.astype(BF16)


def token_out(me, req, wk, wv, sc, ft, qs, rows, gate, gain, arrived, first, so_far):
    heads = qs.shape[0]
    each = arrived[0].shape[0]
    share = STEP * RATIO // each
    steps = len(arrived) // share
    far = first // share

    def tiles(count, *rest):
        return pl.BlockSpec(
            (count,) + rest,
            lambda g, me: ((me[0] // share) ^ (g + far),) + (0,) * len(rest),
        )

    def whole(*shape):
        return pl.BlockSpec(shape, lambda g, me: (0,) * len(shape))

    extra = [] if so_far is None else [so_far]
    return pl.pallas_call(
        token_out_kernel,
        grid_spec=pltpu.PrefetchScalarGridSpec(
            num_scalar_prefetch=1,
            grid=(steps,),
            in_specs=[pl.BlockSpec(memory_space=pltpu.SMEM)]
            + [tiles(STEP * RATIO, 128, 128)] * 2
            + [tiles(STEP, SPAN, RATIO * TILE), tiles(STEP * RATIO, 128, 128)]
            + [tiles(STEP, 128, 128), tiles(STEP, 8, 128), tiles(STEP, 256, TILE), whole(1, 128)]
            + [whole(each, 128, 128)] * len(arrived)
            + [pl.BlockSpec(memory_space=pl.ANY)] * len(extra),
            out_specs=tiles(STEP, 256, TILE),
            scratch_shapes=[pltpu.VMEM((share, each, 128, 128), BF16)],
        ),
        out_shape=jax.ShapeDtypeStruct((heads, 256, TILE), BF16),
        input_output_aliases={10 + len(arrived): 0} if extra else {},
        compiler_params=params(),
        cost_estimate=pl.CostEstimate(flops=10**9, bytes_accessed=4 << 20, transcendentals=10**6),
        name="token_out",
    )(me, req, wk, wv, sc, ft, qs, rows, gate, gain, *arrived, *extra)


def land_kernel(me, *refs):
    got, (states, tails, counts) = refs[:-3], refs[-3:]
    slot = pl.program_id(0)
    heads, own = states.shape[1], tails.shape[2]
    base = heads * 128

    @pl.when(slot == 0)
    def first():
        for i, one in enumerate(got):
            number = jnp.max(one[0, base + own * 16 :].astype(F32))
            counts[i] = number.astype(jnp.int32)

    start = jnp.int32(0)
    source, place = jnp.int32(-1), jnp.int32(0)
    for p in range(len(got)):
        away = me[0] ^ p
        number = counts[away]
        inside = (slot >= start) & (slot < start + number)
        source = jnp.where(inside, away, source)
        place = jnp.where(inside, slot - start, place)
        start = start + number
    place = jnp.clip(place, 0, CAP - 1)
    for i, one in enumerate(got):

        @pl.when(source == i)
        def take():
            for v in range(heads):
                block = one[place, v * 128 : (v + 1) * 128].astype(F32)
                states[0, v] = jnp.transpose(block)
            lines = [one[place, base + h * 16 : base + h * 16 + 16].astype(F32) for h in range(own)]
            for k in range(KERNEL - 1):
                row = [
                    jnp.concatenate([x[4 * k + cg : 4 * k + cg + 1] for cg in range(4)], axis=1)
                    for x in lines
                ]
                tails[0, k] = jnp.concatenate(row, axis=0).astype(BF16)

    @pl.when(source < 0)
    def clear():
        states[...] = jnp.zeros_like(states)
        tails[...] = jnp.zeros_like(tails)


def land(me, got, heads, own):
    lines = got[0].shape[1]
    slots = len(got) * CAP
    smem = pl.BlockSpec(memory_space=pltpu.SMEM)
    return pl.pallas_call(
        land_kernel,
        grid=(slots,),
        in_specs=[smem] + [pl.BlockSpec((CAP, lines, 128), lambda g: (0, 0, 0))] * len(got),
        out_specs=[
            pl.BlockSpec((1, heads, 128, 128), lambda g: (g, 0, 0, 0)),
            pl.BlockSpec((1, KERNEL - 1, own, 512), lambda g: (g, 0, 0, 0)),
        ],
        out_shape=[
            jax.ShapeDtypeStruct((slots, heads, 128, 128), F32),
            jax.ShapeDtypeStruct((slots, KERNEL - 1, own, 512), BF16),
        ],
        scratch_shapes=[pltpu.SMEM((len(got),), jnp.int32)],
        compiler_params=params(),
        cost_estimate=pl.CostEstimate(flops=10**6, bytes_accessed=4 << 20, transcendentals=0),
        name="land",
    )(me, *got)


def exchange(parts, axis):
    count = len(parts)
    got = {0: parts[0]}
    for k in range(count - 1, 0, -1):
        got[k] = lax.ppermute(parts[k], axis, [(i, i ^ k) for i in range(count)])
    return [got[k] for k in range(count)]


def body(
    mixed,
    decay_in,
    beta_in,
    gate_z,
    conv_weight,
    a_log,
    dt_bias,
    norm_gain,
    req_blocks,
    replica_of,
    finished,
):
    n = lax.axis_size("seq")
    replicas = lax.axis_size("rep")
    heads = mixed.shape[1]
    own = heads // n
    me = lax.axis_index("seq").astype(jnp.int32).reshape(1)
    kpack, par = pack_keys(mixed[0], decay_in[0], beta_in[0], conv_weight, a_log, dt_bias)
    halo, *vpack = pack_values(me, mixed[0], n)
    kp = lax.all_to_all(kpack.reshape(n, own, KROWS, TILE), "seq", 0, 0, tiled=True)
    halo = lax.ppermute(halo, "seq", [(i, i + 1) for i in range(n - 1)])
    vp = exchange(vpack, "seq")
    kp, halo = lax.optimization_barrier((kp, halo))
    wk, wv, sc, ft, qs, rows = token_prep(
        req_blocks, me, mixed[0], decay_in[0], beta_in[0], halo, kp.reshape(heads, KROWS, TILE)
    )
    hsol, hft, hgs, hrows = head_prep(req_blocks, kp, par)
    hrows, rows = lax.optimization_barrier((hrows, rows))
    *sin, ends, ktails = head_chain(req_blocks, me, par, hsol, hft, hgs, hrows, vp)
    sin = exchange(sin, "seq")
    my_rep = lax.axis_index("rep").astype(jnp.int32).reshape(1)
    send = choose(req_blocks, replica_of, finished, my_rep, ends, ktails, replicas)
    states, tails = land(my_rep, exchange(send, "rep"), own * RATIO, own)
    out = None
    for first in (0, n // 2):
        out = token_out(
            me,
            req_blocks,
            wk,
            wv,
            sc,
            ft,
            qs,
            rows,
            gate_z[0],
            norm_gain.reshape(1, DV),
            sin[first : first + n // 2],
            first,
            out,
        )
    return (out[None], states[None], tails[None])


def solution(mesh):
    placed = (
        P("rep", None, None, "seq"),
        P("rep", None, None, "seq"),
        P("rep", None, None, "seq"),
        P("rep", None, None, "seq"),
        P(None, "seq", None),
        P("seq"),
        P("seq"),
        P(),
        P("rep", None),
        P("rep", None),
        P("rep", None),
    )
    return jax.shard_map(
        body,
        mesh=mesh,
        in_specs=placed,
        out_specs=(
            P("rep", None, None, "seq"),
            P("rep", None, "seq", None, None),
            P("rep", None, None, "seq", None),
        ),
        check_vma=False,
    )
```

```python
import jax
import jax.numpy as jnp
from jax import lax
from jax.experimental import pallas as pl
from jax.experimental.pallas import tpu as pltpu
from jax.sharding import PartitionSpec as P

DK = 128
DV = 128
KERNEL = 4
SPAN = 64
CAP = 2
RATIO = 2
TILE = 2 * SPAN
KROWS = 160
VROWS = 288
STEP = 4
WIDE = 8
EPSILON = 1e-06
F32 = jnp.float32
BF16 = jnp.bfloat16
VMEM_LIMIT = 56 * 1024 * 1024


def params(**kwargs):
    return pltpu.CompilerParams(vmem_limit_bytes=VMEM_LIMIT, **kwargs)


def iota(shape, dim):
    return lax.broadcasted_iota(jnp.int32, shape, dim)


def dot(left, right):
    return jnp.dot(left, right, preferred_element_type=F32)


def split(wide):
    high = wide.astype(BF16)
    return high, (wide - high.astype(F32)).astype(BF16)


def halves(shape):
    first = iota(shape, len(shape) - 1) < SPAN
    return jnp.where(first, 1.0, 0.0).astype(BF16), jnp.where(first, 0.0, 1.0).astype(BF16)


def corner(first, second):
    none = jnp.zeros_like(first)
    top = jnp.concatenate([first, none], axis=1)
    return jnp.concatenate([top, jnp.concatenate([none, second], axis=1)], axis=0)


def diagonal(packed, masks):
    squares = []
    for r in range(RATIO):
        one = packed[:, r * TILE : (r + 1) * TILE]
        squares.append(jnp.concatenate([one * masks[0], one * masks[1]], axis=0))
    return corner(*squares)


def block_dot(left, right, masks):
    return dot(left, diagonal(right, masks))


def parameter_lines(h, cw, alog, dtb):
    taps = cw[:, h].astype(F32)
    rows = [taps[tap : tap + 1, cg * 128 : (cg + 1) * 128] for tap in range(KERNEL) for cg in range(4)]
    rest = jnp.concatenate(
        [jnp.full((1, 128), ref[h * RATIO + r], F32) for ref in (alog, dtb) for r in range(RATIO)], axis=0
    )
    parts = []
    for _ in range(3):
        part = rest.astype(BF16).astype(F32)
        rest = rest - part
        parts.append(part)
    return jnp.concatenate(rows + parts + [jnp.zeros((4, 128), F32)], axis=0)


def parameters(lines):
    wide = lines.astype(F32)
    rest = wide[16:20] + wide[20:24] + wide[24:28]
    return wide[:16], rest[:RATIO], rest[RATIO:]


def pack_keys_kernel(mixed, dec, beta, cw, alog, dtb, kout, pout):
    row = iota((32, TILE), 0)
    own = pout.shape[0]
    lines = [parameter_lines(h, cw, alog, dtb) for h in range(own)]
    for t in range(mixed.shape[0]):
        kout[t, :DK] = mixed[t]
        rest = lines[t % own]
        d, b = dec[t].astype(F32), beta[t].astype(F32)
        for r in range(RATIO):
            rest = jnp.where(row == 28 + r, d[r : r + 1], rest)
            rest = jnp.where(row == 30 + r, b[r : r + 1], rest)
        kout[t, DK:] = rest.astype(BF16)

    @pl.when(pl.program_id(0) == 0)
    def first():
        for h in range(own):
            pout[h] = lines[h].astype(BF16)


def pack_keys(mixed, dec, beta, cw, alog, dtb):
    heads = mixed.shape[0]
    own = cw.shape[1]
    step = heads // 2
    smem = pl.BlockSpec(memory_space=pltpu.SMEM)
    return pl.pallas_call(
        pack_keys_kernel,
        grid=(heads // step,),
        in_specs=[
            pl.BlockSpec((step, DK, TILE), lambda g: (g, 1, 0)),
            pl.BlockSpec((step, RATIO, TILE), lambda g: (g, 0, 0)),
            pl.BlockSpec((step, RATIO, TILE), lambda g: (g, 0, 0)),
            pl.BlockSpec((KERNEL, own, 512), lambda g: (0, 0, 0)),
            smem,
            smem,
        ],
        out_specs=[
            pl.BlockSpec((step, KROWS, TILE), lambda g: (g, 0, 0)),
            pl.BlockSpec((own, 32, 128), lambda g: (0, 0, 0)),
        ],
        out_shape=[
            jax.ShapeDtypeStruct((heads, KROWS, TILE), BF16),
            jax.ShapeDtypeStruct((own, 32, 128), BF16),
        ],
        compiler_params=params(),
        cost_estimate=pl.CostEstimate(flops=10**6, bytes_accessed=2 << 20, transcendentals=0),
        name="pack_keys",
    )(mixed, dec, beta, cw, alog, dtb)


def pack_values_kernel(me, mixed, hout, *outs):
    step = pl.program_id(0)
    own = outs[0].shape[0]
    row, tok = iota((TILE, 128), 1), iota((TILE, 128), 0)
    place = row & 15
    picks = []
    for cg in range(4):
        hit = (row < 32) & (place < 12) & ((place & 3) == cg)
        hit = hit & (tok == (row >> 4) * SPAN + 61 + (place >> 2))
        picks.append(jnp.where(hit, 1.0, 0.0).astype(BF16))
    all_tails = []
    for h in range(mixed.shape[0]):
        tails = dot(mixed[h, :128], picks[0])
        for cg in range(1, 4):
            tails = tails + dot(mixed[h, cg * 128 : (cg + 1) * 128], picks[cg])
        all_tails.append(jnp.transpose(tails)[:32].astype(BF16))
        hout[h] = all_tails[h][16:]
    for i, out in enumerate(outs):

        @pl.when((step == i // 4) & ((me[0] & 3) == 0))
        def put0():
            put(mixed, all_tails, out, (i & 3) ^ 0, own)

        @pl.when((step == i // 4) & ((me[0] & 3) == 1))
        def put1():
            put(mixed, all_tails, out, (i & 3) ^ 1, own)

        @pl.when((step == i // 4) & ((me[0] & 3) == 2))
        def put2():
            put(mixed, all_tails, out, (i & 3) ^ 2, own)

        @pl.when((step == i // 4) & ((me[0] & 3) == 3))
        def put3():
            put(mixed, all_tails, out, (i & 3) ^ 3, own)


def put(mixed, all_tails, out, place, own):
    for h in range(own):
        out[h, :256] = mixed[place * own + h, 2 * DK :]
        out[h, 256:] = all_tails[place * own + h]


def pack_values(me, mixed, n):
    heads = mixed.shape[0]
    own = heads // n
    return pl.pallas_call(
        pack_values_kernel,
        grid_spec=pltpu.PrefetchScalarGridSpec(
            num_scalar_prefetch=1,
            grid=(n // 4,),
            in_specs=[pl.BlockSpec((4 * own, 512, TILE), lambda g, me: ((me[0] >> 2) ^ g, 0, 0))],
            out_specs=[pl.BlockSpec((4 * own, 16, TILE), lambda g, me: ((me[0] >> 2) ^ g, 0, 0))]
            + [pl.BlockSpec((own, VROWS, TILE), lambda g, me: (0, 0, 0))] * n,
        ),
        out_shape=[jax.ShapeDtypeStruct((heads, 16, TILE), BF16)]
        + [jax.ShapeDtypeStruct((own, VROWS, TILE), BF16)] * n,
        compiler_params=params(),
        cost_estimate=pl.CostEstimate(flops=10**8, bytes_accessed=4 << 20, transcendentals=0),
        name="pack_values",
    )(me, mixed)


def is_fresh(req, block):
    start = jnp.int32(0)
    fresh = jnp.bool_(False)
    for j in range(req.shape[1]):
        fresh = fresh | (start == block)
        start = start + req[0, j]
    return fresh


def tap_tables():
    row, part = iota((16, 4 * 128), 0), iota((16, 4 * 128), 1) >> 7
    hits = [((row & 3) == cg) & ((row >> 2) == part) for cg in range(4)]
    return [jnp.where(hit, 1.0, 0.0).astype(BF16) for hit in hits]


def halo_tables():
    row, lane = iota((48, 128), 0), iota((48, 128), 1)
    token = (row >> 2) % 3
    hits = [((row & 3) == cg) & (row < 36) & (token == lane) for cg in range(4)]
    return [jnp.where(hit, 1.0, 0.0).astype(BF16) for hit in hits]


def turned_dot(rows, table):
    return lax.dot_general(rows, table, (((0,), (0,)), ((), ())), preferred_element_type=F32)


def spread_taps(par, table):
    both = turned_dot(par, table)
    return [both[:, tap * 128 : (tap + 1) * 128] for tap in range(KERNEL)]


def halo_terms(halo, par, not_fresh0):
    x = [halo[4 * k : 4 * k + 4].astype(F32) * not_fresh0 for k in range(3)]
    w = [par[4 * k : 4 * k + 4] for k in range(3)]
    terms = jnp.concatenate(
        [w[0] * x[0] + w[1] * x[1] + w[2] * x[2], w[0] * x[1] + w[1] * x[2], w[0] * x[2]], axis=0
    )
    high = terms.astype(BF16).astype(F32)
    middle = (terms - high).astype(BF16).astype(F32)
    parts = [high, middle, terms - high - middle, jnp.zeros((12, 128), F32)]
    return jnp.concatenate(parts, axis=0).astype(BF16)


def convolve(raw, before, terms, taps, masks):
    lane = iota((1, TILE), 1)
    cur = raw.astype(F32)
    total = taps[KERNEL - 1] * cur
    if terms is not None:
        total = total + terms
    for back in range(1, KERNEL):
        moved = cur if before is None else jnp.where(lane >= TILE - back, before, cur)
        total = total + taps[KERNEL - 1 - back] * (pltpu.roll(moved, back, 1) * masks[back - 1])
    return (total / (1.0 + jnp.exp(-total))).astype(BF16)


def conv_masks(cut0, cut1):
    lane = iota((1, TILE), 1)
    masks = []
    for back in range(1, KERNEL):
        gone = ((lane < back) & cut0) | ((lane >= SPAN) & (lane < SPAN + back) & cut1)
        masks.append(jnp.where(gone, 0.0, 1.0))
    return masks


def row_prep(dec, beta, alog, dtb):
    lane = iota(dec.shape, 1)
    x = dec + dtb
    decay = -jnp.exp(alog) * (jnp.maximum(x, 0.0) + jnp.log1p(jnp.exp(-jnp.abs(x))))
    cum = decay
    for shift in (1, 2, 4, 8, 16, 32):
        cum = cum + jnp.where((lane & (SPAN - 1)) >= shift, pltpu.roll(cum, shift, 1), 0.0)
    strength = 1.0 / (1.0 + jnp.exp(-beta))
    grown = jnp.exp(cum)
    close0, close1 = cum[:, SPAN - 1 : SPAN], cum[:, TILE - 1 :]
    fade = jnp.exp(jnp.where(lane < SPAN, close0, close1) - cum)
    keep0 = jnp.exp(jnp.broadcast_to(close0, cum.shape))
    keep1 = jnp.exp(jnp.broadcast_to(close1, cum.shape))
    return cum, strength, grown, fade, keep0, keep1


def unit_inverses(systems):
    shape = (SPAN, RATIO * TILE)
    row, col = iota(shape, 0), iota(shape, 1) & (SPAN - 1)
    near = (row >> 4) == (col >> 4)
    eye = jnp.where(row == col, 1.0, 0.0)
    masks = halves((SPAN, TILE))

    def low(arrays):
        return [a.astype(BF16) for a in arrays]

    def stack(pair):
        return jnp.concatenate(pair, axis=0)

    total = [jnp.where(near, eye - a, 0.0) for a in systems]
    power = low([jnp.where(near, -a, 0.0) for a in systems])
    power = low([block_dot(p, p, masks) for p in power])
    for _ in range(2):
        both = [block_dot(stack([t, p]), p, masks) for t, p in zip(low(total), power)]
        total = [t + b[:SPAN] for t, b in zip(total, both)]
        power = low([b[SPAN:] for b in both])
    total = [t + block_dot(l, p, masks) for t, l, p in zip(total, low(total), power)]
    small = low(total)
    rest = low([jnp.where(near, 0.0, a) for a in systems])
    cross = low([block_dot(t, r, masks) for t, r in zip(small, rest)])
    total = [t - block_dot(x, l, masks) for t, x, l in zip(total, cross, small)]
    cross = low([block_dot(x, x, masks) for x in cross])
    small = low([t + block_dot(x, l, masks) for t, x, l in zip(total, cross, low(total))])
    solved = []
    for a, x in zip(systems, small):
        wide = x.astype(F32)
        parts = block_dot(stack(split(a)), x, masks)
        miss = eye - wide - (parts[:SPAN] + parts[SPAN:])
        solved.append((wide + block_dot(x, miss.astype(BF16), masks)).astype(BF16))
    return solved


def both_blocks(square):
    none = jnp.zeros((SPAN, square.shape[1]), square.dtype)
    first = jnp.concatenate([square[:SPAN], none], axis=0)
    return jnp.concatenate([first, jnp.concatenate([none, square[SPAN:]], axis=0)], axis=1)


def unit_keys(convolved):
    wide = convolved.astype(F32)
    return (wide * lax.rsqrt(jnp.sum(wide * wide, axis=0, keepdims=True) + EPSILON)).astype(BF16)


def solve_tiles(keys, queries, prep):
    cum, strength, grown, fade, keep0, keep1 = prep
    row, lane = iota((SPAN, TILE), 0), iota((SPAN, TILE), 1)
    early = lane < SPAN
    seen = (lane & (SPAN - 1)) >= row
    later = (lane & (SPAN - 1)) > row
    columns = jnp.transpose(jnp.concatenate([cum, fade], axis=0))
    count = cum.shape[0]

    def beside(tall):
        return jnp.where(early, tall[:SPAN], tall[SPAN:])

    systems, faded, scores = [], [], []
    for t, k in enumerate(keys):
        turned = jnp.transpose(k.astype(F32))
        if queries is None:
            gram = beside(dot(turned.astype(BF16), k))
        else:
            prod = dot(turned.astype(BF16), jnp.concatenate([k, queries[t]], axis=1))
            gram, touch = beside(prod[:, :TILE]), beside(prod[:, TILE:])
        pair = []
        for r in range(RATIO):
            at = t * RATIO + r
            diff = cum[at : at + 1] - beside(columns[:, at : at + 1])
            ratio = jnp.where(seen, jnp.exp(jnp.where(seen, diff, 0.0)), 0.0)
            pair.append(jnp.where(later, strength[at : at + 1] * gram * ratio, 0.0))
            if queries is not None:
                scores.append((touch * ratio).astype(BF16))
            faded.append((turned * columns[:, count + at : count + at + 1]).astype(BF16))
        systems.append(jnp.concatenate(pair, axis=1))
    return unit_inverses(systems), faded, scores


def token_prep_kernel(req, me, mixed, dec, beta, halo, par_lines, wk, wv, sc, ft, qo, rows):
    fresh0, fresh1 = is_fresh(req, me[0] * 2), is_fresh(req, me[0] * 2 + 1)
    not_fresh0 = jnp.where(fresh0, 0.0, 1.0)
    masks = conv_masks(True, fresh1)
    tap_tab, halo_tab = tap_tables(), halo_tables()
    tiles = range(mixed.shape[0])
    par = [parameters(par_lines[t]) for t in tiles]

    def gather(pick):
        return jnp.concatenate([pick(t) for t in tiles], axis=0)

    prep = row_prep(
        gather(lambda t: dec[t].astype(F32)),
        gather(lambda t: beta[t].astype(F32)),
        jnp.concatenate([p[1] for p in par], axis=0),
        jnp.concatenate([p[2] for p in par], axis=0),
    )
    cum, strength, grown, fade, keep0, keep1 = prep
    keys, queries, values = [], [], []
    for t in tiles:
        terms = halo_terms(halo[t], par[t][0], not_fresh0)
        lines = par_lines[t, :16]
        q, k, v0, v1 = [
            convolve(
                mixed[t, c * 128 : (c + 1) * 128],
                None,
                turned_dot(terms, halo_tab[c]),
                spread_taps(lines, tap_tab[c]),
                masks,
            )
            for c in range(4)
        ]
        keys.append(unit_keys(k))
        queries.append(q)
        values.append((v0, v1))
        qo[t] = q
        rows[t] = jnp.concatenate(
            [keep0[2 * t : 2 * t + 2], grown[2 * t : 2 * t + 2], keep1[2 * t : 2 * t + 2], strength[2 * t : 2 * t + 2]],
            axis=0,
        )
    solved, faded, scores = solve_tiles(keys, queries, prep)
    sides = halves((SPAN, TILE))
    for t in tiles:
        stacks = []
        for r in range(RATIO):
            at = t * RATIO + r
            s, lift = strength[at : at + 1], strength[at : at + 1] * grown[at : at + 1]
            stacked = jnp.concatenate(
                [lift * keys[t].astype(F32), s * values[t][r].astype(F32)], axis=0
            )
            stacks.append(stacked.astype(BF16))
            sc[t, :, r * TILE : (r + 1) * TILE] = scores[at]
            ft[at] = faded[at]
        out = block_dot(jnp.concatenate(stacks, axis=1), solved[t], sides).astype(BF16)
        for r in range(RATIO):
            wk[t * RATIO + r] = out[:DK, r * TILE : (r + 1) * TILE]
            wv[t * RATIO + r] = out[DK:, r * TILE : (r + 1) * TILE]


def token_prep(req, me, mixed, dec, beta, halo, par):
    heads = mixed.shape[0]
    smem = pl.BlockSpec(memory_space=pltpu.SMEM)

    def tiles(count, *rest):
        return pl.BlockSpec((count,) + rest, lambda g: (g,) + (0,) * len(rest))

    square = jax.ShapeDtypeStruct((heads * RATIO, 128, 128), BF16)
    return pl.pallas_call(
        token_prep_kernel,
        grid=(heads // WIDE,),
        in_specs=[
            smem,
            smem,
            tiles(WIDE, 512, TILE),
            tiles(WIDE, RATIO, TILE),
            tiles(WIDE, RATIO, TILE),
            tiles(WIDE, 16, TILE),
            pl.BlockSpec((WIDE, 32, 128), lambda g: (g, 4, 0)),
        ],
        out_specs=[tiles(WIDE * RATIO, 128, 128)] * 2
        + [tiles(WIDE, SPAN, RATIO * TILE), tiles(WIDE * RATIO, 128, 128)]
        + [tiles(WIDE, 128, 128), tiles(WIDE, 8, 128)],
        out_shape=[square] * 2
        + [
            jax.ShapeDtypeStruct((heads, SPAN, RATIO * TILE), BF16),
            square,
            jax.ShapeDtypeStruct((heads, 128, 128), BF16),
            jax.ShapeDtypeStruct((heads, 8, 128), F32),
        ],
        compiler_params=params(),
        cost_estimate=pl.CostEstimate(flops=10**10, bytes_accessed=8 << 20, transcendentals=10**6),
        name="token_prep",
    )(req, me, mixed, dec, beta, halo, par)


def head_prep_kernel(req, kp, previous, par_lines, sol, ft, gs, rows):
    step = pl.program_id(0)
    depth, own = kp.shape[0], kp.shape[1]
    tap_tab = tap_tables()
    order = [(d, h) for d in range(depth) for h in range(own)]
    par = [parameters(par_lines[h]) for h in range(own)]

    small = [kp[d, h, DK:].astype(F32) for d, h in order]
    prep = row_prep(
        jnp.concatenate([s[28:30] for s in small], axis=0),
        jnp.concatenate([s[30:32] for s in small], axis=0),
        jnp.concatenate([par[h][1] for d, h in order], axis=0),
        jnp.concatenate([par[h][2] for d, h in order], axis=0),
    )
    cum, strength, grown, fade, keep0, keep1 = prep
    keys = []
    taps = [spread_taps(par_lines[h, :16], tap_tab[1]) for h in range(own)]
    for d in range(depth):
        block = (step * depth + d) * 2
        masks = conv_masks(is_fresh(req, block), is_fresh(req, block + 1))
        for h in range(own):
            before = (kp[d - 1, h, :DK] if d else previous[0, h]).astype(F32)
            keys.append(unit_keys(convolve(kp[d, h, :DK], before, None, taps[h], masks)))
    solved, faded, unused = solve_tiles(keys, None, prep)
    sides = halves((SPAN, TILE))
    for t, (d, h) in enumerate(order):
        rows[d, h] = jnp.concatenate(
            [keep0[2 * t : 2 * t + 2], keep1[2 * t : 2 * t + 2], strength[2 * t : 2 * t + 2], strength[2 * t : 2 * t + 2]],
            axis=0,
        )
        scaled = []
        for r in range(RATIO):
            at = t * RATIO + r
            lift = strength[at : at + 1] * grown[at : at + 1]
            scaled.append((lift * keys[t].astype(F32)).astype(BF16))
        wide = block_dot(jnp.concatenate(scaled, axis=1), solved[t], sides).astype(BF16)
        sol[d, h] = solved[t]
        for r in range(RATIO):
            at = t * RATIO + r
            drop = dot(wide[:, r * TILE : (r + 1) * TILE], both_blocks(faded[at])).astype(BF16)
            gs[d, h, r, 0] = drop[:, :DK]
            gs[d, h, r, 1] = drop[:, DK:]
            ft[d, h, r] = faded[at]


def head_prep(req, kp, par):
    n, own = kp.shape[:2]
    depth = WIDE // own
    smem = pl.BlockSpec(memory_space=pltpu.SMEM)

    def tiles(*rest):
        return pl.BlockSpec((depth, own) + rest, lambda g: (g, 0) + (0,) * len(rest))

    square = jax.ShapeDtypeStruct((n, own, RATIO, 128, 128), BF16)
    return pl.pallas_call(
        head_prep_kernel,
        grid=(n // depth,),
        in_specs=[
            smem,
            tiles(KROWS, TILE),
            pl.BlockSpec((1, own, DK, TILE), lambda g: (jnp.maximum(g * depth - 1, 0), 0, 0, 0)),
            pl.BlockSpec((own, 32, 128), lambda g: (0, 0, 0)),
        ],
        out_specs=[
            tiles(SPAN, RATIO * TILE),
            tiles(RATIO, 128, 128),
            tiles(RATIO, 2, 128, 128),
            tiles(8, 128),
        ],
        out_shape=[
            jax.ShapeDtypeStruct((n, own, SPAN, RATIO * TILE), BF16),
            square,
            jax.ShapeDtypeStruct((n, own, RATIO, 2, 128, 128), BF16),
            jax.ShapeDtypeStruct((n, own, 8, 128), F32),
        ],
        compiler_params=params(),
        cost_estimate=pl.CostEstimate(flops=10**10, bytes_accessed=6 << 20, transcendentals=10**6),
        name="head_prep",
    )(req, kp, kp, par)


def head_chain_kernel(req, me, par_lines, sol, ft, gs, rows, *refs):
    n = refs[-6].shape[0]
    arrived, (sin, ends, tails, state, vp, spread) = refs[:n], refs[n:]
    step = pl.program_id(0)
    depth, own = sol.shape[0], sol.shape[1]

    @pl.when(step == 0)
    def first():
        for k, one in enumerate(arrived):
            vp[me[0] ^ k] = one[...]
            tails[me[0] ^ k] = one[:, 256:]
        tap_tab = tap_tables()
        for h in range(own):
            for r in range(RATIO):
                for tap, wide in enumerate(spread_taps(par_lines[h, :16], tap_tab[2 + r])):
                    spread[h * RATIO + r, tap] = wide

    sides = halves((SPAN, TILE))
    heads = [(h, r) for h in range(own) for r in range(RATIO)]
    taps = [[spread[v, tap] for tap in range(KERNEL)] for v in range(len(heads))]
    current = [state[v] for v in range(len(heads))]
    for d in range(depth):
        tile = step * depth + d
        past = jnp.maximum(tile - 1, 0)
        fresh = [is_fresh(req, tile * 2), is_fresh(req, tile * 2 + 1)]
        masks = conv_masks(fresh[0], fresh[1])
        gains = []
        for h in range(own):
            scaled = []
            for r in range(RATIO):
                raw = vp[tile, h, r * DV : (r + 1) * DV]
                before = vp[past, h, r * DV : (r + 1) * DV].astype(F32)
                value = convolve(raw, before, None, taps[h * RATIO + r], masks)
                scaled.append((rows[d, h, 4 + r : 5 + r] * value.astype(F32)).astype(BF16))
            wide = block_dot(jnp.concatenate(scaled, axis=1), sol[d, h], sides).astype(BF16)
            for r in range(RATIO):
                gains.append(dot(wide[:, r * TILE : (r + 1) * TILE], both_blocks(ft[d, h, r])))
        for half in range(2):
            for h in range(own):
                now = [jnp.where(fresh[half], 0.0, current[h * RATIO + r]) for r in range(RATIO)]
                lost = dot(
                    jnp.concatenate([x.astype(BF16) for x in now], axis=1),
                    corner(gs[d, h, 0, half], gs[d, h, 1, half]),
                )
                for r in range(RATIO):
                    v = h * RATIO + r
                    keep = rows[d, h, 2 * half + r : 2 * half + r + 1]
                    gain = gains[v][:, half * DV : (half + 1) * DV]
                    current[v] = keep * now[r] + (gain - lost[:, r * TILE : (r + 1) * TILE])
                    ends[d * 2 + half, v] = current[v].astype(BF16)
        onward = lax.rem(tile + 1, n)
        for v in range(len(heads)):
            sin[onward, v] = current[v].astype(BF16)
    for v in range(len(heads)):
        state[v] = current[v]


def head_chain(req, me, par, sol, ft, gs, rows, arrived):
    n, own = sol.shape[:2]
    depth = WIDE // own
    smem = pl.BlockSpec(memory_space=pltpu.SMEM)

    def tiles(*rest):
        return pl.BlockSpec((depth, own) + rest, lambda g: (g, 0) + (0,) * len(rest))

    return pl.pallas_call(
        head_chain_kernel,
        grid=(n // depth,),
        in_specs=[
            smem,
            smem,
            pl.BlockSpec((own, 32, 128), lambda g: (0, 0, 0)),
            tiles(SPAN, RATIO * TILE),
            tiles(RATIO, 128, 128),
            tiles(RATIO, 2, 128, 128),
            tiles(8, 128),
        ]
        + [pl.BlockSpec((own, VROWS, TILE), lambda g: (0, 0, 0))] * n,
        out_specs=[
            pl.BlockSpec((n, own * RATIO, 128, 128), lambda g: (0, 0, 0, 0)),
            pl.BlockSpec((2 * depth, own * RATIO, 128, 128), lambda g: (g, 0, 0, 0)),
            pl.BlockSpec((n, own, 32, TILE), lambda g: (0, 0, 0, 0)),
        ],
        out_shape=[
            jax.ShapeDtypeStruct((n, own * RATIO, 128, 128), BF16),
            jax.ShapeDtypeStruct((2 * n, own * RATIO, 128, 128), BF16),
            jax.ShapeDtypeStruct((n, own, 32, TILE), BF16),
        ],
        scratch_shapes=[
            pltpu.VMEM((own * RATIO, 128, 128), F32),
            pltpu.VMEM((n, own, VROWS, TILE), BF16),
            pltpu.VMEM((own * RATIO, KERNEL, 128, 128), F32),
        ],
        compiler_params=params(),
        cost_estimate=pl.CostEstimate(flops=3 * 10**9, bytes_accessed=8 << 20, transcendentals=10**6),
        name="head_chain",
    )(req, me, par, sol, ft, gs, rows, *arrived)


def choose_kernel(req, rep, fin, me, ends, kt, *refs):
    outs, counts = refs[:-1], refs[-1]
    own, heads = kt.shape[1], ends.shape[1]
    base = heads * 128
    for i, out in enumerate(outs):
        out[...] = jnp.zeros_like(out)
        counts[i] = 0
    end = jnp.int32(-1)
    for j in range(req.shape[1]):
        end = end + req[0, j]
        where = rep[0, j] ^ me[0]
        place = jnp.minimum(counts[where], CAP - 1)
        done = fin[0, j] > 0
        counts[where] = counts[where] + jnp.where(done, 1, 0)
        for i, out in enumerate(outs):

            @pl.when(done & (where == i))
            def take():
                for v in range(heads):
                    out[place, v * 128 : (v + 1) * 128] = ends[end, v]
                for h in range(own):
                    lines = kt[end >> 1, h].astype(F32)
                    lines = jnp.where((end & 1) > 0, lines[16:], lines[:16]).astype(BF16)
                    out[place, base + h * 16 : base + h * 16 + 16] = lines

    for i, out in enumerate(outs):
        number = jnp.full((16, 128), counts[i], jnp.int32).astype(F32).astype(BF16)
        for c in range(CAP):
            out[c, base + own * 16 :] = number


def choose(req, rep, fin, me, ends, tails, replicas):
    own = tails.shape[1]
    smem = pl.BlockSpec(memory_space=pltpu.SMEM)
    lines = own * RATIO * 128 + own * 16 + 16
    return pl.pallas_call(
        choose_kernel,
        grid=(1,),
        in_specs=[
            smem,
            smem,
            smem,
            smem,
            pl.BlockSpec(ends.shape, lambda g: (0, 0, 0, 0)),
            pl.BlockSpec(tails.shape, lambda g: (0, 0, 0, 0)),
        ],
        out_specs=[pl.BlockSpec((CAP, lines, 128), lambda g: (0, 0, 0))] * replicas,
        out_shape=[jax.ShapeDtypeStruct((CAP, lines, 128), BF16)] * replicas,
        scratch_shapes=[pltpu.SMEM((replicas,), jnp.int32)],
        compiler_params=params(),
        cost_estimate=pl.CostEstimate(flops=10**6, bytes_accessed=4 << 20, transcendentals=0),
        name="choose",
    )(req, rep, fin, me, ends, tails)


def token_out_kernel(req, me, sin, wk, wv, sc, ft, qs, rows, gate, norm_gain, out):
    gain = jnp.transpose(jnp.broadcast_to(norm_gain[...], (TILE, DV)))
    stay0 = jnp.where(is_fresh(req, me[0] * 2), 0.0, 1.0)
    stay1 = jnp.where(is_fresh(req, me[0] * 2 + 1), 0.0, 1.0)
    lane = iota((DV, TILE), 1)
    early = lane < SPAN
    sides = halves((SPAN, TILE))
    units = [(t, r) for t in range(qs.shape[0]) for r in range(RATIO)]
    both = [jnp.concatenate([wk[t * RATIO + r], qs[t]], axis=1) for t, r in units]
    enter = [sin[t * RATIO + r].astype(F32) * stay0 for t, r in units]
    first = [dot(e.astype(BF16), b) for e, b in zip(enter, both)]
    wide = [wv[t * RATIO + r].astype(F32) for t, r in units]
    new0 = [jnp.where(early, w - f[:, :TILE], 0.0) for w, f in zip(wide, first)]
    tiles = range(qs.shape[0])
    pairs = [
        dot(
            jnp.concatenate([new0[2 * t].astype(BF16), new0[2 * t + 1].astype(BF16)], axis=1),
            corner(ft[2 * t], ft[2 * t + 1]),
        )
        for t in tiles
    ]
    middle = [
        (rows[t, r : r + 1] * e + pairs[t][:, r * TILE : (r + 1) * TILE]) * stay1
        for (t, r), e in zip(units, enter)
    ]
    second = [dot(m.astype(BF16), b) for m, b in zip(middle, both)]
    new = [
        jnp.where(early, x, w - s[:, :TILE]).astype(BF16) for x, w, s in zip(new0, wide, second)
    ]
    near = [
        block_dot(jnp.concatenate([new[2 * t], new[2 * t + 1]], axis=1), sc[t], sides) for t in tiles
    ]
    for at, (t, r) in enumerate(units):
        core = rows[t, 2 + r : 3 + r] * jnp.where(early, first[at][:, TILE:], second[at][:, TILE:])
        core = (core + near[t][:, r * TILE : (r + 1) * TILE]).astype(BF16).astype(F32)
        inverse_rms = lax.rsqrt(jnp.mean(core * core, axis=0, keepdims=True) + EPSILON)
        z = gate[t, r * DV : (r + 1) * DV].astype(F32)
        result = core * inverse_rms * gain * (z / (1.0 + jnp.exp(-z)))
        out[t, r * DV : (r + 1) * DV] = result.astype(BF16)


def token_out(req, me, sin, wk, wv, sc, ft, qs, rows, gate, gain):
    heads = qs.shape[0]
    smem = pl.BlockSpec(memory_space=pltpu.SMEM)

    def tiles(count, *rest):
        return pl.BlockSpec((count,) + rest, lambda g: (g,) + (0,) * len(rest))

    return pl.pallas_call(
        token_out_kernel,
        grid=(heads // STEP,),
        in_specs=[smem, smem]
        + [tiles(STEP * RATIO, 128, 128)] * 3
        + [tiles(STEP, SPAN, RATIO * TILE), tiles(STEP * RATIO, 128, 128)]
        + [
            tiles(STEP, 128, 128),
            tiles(STEP, 8, 128),
            tiles(STEP, 256, TILE),
            pl.BlockSpec((1, 128), lambda g: (0, 0)),
        ],
        out_specs=tiles(STEP, 256, TILE),
        out_shape=jax.ShapeDtypeStruct((heads, 256, TILE), BF16),
        compiler_params=params(),
        cost_estimate=pl.CostEstimate(flops=10**9, bytes_accessed=8 << 20, transcendentals=10**6),
        name="token_out",
    )(req, me, sin, wk, wv, sc, ft, qs, rows, gate, gain)


def land_kernel(me, *refs):
    got, (states, tails, counts) = refs[:-3], refs[-3:]
    slot = pl.program_id(0)
    heads, own = states.shape[1], tails.shape[2]
    base = heads * 128

    @pl.when(slot == 0)
    def first():
        for i, one in enumerate(got):
            number = jnp.max(one[0, base + own * 16 :].astype(F32))
            counts[i] = number.astype(jnp.int32)

    start = jnp.int32(0)
    source, place = jnp.int32(-1), jnp.int32(0)
    for p in range(len(got)):
        away = me[0] ^ p
        number = counts[away]
        inside = (slot >= start) & (slot < start + number)
        source = jnp.where(inside, away, source)
        place = jnp.where(inside, slot - start, place)
        start = start + number
    place = jnp.clip(place, 0, CAP - 1)
    for i, one in enumerate(got):

        @pl.when(source == i)
        def take():
            for v in range(heads):
                block = one[place, v * 128 : (v + 1) * 128].astype(F32)
                states[0, v] = jnp.transpose(block)
            lines = [one[place, base + h * 16 : base + h * 16 + 16].astype(F32) for h in range(own)]
            for k in range(KERNEL - 1):
                row = [
                    jnp.concatenate([x[4 * k + cg : 4 * k + cg + 1] for cg in range(4)], axis=1)
                    for x in lines
                ]
                tails[0, k] = jnp.concatenate(row, axis=0).astype(BF16)

    @pl.when(source < 0)
    def clear():
        states[...] = jnp.zeros_like(states)
        tails[...] = jnp.zeros_like(tails)


def land(me, got, heads, own):
    lines = got[0].shape[1]
    slots = len(got) * CAP
    smem = pl.BlockSpec(memory_space=pltpu.SMEM)
    return pl.pallas_call(
        land_kernel,
        grid=(slots,),
        in_specs=[smem] + [pl.BlockSpec((CAP, lines, 128), lambda g: (0, 0, 0))] * len(got),
        out_specs=[
            pl.BlockSpec((1, heads, 128, 128), lambda g: (g, 0, 0, 0)),
            pl.BlockSpec((1, KERNEL - 1, own, 512), lambda g: (g, 0, 0, 0)),
        ],
        out_shape=[
            jax.ShapeDtypeStruct((slots, heads, 128, 128), F32),
            jax.ShapeDtypeStruct((slots, KERNEL - 1, own, 512), BF16),
        ],
        scratch_shapes=[pltpu.SMEM((len(got),), jnp.int32)],
        compiler_params=params(),
        cost_estimate=pl.CostEstimate(flops=10**6, bytes_accessed=4 << 20, transcendentals=0),
        name="land",
    )(me, *got)


def exchange(parts, axis):
    count = len(parts)
    got = {0: parts[0]}
    for k in range(count - 1, 0, -1):
        got[k] = lax.ppermute(parts[k], axis, [(i, i ^ k) for i in range(count)])
    return [got[k] for k in range(count)]


def body(
    mixed,
    decay_in,
    beta_in,
    gate_z,
    conv_weight,
    a_log,
    dt_bias,
    norm_gain,
    req_blocks,
    replica_of,
    finished,
):
    n = lax.axis_size("seq")
    replicas = lax.axis_size("rep")
    heads = mixed.shape[1]
    own = heads // n
    me = lax.axis_index("seq").astype(jnp.int32).reshape(1)
    kpack, par = pack_keys(mixed[0], decay_in[0], beta_in[0], conv_weight, a_log, dt_bias)
    halo, *vpack = pack_values(me, mixed[0], n)
    kp = lax.all_to_all(kpack.reshape(n, own, KROWS, TILE), "seq", 0, 0, tiled=True)
    halo = lax.ppermute(halo, "seq", [(i, i + 1) for i in range(n - 1)])
    vp = exchange(vpack, "seq")
    kp, halo = lax.optimization_barrier((kp, halo))
    wk, wv, sc, ft, qs, rows = token_prep(
        req_blocks, me, mixed[0], decay_in[0], beta_in[0], halo, kp.reshape(heads, KROWS, TILE)
    )
    hsol, hft, hgs, hrows = head_prep(req_blocks, kp, par)
    sin, ends, ktails = head_chain(req_blocks, me, par, hsol, hft, hgs, hrows, vp)
    sin = lax.all_to_all(sin, "seq", 0, 0, tiled=True)
    my_rep = lax.axis_index("rep").astype(jnp.int32).reshape(1)
    send = choose(req_blocks, replica_of, finished, my_rep, ends, ktails, replicas)
    got = exchange(send, "rep")
    states, tails = land(my_rep, got, own * RATIO, own)
    out = token_out(
        req_blocks,
        me,
        sin.reshape(heads * RATIO, 128, 128),
        wk,
        wv,
        sc,
        ft,
        qs,
        rows,
        gate_z[0],
        norm_gain.reshape(1, DV),
    )
    return (out[None], states[None], tails[None])


def solution(mesh):
    placed = (
        P("rep", None, None, "seq"),
        P("rep", None, None, "seq"),
        P("rep", None, None, "seq"),
        P("rep", None, None, "seq"),
        P(None, "seq", None),
        P("seq"),
        P("seq"),
        P(),
        P("rep", None),
        P("rep", None),
        P("rep", None),
    )
    return jax.shard_map(
        body,
        mesh=mesh,
        in_specs=placed,
        out_specs=(
            P("rep", None, None, "seq"),
            P("rep", None, "seq", None, None),
            P("rep", None, None, "seq", None),
        ),
        check_vma=False,
    )
```

```python
import jax
import jax.numpy as jnp
from jax import lax
from jax.experimental import pallas as pl
from jax.experimental.pallas import tpu as pltpu
from jax.sharding import PartitionSpec as P

DK = 128
DV = 128
KERNEL = 4
SPAN = 64
CAP = 2
RATIO = 2
TILE = 2 * SPAN
KROWS = 160
VROWS = 288
STEP = 4
WIDE = 8
MOST = 16
EPSILON = 1e-06
F32 = jnp.float32
BF16 = jnp.bfloat16
VMEM_LIMIT = 56 * 1024 * 1024


def params(**kwargs):
    return pltpu.CompilerParams(vmem_limit_bytes=VMEM_LIMIT, **kwargs)


def iota(shape, dim):
    return lax.broadcasted_iota(jnp.int32, shape, dim)


def dot(left, right):
    return jnp.dot(left, right, preferred_element_type=F32)


def split(wide):
    high = wide.astype(BF16)
    return high, (wide - high.astype(F32)).astype(BF16)


def halves(shape):
    first = iota(shape, len(shape) - 1) < SPAN
    return jnp.where(first, 1.0, 0.0).astype(BF16), jnp.where(first, 0.0, 1.0).astype(BF16)


def corner(first, second):
    none = jnp.zeros_like(first)
    top = jnp.concatenate([first, none], axis=1)
    return jnp.concatenate([top, jnp.concatenate([none, second], axis=1)], axis=0)


def diagonal(packed, masks):
    squares = []
    for r in range(RATIO):
        one = packed[:, r * TILE : (r + 1) * TILE]
        squares.append(jnp.concatenate([one * masks[0], one * masks[1]], axis=0))
    return corner(*squares)


def block_dot(left, right, masks):
    return dot(left, diagonal(right, masks))


def parameter_lines(h, cw, alog, dtb):
    taps = cw[:, h].astype(F32)
    rows = [taps[tap : tap + 1, cg * 128 : (cg + 1) * 128] for tap in range(KERNEL) for cg in range(4)]
    rest = jnp.concatenate(
        [jnp.full((1, 128), ref[h * RATIO + r], F32) for ref in (alog, dtb) for r in range(RATIO)], axis=0
    )
    parts = []
    for _ in range(3):
        part = rest.astype(BF16).astype(F32)
        rest = rest - part
        parts.append(part)
    return jnp.concatenate(rows + parts + [jnp.zeros((4, 128), F32)], axis=0)


def parameters(lines):
    wide = lines.astype(F32)
    rest = wide[16:20] + wide[20:24] + wide[24:28]
    return wide[:16], rest[:RATIO], rest[RATIO:]


def pack_keys_kernel(me, mixed, dec, beta, cw, alog, dtb, pout, *outs):
    row = iota((32, TILE), 0)
    own = pout.shape[0]
    lines = [parameter_lines(h, cw, alog, dtb) for h in range(own)]
    for h in range(own):
        pout[h] = lines[h].astype(BF16)
    for i, out in enumerate(outs):
        to = me[0] ^ i
        for h in range(own):
            t = to * own + h
            out[h, :DK] = mixed[t]
            d, b = dec[t].astype(F32), beta[t].astype(F32)
            rest = lines[h]
            for r in range(RATIO):
                rest = jnp.where(row == 28 + r, d[r : r + 1], rest)
                rest = jnp.where(row == 30 + r, b[r : r + 1], rest)
            out[h, DK:] = rest.astype(BF16)


def pack_keys(me, mixed, dec, beta, cw, alog, dtb):
    heads = mixed.shape[0]
    own = cw.shape[1]
    n = heads // own
    smem = pl.BlockSpec(memory_space=pltpu.SMEM)

    def whole(*shape):
        return pl.BlockSpec(shape, lambda g: (0,) * len(shape))

    return pl.pallas_call(
        pack_keys_kernel,
        grid=(1,),
        in_specs=[
            smem,
            pl.BlockSpec((heads, DK, TILE), lambda g: (0, 1, 0)),
            whole(heads, RATIO, TILE),
            whole(heads, RATIO, TILE),
            whole(KERNEL, own, 512),
            smem,
            smem,
        ],
        out_specs=[whole(own, 32, 128)] + [whole(own, KROWS, TILE)] * n,
        out_shape=[jax.ShapeDtypeStruct((own, 32, 128), BF16)]
        + [jax.ShapeDtypeStruct((own, KROWS, TILE), BF16)] * n,
        compiler_params=params(),
        cost_estimate=pl.CostEstimate(flops=10**6, bytes_accessed=2 << 20, transcendentals=0),
        name="pack_keys",
    )(me, mixed, dec, beta, cw, alog, dtb)


def pack_values_kernel(me, mixed, hout, *outs):
    step = pl.program_id(0)
    own = outs[0].shape[0]
    row, tok = iota((TILE, 128), 1), iota((TILE, 128), 0)
    place = row & 15
    picks = []
    for cg in range(4):
        hit = (row < 32) & (place < 12) & ((place & 3) == cg)
        hit = hit & (tok == (row >> 4) * SPAN + 61 + (place >> 2))
        picks.append(jnp.where(hit, 1.0, 0.0).astype(BF16))
    all_tails = []
    for h in range(mixed.shape[0]):
        tails = dot(mixed[h, :128], picks[0])
        for cg in range(1, 4):
            tails = tails + dot(mixed[h, cg * 128 : (cg + 1) * 128], picks[cg])
        all_tails.append(jnp.transpose(tails)[:32].astype(BF16))
        hout[h] = all_tails[h][16:]
    for i, out in enumerate(outs):

        @pl.when((step == i // 4) & ((me[0] & 3) == 0))
        def put0():
            put(mixed, all_tails, out, (i & 3) ^ 0, own)

        @pl.when((step == i // 4) & ((me[0] & 3) == 1))
        def put1():
            put(mixed, all_tails, out, (i & 3) ^ 1, own)

        @pl.when((step == i // 4) & ((me[0] & 3) == 2))
        def put2():
            put(mixed, all_tails, out, (i & 3) ^ 2, own)

        @pl.when((step == i // 4) & ((me[0] & 3) == 3))
        def put3():
            put(mixed, all_tails, out, (i & 3) ^ 3, own)


def put(mixed, all_tails, out, place, own):
    for h in range(own):
        out[h, :256] = mixed[place * own + h, 2 * DK :]
        out[h, 256:] = all_tails[place * own + h]


def pack_values(me, mixed, n):
    heads = mixed.shape[0]
    own = heads // n
    return pl.pallas_call(
        pack_values_kernel,
        grid_spec=pltpu.PrefetchScalarGridSpec(
            num_scalar_prefetch=1,
            grid=(n // 4,),
            in_specs=[pl.BlockSpec((4 * own, 512, TILE), lambda g, me: ((me[0] >> 2) ^ g, 0, 0))],
            out_specs=[pl.BlockSpec((4 * own, 16, TILE), lambda g, me: ((me[0] >> 2) ^ g, 0, 0))]
            + [pl.BlockSpec((own, VROWS, TILE), lambda g, me: (0, 0, 0))] * n,
        ),
        out_shape=[jax.ShapeDtypeStruct((heads, 16, TILE), BF16)]
        + [jax.ShapeDtypeStruct((own, VROWS, TILE), BF16)] * n,
        compiler_params=params(),
        cost_estimate=pl.CostEstimate(flops=10**8, bytes_accessed=4 << 20, transcendentals=0),
        name="pack_values",
    )(me, mixed)


def is_fresh(req, block):
    start = jnp.int32(0)
    fresh = jnp.bool_(False)
    for j in range(req.shape[1]):
        fresh = fresh | (start == block)
        start = start + req[0, j]
    return fresh


def tap_tables():
    row, part = iota((16, 4 * 128), 0), iota((16, 4 * 128), 1) >> 7
    hits = [((row & 3) == cg) & ((row >> 2) == part) for cg in range(4)]
    return [jnp.where(hit, 1.0, 0.0).astype(BF16) for hit in hits]


def halo_tables():
    row, lane = iota((48, 128), 0), iota((48, 128), 1)
    token = (row >> 2) % 3
    hits = [((row & 3) == cg) & (row < 36) & (token == lane) for cg in range(4)]
    return [jnp.where(hit, 1.0, 0.0).astype(BF16) for hit in hits]


def turned_dot(rows, table):
    return lax.dot_general(rows, table, (((0,), (0,)), ((), ())), preferred_element_type=F32)


def spread_taps(par, table):
    both = turned_dot(par, table)
    return [both[:, tap * 128 : (tap + 1) * 128] for tap in range(KERNEL)]


def halo_terms(halo, par, not_fresh0):
    x = [halo[4 * k : 4 * k + 4].astype(F32) * not_fresh0 for k in range(3)]
    w = [par[4 * k : 4 * k + 4] for k in range(3)]
    terms = jnp.concatenate(
        [w[0] * x[0] + w[1] * x[1] + w[2] * x[2], w[0] * x[1] + w[1] * x[2], w[0] * x[2]], axis=0
    )
    high = terms.astype(BF16).astype(F32)
    middle = (terms - high).astype(BF16).astype(F32)
    parts = [high, middle, terms - high - middle, jnp.zeros((12, 128), F32)]
    return jnp.concatenate(parts, axis=0).astype(BF16)


def convolve(raw, before, terms, taps, masks):
    lane = iota((1, TILE), 1)
    cur = raw.astype(F32)
    total = taps[KERNEL - 1] * cur
    if terms is not None:
        total = total + terms
    for back in range(1, KERNEL):
        moved = cur if before is None else jnp.where(lane >= TILE - back, before, cur)
        total = total + taps[KERNEL - 1 - back] * (pltpu.roll(moved, back, 1) * masks[back - 1])
    return (total / (1.0 + jnp.exp(-total))).astype(BF16)


def conv_masks(cut0, cut1):
    lane = iota((1, TILE), 1)
    masks = []
    for back in range(1, KERNEL):
        gone = ((lane < back) & cut0) | ((lane >= SPAN) & (lane < SPAN + back) & cut1)
        masks.append(jnp.where(gone, 0.0, 1.0))
    return masks


def row_prep(dec, beta, alog, dtb):
    lane = iota(dec.shape, 1)
    x = dec + dtb
    decay = -jnp.exp(alog) * (jnp.maximum(x, 0.0) + jnp.log1p(jnp.exp(-jnp.abs(x))))
    cum = decay
    for shift in (1, 2, 4, 8, 16, 32):
        cum = cum + jnp.where((lane & (SPAN - 1)) >= shift, pltpu.roll(cum, shift, 1), 0.0)
    strength = 1.0 / (1.0 + jnp.exp(-beta))
    grown = jnp.exp(cum)
    close0, close1 = cum[:, SPAN - 1 : SPAN], cum[:, TILE - 1 :]
    fade = jnp.exp(jnp.where(lane < SPAN, close0, close1) - cum)
    keep0 = jnp.exp(jnp.broadcast_to(close0, cum.shape))
    keep1 = jnp.exp(jnp.broadcast_to(close1, cum.shape))
    return cum, strength, grown, fade, keep0, keep1


def unit_inverses(systems):
    shape = (SPAN, RATIO * TILE)
    row, col = iota(shape, 0), iota(shape, 1) & (SPAN - 1)
    near = (row >> 4) == (col >> 4)
    eye = jnp.where(row == col, 1.0, 0.0)
    masks = halves((SPAN, TILE))

    def low(arrays):
        return [a.astype(BF16) for a in arrays]

    def stack(pair):
        return jnp.concatenate(pair, axis=0)

    total = [jnp.where(near, eye - a, 0.0) for a in systems]
    power = low([jnp.where(near, -a, 0.0) for a in systems])
    power = low([block_dot(p, p, masks) for p in power])
    for _ in range(2):
        both = [block_dot(stack([t, p]), p, masks) for t, p in zip(low(total), power)]
        total = [t + b[:SPAN] for t, b in zip(total, both)]
        power = low([b[SPAN:] for b in both])
    total = [t + block_dot(l, p, masks) for t, l, p in zip(total, low(total), power)]
    small = low(total)
    rest = low([jnp.where(near, 0.0, a) for a in systems])
    cross = low([block_dot(t, r, masks) for t, r in zip(small, rest)])
    total = [t - block_dot(x, l, masks) for t, x, l in zip(total, cross, small)]
    small = low(total)
    solved = []
    for a, x in zip(systems, small):
        wide = x.astype(F32)
        parts = block_dot(stack(split(a)), x, masks)
        miss = eye - wide - (parts[:SPAN] + parts[SPAN:])
        solved.append((wide + block_dot(x, miss.astype(BF16), masks)).astype(BF16))
    return solved


def both_blocks(square):
    none = jnp.zeros((SPAN, square.shape[1]), square.dtype)
    first = jnp.concatenate([square[:SPAN], none], axis=0)
    return jnp.concatenate([first, jnp.concatenate([none, square[SPAN:]], axis=0)], axis=1)


def unit_keys(convolved):
    wide = convolved.astype(F32)
    return (wide * lax.rsqrt(jnp.sum(wide * wide, axis=0, keepdims=True) + EPSILON)).astype(BF16)


def solve_tiles(keys, queries, prep):
    cum, strength, grown, fade, keep0, keep1 = prep
    row, lane = iota((SPAN, TILE), 0), iota((SPAN, TILE), 1)
    early = lane < SPAN
    seen = (lane & (SPAN - 1)) >= row
    later = (lane & (SPAN - 1)) > row
    columns = jnp.transpose(jnp.concatenate([cum, fade], axis=0))
    count = cum.shape[0]

    def beside(tall):
        return jnp.where(early, tall[:SPAN], tall[SPAN:])

    systems, faded, scores = [], [], []
    for t, k in enumerate(keys):
        turned = jnp.transpose(k.astype(F32))
        if queries is None:
            gram = beside(dot(turned.astype(BF16), k))
        else:
            prod = dot(turned.astype(BF16), jnp.concatenate([k, queries[t]], axis=1))
            gram, touch = beside(prod[:, :TILE]), beside(prod[:, TILE:])
        pair = []
        for r in range(RATIO):
            at = t * RATIO + r
            diff = cum[at : at + 1] - beside(columns[:, at : at + 1])
            ratio = jnp.where(seen, jnp.exp(jnp.where(seen, diff, 0.0)), 0.0)
            pair.append(jnp.where(later, strength[at : at + 1] * gram * ratio, 0.0))
            if queries is not None:
                scores.append((touch * ratio).astype(BF16))
            faded.append((turned * columns[:, count + at : count + at + 1]).astype(BF16))
        systems.append(jnp.concatenate(pair, axis=1))
    return unit_inverses(systems), faded, scores


def token_prep_kernel(req, me, mixed, dec, beta, halo, par_lines, wk, wv, sc, ft, qo, rows):
    fresh0, fresh1 = is_fresh(req, me[0] * 2), is_fresh(req, me[0] * 2 + 1)
    not_fresh0 = jnp.where(fresh0, 0.0, 1.0)
    masks = conv_masks(True, fresh1)
    tap_tab, halo_tab = tap_tables(), halo_tables()
    tiles = range(mixed.shape[0])
    par = [parameters(par_lines[t]) for t in tiles]

    def gather(pick):
        return jnp.concatenate([pick(t) for t in tiles], axis=0)

    prep = row_prep(
        gather(lambda t: dec[t].astype(F32)),
        gather(lambda t: beta[t].astype(F32)),
        jnp.concatenate([p[1] for p in par], axis=0),
        jnp.concatenate([p[2] for p in par], axis=0),
    )
    cum, strength, grown, fade, keep0, keep1 = prep
    keys, queries, values = [], [], []
    for t in tiles:
        terms = halo_terms(halo[t], par[t][0], not_fresh0)
        lines = par_lines[t, :16]
        q, k, v0, v1 = [
            convolve(
                mixed[t, c * 128 : (c + 1) * 128],
                None,
                turned_dot(terms, halo_tab[c]),
                spread_taps(lines, tap_tab[c]),
                masks,
            )
            for c in range(4)
        ]
        keys.append(unit_keys(k))
        queries.append(q)
        values.append((v0, v1))
        qo[t] = q
        rows[t] = jnp.concatenate(
            [keep0[2 * t : 2 * t + 2], grown[2 * t : 2 * t + 2], keep1[2 * t : 2 * t + 2], strength[2 * t : 2 * t + 2]],
            axis=0,
        )
    solved, faded, scores = solve_tiles(keys, queries, prep)
    sides = halves((SPAN, TILE))
    for t in tiles:
        stacks = []
        for r in range(RATIO):
            at = t * RATIO + r
            s, lift = strength[at : at + 1], strength[at : at + 1] * grown[at : at + 1]
            stacked = jnp.concatenate(
                [lift * keys[t].astype(F32), s * values[t][r].astype(F32)], axis=0
            )
            stacks.append(stacked.astype(BF16))
            sc[t, :, r * TILE : (r + 1) * TILE] = scores[at]
            ft[at] = faded[at]
        out = block_dot(jnp.concatenate(stacks, axis=1), solved[t], sides).astype(BF16)
        for r in range(RATIO):
            wk[t * RATIO + r] = out[:DK, r * TILE : (r + 1) * TILE]
            wv[t * RATIO + r] = out[DK:, r * TILE : (r + 1) * TILE]


def token_prep(req, me, mixed, dec, beta, halo, par):
    heads = mixed.shape[0]
    smem = pl.BlockSpec(memory_space=pltpu.SMEM)

    def tiles(count, *rest):
        return pl.BlockSpec((count,) + rest, lambda g: (g,) + (0,) * len(rest))

    square = jax.ShapeDtypeStruct((heads * RATIO, 128, 128), BF16)
    return pl.pallas_call(
        token_prep_kernel,
        grid=(heads // WIDE,),
        in_specs=[
            smem,
            smem,
            tiles(WIDE, 512, TILE),
            tiles(WIDE, RATIO, TILE),
            tiles(WIDE, RATIO, TILE),
            tiles(WIDE, 16, TILE),
            tiles(WIDE, 32, 128),
        ],
        out_specs=[tiles(WIDE * RATIO, 128, 128)] * 2
        + [tiles(WIDE, SPAN, RATIO * TILE), tiles(WIDE * RATIO, 128, 128)]
        + [tiles(WIDE, 128, 128), tiles(WIDE, 8, 128)],
        out_shape=[square] * 2
        + [
            jax.ShapeDtypeStruct((heads, SPAN, RATIO * TILE), BF16),
            square,
            jax.ShapeDtypeStruct((heads, 128, 128), BF16),
            jax.ShapeDtypeStruct((heads, 8, 128), F32),
        ],
        compiler_params=params(),
        cost_estimate=pl.CostEstimate(flops=10**10, bytes_accessed=8 << 20, transcendentals=10**6),
        name="token_prep",
    )(req, me, mixed, dec, beta, halo, par)


def head_prep_kernel(req, me, par_lines, *refs):
    n = len(refs) - 6
    arrived, (sol, ft, gs, rows, all_par, kp) = refs[:n], refs[n:]
    step = pl.program_id(0)
    depth, own = sol.shape[0], sol.shape[1]
    start = step * depth

    @pl.when(step == 0)
    def first():
        for k, one in enumerate(arrived):
            kp[me[0] ^ k] = one[...]
            all_par[me[0] ^ k] = one[:, DK:]

    tap_tab = tap_tables()
    order = [(d, h) for d in range(depth) for h in range(own)]
    par = [parameters(par_lines[h]) for h in range(own)]

    small = [kp[start + d, h, DK:].astype(F32) for d, h in order]
    prep = row_prep(
        jnp.concatenate([s[28:30] for s in small], axis=0),
        jnp.concatenate([s[30:32] for s in small], axis=0),
        jnp.concatenate([par[h][1] for d, h in order], axis=0),
        jnp.concatenate([par[h][2] for d, h in order], axis=0),
    )
    cum, strength, grown, fade, keep0, keep1 = prep
    keys = []
    taps = [spread_taps(par_lines[h, :16], tap_tab[1]) for h in range(own)]
    for d in range(depth):
        block = (step * depth + d) * 2
        masks = conv_masks(is_fresh(req, block), is_fresh(req, block + 1))
        for h in range(own):
            before = kp[jnp.maximum(start + d - 1, 0), h, :DK].astype(F32)
            keys.append(unit_keys(convolve(kp[start + d, h, :DK], before, None, taps[h], masks)))
    solved, faded, unused = solve_tiles(keys, None, prep)
    sides = halves((SPAN, TILE))
    for t, (d, h) in enumerate(order):
        rows[d, h] = jnp.concatenate(
            [keep0[2 * t : 2 * t + 2], keep1[2 * t : 2 * t + 2], strength[2 * t : 2 * t + 2], strength[2 * t : 2 * t + 2]],
            axis=0,
        )
        scaled = []
        for r in range(RATIO):
            at = t * RATIO + r
            lift = strength[at : at + 1] * grown[at : at + 1]
            scaled.append((lift * keys[t].astype(F32)).astype(BF16))
        wide = block_dot(jnp.concatenate(scaled, axis=1), solved[t], sides).astype(BF16)
        sol[d, h] = solved[t]
        for r in range(RATIO):
            at = t * RATIO + r
            drop = dot(wide[:, r * TILE : (r + 1) * TILE], both_blocks(faded[at])).astype(BF16)
            gs[d, h, r, 0] = drop[:, :DK]
            gs[d, h, r, 1] = drop[:, DK:]
            ft[d, h, r] = faded[at]


def head_prep(req, me, par, arrived):
    n, own = len(arrived), par.shape[0]
    depth = MOST // own
    smem = pl.BlockSpec(memory_space=pltpu.SMEM)

    def tiles(*rest):
        return pl.BlockSpec((depth, own) + rest, lambda g: (g, 0) + (0,) * len(rest))

    def whole(*shape):
        return pl.BlockSpec(shape, lambda g: (0,) * len(shape))

    square = jax.ShapeDtypeStruct((n, own, RATIO, 128, 128), BF16)
    return pl.pallas_call(
        head_prep_kernel,
        grid=(n // depth,),
        in_specs=[smem, smem, whole(own, 32, 128)] + [whole(own, KROWS, TILE)] * n,
        out_specs=[
            tiles(SPAN, RATIO * TILE),
            tiles(RATIO, 128, 128),
            tiles(RATIO, 2, 128, 128),
            tiles(8, 128),
            whole(n, own, 32, 128),
        ],
        out_shape=[
            jax.ShapeDtypeStruct((n, own, SPAN, RATIO * TILE), BF16),
            square,
            jax.ShapeDtypeStruct((n, own, RATIO, 2, 128, 128), BF16),
            jax.ShapeDtypeStruct((n, own, 8, 128), F32),
            jax.ShapeDtypeStruct((n, own, 32, 128), BF16),
        ],
        scratch_shapes=[pltpu.VMEM((n, own, KROWS, TILE), BF16)],
        compiler_params=params(),
        cost_estimate=pl.CostEstimate(flops=10**10, bytes_accessed=6 << 20, transcendentals=10**6),
        name="head_prep",
    )(req, me, par, *arrived)


def head_chain_kernel(req, me, par_lines, sol, ft, gs, rows, *refs):
    n = refs[-6].shape[0]
    arrived, (sin, ends, tails, state, vp, spread) = refs[:n], refs[n:]
    step = pl.program_id(0)
    depth, own = sol.shape[0], sol.shape[1]

    @pl.when(step == 0)
    def first():
        for k, one in enumerate(arrived):
            vp[me[0] ^ k] = one[...]
            tails[me[0] ^ k] = one[:, 256:]
        tap_tab = tap_tables()
        for h in range(own):
            for r in range(RATIO):
                for tap, wide in enumerate(spread_taps(par_lines[h, :16], tap_tab[2 + r])):
                    spread[h * RATIO + r, tap] = wide

    sides = halves((SPAN, TILE))
    heads = [(h, r) for h in range(own) for r in range(RATIO)]
    taps = [[spread[v, tap] for tap in range(KERNEL)] for v in range(len(heads))]
    current = [state[v] for v in range(len(heads))]
    for d in range(depth):
        tile = step * depth + d
        past = jnp.maximum(tile - 1, 0)
        fresh = [is_fresh(req, tile * 2), is_fresh(req, tile * 2 + 1)]
        masks = conv_masks(fresh[0], fresh[1])
        gains = []
        for h in range(own):
            scaled = []
            for r in range(RATIO):
                raw = vp[tile, h, r * DV : (r + 1) * DV]
                before = vp[past, h, r * DV : (r + 1) * DV].astype(F32)
                value = convolve(raw, before, None, taps[h * RATIO + r], masks)
                scaled.append((rows[d, h, 4 + r : 5 + r] * value.astype(F32)).astype(BF16))
            wide = block_dot(jnp.concatenate(scaled, axis=1), sol[d, h], sides).astype(BF16)
            for r in range(RATIO):
                gains.append(dot(wide[:, r * TILE : (r + 1) * TILE], both_blocks(ft[d, h, r])))
        for half in range(2):
            for h in range(own):
                now = [jnp.where(fresh[half], 0.0, current[h * RATIO + r]) for r in range(RATIO)]
                lost = dot(
                    jnp.concatenate([x.astype(BF16) for x in now], axis=1),
                    corner(gs[d, h, 0, half], gs[d, h, 1, half]),
                )
                for r in range(RATIO):
                    v = h * RATIO + r
                    keep = rows[d, h, 2 * half + r : 2 * half + r + 1]
                    gain = gains[v][:, half * DV : (half + 1) * DV]
                    current[v] = keep * now[r] + (gain - lost[:, r * TILE : (r + 1) * TILE])
                    ends[d * 2 + half, v] = current[v].astype(BF16)
        onward = lax.rem(tile + 1, n)
        for v in range(len(heads)):
            sin[onward, v] = current[v].astype(BF16)
    for v in range(len(heads)):
        state[v] = current[v]


def head_chain(req, me, par, sol, ft, gs, rows, arrived):
    n, own = sol.shape[:2]
    depth = MOST // own
    smem = pl.BlockSpec(memory_space=pltpu.SMEM)

    def tiles(*rest):
        return pl.BlockSpec((depth, own) + rest, lambda g: (g, 0) + (0,) * len(rest))

    return pl.pallas_call(
        head_chain_kernel,
        grid=(n // depth,),
        in_specs=[
            smem,
            smem,
            pl.BlockSpec((own, 32, 128), lambda g: (0, 0, 0)),
            tiles(SPAN, RATIO * TILE),
            tiles(RATIO, 128, 128),
            tiles(RATIO, 2, 128, 128),
            tiles(8, 128),
        ]
        + [pl.BlockSpec((own, VROWS, TILE), lambda g: (0, 0, 0))] * n,
        out_specs=[
            pl.BlockSpec((n, own * RATIO, 128, 128), lambda g: (0, 0, 0, 0)),
            pl.BlockSpec((2 * depth, own * RATIO, 128, 128), lambda g: (g, 0, 0, 0)),
            pl.BlockSpec((n, own, 32, TILE), lambda g: (0, 0, 0, 0)),
        ],
        out_shape=[
            jax.ShapeDtypeStruct((n, own * RATIO, 128, 128), BF16),
            jax.ShapeDtypeStruct((2 * n, own * RATIO, 128, 128), BF16),
            jax.ShapeDtypeStruct((n, own, 32, TILE), BF16),
        ],
        scratch_shapes=[
            pltpu.VMEM((own * RATIO, 128, 128), F32),
            pltpu.VMEM((n, own, VROWS, TILE), BF16),
            pltpu.VMEM((own * RATIO, KERNEL, 128, 128), F32),
        ],
        compiler_params=params(),
        cost_estimate=pl.CostEstimate(flops=3 * 10**9, bytes_accessed=8 << 20, transcendentals=10**6),
        name="head_chain",
    )(req, me, par, sol, ft, gs, rows, *arrived)


def choose_kernel(req, rep, fin, me, ends, kt, *refs):
    outs, counts = refs[:-1], refs[-1]
    own, heads = kt.shape[1], ends.shape[1]
    base = heads * 128
    for i, out in enumerate(outs):
        out[...] = jnp.zeros_like(out)
        counts[i] = 0
    end = jnp.int32(-1)
    for j in range(req.shape[1]):
        end = end + req[0, j]
        where = rep[0, j] ^ me[0]
        place = jnp.minimum(counts[where], CAP - 1)
        done = fin[0, j] > 0
        counts[where] = counts[where] + jnp.where(done, 1, 0)
        for i, out in enumerate(outs):

            @pl.when(done & (where == i))
            def take():
                for v in range(heads):
                    out[place, v * 128 : (v + 1) * 128] = ends[end, v]
                for h in range(own):
                    lines = kt[end >> 1, h].astype(F32)
                    lines = jnp.where((end & 1) > 0, lines[16:], lines[:16]).astype(BF16)
                    out[place, base + h * 16 : base + h * 16 + 16] = lines

    for i, out in enumerate(outs):
        number = jnp.full((16, 128), counts[i], jnp.int32).astype(F32).astype(BF16)
        for c in range(CAP):
            out[c, base + own * 16 :] = number


def choose(req, rep, fin, me, ends, tails, replicas):
    own = tails.shape[1]
    smem = pl.BlockSpec(memory_space=pltpu.SMEM)
    lines = own * RATIO * 128 + own * 16 + 16
    return pl.pallas_call(
        choose_kernel,
        grid=(1,),
        in_specs=[
            smem,
            smem,
            smem,
            smem,
            pl.BlockSpec(ends.shape, lambda g: (0, 0, 0, 0)),
            pl.BlockSpec(tails.shape, lambda g: (0, 0, 0, 0)),
        ],
        out_specs=[pl.BlockSpec((CAP, lines, 128), lambda g: (0, 0, 0))] * replicas,
        out_shape=[jax.ShapeDtypeStruct((CAP, lines, 128), BF16)] * replicas,
        scratch_shapes=[pltpu.SMEM((replicas,), jnp.int32)],
        compiler_params=params(),
        cost_estimate=pl.CostEstimate(flops=10**6, bytes_accessed=4 << 20, transcendentals=0),
        name="choose",
    )(req, rep, fin, me, ends, tails)


def token_out_kernel(req, me, sin, wk, wv, sc, ft, qs, rows, gate, norm_gain, out):
    gain = jnp.transpose(jnp.broadcast_to(norm_gain[...], (TILE, DV)))
    stay0 = jnp.where(is_fresh(req, me[0] * 2), 0.0, 1.0)
    stay1 = jnp.where(is_fresh(req, me[0] * 2 + 1), 0.0, 1.0)
    lane = iota((DV, TILE), 1)
    early = lane < SPAN
    sides = halves((SPAN, TILE))
    units = [(t, r) for t in range(qs.shape[0]) for r in range(RATIO)]
    both = [jnp.concatenate([wk[t * RATIO + r], qs[t]], axis=1) for t, r in units]
    enter = [sin[t * RATIO + r].astype(F32) * stay0 for t, r in units]
    first = [dot(e.astype(BF16), b) for e, b in zip(enter, both)]
    wide = [wv[t * RATIO + r].astype(F32) for t, r in units]
    new0 = [jnp.where(early, w - f[:, :TILE], 0.0) for w, f in zip(wide, first)]
    tiles = range(qs.shape[0])
    pairs = [
        dot(
            jnp.concatenate([new0[2 * t].astype(BF16), new0[2 * t + 1].astype(BF16)], axis=1),
            corner(ft[2 * t], ft[2 * t + 1]),
        )
        for t in tiles
    ]
    middle = [
        (rows[t, r : r + 1] * e + pairs[t][:, r * TILE : (r + 1) * TILE]) * stay1
        for (t, r), e in zip(units, enter)
    ]
    second = [dot(m.astype(BF16), b) for m, b in zip(middle, both)]
    new = [
        jnp.where(early, x, w - s[:, :TILE]).astype(BF16) for x, w, s in zip(new0, wide, second)
    ]
    near = [
        block_dot(jnp.concatenate([new[2 * t], new[2 * t + 1]], axis=1), sc[t], sides) for t in tiles
    ]
    for at, (t, r) in enumerate(units):
        core = rows[t, 2 + r : 3 + r] * jnp.where(early, first[at][:, TILE:], second[at][:, TILE:])
        core = (core + near[t][:, r * TILE : (r + 1) * TILE]).astype(BF16).astype(F32)
        inverse_rms = lax.rsqrt(jnp.mean(core * core, axis=0, keepdims=True) + EPSILON)
        z = gate[t, r * DV : (r + 1) * DV].astype(F32)
        result = core * inverse_rms * gain * (z / (1.0 + jnp.exp(-z)))
        out[t, r * DV : (r + 1) * DV] = result.astype(BF16)


def token_out(req, me, sin, wk, wv, sc, ft, qs, rows, gate, gain):
    heads = qs.shape[0]
    smem = pl.BlockSpec(memory_space=pltpu.SMEM)

    def tiles(count, *rest):
        return pl.BlockSpec((count,) + rest, lambda g: (g,) + (0,) * len(rest))

    return pl.pallas_call(
        token_out_kernel,
        grid=(heads // STEP,),
        in_specs=[smem, smem]
        + [tiles(STEP * RATIO, 128, 128)] * 3
        + [tiles(STEP, SPAN, RATIO * TILE), tiles(STEP * RATIO, 128, 128)]
        + [
            tiles(STEP, 128, 128),
            tiles(STEP, 8, 128),
            tiles(STEP, 256, TILE),
            pl.BlockSpec((1, 128), lambda g: (0, 0)),
        ],
        out_specs=tiles(STEP, 256, TILE),
        out_shape=jax.ShapeDtypeStruct((heads, 256, TILE), BF16),
        compiler_params=params(),
        cost_estimate=pl.CostEstimate(flops=10**9, bytes_accessed=8 << 20, transcendentals=10**6),
        name="token_out",
    )(req, me, sin, wk, wv, sc, ft, qs, rows, gate, gain)


def land_kernel(me, *refs):
    got, (states, tails, counts) = refs[:-3], refs[-3:]
    slot = pl.program_id(0)
    heads, own = states.shape[1], tails.shape[2]
    base = heads * 128

    @pl.when(slot == 0)
    def first():
        for i, one in enumerate(got):
            number = jnp.max(one[0, base + own * 16 :].astype(F32))
            counts[i] = number.astype(jnp.int32)

    start = jnp.int32(0)
    source, place = jnp.int32(-1), jnp.int32(0)
    for p in range(len(got)):
        away = me[0] ^ p
        number = counts[away]
        inside = (slot >= start) & (slot < start + number)
        source = jnp.where(inside, away, source)
        place = jnp.where(inside, slot - start, place)
        start = start + number
    place = jnp.clip(place, 0, CAP - 1)
    for i, one in enumerate(got):

        @pl.when(source == i)
        def take():
            for v in range(heads):
                states[0, v] = jnp.transpose(one[place, v * 128 : (v + 1) * 128]).astype(F32)
            lines = [one[place, base + h * 16 : base + h * 16 + 16].astype(F32) for h in range(own)]
            for k in range(KERNEL - 1):
                row = [
                    jnp.concatenate([x[4 * k + cg : 4 * k + cg + 1] for cg in range(4)], axis=1)
                    for x in lines
                ]
                tails[0, k] = jnp.concatenate(row, axis=0).astype(BF16)

    @pl.when(source < 0)
    def clear():
        states[...] = jnp.zeros_like(states)
        tails[...] = jnp.zeros_like(tails)


def land(me, got, heads, own):
    lines = got[0].shape[1]
    slots = len(got) * CAP
    smem = pl.BlockSpec(memory_space=pltpu.SMEM)
    return pl.pallas_call(
        land_kernel,
        grid=(slots,),
        in_specs=[smem] + [pl.BlockSpec((CAP, lines, 128), lambda g: (0, 0, 0))] * len(got),
        out_specs=[
            pl.BlockSpec((1, heads, 128, 128), lambda g: (g, 0, 0, 0)),
            pl.BlockSpec((1, KERNEL - 1, own, 512), lambda g: (g, 0, 0, 0)),
        ],
        out_shape=[
            jax.ShapeDtypeStruct((slots, heads, 128, 128), F32),
            jax.ShapeDtypeStruct((slots, KERNEL - 1, own, 512), BF16),
        ],
        scratch_shapes=[pltpu.SMEM((len(got),), jnp.int32)],
        compiler_params=params(),
        cost_estimate=pl.CostEstimate(flops=10**6, bytes_accessed=4 << 20, transcendentals=0),
        name="land",
    )(me, *got)


def exchange(parts, axis):
    count = len(parts)
    got = {0: parts[0]}
    for k in range(count - 1, 0, -1):
        got[k] = lax.ppermute(parts[k], axis, [(i, i ^ k) for i in range(count)])
    return [got[k] for k in range(count)]


def body(
    mixed,
    decay_in,
    beta_in,
    gate_z,
    conv_weight,
    a_log,
    dt_bias,
    norm_gain,
    req_blocks,
    replica_of,
    finished,
):
    n = lax.axis_size("seq")
    replicas = lax.axis_size("rep")
    heads = mixed.shape[1]
    own = heads // n
    me = lax.axis_index("seq").astype(jnp.int32).reshape(1)
    par, *kpack = pack_keys(
        me, mixed[0], decay_in[0], beta_in[0], conv_weight, a_log, dt_bias
    )
    kp = exchange(kpack, "seq")
    halo, *vpack = pack_values(me, mixed[0], n)
    halo = lax.ppermute(halo, "seq", [(i, i + 1) for i in range(n - 1)])
    vp = exchange(vpack, "seq")
    par, halo = lax.optimization_barrier((par, halo))
    hsol, hft, hgs, hrows, all_par = head_prep(req_blocks, me, par, kp)
    wk, wv, sc, ft, qs, rows = token_prep(
        req_blocks, me, mixed[0], decay_in[0], beta_in[0], halo, all_par.reshape(heads, 32, 128)
    )
    sin, ends, ktails = head_chain(req_blocks, me, par, hsol, hft, hgs, hrows, vp)
    sin = lax.all_to_all(sin, "seq", 0, 0, tiled=True)
    my_rep = lax.axis_index("rep").astype(jnp.int32).reshape(1)
    send = choose(req_blocks, replica_of, finished, my_rep, ends, ktails, replicas)
    got = exchange(send, "rep")
    states, tails = land(my_rep, got, own * RATIO, own)
    out = token_out(
        req_blocks,
        me,
        sin.reshape(heads * RATIO, 128, 128),
        wk,
        wv,
        sc,
        ft,
        qs,
        rows,
        gate_z[0],
        norm_gain.reshape(1, DV),
    )
    return (out[None], states[None], tails[None])


def solution(mesh):
    placed = (
        P("rep", None, None, "seq"),
        P("rep", None, None, "seq"),
        P("rep", None, None, "seq"),
        P("rep", None, None, "seq"),
        P(None, "seq", None),
        P("seq"),
        P("seq"),
        P(),
        P("rep", None),
        P("rep", None),
        P("rep", None),
    )
    return jax.shard_map(
        body,
        mesh=mesh,
        in_specs=placed,
        out_specs=(
            P("rep", None, None, "seq"),
            P("rep", None, "seq", None, None),
            P("rep", None, None, "seq", None),
        ),
        check_vma=False,
    )
```

```python
import jax
import jax.numpy as jnp
from jax import lax
from jax.experimental import pallas as pl
from jax.experimental.pallas import tpu as pltpu
from jax.sharding import PartitionSpec as P

DK = 128
DV = 128
KERNEL = 4
SPAN = 64
CAP = 2
RATIO = 2
TILE = 2 * SPAN
KROWS = 160
VROWS = 288
STEP = 4
WIDE = 8
MOST = 16
EPSILON = 1e-06
F32 = jnp.float32
BF16 = jnp.bfloat16
VMEM_LIMIT = 56 * 1024 * 1024


def params(**kwargs):
    return pltpu.CompilerParams(vmem_limit_bytes=VMEM_LIMIT, **kwargs)


def iota(shape, dim):
    return lax.broadcasted_iota(jnp.int32, shape, dim)


def dot(left, right):
    return jnp.dot(left, right, preferred_element_type=F32)


def split(wide):
    high = wide.astype(BF16)
    return high, (wide - high.astype(F32)).astype(BF16)


def halves(shape):
    first = iota(shape, len(shape) - 1) < SPAN
    return jnp.where(first, 1.0, 0.0).astype(BF16), jnp.where(first, 0.0, 1.0).astype(BF16)


def corner(first, second):
    none = jnp.zeros_like(first)
    top = jnp.concatenate([first, none], axis=1)
    return jnp.concatenate([top, jnp.concatenate([none, second], axis=1)], axis=0)


def diagonal(packed, masks):
    squares = []
    for r in range(RATIO):
        one = packed[:, r * TILE : (r + 1) * TILE]
        squares.append(jnp.concatenate([one * masks[0], one * masks[1]], axis=0))
    return corner(*squares)


def block_dot(left, right, masks):
    return dot(left, diagonal(right, masks))


def parameter_lines(h, cw, alog, dtb):
    taps = cw[:, h].astype(F32)
    rows = [taps[tap : tap + 1, cg * 128 : (cg + 1) * 128] for tap in range(KERNEL) for cg in range(4)]
    rest = jnp.concatenate(
        [jnp.full((1, 128), ref[h * RATIO + r], F32) for ref in (alog, dtb) for r in range(RATIO)], axis=0
    )
    parts = []
    for _ in range(3):
        part = rest.astype(BF16).astype(F32)
        rest = rest - part
        parts.append(part)
    return jnp.concatenate(rows + parts + [jnp.zeros((4, 128), F32)], axis=0)


def parameters(lines):
    wide = lines.astype(F32)
    rest = wide[16:20] + wide[20:24] + wide[24:28]
    return wide[:16], rest[:RATIO], rest[RATIO:]


def pack_keys_kernel(mixed, dec, beta, cw, alog, dtb, after, kout, pout):
    row = iota((32, TILE), 0)
    own = pout.shape[0]
    lines = [parameter_lines(h, cw, alog, dtb) for h in range(own)]
    for t in range(mixed.shape[0]):
        kout[t, :DK] = mixed[t]
        rest = lines[t % own]
        d, b = dec[t].astype(F32), beta[t].astype(F32)
        for r in range(RATIO):
            rest = jnp.where(row == 28 + r, d[r : r + 1], rest)
            rest = jnp.where(row == 30 + r, b[r : r + 1], rest)
        kout[t, DK:] = rest.astype(BF16)

    @pl.when(pl.program_id(0) == 0)
    def first():
        for h in range(own):
            pout[h] = lines[h].astype(BF16)


def pack_keys(mixed, dec, beta, cw, alog, dtb, after):
    heads = mixed.shape[0]
    own = cw.shape[1]
    step = heads // 2
    smem = pl.BlockSpec(memory_space=pltpu.SMEM)
    return pl.pallas_call(
        pack_keys_kernel,
        grid=(heads // step,),
        in_specs=[
            pl.BlockSpec((step, DK, TILE), lambda g: (g, 1, 0)),
            pl.BlockSpec((step, RATIO, TILE), lambda g: (g, 0, 0)),
            pl.BlockSpec((step, RATIO, TILE), lambda g: (g, 0, 0)),
            pl.BlockSpec((KERNEL, own, 512), lambda g: (0, 0, 0)),
            smem,
            smem,
            pl.BlockSpec(memory_space=pl.ANY),
        ],
        out_specs=[
            pl.BlockSpec((step, KROWS, TILE), lambda g: (g, 0, 0)),
            pl.BlockSpec((own, 32, 128), lambda g: (0, 0, 0)),
        ],
        out_shape=[
            jax.ShapeDtypeStruct((heads, KROWS, TILE), BF16),
            jax.ShapeDtypeStruct((own, 32, 128), BF16),
        ],
        compiler_params=params(),
        cost_estimate=pl.CostEstimate(flops=10**6, bytes_accessed=2 << 20, transcendentals=0),
        name="pack_keys",
    )(mixed, dec, beta, cw, alog, dtb, after)


def pack_values_kernel(me, mixed, *refs):
    step = pl.program_id(0)
    outs = refs[-2 * pl.num_programs(0) :]
    hout = refs[-2 * pl.num_programs(0) - 1]
    own = outs[0].shape[0]
    row, tok = iota((TILE, 128), 1), iota((TILE, 128), 0)
    place = row & 15
    picks = []
    for cg in range(4):
        hit = (row < 32) & (place < 12) & ((place & 3) == cg)
        hit = hit & (tok == (row >> 4) * SPAN + 61 + (place >> 2))
        picks.append(jnp.where(hit, 1.0, 0.0).astype(BF16))
    all_tails = []
    for h in range(mixed.shape[0]):
        tails = dot(mixed[h, :128], picks[0])
        for cg in range(1, 4):
            tails = tails + dot(mixed[h, cg * 128 : (cg + 1) * 128], picks[cg])
        all_tails.append(jnp.transpose(tails)[:32].astype(BF16))
        hout[h] = all_tails[h][16:]
    for i, out in enumerate(outs):
        for odd in range(2):

            @pl.when((step == i // 2) & ((me[0] & 1) == odd))
            def put():
                for h in range(own):
                    t = ((i & 1) ^ odd) * own + h
                    out[h, :256] = mixed[t, 2 * DK :]
                    out[h, 256:] = all_tails[t]


def pack_values(me, mixed, n, first, pairs, halo):
    heads = mixed.shape[0]
    own = heads // n
    extra = [] if halo is None else [halo]

    def place(g, me):
        return ((me[0] >> 1) ^ (g + first), 0, 0)

    return pl.pallas_call(
        pack_values_kernel,
        grid_spec=pltpu.PrefetchScalarGridSpec(
            num_scalar_prefetch=1,
            grid=(pairs,),
            in_specs=[pl.BlockSpec((2 * own, 512, TILE), place)]
            + [pl.BlockSpec(memory_space=pl.ANY)] * len(extra),
            out_specs=[pl.BlockSpec((2 * own, 16, TILE), place)]
            + [pl.BlockSpec((own, VROWS, TILE), lambda g, me: (0, 0, 0))] * (2 * pairs),
        ),
        out_shape=[jax.ShapeDtypeStruct((heads, 16, TILE), BF16)]
        + [jax.ShapeDtypeStruct((own, VROWS, TILE), BF16)] * (2 * pairs),
        input_output_aliases={2: 0} if extra else {},
        compiler_params=params(),
        cost_estimate=pl.CostEstimate(flops=10**8, bytes_accessed=4 << 20, transcendentals=0),
        name="pack_values",
    )(me, mixed, *extra)


def is_fresh(req, block):
    start = jnp.int32(0)
    fresh = jnp.bool_(False)
    for j in range(req.shape[1]):
        fresh = fresh | (start == block)
        start = start + req[0, j]
    return fresh


def tap_tables():
    row, part = iota((16, 4 * 128), 0), iota((16, 4 * 128), 1) >> 7
    hits = [((row & 3) == cg) & ((row >> 2) == part) for cg in range(4)]
    return [jnp.where(hit, 1.0, 0.0).astype(BF16) for hit in hits]


def halo_tables():
    row, lane = iota((48, 128), 0), iota((48, 128), 1)
    token = (row >> 2) % 3
    hits = [((row & 3) == cg) & (row < 36) & (token == lane) for cg in range(4)]
    return [jnp.where(hit, 1.0, 0.0).astype(BF16) for hit in hits]


def turned_dot(rows, table):
    return lax.dot_general(rows, table, (((0,), (0,)), ((), ())), preferred_element_type=F32)


def spread_taps(par, table):
    both = turned_dot(par, table)
    return [both[:, tap * 128 : (tap + 1) * 128] for tap in range(KERNEL)]


def halo_terms(halo, par, not_fresh0):
    x = [halo[4 * k : 4 * k + 4].astype(F32) * not_fresh0 for k in range(3)]
    w = [par[4 * k : 4 * k + 4] for k in range(3)]
    terms = jnp.concatenate(
        [w[0] * x[0] + w[1] * x[1] + w[2] * x[2], w[0] * x[1] + w[1] * x[2], w[0] * x[2]], axis=0
    )
    high = terms.astype(BF16).astype(F32)
    middle = (terms - high).astype(BF16).astype(F32)
    parts = [high, middle, terms - high - middle, jnp.zeros((12, 128), F32)]
    return jnp.concatenate(parts, axis=0).astype(BF16)


def convolve(raw, before, terms, taps, masks):
    lane = iota((1, TILE), 1)
    cur = raw.astype(F32)
    total = taps[KERNEL - 1] * cur
    if terms is not None:
        total = total + terms
    for back in range(1, KERNEL):
        moved = cur if before is None else jnp.where(lane >= TILE - back, before, cur)
        total = total + taps[KERNEL - 1 - back] * (pltpu.roll(moved, back, 1) * masks[back - 1])
    return (total / (1.0 + jnp.exp(-total))).astype(BF16)


def conv_masks(cut0, cut1):
    lane = iota((1, TILE), 1)
    masks = []
    for back in range(1, KERNEL):
        gone = ((lane < back) & cut0) | ((lane >= SPAN) & (lane < SPAN + back) & cut1)
        masks.append(jnp.where(gone, 0.0, 1.0))
    return masks


def row_prep(dec, beta, alog, dtb):
    lane = iota(dec.shape, 1)
    x = dec + dtb
    decay = -jnp.exp(alog) * (jnp.maximum(x, 0.0) + jnp.log1p(jnp.exp(-jnp.abs(x))))
    cum = decay
    for shift in (1, 2, 4, 8, 16, 32):
        cum = cum + jnp.where((lane & (SPAN - 1)) >= shift, pltpu.roll(cum, shift, 1), 0.0)
    strength = 1.0 / (1.0 + jnp.exp(-beta))
    grown = jnp.exp(cum)
    close0, close1 = cum[:, SPAN - 1 : SPAN], cum[:, TILE - 1 :]
    fade = jnp.exp(jnp.where(lane < SPAN, close0, close1) - cum)
    keep0 = jnp.exp(jnp.broadcast_to(close0, cum.shape))
    keep1 = jnp.exp(jnp.broadcast_to(close1, cum.shape))
    return cum, strength, grown, fade, keep0, keep1


def unit_inverses(systems):
    shape = (SPAN, RATIO * TILE)
    row, col = iota(shape, 0), iota(shape, 1) & (SPAN - 1)
    near = (row >> 4) == (col >> 4)
    eye = jnp.where(row == col, 1.0, 0.0)
    masks = halves((SPAN, TILE))

    def low(arrays):
        return [a.astype(BF16) for a in arrays]

    def stack(pair):
        return jnp.concatenate(pair, axis=0)

    total = [jnp.where(near, eye - a, 0.0) for a in systems]
    power = low([jnp.where(near, -a, 0.0) for a in systems])
    power = low([block_dot(p, p, masks) for p in power])
    for _ in range(2):
        both = [block_dot(stack([t, p]), p, masks) for t, p in zip(low(total), power)]
        total = [t + b[:SPAN] for t, b in zip(total, both)]
        power = low([b[SPAN:] for b in both])
    total = [t + block_dot(l, p, masks) for t, l, p in zip(total, low(total), power)]
    small = low(total)
    rest = low([jnp.where(near, 0.0, a) for a in systems])
    cross = low([block_dot(t, r, masks) for t, r in zip(small, rest)])
    total = [t - block_dot(x, l, masks) for t, x, l in zip(total, cross, small)]
    small = low(total)
    solved = []
    for a, x in zip(systems, small):
        wide = x.astype(F32)
        parts = block_dot(stack(split(a)), x, masks)
        miss = eye - wide - (parts[:SPAN] + parts[SPAN:])
        solved.append((wide + block_dot(x, miss.astype(BF16), masks)).astype(BF16))
    return solved


def both_blocks(square):
    none = jnp.zeros((SPAN, square.shape[1]), square.dtype)
    first = jnp.concatenate([square[:SPAN], none], axis=0)
    return jnp.concatenate([first, jnp.concatenate([none, square[SPAN:]], axis=0)], axis=1)


def unit_keys(convolved):
    wide = convolved.astype(F32)
    return (wide * lax.rsqrt(jnp.sum(wide * wide, axis=0, keepdims=True) + EPSILON)).astype(BF16)


def solve_tiles(keys, queries, prep):
    cum, strength, grown, fade, keep0, keep1 = prep
    row, lane = iota((SPAN, TILE), 0), iota((SPAN, TILE), 1)
    early = lane < SPAN
    seen = (lane & (SPAN - 1)) >= row
    later = (lane & (SPAN - 1)) > row
    columns = jnp.transpose(jnp.concatenate([cum, fade], axis=0))
    count = cum.shape[0]

    def beside(tall):
        return jnp.where(early, tall[:SPAN], tall[SPAN:])

    systems, faded, scores = [], [], []
    for t, k in enumerate(keys):
        turned = jnp.transpose(k.astype(F32))
        if queries is None:
            gram = beside(dot(turned.astype(BF16), k))
        else:
            prod = dot(turned.astype(BF16), jnp.concatenate([k, queries[t]], axis=1))
            gram, touch = beside(prod[:, :TILE]), beside(prod[:, TILE:])
        pair = []
        for r in range(RATIO):
            at = t * RATIO + r
            diff = cum[at : at + 1] - beside(columns[:, at : at + 1])
            ratio = jnp.where(seen, jnp.exp(jnp.where(seen, diff, 0.0)), 0.0)
            pair.append(jnp.where(later, strength[at : at + 1] * gram * ratio, 0.0))
            if queries is not None:
                scores.append((touch * ratio).astype(BF16))
            faded.append((turned * columns[:, count + at : count + at + 1]).astype(BF16))
        systems.append(jnp.concatenate(pair, axis=1))
    return unit_inverses(systems), faded, scores


def token_prep_kernel(req, me, mixed, dec, beta, halo, par_lines, wk, wv, sc, ft, qo, rows):
    fresh0, fresh1 = is_fresh(req, me[0] * 2), is_fresh(req, me[0] * 2 + 1)
    not_fresh0 = jnp.where(fresh0, 0.0, 1.0)
    masks = conv_masks(True, fresh1)
    tap_tab, halo_tab = tap_tables(), halo_tables()
    tiles = range(mixed.shape[0])
    par = [parameters(par_lines[t]) for t in tiles]

    def gather(pick):
        return jnp.concatenate([pick(t) for t in tiles], axis=0)

    prep = row_prep(
        gather(lambda t: dec[t].astype(F32)),
        gather(lambda t: beta[t].astype(F32)),
        jnp.concatenate([p[1] for p in par], axis=0),
        jnp.concatenate([p[2] for p in par], axis=0),
    )
    cum, strength, grown, fade, keep0, keep1 = prep
    keys, queries, values = [], [], []
    for t in tiles:
        terms = halo_terms(halo[t], par[t][0], not_fresh0)
        lines = par_lines[t, :16]
        q, k, v0, v1 = [
            convolve(
                mixed[t, c * 128 : (c + 1) * 128],
                None,
                turned_dot(terms, halo_tab[c]),
                spread_taps(lines, tap_tab[c]),
                masks,
            )
            for c in range(4)
        ]
        keys.append(unit_keys(k))
        queries.append(q)
        values.append((v0, v1))
        qo[t] = q
        rows[t] = jnp.concatenate(
            [keep0[2 * t : 2 * t + 2], grown[2 * t : 2 * t + 2], keep1[2 * t : 2 * t + 2], strength[2 * t : 2 * t + 2]],
            axis=0,
        )
    solved, faded, scores = solve_tiles(keys, queries, prep)
    sides = halves((SPAN, TILE))
    for t in tiles:
        stacks = []
        for r in range(RATIO):
            at = t * RATIO + r
            s, lift = strength[at : at + 1], strength[at : at + 1] * grown[at : at + 1]
            stacked = jnp.concatenate(
                [lift * keys[t].astype(F32), s * values[t][r].astype(F32)], axis=0
            )
            stacks.append(stacked.astype(BF16))
            sc[t, :, r * TILE : (r + 1) * TILE] = scores[at]
            ft[at] = faded[at]
        out = block_dot(jnp.concatenate(stacks, axis=1), solved[t], sides).astype(BF16)
        for r in range(RATIO):
            wk[t * RATIO + r] = out[:DK, r * TILE : (r + 1) * TILE]
            wv[t * RATIO + r] = out[DK:, r * TILE : (r + 1) * TILE]


def token_prep(req, me, mixed, dec, beta, halo, par):
    heads = mixed.shape[0]
    smem = pl.BlockSpec(memory_space=pltpu.SMEM)

    def tiles(count, *rest):
        return pl.BlockSpec((count,) + rest, lambda g: (g,) + (0,) * len(rest))

    square = jax.ShapeDtypeStruct((heads * RATIO, 128, 128), BF16)
    return pl.pallas_call(
        token_prep_kernel,
        grid=(heads // WIDE,),
        in_specs=[
            smem,
            smem,
            tiles(WIDE, 512, TILE),
            tiles(WIDE, RATIO, TILE),
            tiles(WIDE, RATIO, TILE),
            tiles(WIDE, 16, TILE),
            pl.BlockSpec((WIDE, 32, 128), lambda g: (g, 4, 0)),
        ],
        out_specs=[tiles(WIDE * RATIO, 128, 128)] * 2
        + [tiles(WIDE, SPAN, RATIO * TILE), tiles(WIDE * RATIO, 128, 128)]
        + [tiles(WIDE, 128, 128), tiles(WIDE, 8, 128)],
        out_shape=[square] * 2
        + [
            jax.ShapeDtypeStruct((heads, SPAN, RATIO * TILE), BF16),
            square,
            jax.ShapeDtypeStruct((heads, 128, 128), BF16),
            jax.ShapeDtypeStruct((heads, 8, 128), F32),
        ],
        compiler_params=params(),
        cost_estimate=pl.CostEstimate(flops=10**10, bytes_accessed=8 << 20, transcendentals=10**6),
        name="token_prep",
    )(req, me, mixed, dec, beta, halo, par)


def head_prep_kernel(req, kp, previous, par_lines, sol, ft, gs, rows):
    step = pl.program_id(0)
    depth, own = kp.shape[0], kp.shape[1]
    tap_tab = tap_tables()
    order = [(d, h) for d in range(depth) for h in range(own)]
    par = [parameters(par_lines[h]) for h in range(own)]

    small = [kp[d, h, DK:].astype(F32) for d, h in order]
    prep = row_prep(
        jnp.concatenate([s[28:30] for s in small], axis=0),
        jnp.concatenate([s[30:32] for s in small], axis=0),
        jnp.concatenate([par[h][1] for d, h in order], axis=0),
        jnp.concatenate([par[h][2] for d, h in order], axis=0),
    )
    cum, strength, grown, fade, keep0, keep1 = prep
    keys = []
    taps = [spread_taps(par_lines[h, :16], tap_tab[1]) for h in range(own)]
    for d in range(depth):
        block = (step * depth + d) * 2
        masks = conv_masks(is_fresh(req, block), is_fresh(req, block + 1))
        for h in range(own):
            before = (kp[d - 1, h, :DK] if d else previous[0, h]).astype(F32)
            keys.append(unit_keys(convolve(kp[d, h, :DK], before, None, taps[h], masks)))
    solved, faded, unused = solve_tiles(keys, None, prep)
    sides = halves((SPAN, TILE))
    for t, (d, h) in enumerate(order):
        rows[d, h] = jnp.concatenate(
            [keep0[2 * t : 2 * t + 2], keep1[2 * t : 2 * t + 2], strength[2 * t : 2 * t + 2], strength[2 * t : 2 * t + 2]],
            axis=0,
        )
        scaled = []
        for r in range(RATIO):
            at = t * RATIO + r
            lift = strength[at : at + 1] * grown[at : at + 1]
            scaled.append((lift * keys[t].astype(F32)).astype(BF16))
        wide = block_dot(jnp.concatenate(scaled, axis=1), solved[t], sides).astype(BF16)
        sol[d, h] = solved[t]
        for r in range(RATIO):
            at = t * RATIO + r
            drop = dot(wide[:, r * TILE : (r + 1) * TILE], both_blocks(faded[at])).astype(BF16)
            gs[d, h, r, 0] = drop[:, :DK]
            gs[d, h, r, 1] = drop[:, DK:]
            ft[d, h, r] = faded[at]


def head_prep(req, kp, par):
    n, own = kp.shape[:2]
    depth = MOST // own
    smem = pl.BlockSpec(memory_space=pltpu.SMEM)

    def tiles(*rest):
        return pl.BlockSpec((depth, own) + rest, lambda g: (g, 0) + (0,) * len(rest))

    square = jax.ShapeDtypeStruct((n, own, RATIO, 128, 128), BF16)
    return pl.pallas_call(
        head_prep_kernel,
        grid=(n // depth,),
        in_specs=[
            smem,
            tiles(KROWS, TILE),
            pl.BlockSpec((1, own, DK, TILE), lambda g: (jnp.maximum(g * depth - 1, 0), 0, 0, 0)),
            pl.BlockSpec((own, 32, 128), lambda g: (0, 0, 0)),
        ],
        out_specs=[
            tiles(SPAN, RATIO * TILE),
            tiles(RATIO, 128, 128),
            tiles(RATIO, 2, 128, 128),
            tiles(8, 128),
        ],
        out_shape=[
            jax.ShapeDtypeStruct((n, own, SPAN, RATIO * TILE), BF16),
            square,
            jax.ShapeDtypeStruct((n, own, RATIO, 2, 128, 128), BF16),
            jax.ShapeDtypeStruct((n, own, 8, 128), F32),
        ],
        compiler_params=params(),
        cost_estimate=pl.CostEstimate(flops=10**10, bytes_accessed=6 << 20, transcendentals=10**6),
        name="head_prep",
    )(req, kp, kp, par)


def head_chain_kernel(req, me, par_lines, sol, ft, gs, rows, *refs):
    n = refs[-6].shape[0]
    arrived, (sin, ends, tails, state, vp, spread) = refs[:n], refs[n:]
    step = pl.program_id(0)
    depth, own = sol.shape[0], sol.shape[1]

    @pl.when(step == 0)
    def first():
        for k, one in enumerate(arrived):
            vp[me[0] ^ k] = one[...]
            tails[me[0] ^ k] = one[:, 256:]
        tap_tab = tap_tables()
        for h in range(own):
            for r in range(RATIO):
                for tap, wide in enumerate(spread_taps(par_lines[h, :16], tap_tab[2 + r])):
                    spread[h * RATIO + r, tap] = wide

    sides = halves((SPAN, TILE))
    heads = [(h, r) for h in range(own) for r in range(RATIO)]
    taps = [[spread[v, tap] for tap in range(KERNEL)] for v in range(len(heads))]
    current = [state[v] for v in range(len(heads))]
    for d in range(depth):
        tile = step * depth + d
        past = jnp.maximum(tile - 1, 0)
        fresh = [is_fresh(req, tile * 2), is_fresh(req, tile * 2 + 1)]
        masks = conv_masks(fresh[0], fresh[1])
        gains = []
        for h in range(own):
            scaled = []
            for r in range(RATIO):
                raw = vp[tile, h, r * DV : (r + 1) * DV]
                before = vp[past, h, r * DV : (r + 1) * DV].astype(F32)
                value = convolve(raw, before, None, taps[h * RATIO + r], masks)
                scaled.append((rows[d, h, 4 + r : 5 + r] * value.astype(F32)).astype(BF16))
            wide = block_dot(jnp.concatenate(scaled, axis=1), sol[d, h], sides).astype(BF16)
            for r in range(RATIO):
                gains.append(dot(wide[:, r * TILE : (r + 1) * TILE], both_blocks(ft[d, h, r])))
        for half in range(2):
            for h in range(own):
                now = [jnp.where(fresh[half], 0.0, current[h * RATIO + r]) for r in range(RATIO)]
                lost = dot(
                    jnp.concatenate([x.astype(BF16) for x in now], axis=1),
                    corner(gs[d, h, 0, half], gs[d, h, 1, half]),
                )
                for r in range(RATIO):
                    v = h * RATIO + r
                    keep = rows[d, h, 2 * half + r : 2 * half + r + 1]
                    gain = gains[v][:, half * DV : (half + 1) * DV]
                    current[v] = keep * now[r] + (gain - lost[:, r * TILE : (r + 1) * TILE])
                    ends[d * 2 + half, v] = current[v].astype(BF16)
        onward = lax.rem(tile + 1, n)
        for v in range(len(heads)):
            sin[onward, v] = current[v].astype(BF16)
    for v in range(len(heads)):
        state[v] = current[v]


def head_chain(req, me, par, sol, ft, gs, rows, arrived):
    n, own = sol.shape[:2]
    depth = WIDE // own
    smem = pl.BlockSpec(memory_space=pltpu.SMEM)

    def tiles(*rest):
        return pl.BlockSpec((depth, own) + rest, lambda g: (g, 0) + (0,) * len(rest))

    return pl.pallas_call(
        head_chain_kernel,
        grid=(n // depth,),
        in_specs=[
            smem,
            smem,
            pl.BlockSpec((own, 32, 128), lambda g: (0, 0, 0)),
            tiles(SPAN, RATIO * TILE),
            tiles(RATIO, 128, 128),
            tiles(RATIO, 2, 128, 128),
            tiles(8, 128),
        ]
        + [pl.BlockSpec((own, VROWS, TILE), lambda g: (0, 0, 0))] * n,
        out_specs=[
            pl.BlockSpec((n, own * RATIO, 128, 128), lambda g: (0, 0, 0, 0)),
            pl.BlockSpec((2 * depth, own * RATIO, 128, 128), lambda g: (g, 0, 0, 0)),
            pl.BlockSpec((n, own, 32, TILE), lambda g: (0, 0, 0, 0)),
        ],
        out_shape=[
            jax.ShapeDtypeStruct((n, own * RATIO, 128, 128), BF16),
            jax.ShapeDtypeStruct((2 * n, own * RATIO, 128, 128), BF16),
            jax.ShapeDtypeStruct((n, own, 32, TILE), BF16),
        ],
        scratch_shapes=[
            pltpu.VMEM((own * RATIO, 128, 128), F32),
            pltpu.VMEM((n, own, VROWS, TILE), BF16),
            pltpu.VMEM((own * RATIO, KERNEL, 128, 128), F32),
        ],
        compiler_params=params(),
        cost_estimate=pl.CostEstimate(flops=3 * 10**9, bytes_accessed=8 << 20, transcendentals=10**6),
        name="head_chain",
    )(req, me, par, sol, ft, gs, rows, *arrived)


def choose_kernel(req, rep, fin, me, ends, kt, *refs):
    outs, counts = refs[:-1], refs[-1]
    own, heads = kt.shape[1], ends.shape[1]
    base = heads * 128
    for i, out in enumerate(outs):
        out[...] = jnp.zeros_like(out)
        counts[i] = 0
    end = jnp.int32(-1)
    for j in range(req.shape[1]):
        end = end + req[0, j]
        where = rep[0, j] ^ me[0]
        place = jnp.minimum(counts[where], CAP - 1)
        done = fin[0, j] > 0
        counts[where] = counts[where] + jnp.where(done, 1, 0)
        for i, out in enumerate(outs):

            @pl.when(done & (where == i))
            def take():
                for v in range(heads):
                    out[place, v * 128 : (v + 1) * 128] = ends[end, v]
                for h in range(own):
                    lines = kt[end >> 1, h].astype(F32)
                    lines = jnp.where((end & 1) > 0, lines[16:], lines[:16]).astype(BF16)
                    out[place, base + h * 16 : base + h * 16 + 16] = lines

    for i, out in enumerate(outs):
        number = jnp.full((16, 128), counts[i], jnp.int32).astype(F32).astype(BF16)
        for c in range(CAP):
            out[c, base + own * 16 :] = number


def choose(req, rep, fin, me, ends, tails, replicas):
    own = tails.shape[1]
    smem = pl.BlockSpec(memory_space=pltpu.SMEM)
    lines = own * RATIO * 128 + own * 16 + 16
    return pl.pallas_call(
        choose_kernel,
        grid=(1,),
        in_specs=[
            smem,
            smem,
            smem,
            smem,
            pl.BlockSpec(ends.shape, lambda g: (0, 0, 0, 0)),
            pl.BlockSpec(tails.shape, lambda g: (0, 0, 0, 0)),
        ],
        out_specs=[pl.BlockSpec((CAP, lines, 128), lambda g: (0, 0, 0))] * replicas,
        out_shape=[jax.ShapeDtypeStruct((CAP, lines, 128), BF16)] * replicas,
        scratch_shapes=[pltpu.SMEM((replicas,), jnp.int32)],
        compiler_params=params(),
        cost_estimate=pl.CostEstimate(flops=10**6, bytes_accessed=4 << 20, transcendentals=0),
        name="choose",
    )(req, rep, fin, me, ends, tails)


def token_out_kernel(req, me, sin, wk, wv, sc, ft, qs, rows, gate, norm_gain, out):
    gain = jnp.transpose(jnp.broadcast_to(norm_gain[...], (TILE, DV)))
    stay0 = jnp.where(is_fresh(req, me[0] * 2), 0.0, 1.0)
    stay1 = jnp.where(is_fresh(req, me[0] * 2 + 1), 0.0, 1.0)
    lane = iota((DV, TILE), 1)
    early = lane < SPAN
    sides = halves((SPAN, TILE))
    units = [(t, r) for t in range(qs.shape[0]) for r in range(RATIO)]
    both = [jnp.concatenate([wk[t * RATIO + r], qs[t]], axis=1) for t, r in units]
    enter = [sin[t * RATIO + r].astype(F32) * stay0 for t, r in units]
    first = [dot(e.astype(BF16), b) for e, b in zip(enter, both)]
    wide = [wv[t * RATIO + r].astype(F32) for t, r in units]
    new0 = [jnp.where(early, w - f[:, :TILE], 0.0) for w, f in zip(wide, first)]
    tiles = range(qs.shape[0])
    pairs = [
        dot(
            jnp.concatenate([new0[2 * t].astype(BF16), new0[2 * t + 1].astype(BF16)], axis=1),
            corner(ft[2 * t], ft[2 * t + 1]),
        )
        for t in tiles
    ]
    middle = [
        (rows[t, r : r + 1] * e + pairs[t][:, r * TILE : (r + 1) * TILE]) * stay1
        for (t, r), e in zip(units, enter)
    ]
    second = [dot(m.astype(BF16), b) for m, b in zip(middle, both)]
    new = [
        jnp.where(early, x, w - s[:, :TILE]).astype(BF16) for x, w, s in zip(new0, wide, second)
    ]
    near = [
        block_dot(jnp.concatenate([new[2 * t], new[2 * t + 1]], axis=1), sc[t], sides) for t in tiles
    ]
    for at, (t, r) in enumerate(units):
        core = rows[t, 2 + r : 3 + r] * jnp.where(early, first[at][:, TILE:], second[at][:, TILE:])
        core = (core + near[t][:, r * TILE : (r + 1) * TILE]).astype(BF16).astype(F32)
        inverse_rms = lax.rsqrt(jnp.mean(core * core, axis=0, keepdims=True) + EPSILON)
        z = gate[t, r * DV : (r + 1) * DV].astype(F32)
        result = core * inverse_rms * gain * (z / (1.0 + jnp.exp(-z)))
        out[t, r * DV : (r + 1) * DV] = result.astype(BF16)


def token_out(req, me, sin, wk, wv, sc, ft, qs, rows, gate, gain):
    heads = qs.shape[0]
    smem = pl.BlockSpec(memory_space=pltpu.SMEM)

    def tiles(count, *rest):
        return pl.BlockSpec((count,) + rest, lambda g: (g,) + (0,) * len(rest))

    return pl.pallas_call(
        token_out_kernel,
        grid=(heads // STEP,),
        in_specs=[smem, smem]
        + [tiles(STEP * RATIO, 128, 128)] * 3
        + [tiles(STEP, SPAN, RATIO * TILE), tiles(STEP * RATIO, 128, 128)]
        + [
            tiles(STEP, 128, 128),
            tiles(STEP, 8, 128),
            tiles(STEP, 256, TILE),
            pl.BlockSpec((1, 128), lambda g: (0, 0)),
        ],
        out_specs=tiles(STEP, 256, TILE),
        out_shape=jax.ShapeDtypeStruct((heads, 256, TILE), BF16),
        compiler_params=params(),
        cost_estimate=pl.CostEstimate(flops=10**9, bytes_accessed=8 << 20, transcendentals=10**6),
        name="token_out",
    )(req, me, sin, wk, wv, sc, ft, qs, rows, gate, gain)


def land_kernel(me, *refs):
    got, (states, tails, counts) = refs[:-3], refs[-3:]
    slot = pl.program_id(0)
    heads, own = states.shape[1], tails.shape[2]
    base = heads * 128

    @pl.when(slot == 0)
    def first():
        for i, one in enumerate(got):
            number = jnp.max(one[0, base + own * 16 :].astype(F32))
            counts[i] = number.astype(jnp.int32)

    start = jnp.int32(0)
    source, place = jnp.int32(-1), jnp.int32(0)
    for p in range(len(got)):
        away = me[0] ^ p
        number = counts[away]
        inside = (slot >= start) & (slot < start + number)
        source = jnp.where(inside, away, source)
        place = jnp.where(inside, slot - start, place)
        start = start + number
    place = jnp.clip(place, 0, CAP - 1)
    for i, one in enumerate(got):

        @pl.when(source == i)
        def take():
            for v in range(heads):
                states[0, v] = jnp.transpose(one[place, v * 128 : (v + 1) * 128]).astype(F32)
            lines = [one[place, base + h * 16 : base + h * 16 + 16].astype(F32) for h in range(own)]
            for k in range(KERNEL - 1):
                row = [
                    jnp.concatenate([x[4 * k + cg : 4 * k + cg + 1] for cg in range(4)], axis=1)
                    for x in lines
                ]
                tails[0, k] = jnp.concatenate(row, axis=0).astype(BF16)

    @pl.when(source < 0)
    def clear():
        states[...] = jnp.zeros_like(states)
        tails[...] = jnp.zeros_like(tails)


def land(me, got, heads, own):
    lines = got[0].shape[1]
    slots = len(got) * CAP
    smem = pl.BlockSpec(memory_space=pltpu.SMEM)
    return pl.pallas_call(
        land_kernel,
        grid=(slots,),
        in_specs=[smem] + [pl.BlockSpec((CAP, lines, 128), lambda g: (0, 0, 0))] * len(got),
        out_specs=[
            pl.BlockSpec((1, heads, 128, 128), lambda g: (g, 0, 0, 0)),
            pl.BlockSpec((1, KERNEL - 1, own, 512), lambda g: (g, 0, 0, 0)),
        ],
        out_shape=[
            jax.ShapeDtypeStruct((slots, heads, 128, 128), F32),
            jax.ShapeDtypeStruct((slots, KERNEL - 1, own, 512), BF16),
        ],
        scratch_shapes=[pltpu.SMEM((len(got),), jnp.int32)],
        compiler_params=params(),
        cost_estimate=pl.CostEstimate(flops=10**6, bytes_accessed=4 << 20, transcendentals=0),
        name="land",
    )(me, *got)


def exchange(parts, axis):
    count = len(parts)
    got = {0: parts[0]}
    for k in range(count - 1, 0, -1):
        got[k] = lax.ppermute(parts[k], axis, [(i, i ^ k) for i in range(count)])
    return [got[k] for k in range(count)]


def body(
    mixed,
    decay_in,
    beta_in,
    gate_z,
    conv_weight,
    a_log,
    dt_bias,
    norm_gain,
    req_blocks,
    replica_of,
    finished,
):
    n = lax.axis_size("seq")
    replicas = lax.axis_size("rep")
    heads = mixed.shape[1]
    own = heads // n
    me = lax.axis_index("seq").astype(jnp.int32).reshape(1)
    ahead = max(1, n // 8)
    near = n // 2 - ahead
    halo, *vfar = pack_values(me, mixed[0], n, near, ahead, None)
    kpack, par = pack_keys(
        mixed[0], decay_in[0], beta_in[0], conv_weight, a_log, dt_bias, vfar[-1]
    )
    halo, *vnear = pack_values(me, mixed[0], n, 0, near, halo)
    kp = lax.all_to_all(kpack.reshape(n, own, KROWS, TILE), "seq", 0, 0, tiled=True)
    halo = lax.ppermute(halo, "seq", [(i, i + 1) for i in range(n - 1)])
    vp = exchange(vnear + vfar, "seq")
    kp, halo = lax.optimization_barrier((kp, halo))
    wk, wv, sc, ft, qs, rows = token_prep(
        req_blocks, me, mixed[0], decay_in[0], beta_in[0], halo, kp.reshape(heads, KROWS, TILE)
    )
    hsol, hft, hgs, hrows = head_prep(req_blocks, kp, par)
    sin, ends, ktails = head_chain(req_blocks, me, par, hsol, hft, hgs, hrows, vp)
    sin = lax.all_to_all(sin, "seq", 0, 0, tiled=True)
    my_rep = lax.axis_index("rep").astype(jnp.int32).reshape(1)
    send = choose(req_blocks, replica_of, finished, my_rep, ends, ktails, replicas)
    got = exchange(send, "rep")
    states, tails = land(my_rep, got, own * RATIO, own)
    out = token_out(
        req_blocks,
        me,
        sin.reshape(heads * RATIO, 128, 128),
        wk,
        wv,
        sc,
        ft,
        qs,
        rows,
        gate_z[0],
        norm_gain.reshape(1, DV),
    )
    return (out[None], states[None], tails[None])


def solution(mesh):
    placed = (
        P("rep", None, None, "seq"),
        P("rep", None, None, "seq"),
        P("rep", None, None, "seq"),
        P("rep", None, None, "seq"),
        P(None, "seq", None),
        P("seq"),
        P("seq"),
        P(),
        P("rep", None),
        P("rep", None),
        P("rep", None),
    )
    return jax.shard_map(
        body,
        mesh=mesh,
        in_specs=placed,
        out_specs=(
            P("rep", None, None, "seq"),
            P("rep", None, "seq", None, None),
            P("rep", None, None, "seq", None),
        ),
        check_vma=False,
    )
```

```python
import jax
import jax.numpy as jnp
from jax import lax
from jax.experimental import pallas as pl
from jax.experimental.pallas import tpu as pltpu
from jax.sharding import PartitionSpec as P

DK = 128
DV = 128
KERNEL = 4
SPAN = 64
CAP = 2
RATIO = 2
TILE = 2 * SPAN
KROWS = 160
VROWS = 288
WIDE = 8
MOST = 16
EPSILON = 1e-06
F32 = jnp.float32
BF16 = jnp.bfloat16
VMEM_LIMIT = 56 * 1024 * 1024
ALL_VMEM = 63 * 1024 * 1024


def params(limit=VMEM_LIMIT):
    return pltpu.CompilerParams(vmem_limit_bytes=limit)


def iota(shape, dim):
    return lax.broadcasted_iota(jnp.int32, shape, dim)


def dot(left, right):
    return jnp.dot(left, right, preferred_element_type=F32)


def split(wide):
    high = wide.astype(BF16)
    return high, (wide - high.astype(F32)).astype(BF16)


def halves(shape):
    first = iota(shape, len(shape) - 1) < SPAN
    return jnp.where(first, 1.0, 0.0).astype(BF16), jnp.where(first, 0.0, 1.0).astype(BF16)


def corner(first, second):
    none = jnp.zeros_like(first)
    top = jnp.concatenate([first, none], axis=1)
    return jnp.concatenate([top, jnp.concatenate([none, second], axis=1)], axis=0)


def diagonal(packed, masks):
    squares = []
    for r in range(RATIO):
        one = packed[:, r * TILE : (r + 1) * TILE]
        squares.append(jnp.concatenate([one * masks[0], one * masks[1]], axis=0))
    return corner(*squares)


def block_dot(left, right, masks):
    return dot(left, diagonal(right, masks))


def parameter_lines(h, cw, alog, dtb):
    taps = cw[:, h].astype(F32)
    rows = [taps[tap : tap + 1, cg * 128 : (cg + 1) * 128] for tap in range(KERNEL) for cg in range(4)]
    rest = jnp.concatenate(
        [jnp.full((1, 128), ref[h * RATIO + r], F32) for ref in (alog, dtb) for r in range(RATIO)], axis=0
    )
    parts = []
    for _ in range(3):
        part = rest.astype(BF16).astype(F32)
        rest = rest - part
        parts.append(part)
    return jnp.concatenate(rows + parts + [jnp.zeros((4, 128), F32)], axis=0)


def parameters(lines):
    wide = lines.astype(F32)
    rest = wide[16:20] + wide[20:24] + wide[24:28]
    return wide[:16], rest[:RATIO], rest[RATIO:]


def pack_keys_kernel(mixed, dec, beta, cw, alog, dtb, kout, pout):
    row = iota((32, TILE), 0)
    own = pout.shape[0]
    lines = [parameter_lines(h, cw, alog, dtb) for h in range(own)]
    for t in range(mixed.shape[0]):
        kout[t, :DK] = mixed[t]
        rest = lines[t % own]
        d, b = dec[t].astype(F32), beta[t].astype(F32)
        for r in range(RATIO):
            rest = jnp.where(row == 28 + r, d[r : r + 1], rest)
            rest = jnp.where(row == 30 + r, b[r : r + 1], rest)
        kout[t, DK:] = rest.astype(BF16)

    @pl.when(pl.program_id(0) == 0)
    def first():
        for h in range(own):
            pout[h] = lines[h].astype(BF16)


def pack_keys(mixed, dec, beta, cw, alog, dtb):
    heads = mixed.shape[0]
    own = cw.shape[1]
    step = heads // 2
    smem = pl.BlockSpec(memory_space=pltpu.SMEM)
    return pl.pallas_call(
        pack_keys_kernel,
        grid=(heads // step,),
        in_specs=[
            pl.BlockSpec((step, DK, TILE), lambda g: (g, 1, 0)),
            pl.BlockSpec((step, RATIO, TILE), lambda g: (g, 0, 0)),
            pl.BlockSpec((step, RATIO, TILE), lambda g: (g, 0, 0)),
            pl.BlockSpec((KERNEL, own, 512), lambda g: (0, 0, 0)),
            smem,
            smem,
        ],
        out_specs=[
            pl.BlockSpec((step, KROWS, TILE), lambda g: (g, 0, 0)),
            pl.BlockSpec((own, 32, 128), lambda g: (0, 0, 0)),
        ],
        out_shape=[
            jax.ShapeDtypeStruct((heads, KROWS, TILE), BF16),
            jax.ShapeDtypeStruct((own, 32, 128), BF16),
        ],
        compiler_params=params(),
        cost_estimate=pl.CostEstimate(flops=10**6, bytes_accessed=2 << 20, transcendentals=0),
        name="pack_keys",
    )(mixed, dec, beta, cw, alog, dtb)


def pack_values_kernel(me, mixed, hout, *outs):
    step = pl.program_id(0)
    own = outs[0].shape[0]
    row, tok = iota((TILE, 128), 1), iota((TILE, 128), 0)
    place = row & 15
    picks = []
    for cg in range(4):
        hit = (row < 32) & (place < 12) & ((place & 3) == cg)
        hit = hit & (tok == (row >> 4) * SPAN + 61 + (place >> 2))
        picks.append(jnp.where(hit, 1.0, 0.0).astype(BF16))
    all_tails = []
    for h in range(mixed.shape[0]):
        tails = dot(mixed[h, :128], picks[0])
        for cg in range(1, 4):
            tails = tails + dot(mixed[h, cg * 128 : (cg + 1) * 128], picks[cg])
        all_tails.append(jnp.transpose(tails)[:32].astype(BF16))
        hout[h] = all_tails[h][16:]
    for i, out in enumerate(outs):

        @pl.when((step == i // 4) & ((me[0] & 3) == 0))
        def put0():
            put(mixed, all_tails, out, (i & 3) ^ 0, own)

        @pl.when((step == i // 4) & ((me[0] & 3) == 1))
        def put1():
            put(mixed, all_tails, out, (i & 3) ^ 1, own)

        @pl.when((step == i // 4) & ((me[0] & 3) == 2))
        def put2():
            put(mixed, all_tails, out, (i & 3) ^ 2, own)

        @pl.when((step == i // 4) & ((me[0] & 3) == 3))
        def put3():
            put(mixed, all_tails, out, (i & 3) ^ 3, own)


def put(mixed, all_tails, out, place, own):
    for h in range(own):
        out[h, :256] = mixed[place * own + h, 2 * DK :]
        out[h, 256:] = all_tails[place * own + h]


def pack_values(me, mixed, n):
    heads = mixed.shape[0]
    own = heads // n
    return pl.pallas_call(
        pack_values_kernel,
        grid_spec=pltpu.PrefetchScalarGridSpec(
            num_scalar_prefetch=1,
            grid=(n // 4,),
            in_specs=[pl.BlockSpec((4 * own, 512, TILE), lambda g, me: ((me[0] >> 2) ^ g, 0, 0))],
            out_specs=[pl.BlockSpec((4 * own, 16, TILE), lambda g, me: ((me[0] >> 2) ^ g, 0, 0))]
            + [pl.BlockSpec((own, VROWS, TILE), lambda g, me: (0, 0, 0))] * n,
        ),
        out_shape=[jax.ShapeDtypeStruct((heads, 16, TILE), BF16)]
        + [jax.ShapeDtypeStruct((own, VROWS, TILE), BF16)] * n,
        compiler_params=params(),
        cost_estimate=pl.CostEstimate(flops=10**8, bytes_accessed=4 << 20, transcendentals=0),
        name="pack_values",
    )(me, mixed)


def is_fresh(req, block):
    start = jnp.int32(0)
    fresh = jnp.bool_(False)
    for j in range(req.shape[1]):
        fresh = fresh | (start == block)
        start = start + req[0, j]
    return fresh


def tap_tables():
    row, part = iota((16, 4 * 128), 0), iota((16, 4 * 128), 1) >> 7
    hits = [((row & 3) == cg) & ((row >> 2) == part) for cg in range(4)]
    return [jnp.where(hit, 1.0, 0.0).astype(BF16) for hit in hits]


def halo_tables():
    row, lane = iota((48, 128), 0), iota((48, 128), 1)
    token = (row >> 2) % 3
    hits = [((row & 3) == cg) & (row < 36) & (token == lane) for cg in range(4)]
    return [jnp.where(hit, 1.0, 0.0).astype(BF16) for hit in hits]


def turned_dot(rows, table):
    return lax.dot_general(rows, table, (((0,), (0,)), ((), ())), preferred_element_type=F32)


def spread_taps(par, table):
    both = turned_dot(par, table)
    return [both[:, tap * 128 : (tap + 1) * 128] for tap in range(KERNEL)]


def halo_terms(halo, par, not_fresh0):
    x = [halo[4 * k : 4 * k + 4].astype(F32) * not_fresh0 for k in range(3)]
    w = [par[4 * k : 4 * k + 4] for k in range(3)]
    terms = jnp.concatenate(
        [w[0] * x[0] + w[1] * x[1] + w[2] * x[2], w[0] * x[1] + w[1] * x[2], w[0] * x[2]], axis=0
    )
    high = terms.astype(BF16).astype(F32)
    middle = (terms - high).astype(BF16).astype(F32)
    parts = [high, middle, terms - high - middle, jnp.zeros((12, 128), F32)]
    return jnp.concatenate(parts, axis=0).astype(BF16)


def convolve(raw, before, terms, taps, masks):
    lane = iota((1, TILE), 1)
    cur = raw.astype(F32)
    total = taps[KERNEL - 1] * cur
    if terms is not None:
        total = total + terms
    for back in range(1, KERNEL):
        moved = cur if before is None else jnp.where(lane >= TILE - back, before, cur)
        total = total + taps[KERNEL - 1 - back] * (pltpu.roll(moved, back, 1) * masks[back - 1])
    return (total / (1.0 + jnp.exp(-total))).astype(BF16)


def conv_masks(cut0, cut1):
    lane = iota((1, TILE), 1)
    masks = []
    for back in range(1, KERNEL):
        gone = ((lane < back) & cut0) | ((lane >= SPAN) & (lane < SPAN + back) & cut1)
        masks.append(jnp.where(gone, 0.0, 1.0))
    return masks


def row_prep(dec, beta, alog, dtb):
    lane = iota(dec.shape, 1)
    x = dec + dtb
    decay = -jnp.exp(alog) * (jnp.maximum(x, 0.0) + jnp.log1p(jnp.exp(-jnp.abs(x))))
    cum = decay
    for shift in (1, 2, 4, 8, 16, 32):
        cum = cum + jnp.where((lane & (SPAN - 1)) >= shift, pltpu.roll(cum, shift, 1), 0.0)
    strength = 1.0 / (1.0 + jnp.exp(-beta))
    grown = jnp.exp(cum)
    close0, close1 = cum[:, SPAN - 1 : SPAN], cum[:, TILE - 1 :]
    fade = jnp.exp(jnp.where(lane < SPAN, close0, close1) - cum)
    keep0 = jnp.exp(jnp.broadcast_to(close0, cum.shape))
    keep1 = jnp.exp(jnp.broadcast_to(close1, cum.shape))
    return cum, strength, grown, fade, keep0, keep1


def unit_inverses(systems):
    shape = (SPAN, RATIO * TILE)
    row, col = iota(shape, 0), iota(shape, 1) & (SPAN - 1)
    near = (row >> 4) == (col >> 4)
    eye = jnp.where(row == col, 1.0, 0.0)
    masks = halves((SPAN, TILE))

    def low(arrays):
        return [a.astype(BF16) for a in arrays]

    def stack(pair):
        return jnp.concatenate(pair, axis=0)

    total = [jnp.where(near, eye - a, 0.0) for a in systems]
    power = low([jnp.where(near, -a, 0.0) for a in systems])
    power = low([block_dot(p, p, masks) for p in power])
    for _ in range(2):
        both = [block_dot(stack([t, p]), p, masks) for t, p in zip(low(total), power)]
        total = [t + b[:SPAN] for t, b in zip(total, both)]
        power = low([b[SPAN:] for b in both])
    total = [t + block_dot(l, p, masks) for t, l, p in zip(total, low(total), power)]
    small = low(total)
    rest = low([jnp.where(near, 0.0, a) for a in systems])
    cross = low([block_dot(t, r, masks) for t, r in zip(small, rest)])
    total = [t - block_dot(x, l, masks) for t, x, l in zip(total, cross, small)]
    small = low(total)
    solved = []
    for a, x in zip(systems, small):
        wide = x.astype(F32)
        parts = block_dot(stack(split(a)), x, masks)
        miss = eye - wide - (parts[:SPAN] + parts[SPAN:])
        solved.append((wide + block_dot(x, miss.astype(BF16), masks)).astype(BF16))
    return solved


def both_blocks(square):
    none = jnp.zeros((SPAN, square.shape[1]), square.dtype)
    first = jnp.concatenate([square[:SPAN], none], axis=0)
    return jnp.concatenate([first, jnp.concatenate([none, square[SPAN:]], axis=0)], axis=1)


def unit_keys(convolved):
    wide = convolved.astype(F32)
    return (wide * lax.rsqrt(jnp.sum(wide * wide, axis=0, keepdims=True) + EPSILON)).astype(BF16)


def solve_tiles(keys, queries, prep):
    cum, strength, grown, fade, keep0, keep1 = prep
    row, lane = iota((SPAN, TILE), 0), iota((SPAN, TILE), 1)
    early = lane < SPAN
    seen = (lane & (SPAN - 1)) >= row
    later = (lane & (SPAN - 1)) > row
    columns = jnp.transpose(jnp.concatenate([cum, fade], axis=0))
    count = cum.shape[0]

    def beside(tall):
        return jnp.where(early, tall[:SPAN], tall[SPAN:])

    systems, faded, scores = [], [], []
    for t, k in enumerate(keys):
        turned = jnp.transpose(k.astype(F32))
        if queries is None:
            gram = beside(dot(turned.astype(BF16), k))
        else:
            prod = dot(turned.astype(BF16), jnp.concatenate([k, queries[t]], axis=1))
            gram, touch = beside(prod[:, :TILE]), beside(prod[:, TILE:])
        pair = []
        for r in range(RATIO):
            at = t * RATIO + r
            diff = cum[at : at + 1] - beside(columns[:, at : at + 1])
            ratio = jnp.where(seen, jnp.exp(jnp.where(seen, diff, 0.0)), 0.0)
            pair.append(jnp.where(later, strength[at : at + 1] * gram * ratio, 0.0))
            if queries is not None:
                scores.append((touch * ratio).astype(BF16))
            faded.append((turned * columns[:, count + at : count + at + 1]).astype(BF16))
        systems.append(jnp.concatenate(pair, axis=1))
    return unit_inverses(systems), faded, scores


def token_prep_kernel(req, me, mixed, dec, beta, halo, par_lines, wk, wv, sc, ft, qo, rows):
    fresh0, fresh1 = is_fresh(req, me[0] * 2), is_fresh(req, me[0] * 2 + 1)
    not_fresh0 = jnp.where(fresh0, 0.0, 1.0)
    masks = conv_masks(True, fresh1)
    tap_tab, halo_tab = tap_tables(), halo_tables()
    tiles = range(mixed.shape[0])
    par = [parameters(par_lines[t]) for t in tiles]

    def gather(pick):
        return jnp.concatenate([pick(t) for t in tiles], axis=0)

    prep = row_prep(
        gather(lambda t: dec[t].astype(F32)),
        gather(lambda t: beta[t].astype(F32)),
        jnp.concatenate([p[1] for p in par], axis=0),
        jnp.concatenate([p[2] for p in par], axis=0),
    )
    cum, strength, grown, fade, keep0, keep1 = prep
    keys, queries, values = [], [], []
    for t in tiles:
        terms = halo_terms(halo[t], par[t][0], not_fresh0)
        lines = par_lines[t, :16]
        q, k, v0, v1 = [
            convolve(
                mixed[t, c * 128 : (c + 1) * 128],
                None,
                turned_dot(terms, halo_tab[c]),
                spread_taps(lines, tap_tab[c]),
                masks,
            )
            for c in range(4)
        ]
        keys.append(unit_keys(k))
        queries.append(q)
        values.append((v0, v1))
        qo[t] = q
        rows[t] = jnp.concatenate(
            [keep0[2 * t : 2 * t + 2], grown[2 * t : 2 * t + 2], keep1[2 * t : 2 * t + 2], strength[2 * t : 2 * t + 2]],
            axis=0,
        )
    solved, faded, scores = solve_tiles(keys, queries, prep)
    sides = halves((SPAN, TILE))
    for t in tiles:
        stacks = []
        for r in range(RATIO):
            at = t * RATIO + r
            s, lift = strength[at : at + 1], strength[at : at + 1] * grown[at : at + 1]
            stacked = jnp.concatenate(
                [lift * keys[t].astype(F32), s * values[t][r].astype(F32)], axis=0
            )
            stacks.append(stacked.astype(BF16))
            sc[t, :, r * TILE : (r + 1) * TILE] = scores[at]
            ft[at] = faded[at]
        out = block_dot(jnp.concatenate(stacks, axis=1), solved[t], sides).astype(BF16)
        for r in range(RATIO):
            wk[t * RATIO + r] = out[:DK, r * TILE : (r + 1) * TILE]
            wv[t * RATIO + r] = out[DK:, r * TILE : (r + 1) * TILE]


def token_prep(req, me, mixed, dec, beta, halo, par):
    heads = mixed.shape[0]
    smem = pl.BlockSpec(memory_space=pltpu.SMEM)

    def tiles(count, *rest):
        return pl.BlockSpec((count,) + rest, lambda g: (g,) + (0,) * len(rest))

    square = jax.ShapeDtypeStruct((heads * RATIO, 128, 128), BF16)
    return pl.pallas_call(
        token_prep_kernel,
        grid=(heads // WIDE,),
        in_specs=[
            smem,
            smem,
            tiles(WIDE, 512, TILE),
            tiles(WIDE, RATIO, TILE),
            tiles(WIDE, RATIO, TILE),
            tiles(WIDE, 16, TILE),
            pl.BlockSpec((WIDE, 32, 128), lambda g: (g, 4, 0)),
        ],
        out_specs=[tiles(WIDE * RATIO, 128, 128)] * 2
        + [tiles(WIDE, SPAN, RATIO * TILE), tiles(WIDE * RATIO, 128, 128)]
        + [tiles(WIDE, 128, 128), tiles(WIDE, 8, 128)],
        out_shape=[square] * 2
        + [
            jax.ShapeDtypeStruct((heads, SPAN, RATIO * TILE), BF16),
            square,
            jax.ShapeDtypeStruct((heads, 128, 128), BF16),
            jax.ShapeDtypeStruct((heads, 8, 128), F32),
        ],
        compiler_params=params(),
        cost_estimate=pl.CostEstimate(flops=10**10, bytes_accessed=8 << 20, transcendentals=10**6),
        name="token_prep",
    )(req, me, mixed, dec, beta, halo, par)


def head_prep_kernel(req, kp, previous, par_lines, sol, ft, gs, rows):
    step = pl.program_id(0)
    depth, own = kp.shape[0], kp.shape[1]
    tap_tab = tap_tables()
    order = [(d, h) for d in range(depth) for h in range(own)]
    par = [parameters(par_lines[h]) for h in range(own)]

    small = [kp[d, h, DK:].astype(F32) for d, h in order]
    prep = row_prep(
        jnp.concatenate([s[28:30] for s in small], axis=0),
        jnp.concatenate([s[30:32] for s in small], axis=0),
        jnp.concatenate([par[h][1] for d, h in order], axis=0),
        jnp.concatenate([par[h][2] for d, h in order], axis=0),
    )
    cum, strength, grown, fade, keep0, keep1 = prep
    keys = []
    taps = [spread_taps(par_lines[h, :16], tap_tab[1]) for h in range(own)]
    for d in range(depth):
        block = (step * depth + d) * 2
        masks = conv_masks(is_fresh(req, block), is_fresh(req, block + 1))
        for h in range(own):
            before = (kp[d - 1, h, :DK] if d else previous[0, h]).astype(F32)
            keys.append(unit_keys(convolve(kp[d, h, :DK], before, None, taps[h], masks)))
    solved, faded, unused = solve_tiles(keys, None, prep)
    sides = halves((SPAN, TILE))
    for t, (d, h) in enumerate(order):
        rows[d, h] = jnp.concatenate(
            [keep0[2 * t : 2 * t + 2], keep1[2 * t : 2 * t + 2], strength[2 * t : 2 * t + 2], strength[2 * t : 2 * t + 2]],
            axis=0,
        )
        scaled = []
        for r in range(RATIO):
            at = t * RATIO + r
            lift = strength[at : at + 1] * grown[at : at + 1]
            scaled.append((lift * keys[t].astype(F32)).astype(BF16))
        wide = block_dot(jnp.concatenate(scaled, axis=1), solved[t], sides).astype(BF16)
        sol[d, h] = solved[t]
        for r in range(RATIO):
            at = t * RATIO + r
            drop = dot(wide[:, r * TILE : (r + 1) * TILE], both_blocks(faded[at])).astype(BF16)
            gs[d, h, r, 0] = drop[:, :DK]
            gs[d, h, r, 1] = drop[:, DK:]
            ft[d, h, r] = faded[at]


def head_prep(req, kp, par):
    n, own = kp.shape[:2]
    depth = MOST // own
    smem = pl.BlockSpec(memory_space=pltpu.SMEM)

    def tiles(*rest):
        return pl.BlockSpec((depth, own) + rest, lambda g: (g, 0) + (0,) * len(rest))

    square = jax.ShapeDtypeStruct((n, own, RATIO, 128, 128), BF16)
    return pl.pallas_call(
        head_prep_kernel,
        grid=(n // depth,),
        in_specs=[
            smem,
            tiles(KROWS, TILE),
            pl.BlockSpec((1, own, DK, TILE), lambda g: (jnp.maximum(g * depth - 1, 0), 0, 0, 0)),
            pl.BlockSpec((own, 32, 128), lambda g: (0, 0, 0)),
        ],
        out_specs=[
            tiles(SPAN, RATIO * TILE),
            tiles(RATIO, 128, 128),
            tiles(RATIO, 2, 128, 128),
            tiles(8, 128),
        ],
        out_shape=[
            jax.ShapeDtypeStruct((n, own, SPAN, RATIO * TILE), BF16),
            square,
            jax.ShapeDtypeStruct((n, own, RATIO, 2, 128, 128), BF16),
            jax.ShapeDtypeStruct((n, own, 8, 128), F32),
        ],
        compiler_params=params(),
        cost_estimate=pl.CostEstimate(flops=10**10, bytes_accessed=6 << 20, transcendentals=10**6),
        name="head_prep",
    )(req, kp, kp, par)


def head_chain_kernel(req, me, par_lines, sol, ft, gs, rows, *refs):
    n = refs[-6].shape[0]
    arrived, (sin, ends, tails, state, vp, spread) = refs[:n], refs[n:]
    step = pl.program_id(0)
    depth, own = sol.shape[0], sol.shape[1]

    @pl.when(step == 0)
    def first():
        for k, one in enumerate(arrived):
            vp[me[0] ^ k] = one[...]
            tails[me[0] ^ k] = one[:, 256:]
        tap_tab = tap_tables()
        for h in range(own):
            for r in range(RATIO):
                for tap, wide in enumerate(spread_taps(par_lines[h, :16], tap_tab[2 + r])):
                    spread[h * RATIO + r, tap] = wide

    sides = halves((SPAN, TILE))
    heads = [(h, r) for h in range(own) for r in range(RATIO)]
    taps = [[spread[v, tap] for tap in range(KERNEL)] for v in range(len(heads))]
    current = [state[v] for v in range(len(heads))]
    for d in range(depth):
        tile = step * depth + d
        past = jnp.maximum(tile - 1, 0)
        fresh = [is_fresh(req, tile * 2), is_fresh(req, tile * 2 + 1)]
        masks = conv_masks(fresh[0], fresh[1])
        gains = []
        for h in range(own):
            scaled = []
            for r in range(RATIO):
                raw = vp[tile, h, r * DV : (r + 1) * DV]
                before = vp[past, h, r * DV : (r + 1) * DV].astype(F32)
                value = convolve(raw, before, None, taps[h * RATIO + r], masks)
                scaled.append((rows[d, h, 4 + r : 5 + r] * value.astype(F32)).astype(BF16))
            wide = block_dot(jnp.concatenate(scaled, axis=1), sol[d, h], sides).astype(BF16)
            for r in range(RATIO):
                gains.append(dot(wide[:, r * TILE : (r + 1) * TILE], both_blocks(ft[d, h, r])))
        for half in range(2):
            for h in range(own):
                now = [jnp.where(fresh[half], 0.0, current[h * RATIO + r]) for r in range(RATIO)]
                lost = dot(
                    jnp.concatenate([x.astype(BF16) for x in now], axis=1),
                    corner(gs[d, h, 0, half], gs[d, h, 1, half]),
                )
                for r in range(RATIO):
                    v = h * RATIO + r
                    keep = rows[d, h, 2 * half + r : 2 * half + r + 1]
                    gain = gains[v][:, half * DV : (half + 1) * DV]
                    current[v] = keep * now[r] + (gain - lost[:, r * TILE : (r + 1) * TILE])
                    ends[d * 2 + half, v] = current[v].astype(BF16)
        onward = lax.rem(tile + 1, n)
        for v in range(len(heads)):
            sin[onward, v] = current[v].astype(BF16)
    for v in range(len(heads)):
        state[v] = current[v]


def head_chain(req, me, par, sol, ft, gs, rows, arrived):
    n, own = sol.shape[:2]
    depth = WIDE // own
    smem = pl.BlockSpec(memory_space=pltpu.SMEM)

    def tiles(*rest):
        return pl.BlockSpec((depth, own) + rest, lambda g: (g, 0) + (0,) * len(rest))

    return pl.pallas_call(
        head_chain_kernel,
        grid=(n // depth,),
        in_specs=[
            smem,
            smem,
            pl.BlockSpec((own, 32, 128), lambda g: (0, 0, 0)),
            tiles(SPAN, RATIO * TILE),
            tiles(RATIO, 128, 128),
            tiles(RATIO, 2, 128, 128),
            tiles(8, 128),
        ]
        + [pl.BlockSpec((own, VROWS, TILE), lambda g: (0, 0, 0))] * n,
        out_specs=[
            pl.BlockSpec((n, own * RATIO, 128, 128), lambda g: (0, 0, 0, 0)),
            pl.BlockSpec((2 * depth, own * RATIO, 128, 128), lambda g: (g, 0, 0, 0)),
            pl.BlockSpec((n, own, 32, TILE), lambda g: (0, 0, 0, 0)),
        ],
        out_shape=[
            jax.ShapeDtypeStruct((n, own * RATIO, 128, 128), BF16),
            jax.ShapeDtypeStruct((2 * n, own * RATIO, 128, 128), BF16),
            jax.ShapeDtypeStruct((n, own, 32, TILE), BF16),
        ],
        scratch_shapes=[
            pltpu.VMEM((own * RATIO, 128, 128), F32),
            pltpu.VMEM((n, own, VROWS, TILE), BF16),
            pltpu.VMEM((own * RATIO, KERNEL, 128, 128), F32),
        ],
        compiler_params=params(),
        cost_estimate=pl.CostEstimate(flops=3 * 10**9, bytes_accessed=8 << 20, transcendentals=10**6),
        name="head_chain",
    )(req, me, par, sol, ft, gs, rows, *arrived)


def choose_kernel(req, rep, fin, me, ends, kt, *refs):
    outs, counts = refs[:-1], refs[-1]
    own, heads = kt.shape[1], ends.shape[1]
    base = heads * 128
    for i, out in enumerate(outs):
        out[...] = jnp.zeros_like(out)
        counts[i] = 0
    end = jnp.int32(-1)
    for j in range(req.shape[1]):
        end = end + req[0, j]
        where = rep[0, j] ^ me[0]
        place = jnp.minimum(counts[where], CAP - 1)
        done = fin[0, j] > 0
        counts[where] = counts[where] + jnp.where(done, 1, 0)
        for i, out in enumerate(outs):

            @pl.when(done & (where == i))
            def take():
                for v in range(heads):
                    out[place, v * 128 : (v + 1) * 128] = ends[end, v]
                for h in range(own):
                    lines = kt[end >> 1, h].astype(F32)
                    lines = jnp.where((end & 1) > 0, lines[16:], lines[:16]).astype(BF16)
                    out[place, base + h * 16 : base + h * 16 + 16] = lines

    for i, out in enumerate(outs):
        number = jnp.full((16, 128), counts[i], jnp.int32).astype(F32).astype(BF16)
        for c in range(CAP):
            out[c, base + own * 16 :] = number


def choose(req, rep, fin, me, ends, tails, replicas):
    own = tails.shape[1]
    smem = pl.BlockSpec(memory_space=pltpu.SMEM)
    lines = own * RATIO * 128 + own * 16 + 16
    return pl.pallas_call(
        choose_kernel,
        grid=(1,),
        in_specs=[
            smem,
            smem,
            smem,
            smem,
            pl.BlockSpec(ends.shape, lambda g: (0, 0, 0, 0)),
            pl.BlockSpec(tails.shape, lambda g: (0, 0, 0, 0)),
        ],
        out_specs=[pl.BlockSpec((CAP, lines, 128), lambda g: (0, 0, 0))] * replicas,
        out_shape=[jax.ShapeDtypeStruct((CAP, lines, 128), BF16)] * replicas,
        scratch_shapes=[pltpu.SMEM((replicas,), jnp.int32)],
        compiler_params=params(),
        cost_estimate=pl.CostEstimate(flops=10**6, bytes_accessed=4 << 20, transcendentals=0),
        name="choose",
    )(req, rep, fin, me, ends, tails)


def token_out_kernel(req, me, sin, wk, wv, sc, ft, qs, rows, gate, norm_gain, out):
    gain = jnp.transpose(jnp.broadcast_to(norm_gain[...], (TILE, DV)))
    stay0 = jnp.where(is_fresh(req, me[0] * 2), 0.0, 1.0)
    stay1 = jnp.where(is_fresh(req, me[0] * 2 + 1), 0.0, 1.0)
    lane = iota((DV, TILE), 1)
    early = lane < SPAN
    sides = halves((SPAN, TILE))
    units = [(t, r) for t in range(qs.shape[0]) for r in range(RATIO)]
    both = [jnp.concatenate([wk[t * RATIO + r], qs[t]], axis=1) for t, r in units]
    enter = [sin[t * RATIO + r].astype(F32) * stay0 for t, r in units]
    first = [dot(e.astype(BF16), b) for e, b in zip(enter, both)]
    wide = [wv[t * RATIO + r].astype(F32) for t, r in units]
    new0 = [jnp.where(early, w - f[:, :TILE], 0.0) for w, f in zip(wide, first)]
    tiles = range(qs.shape[0])
    pairs = [
        dot(
            jnp.concatenate([new0[2 * t].astype(BF16), new0[2 * t + 1].astype(BF16)], axis=1),
            corner(ft[2 * t], ft[2 * t + 1]),
        )
        for t in tiles
    ]
    middle = [
        (rows[t, r : r + 1] * e + pairs[t][:, r * TILE : (r + 1) * TILE]) * stay1
        for (t, r), e in zip(units, enter)
    ]
    second = [dot(m.astype(BF16), b) for m, b in zip(middle, both)]
    new = [
        jnp.where(early, x, w - s[:, :TILE]).astype(BF16) for x, w, s in zip(new0, wide, second)
    ]
    near = [
        block_dot(jnp.concatenate([new[2 * t], new[2 * t + 1]], axis=1), sc[t], sides) for t in tiles
    ]
    for at, (t, r) in enumerate(units):
        core = rows[t, 2 + r : 3 + r] * jnp.where(early, first[at][:, TILE:], second[at][:, TILE:])
        core = (core + near[t][:, r * TILE : (r + 1) * TILE]).astype(BF16).astype(F32)
        inverse_rms = lax.rsqrt(jnp.mean(core * core, axis=0, keepdims=True) + EPSILON)
        z = gate[t, r * DV : (r + 1) * DV].astype(F32)
        result = core * inverse_rms * gain * (z / (1.0 + jnp.exp(-z)))
        out[t, r * DV : (r + 1) * DV] = result.astype(BF16)


def token_out(req, me, sin, wk, wv, sc, ft, qs, rows, gate, gain):
    heads = qs.shape[0]
    smem = pl.BlockSpec(memory_space=pltpu.SMEM)

    def tiles(count, *rest):
        return pl.BlockSpec((count,) + rest, lambda g: (g,) + (0,) * len(rest))

    return pl.pallas_call(
        token_out_kernel,
        grid=(heads // WIDE,),
        in_specs=[smem, smem]
        + [tiles(WIDE * RATIO, 128, 128)] * 3
        + [tiles(WIDE, SPAN, RATIO * TILE), tiles(WIDE * RATIO, 128, 128)]
        + [
            tiles(WIDE, 128, 128),
            tiles(WIDE, 8, 128),
            tiles(WIDE, 256, TILE),
            pl.BlockSpec((1, 128), lambda g: (0, 0)),
        ],
        out_specs=tiles(WIDE, 256, TILE),
        out_shape=jax.ShapeDtypeStruct((heads, 256, TILE), BF16),
        compiler_params=params(ALL_VMEM),
        cost_estimate=pl.CostEstimate(flops=10**9, bytes_accessed=8 << 20, transcendentals=10**6),
        name="token_out",
    )(req, me, sin, wk, wv, sc, ft, qs, rows, gate, gain)


def land_kernel(me, *refs):
    got, (states, tails, counts) = refs[:-3], refs[-3:]
    slot = pl.program_id(0)
    heads, own = states.shape[1], tails.shape[2]
    base = heads * 128

    @pl.when(slot == 0)
    def first():
        for i, one in enumerate(got):
            number = jnp.max(one[0, base + own * 16 :].astype(F32))
            counts[i] = number.astype(jnp.int32)

    start = jnp.int32(0)
    source, place = jnp.int32(-1), jnp.int32(0)
    for p in range(len(got)):
        away = me[0] ^ p
        number = counts[away]
        inside = (slot >= start) & (slot < start + number)
        source = jnp.where(inside, away, source)
        place = jnp.where(inside, slot - start, place)
        start = start + number
    place = jnp.clip(place, 0, CAP - 1)
    for i, one in enumerate(got):

        @pl.when(source == i)
        def take():
            for v in range(heads):
                states[0, v] = jnp.transpose(one[place, v * 128 : (v + 1) * 128]).astype(F32)
            lines = [one[place, base + h * 16 : base + h * 16 + 16].astype(F32) for h in range(own)]
            for k in range(KERNEL - 1):
                row = [
                    jnp.concatenate([x[4 * k + cg : 4 * k + cg + 1] for cg in range(4)], axis=1)
                    for x in lines
                ]
                tails[0, k] = jnp.concatenate(row, axis=0).astype(BF16)

    @pl.when(source < 0)
    def clear():
        states[...] = jnp.zeros_like(states)
        tails[...] = jnp.zeros_like(tails)


def land(me, got, heads, own):
    lines = got[0].shape[1]
    slots = len(got) * CAP
    smem = pl.BlockSpec(memory_space=pltpu.SMEM)
    return pl.pallas_call(
        land_kernel,
        grid=(slots,),
        in_specs=[smem] + [pl.BlockSpec((CAP, lines, 128), lambda g: (0, 0, 0))] * len(got),
        out_specs=[
            pl.BlockSpec((1, heads, 128, 128), lambda g: (g, 0, 0, 0)),
            pl.BlockSpec((1, KERNEL - 1, own, 512), lambda g: (g, 0, 0, 0)),
        ],
        out_shape=[
            jax.ShapeDtypeStruct((slots, heads, 128, 128), F32),
            jax.ShapeDtypeStruct((slots, KERNEL - 1, own, 512), BF16),
        ],
        scratch_shapes=[pltpu.SMEM((len(got),), jnp.int32)],
        compiler_params=params(ALL_VMEM),
        cost_estimate=pl.CostEstimate(flops=10**6, bytes_accessed=4 << 20, transcendentals=0),
        name="land",
    )(me, *got)


def exchange(parts, axis):
    count = len(parts)
    got = {0: parts[0]}
    for k in range(count - 1, 0, -1):
        got[k] = lax.ppermute(parts[k], axis, [(i, i ^ k) for i in range(count)])
    return [got[k] for k in range(count)]


def body(
    mixed,
    decay_in,
    beta_in,
    gate_z,
    conv_weight,
    a_log,
    dt_bias,
    norm_gain,
    req_blocks,
    replica_of,
    finished,
):
    n = lax.axis_size("seq")
    replicas = lax.axis_size("rep")
    heads = mixed.shape[1]
    own = heads // n
    me = lax.axis_index("seq").astype(jnp.int32).reshape(1)
    kpack, par = pack_keys(mixed[0], decay_in[0], beta_in[0], conv_weight, a_log, dt_bias)
    halo, *vpack = pack_values(me, mixed[0], n)
    kp = lax.all_to_all(kpack.reshape(n, own, KROWS, TILE), "seq", 0, 0, tiled=True)
    halo = lax.ppermute(halo, "seq", [(i, i + 1) for i in range(n - 1)])
    vp = exchange(vpack, "seq")
    hsol, hft, hgs, hrows = head_prep(req_blocks, kp, par)
    hrows, halo = lax.optimization_barrier((hrows, halo))
    wk, wv, sc, ft, qs, rows = token_prep(
        req_blocks, me, mixed[0], decay_in[0], beta_in[0], halo, kp.reshape(heads, KROWS, TILE)
    )
    sin, ends, ktails = head_chain(req_blocks, me, par, hsol, hft, hgs, hrows, vp)
    sin = lax.all_to_all(sin, "seq", 0, 0, tiled=True)
    my_rep = lax.axis_index("rep").astype(jnp.int32).reshape(1)
    send = choose(req_blocks, replica_of, finished, my_rep, ends, ktails, replicas)
    got = exchange(send, "rep")
    states, tails = land(my_rep, got, own * RATIO, own)
    out = token_out(
        req_blocks,
        me,
        sin.reshape(heads * RATIO, 128, 128),
        wk,
        wv,
        sc,
        ft,
        qs,
        rows,
        gate_z[0],
        norm_gain.reshape(1, DV),
    )
    return (out[None], states[None], tails[None])


def solution(mesh):
    placed = (
        P("rep", None, None, "seq"),
        P("rep", None, None, "seq"),
        P("rep", None, None, "seq"),
        P("rep", None, None, "seq"),
        P(None, "seq", None),
        P("seq"),
        P("seq"),
        P(),
        P("rep", None),
        P("rep", None),
        P("rep", None),
    )
    return jax.shard_map(
        body,
        mesh=mesh,
        in_specs=placed,
        out_specs=(
            P("rep", None, None, "seq"),
            P("rep", None, "seq", None, None),
            P("rep", None, None, "seq", None),
        ),
        check_vma=False,
    )
```

```python
import jax
import jax.numpy as jnp
from jax import lax
from jax.experimental import pallas as pl
from jax.experimental.pallas import tpu as pltpu
from jax.sharding import PartitionSpec as P

DK = 128
DV = 128
KERNEL = 4
SPAN = 64
CAP = 2
RATIO = 2
TILE = 2 * SPAN
KROWS = 160
VROWS = 288
WIDE = 8
MOST = 16
EPSILON = 1e-06
F32 = jnp.float32
BF16 = jnp.bfloat16
VMEM_LIMIT = 56 * 1024 * 1024
ALL_VMEM = 63 * 1024 * 1024


def params(limit=VMEM_LIMIT):
    return pltpu.CompilerParams(vmem_limit_bytes=limit)


def iota(shape, dim):
    return lax.broadcasted_iota(jnp.int32, shape, dim)


def dot(left, right):
    return jnp.dot(left, right, preferred_element_type=F32)


def split(wide):
    high = wide.astype(BF16)
    return high, (wide - high.astype(F32)).astype(BF16)


def halves(shape):
    first = iota(shape, len(shape) - 1) < SPAN
    return jnp.where(first, 1.0, 0.0).astype(BF16), jnp.where(first, 0.0, 1.0).astype(BF16)


def corner(first, second):
    none = jnp.zeros_like(first)
    top = jnp.concatenate([first, none], axis=1)
    return jnp.concatenate([top, jnp.concatenate([none, second], axis=1)], axis=0)


def diagonal(packed, masks):
    squares = []
    for r in range(RATIO):
        one = packed[:, r * TILE : (r + 1) * TILE]
        squares.append(jnp.concatenate([one * masks[0], one * masks[1]], axis=0))
    return corner(*squares)


def block_dot(left, right, masks):
    return dot(left, diagonal(right, masks))


def parameter_lines(h, cw, alog, dtb):
    taps = cw[:, h].astype(F32)
    rows = [taps[tap : tap + 1, cg * 128 : (cg + 1) * 128] for tap in range(KERNEL) for cg in range(4)]
    rest = jnp.concatenate(
        [jnp.full((1, 128), ref[h * RATIO + r], F32) for ref in (alog, dtb) for r in range(RATIO)], axis=0
    )
    parts = []
    for _ in range(3):
        part = rest.astype(BF16).astype(F32)
        rest = rest - part
        parts.append(part)
    return jnp.concatenate(rows + parts + [jnp.zeros((4, 128), F32)], axis=0)


def parameters(lines):
    wide = lines.astype(F32)
    rest = wide[16:20] + wide[20:24] + wide[24:28]
    return wide[:16], rest[:RATIO], rest[RATIO:]


def pack_keys_kernel(mixed, dec, beta, cw, alog, dtb, kout, pout):
    row = iota((32, TILE), 0)
    own = pout.shape[0]
    lines = [parameter_lines(h, cw, alog, dtb) for h in range(own)]
    for t in range(mixed.shape[0]):
        kout[t, :DK] = mixed[t]
        rest = lines[t % own]
        d, b = dec[t].astype(F32), beta[t].astype(F32)
        for r in range(RATIO):
            rest = jnp.where(row == 28 + r, d[r : r + 1], rest)
            rest = jnp.where(row == 30 + r, b[r : r + 1], rest)
        kout[t, DK:] = rest.astype(BF16)

    @pl.when(pl.program_id(0) == 0)
    def first():
        for h in range(own):
            pout[h] = lines[h].astype(BF16)


def pack_keys(mixed, dec, beta, cw, alog, dtb):
    heads = mixed.shape[0]
    own = cw.shape[1]
    step = heads // 2
    smem = pl.BlockSpec(memory_space=pltpu.SMEM)
    return pl.pallas_call(
        pack_keys_kernel,
        grid=(heads // step,),
        in_specs=[
            pl.BlockSpec((step, DK, TILE), lambda g: (g, 1, 0)),
            pl.BlockSpec((step, RATIO, TILE), lambda g: (g, 0, 0)),
            pl.BlockSpec((step, RATIO, TILE), lambda g: (g, 0, 0)),
            pl.BlockSpec((KERNEL, own, 512), lambda g: (0, 0, 0)),
            smem,
            smem,
        ],
        out_specs=[
            pl.BlockSpec((step, KROWS, TILE), lambda g: (g, 0, 0)),
            pl.BlockSpec((own, 32, 128), lambda g: (0, 0, 0)),
        ],
        out_shape=[
            jax.ShapeDtypeStruct((heads, KROWS, TILE), BF16),
            jax.ShapeDtypeStruct((own, 32, 128), BF16),
        ],
        compiler_params=params(),
        cost_estimate=pl.CostEstimate(flops=10**6, bytes_accessed=2 << 20, transcendentals=0),
        name="pack_keys",
    )(mixed, dec, beta, cw, alog, dtb)


def pack_values_kernel(me, mixed, hout, *outs):
    step = pl.program_id(0)
    own = outs[0].shape[0]
    row, tok = iota((TILE, 128), 1), iota((TILE, 128), 0)
    place = row & 15
    picks = []
    for cg in range(4):
        hit = (row < 32) & (place < 12) & ((place & 3) == cg)
        hit = hit & (tok == (row >> 4) * SPAN + 61 + (place >> 2))
        picks.append(jnp.where(hit, 1.0, 0.0).astype(BF16))
    all_tails = []
    for h in range(mixed.shape[0]):
        tails = dot(mixed[h, :128], picks[0])
        for cg in range(1, 4):
            tails = tails + dot(mixed[h, cg * 128 : (cg + 1) * 128], picks[cg])
        all_tails.append(jnp.transpose(tails)[:32].astype(BF16))
        hout[h] = all_tails[h][16:]
    for i, out in enumerate(outs):

        @pl.when((step == i // 4) & ((me[0] & 3) == 0))
        def put0():
            put(mixed, all_tails, out, (i & 3) ^ 0, own)

        @pl.when((step == i // 4) & ((me[0] & 3) == 1))
        def put1():
            put(mixed, all_tails, out, (i & 3) ^ 1, own)

        @pl.when((step == i // 4) & ((me[0] & 3) == 2))
        def put2():
            put(mixed, all_tails, out, (i & 3) ^ 2, own)

        @pl.when((step == i // 4) & ((me[0] & 3) == 3))
        def put3():
            put(mixed, all_tails, out, (i & 3) ^ 3, own)


def put(mixed, all_tails, out, place, own):
    for h in range(own):
        out[h, :256] = mixed[place * own + h, 2 * DK :]
        out[h, 256:] = all_tails[place * own + h]


def pack_values(me, mixed, n):
    heads = mixed.shape[0]
    own = heads // n
    return pl.pallas_call(
        pack_values_kernel,
        grid_spec=pltpu.PrefetchScalarGridSpec(
            num_scalar_prefetch=1,
            grid=(n // 4,),
            in_specs=[pl.BlockSpec((4 * own, 512, TILE), lambda g, me: ((me[0] >> 2) ^ g, 0, 0))],
            out_specs=[pl.BlockSpec((4 * own, 16, TILE), lambda g, me: ((me[0] >> 2) ^ g, 0, 0))]
            + [pl.BlockSpec((own, VROWS, TILE), lambda g, me: (0, 0, 0))] * n,
        ),
        out_shape=[jax.ShapeDtypeStruct((heads, 16, TILE), BF16)]
        + [jax.ShapeDtypeStruct((own, VROWS, TILE), BF16)] * n,
        compiler_params=params(),
        cost_estimate=pl.CostEstimate(flops=10**8, bytes_accessed=4 << 20, transcendentals=0),
        name="pack_values",
    )(me, mixed)


def is_fresh(req, block):
    start = jnp.int32(0)
    fresh = jnp.bool_(False)
    for j in range(req.shape[1]):
        fresh = fresh | (start == block)
        start = start + req[0, j]
    return fresh


def tap_tables():
    row, part = iota((16, 4 * 128), 0), iota((16, 4 * 128), 1) >> 7
    hits = [((row & 3) == cg) & ((row >> 2) == part) for cg in range(4)]
    return [jnp.where(hit, 1.0, 0.0).astype(BF16) for hit in hits]


def halo_tables():
    row, lane = iota((48, 128), 0), iota((48, 128), 1)
    token = (row >> 2) % 3
    hits = [((row & 3) == cg) & (row < 36) & (token == lane) for cg in range(4)]
    return [jnp.where(hit, 1.0, 0.0).astype(BF16) for hit in hits]


def turned_dot(rows, table):
    return lax.dot_general(rows, table, (((0,), (0,)), ((), ())), preferred_element_type=F32)


def spread_taps(par, table):
    both = turned_dot(par, table)
    return [both[:, tap * 128 : (tap + 1) * 128] for tap in range(KERNEL)]


def halo_terms(halo, par, not_fresh0):
    x = [halo[4 * k : 4 * k + 4].astype(F32) * not_fresh0 for k in range(3)]
    w = [par[4 * k : 4 * k + 4] for k in range(3)]
    terms = jnp.concatenate(
        [w[0] * x[0] + w[1] * x[1] + w[2] * x[2], w[0] * x[1] + w[1] * x[2], w[0] * x[2]], axis=0
    )
    high = terms.astype(BF16).astype(F32)
    middle = (terms - high).astype(BF16).astype(F32)
    parts = [high, middle, terms - high - middle, jnp.zeros((12, 128), F32)]
    return jnp.concatenate(parts, axis=0).astype(BF16)


def convolve(raw, before, terms, taps, masks):
    lane = iota((1, TILE), 1)
    cur = raw.astype(F32)
    total = taps[KERNEL - 1] * cur
    if terms is not None:
        total = total + terms
    for back in range(1, KERNEL):
        moved = cur if before is None else jnp.where(lane >= TILE - back, before, cur)
        total = total + taps[KERNEL - 1 - back] * (pltpu.roll(moved, back, 1) * masks[back - 1])
    return (total / (1.0 + jnp.exp(-total))).astype(BF16)


def conv_masks(cut0, cut1):
    lane = iota((1, TILE), 1)
    masks = []
    for back in range(1, KERNEL):
        gone = ((lane < back) & cut0) | ((lane >= SPAN) & (lane < SPAN + back) & cut1)
        masks.append(jnp.where(gone, 0.0, 1.0))
    return masks


def row_prep(dec, beta, alog, dtb):
    lane = iota(dec.shape, 1)
    x = dec + dtb
    decay = -jnp.exp(alog) * (jnp.maximum(x, 0.0) + jnp.log1p(jnp.exp(-jnp.abs(x))))
    cum = decay
    for shift in (1, 2, 4, 8, 16, 32):
        cum = cum + jnp.where((lane & (SPAN - 1)) >= shift, pltpu.roll(cum, shift, 1), 0.0)
    strength = 1.0 / (1.0 + jnp.exp(-beta))
    grown = jnp.exp(cum)
    close0, close1 = cum[:, SPAN - 1 : SPAN], cum[:, TILE - 1 :]
    fade = jnp.exp(jnp.where(lane < SPAN, close0, close1) - cum)
    keep0 = jnp.exp(jnp.broadcast_to(close0, cum.shape))
    keep1 = jnp.exp(jnp.broadcast_to(close1, cum.shape))
    return cum, strength, grown, fade, keep0, keep1


def unit_inverses(systems):
    shape = (SPAN, RATIO * TILE)
    row, col = iota(shape, 0), iota(shape, 1) & (SPAN - 1)
    near = (row >> 4) == (col >> 4)
    eye = jnp.where(row == col, 1.0, 0.0)
    masks = halves((SPAN, TILE))

    def low(arrays):
        return [a.astype(BF16) for a in arrays]

    def stack(pair):
        return jnp.concatenate(pair, axis=0)

    total = [jnp.where(near, eye - a, 0.0) for a in systems]
    power = low([jnp.where(near, -a, 0.0) for a in systems])
    power = low([block_dot(p, p, masks) for p in power])
    for _ in range(2):
        both = [block_dot(stack([t, p]), p, masks) for t, p in zip(low(total), power)]
        total = [t + b[:SPAN] for t, b in zip(total, both)]
        power = low([b[SPAN:] for b in both])
    total = [t + block_dot(l, p, masks) for t, l, p in zip(total, low(total), power)]
    small = low(total)
    rest = low([jnp.where(near, 0.0, a) for a in systems])
    cross = low([block_dot(t, r, masks) for t, r in zip(small, rest)])
    total = [t - block_dot(x, l, masks) for t, x, l in zip(total, cross, small)]
    small = low(total)
    solved = []
    for a, x in zip(systems, small):
        wide = x.astype(F32)
        parts = block_dot(stack(split(a)), x, masks)
        miss = eye - wide - (parts[:SPAN] + parts[SPAN:])
        solved.append((wide + block_dot(x, miss.astype(BF16), masks)).astype(BF16))
    return solved


def both_blocks(square):
    none = jnp.zeros((SPAN, square.shape[1]), square.dtype)
    first = jnp.concatenate([square[:SPAN], none], axis=0)
    return jnp.concatenate([first, jnp.concatenate([none, square[SPAN:]], axis=0)], axis=1)


def unit_keys(convolved):
    wide = convolved.astype(F32)
    return (wide * lax.rsqrt(jnp.sum(wide * wide, axis=0, keepdims=True) + EPSILON)).astype(BF16)


def solve_tiles(keys, queries, prep):
    cum, strength, grown, fade, keep0, keep1 = prep
    row, lane = iota((SPAN, TILE), 0), iota((SPAN, TILE), 1)
    early = lane < SPAN
    seen = (lane & (SPAN - 1)) >= row
    later = (lane & (SPAN - 1)) > row
    columns = jnp.transpose(jnp.concatenate([cum, fade], axis=0))
    count = cum.shape[0]

    def beside(tall):
        return jnp.where(early, tall[:SPAN], tall[SPAN:])

    systems, faded, scores = [], [], []
    for t, k in enumerate(keys):
        turned = jnp.transpose(k.astype(F32))
        if queries is None:
            gram = beside(dot(turned.astype(BF16), k))
        else:
            prod = dot(turned.astype(BF16), jnp.concatenate([k, queries[t]], axis=1))
            gram, touch = beside(prod[:, :TILE]), beside(prod[:, TILE:])
        pair = []
        for r in range(RATIO):
            at = t * RATIO + r
            diff = cum[at : at + 1] - beside(columns[:, at : at + 1])
            ratio = jnp.where(seen, jnp.exp(jnp.where(seen, diff, 0.0)), 0.0)
            pair.append(jnp.where(later, strength[at : at + 1] * gram * ratio, 0.0))
            if queries is not None:
                scores.append((touch * ratio).astype(BF16))
            faded.append((turned * columns[:, count + at : count + at + 1]).astype(BF16))
        systems.append(jnp.concatenate(pair, axis=1))
    return unit_inverses(systems), faded, scores


def token_prep_kernel(req, me, mixed, dec, beta, halo, par_lines, wk, wv, sc, ft, qo, rows):
    fresh0, fresh1 = is_fresh(req, me[0] * 2), is_fresh(req, me[0] * 2 + 1)
    not_fresh0 = jnp.where(fresh0, 0.0, 1.0)
    masks = conv_masks(True, fresh1)
    tap_tab, halo_tab = tap_tables(), halo_tables()
    tiles = range(mixed.shape[0])
    par = [parameters(par_lines[t]) for t in tiles]

    def gather(pick):
        return jnp.concatenate([pick(t) for t in tiles], axis=0)

    prep = row_prep(
        gather(lambda t: dec[t].astype(F32)),
        gather(lambda t: beta[t].astype(F32)),
        jnp.concatenate([p[1] for p in par], axis=0),
        jnp.concatenate([p[2] for p in par], axis=0),
    )
    cum, strength, grown, fade, keep0, keep1 = prep
    keys, queries, values = [], [], []
    for t in tiles:
        terms = halo_terms(halo[t], par[t][0], not_fresh0)
        lines = par_lines[t, :16]
        q, k, v0, v1 = [
            convolve(
                mixed[t, c * 128 : (c + 1) * 128],
                None,
                turned_dot(terms, halo_tab[c]),
                spread_taps(lines, tap_tab[c]),
                masks,
            )
            for c in range(4)
        ]
        keys.append(unit_keys(k))
        queries.append(q)
        values.append((v0, v1))
        qo[t] = q
        rows[t] = jnp.concatenate(
            [keep0[2 * t : 2 * t + 2], grown[2 * t : 2 * t + 2], keep1[2 * t : 2 * t + 2], strength[2 * t : 2 * t + 2]],
            axis=0,
        )
    solved, faded, scores = solve_tiles(keys, queries, prep)
    sides = halves((SPAN, TILE))
    for t in tiles:
        stacks = []
        for r in range(RATIO):
            at = t * RATIO + r
            s, lift = strength[at : at + 1], strength[at : at + 1] * grown[at : at + 1]
            stacked = jnp.concatenate(
                [lift * keys[t].astype(F32), s * values[t][r].astype(F32)], axis=0
            )
            stacks.append(stacked.astype(BF16))
            sc[t, :, r * TILE : (r + 1) * TILE] = scores[at]
            ft[at] = faded[at]
        out = block_dot(jnp.concatenate(stacks, axis=1), solved[t], sides).astype(BF16)
        for r in range(RATIO):
            wk[t * RATIO + r] = out[:DK, r * TILE : (r + 1) * TILE]
            wv[t * RATIO + r] = out[DK:, r * TILE : (r + 1) * TILE]


def token_prep(req, me, mixed, dec, beta, halo, par):
    heads = mixed.shape[0]
    smem = pl.BlockSpec(memory_space=pltpu.SMEM)

    def tiles(count, *rest):
        return pl.BlockSpec((count,) + rest, lambda g: (g,) + (0,) * len(rest))

    square = jax.ShapeDtypeStruct((heads * RATIO, 128, 128), BF16)
    return pl.pallas_call(
        token_prep_kernel,
        grid=(heads // WIDE,),
        in_specs=[
            smem,
            smem,
            tiles(WIDE, 512, TILE),
            tiles(WIDE, RATIO, TILE),
            tiles(WIDE, RATIO, TILE),
            tiles(WIDE, 16, TILE),
            pl.BlockSpec((WIDE, 32, 128), lambda g: (g, 4, 0)),
        ],
        out_specs=[tiles(WIDE * RATIO, 128, 128)] * 2
        + [tiles(WIDE, SPAN, RATIO * TILE), tiles(WIDE * RATIO, 128, 128)]
        + [tiles(WIDE, 128, 128), tiles(WIDE, 8, 128)],
        out_shape=[square] * 2
        + [
            jax.ShapeDtypeStruct((heads, SPAN, RATIO * TILE), BF16),
            square,
            jax.ShapeDtypeStruct((heads, 128, 128), BF16),
            jax.ShapeDtypeStruct((heads, 8, 128), F32),
        ],
        compiler_params=params(),
        cost_estimate=pl.CostEstimate(flops=10**10, bytes_accessed=8 << 20, transcendentals=10**6),
        name="token_prep",
    )(req, me, mixed, dec, beta, halo, par)


def head_prep_kernel(req, kp, previous, par_lines, sol, ft, gs, rows):
    step = pl.program_id(0)
    depth, own = kp.shape[0], kp.shape[1]
    tap_tab = tap_tables()
    order = [(d, h) for d in range(depth) for h in range(own)]
    par = [parameters(par_lines[h]) for h in range(own)]

    small = [kp[d, h, DK:].astype(F32) for d, h in order]
    prep = row_prep(
        jnp.concatenate([s[28:30] for s in small], axis=0),
        jnp.concatenate([s[30:32] for s in small], axis=0),
        jnp.concatenate([par[h][1] for d, h in order], axis=0),
        jnp.concatenate([par[h][2] for d, h in order], axis=0),
    )
    cum, strength, grown, fade, keep0, keep1 = prep
    keys = []
    taps = [spread_taps(par_lines[h, :16], tap_tab[1]) for h in range(own)]
    for d in range(depth):
        block = (step * depth + d) * 2
        masks = conv_masks(is_fresh(req, block), is_fresh(req, block + 1))
        for h in range(own):
            before = (kp[d - 1, h, :DK] if d else previous[0, h]).astype(F32)
            keys.append(unit_keys(convolve(kp[d, h, :DK], before, None, taps[h], masks)))
    solved, faded, unused = solve_tiles(keys, None, prep)
    sides = halves((SPAN, TILE))
    for t, (d, h) in enumerate(order):
        rows[d, h] = jnp.concatenate(
            [keep0[2 * t : 2 * t + 2], keep1[2 * t : 2 * t + 2], strength[2 * t : 2 * t + 2], strength[2 * t : 2 * t + 2]],
            axis=0,
        )
        scaled = []
        for r in range(RATIO):
            at = t * RATIO + r
            lift = strength[at : at + 1] * grown[at : at + 1]
            scaled.append((lift * keys[t].astype(F32)).astype(BF16))
        wide = block_dot(jnp.concatenate(scaled, axis=1), solved[t], sides).astype(BF16)
        sol[d, h] = solved[t]
        for r in range(RATIO):
            at = t * RATIO + r
            drop = dot(wide[:, r * TILE : (r + 1) * TILE], both_blocks(faded[at])).astype(BF16)
            gs[d, h, r, 0] = drop[:, :DK]
            gs[d, h, r, 1] = drop[:, DK:]
            ft[d, h, r] = faded[at]


def head_prep(req, kp, par):
    n, own = kp.shape[:2]
    depth = MOST // own
    smem = pl.BlockSpec(memory_space=pltpu.SMEM)

    def tiles(*rest):
        return pl.BlockSpec((depth, own) + rest, lambda g: (g, 0) + (0,) * len(rest))

    square = jax.ShapeDtypeStruct((n, own, RATIO, 128, 128), BF16)
    return pl.pallas_call(
        head_prep_kernel,
        grid=(n // depth,),
        in_specs=[
            smem,
            tiles(KROWS, TILE),
            pl.BlockSpec((1, own, DK, TILE), lambda g: (jnp.maximum(g * depth - 1, 0), 0, 0, 0)),
            pl.BlockSpec((own, 32, 128), lambda g: (0, 0, 0)),
        ],
        out_specs=[
            tiles(SPAN, RATIO * TILE),
            tiles(RATIO, 128, 128),
            tiles(RATIO, 2, 128, 128),
            tiles(8, 128),
        ],
        out_shape=[
            jax.ShapeDtypeStruct((n, own, SPAN, RATIO * TILE), BF16),
            square,
            jax.ShapeDtypeStruct((n, own, RATIO, 2, 128, 128), BF16),
            jax.ShapeDtypeStruct((n, own, 8, 128), F32),
        ],
        compiler_params=params(),
        cost_estimate=pl.CostEstimate(flops=10**10, bytes_accessed=6 << 20, transcendentals=10**6),
        name="head_prep",
    )(req, kp, kp, par)


def head_chain_kernel(req, me, par_lines, sol, ft, gs, rows, *refs):
    n = refs[-6].shape[0]
    arrived, (sin, ends, tails, state, vp, spread) = refs[:n], refs[n:]
    step = pl.program_id(0)
    depth, own = sol.shape[0], sol.shape[1]

    @pl.when(step == 0)
    def first():
        for i, one in enumerate(arrived):
            tile = me[0] ^ ((n - i) % n)
            vp[tile] = one[...]
            tails[tile] = one[:, 256:]
        tap_tab = tap_tables()
        for h in range(own):
            for r in range(RATIO):
                for tap, wide in enumerate(spread_taps(par_lines[h, :16], tap_tab[2 + r])):
                    spread[h * RATIO + r, tap] = wide

    sides = halves((SPAN, TILE))
    heads = [(h, r) for h in range(own) for r in range(RATIO)]
    taps = [[spread[v, tap] for tap in range(KERNEL)] for v in range(len(heads))]
    current = [state[v] for v in range(len(heads))]
    for d in range(depth):
        tile = step * depth + d
        past = jnp.maximum(tile - 1, 0)
        fresh = [is_fresh(req, tile * 2), is_fresh(req, tile * 2 + 1)]
        masks = conv_masks(fresh[0], fresh[1])
        gains = []
        for h in range(own):
            scaled = []
            for r in range(RATIO):
                raw = vp[tile, h, r * DV : (r + 1) * DV]
                before = vp[past, h, r * DV : (r + 1) * DV].astype(F32)
                value = convolve(raw, before, None, taps[h * RATIO + r], masks)
                scaled.append((rows[d, h, 4 + r : 5 + r] * value.astype(F32)).astype(BF16))
            wide = block_dot(jnp.concatenate(scaled, axis=1), sol[d, h], sides).astype(BF16)
            for r in range(RATIO):
                gains.append(dot(wide[:, r * TILE : (r + 1) * TILE], both_blocks(ft[d, h, r])))
        for half in range(2):
            for h in range(own):
                now = [jnp.where(fresh[half], 0.0, current[h * RATIO + r]) for r in range(RATIO)]
                lost = dot(
                    jnp.concatenate([x.astype(BF16) for x in now], axis=1),
                    corner(gs[d, h, 0, half], gs[d, h, 1, half]),
                )
                for r in range(RATIO):
                    v = h * RATIO + r
                    keep = rows[d, h, 2 * half + r : 2 * half + r + 1]
                    gain = gains[v][:, half * DV : (half + 1) * DV]
                    current[v] = keep * now[r] + (gain - lost[:, r * TILE : (r + 1) * TILE])
                    ends[d * 2 + half, v] = current[v].astype(BF16)
        onward = lax.rem(tile + 1, n)
        for v in range(len(heads)):
            sin[onward, v] = current[v].astype(BF16)
    for v in range(len(heads)):
        state[v] = current[v]


def head_chain(req, me, par, sol, ft, gs, rows, arrived):
    n, own = sol.shape[:2]
    depth = WIDE // own
    smem = pl.BlockSpec(memory_space=pltpu.SMEM)

    def tiles(*rest):
        return pl.BlockSpec((depth, own) + rest, lambda g: (g, 0) + (0,) * len(rest))

    return pl.pallas_call(
        head_chain_kernel,
        grid=(n // depth,),
        in_specs=[
            smem,
            smem,
            pl.BlockSpec((own, 32, 128), lambda g: (0, 0, 0)),
            tiles(SPAN, RATIO * TILE),
            tiles(RATIO, 128, 128),
            tiles(RATIO, 2, 128, 128),
            tiles(8, 128),
        ]
        + [pl.BlockSpec((own, VROWS, TILE), lambda g: (0, 0, 0))] * n,
        out_specs=[
            pl.BlockSpec((n, own * RATIO, 128, 128), lambda g: (0, 0, 0, 0)),
            pl.BlockSpec((2 * depth, own * RATIO, 128, 128), lambda g: (g, 0, 0, 0)),
            pl.BlockSpec((n, own, 32, TILE), lambda g: (0, 0, 0, 0)),
        ],
        out_shape=[
            jax.ShapeDtypeStruct((n, own * RATIO, 128, 128), BF16),
            jax.ShapeDtypeStruct((2 * n, own * RATIO, 128, 128), BF16),
            jax.ShapeDtypeStruct((n, own, 32, TILE), BF16),
        ],
        scratch_shapes=[
            pltpu.VMEM((own * RATIO, 128, 128), F32),
            pltpu.VMEM((n, own, VROWS, TILE), BF16),
            pltpu.VMEM((own * RATIO, KERNEL, 128, 128), F32),
        ],
        compiler_params=params(),
        cost_estimate=pl.CostEstimate(flops=3 * 10**9, bytes_accessed=8 << 20, transcendentals=10**6),
        name="head_chain",
    )(req, me, par, sol, ft, gs, rows, arrived[0], *arrived[:0:-1])


def choose_kernel(req, rep, fin, me, ends, kt, *refs):
    outs, counts = refs[:-1], refs[-1]
    own, heads = kt.shape[1], ends.shape[1]
    base = heads * 128
    for i, out in enumerate(outs):
        out[...] = jnp.zeros_like(out)
        counts[i] = 0
    end = jnp.int32(-1)
    for j in range(req.shape[1]):
        end = end + req[0, j]
        where = rep[0, j] ^ me[0]
        place = jnp.minimum(counts[where], CAP - 1)
        done = fin[0, j] > 0
        counts[where] = counts[where] + jnp.where(done, 1, 0)
        for i, out in enumerate(outs):

            @pl.when(done & (where == i))
            def take():
                for v in range(heads):
                    out[place, v * 128 : (v + 1) * 128] = ends[end, v]
                for h in range(own):
                    lines = kt[end >> 1, h].astype(F32)
                    lines = jnp.where((end & 1) > 0, lines[16:], lines[:16]).astype(BF16)
                    out[place, base + h * 16 : base + h * 16 + 16] = lines

    for i, out in enumerate(outs):
        number = jnp.full((16, 128), counts[i], jnp.int32).astype(F32).astype(BF16)
        for c in range(CAP):
            out[c, base + own * 16 :] = number


def choose(req, rep, fin, me, ends, tails, replicas):
    own = tails.shape[1]
    smem = pl.BlockSpec(memory_space=pltpu.SMEM)
    lines = own * RATIO * 128 + own * 16 + 16
    return pl.pallas_call(
        choose_kernel,
        grid=(1,),
        in_specs=[
            smem,
            smem,
            smem,
            smem,
            pl.BlockSpec(ends.shape, lambda g: (0, 0, 0, 0)),
            pl.BlockSpec(tails.shape, lambda g: (0, 0, 0, 0)),
        ],
        out_specs=[pl.BlockSpec((CAP, lines, 128), lambda g: (0, 0, 0))] * replicas,
        out_shape=[jax.ShapeDtypeStruct((CAP, lines, 128), BF16)] * replicas,
        scratch_shapes=[pltpu.SMEM((replicas,), jnp.int32)],
        compiler_params=params(),
        cost_estimate=pl.CostEstimate(flops=10**6, bytes_accessed=4 << 20, transcendentals=0),
        name="choose",
    )(req, rep, fin, me, ends, tails)


def token_out_kernel(req, me, sin, wk, wv, sc, ft, qs, rows, gate, norm_gain, out):
    gain = jnp.transpose(jnp.broadcast_to(norm_gain[...], (TILE, DV)))
    stay0 = jnp.where(is_fresh(req, me[0] * 2), 0.0, 1.0)
    stay1 = jnp.where(is_fresh(req, me[0] * 2 + 1), 0.0, 1.0)
    lane = iota((DV, TILE), 1)
    early = lane < SPAN
    sides = halves((SPAN, TILE))
    units = [(t, r) for t in range(qs.shape[0]) for r in range(RATIO)]
    both = [jnp.concatenate([wk[t * RATIO + r], qs[t]], axis=1) for t, r in units]
    enter = [sin[t * RATIO + r].astype(F32) * stay0 for t, r in units]
    first = [dot(e.astype(BF16), b) for e, b in zip(enter, both)]
    wide = [wv[t * RATIO + r].astype(F32) for t, r in units]
    new0 = [jnp.where(early, w - f[:, :TILE], 0.0) for w, f in zip(wide, first)]
    tiles = range(qs.shape[0])
    pairs = [
        dot(
            jnp.concatenate([new0[2 * t].astype(BF16), new0[2 * t + 1].astype(BF16)], axis=1),
            corner(ft[2 * t], ft[2 * t + 1]),
        )
        for t in tiles
    ]
    middle = [
        (rows[t, r : r + 1] * e + pairs[t][:, r * TILE : (r + 1) * TILE]) * stay1
        for (t, r), e in zip(units, enter)
    ]
    second = [dot(m.astype(BF16), b) for m, b in zip(middle, both)]
    new = [
        jnp.where(early, x, w - s[:, :TILE]).astype(BF16) for x, w, s in zip(new0, wide, second)
    ]
    near = [
        block_dot(jnp.concatenate([new[2 * t], new[2 * t + 1]], axis=1), sc[t], sides) for t in tiles
    ]
    for at, (t, r) in enumerate(units):
        core = rows[t, 2 + r : 3 + r] * jnp.where(early, first[at][:, TILE:], second[at][:, TILE:])
        core = (core + near[t][:, r * TILE : (r + 1) * TILE]).astype(BF16).astype(F32)
        inverse_rms = lax.rsqrt(jnp.mean(core * core, axis=0, keepdims=True) + EPSILON)
        z = gate[t, r * DV : (r + 1) * DV].astype(F32)
        result = core * inverse_rms * gain * (z / (1.0 + jnp.exp(-z)))
        out[t, r * DV : (r + 1) * DV] = result.astype(BF16)


def token_out(req, me, sin, wk, wv, sc, ft, qs, rows, gate, gain):
    heads = qs.shape[0]
    smem = pl.BlockSpec(memory_space=pltpu.SMEM)

    def tiles(count, *rest):
        return pl.BlockSpec((count,) + rest, lambda g: (g,) + (0,) * len(rest))

    return pl.pallas_call(
        token_out_kernel,
        grid=(heads // WIDE,),
        in_specs=[smem, smem]
        + [tiles(WIDE * RATIO, 128, 128)] * 3
        + [tiles(WIDE, SPAN, RATIO * TILE), tiles(WIDE * RATIO, 128, 128)]
        + [
            tiles(WIDE, 128, 128),
            tiles(WIDE, 8, 128),
            tiles(WIDE, 256, TILE),
            pl.BlockSpec((1, 128), lambda g: (0, 0)),
        ],
        out_specs=tiles(WIDE, 256, TILE),
        out_shape=jax.ShapeDtypeStruct((heads, 256, TILE), BF16),
        compiler_params=params(ALL_VMEM),
        cost_estimate=pl.CostEstimate(flops=10**9, bytes_accessed=8 << 20, transcendentals=10**6),
        name="token_out",
    )(req, me, sin, wk, wv, sc, ft, qs, rows, gate, gain)


def land_kernel(me, *refs):
    got, (states, tails, counts) = refs[:-3], refs[-3:]
    slot = pl.program_id(0)
    heads, own = states.shape[1], tails.shape[2]
    base = heads * 128

    @pl.when(slot == 0)
    def first():
        for i, one in enumerate(got):
            number = jnp.max(one[0, base + own * 16 :].astype(F32))
            counts[i] = number.astype(jnp.int32)

    start = jnp.int32(0)
    source, place = jnp.int32(-1), jnp.int32(0)
    for p in range(len(got)):
        away = me[0] ^ p
        number = counts[away]
        inside = (slot >= start) & (slot < start + number)
        source = jnp.where(inside, away, source)
        place = jnp.where(inside, slot - start, place)
        start = start + number
    place = jnp.clip(place, 0, CAP - 1)
    for i, one in enumerate(got):

        @pl.when(source == i)
        def take():
            for v in range(heads):
                states[0, v] = jnp.transpose(one[place, v * 128 : (v + 1) * 128]).astype(F32)
            lines = [one[place, base + h * 16 : base + h * 16 + 16].astype(F32) for h in range(own)]
            for k in range(KERNEL - 1):
                row = [
                    jnp.concatenate([x[4 * k + cg : 4 * k + cg + 1] for cg in range(4)], axis=1)
                    for x in lines
                ]
                tails[0, k] = jnp.concatenate(row, axis=0).astype(BF16)

    @pl.when(source < 0)
    def clear():
        states[...] = jnp.zeros_like(states)
        tails[...] = jnp.zeros_like(tails)


def land(me, got, heads, own):
    lines = got[0].shape[1]
    slots = len(got) * CAP
    smem = pl.BlockSpec(memory_space=pltpu.SMEM)
    return pl.pallas_call(
        land_kernel,
        grid=(slots,),
        in_specs=[smem] + [pl.BlockSpec((CAP, lines, 128), lambda g: (0, 0, 0))] * len(got),
        out_specs=[
            pl.BlockSpec((1, heads, 128, 128), lambda g: (g, 0, 0, 0)),
            pl.BlockSpec((1, KERNEL - 1, own, 512), lambda g: (g, 0, 0, 0)),
        ],
        out_shape=[
            jax.ShapeDtypeStruct((slots, heads, 128, 128), F32),
            jax.ShapeDtypeStruct((slots, KERNEL - 1, own, 512), BF16),
        ],
        scratch_shapes=[pltpu.SMEM((len(got),), jnp.int32)],
        compiler_params=params(ALL_VMEM),
        cost_estimate=pl.CostEstimate(flops=10**6, bytes_accessed=4 << 20, transcendentals=0),
        name="land",
    )(me, *got)


def exchange(parts, axis):
    count = len(parts)
    got = {0: parts[0]}
    for k in range(count - 1, 0, -1):
        got[k] = lax.ppermute(parts[k], axis, [(i, i ^ k) for i in range(count)])
    return [got[k] for k in range(count)]


def body(
    mixed,
    decay_in,
    beta_in,
    gate_z,
    conv_weight,
    a_log,
    dt_bias,
    norm_gain,
    req_blocks,
    replica_of,
    finished,
):
    n = lax.axis_size("seq")
    replicas = lax.axis_size("rep")
    heads = mixed.shape[1]
    own = heads // n
    me = lax.axis_index("seq").astype(jnp.int32).reshape(1)
    kpack, par = pack_keys(mixed[0], decay_in[0], beta_in[0], conv_weight, a_log, dt_bias)
    halo, *vpack = pack_values(me, mixed[0], n)
    kp = lax.all_to_all(kpack.reshape(n, own, KROWS, TILE), "seq", 0, 0, tiled=True)
    halo = lax.ppermute(halo, "seq", [(i, i + 1) for i in range(n - 1)])
    vp = exchange(vpack, "seq")
    hsol, hft, hgs, hrows = head_prep(req_blocks, kp, par)
    hrows, halo = lax.optimization_barrier((hrows, halo))
    wk, wv, sc, ft, qs, rows = token_prep(
        req_blocks, me, mixed[0], decay_in[0], beta_in[0], halo, kp.reshape(heads, KROWS, TILE)
    )
    sin, ends, ktails = head_chain(req_blocks, me, par, hsol, hft, hgs, hrows, vp)
    sin = lax.all_to_all(sin, "seq", 0, 0, tiled=True)
    my_rep = lax.axis_index("rep").astype(jnp.int32).reshape(1)
    send = choose(req_blocks, replica_of, finished, my_rep, ends, ktails, replicas)
    got = exchange(send, "rep")
    states, tails = land(my_rep, got, own * RATIO, own)
    out = token_out(
        req_blocks,
        me,
        sin.reshape(heads * RATIO, 128, 128),
        wk,
        wv,
        sc,
        ft,
        qs,
        rows,
        gate_z[0],
        norm_gain.reshape(1, DV),
    )
    return (out[None], states[None], tails[None])


def solution(mesh):
    placed = (
        P("rep", None, None, "seq"),
        P("rep", None, None, "seq"),
        P("rep", None, None, "seq"),
        P("rep", None, None, "seq"),
        P(None, "seq", None),
        P("seq"),
        P("seq"),
        P(),
        P("rep", None),
        P("rep", None),
        P("rep", None),
    )
    return jax.shard_map(
        body,
        mesh=mesh,
        in_specs=placed,
        out_specs=(
            P("rep", None, None, "seq"),
            P("rep", None, "seq", None, None),
            P("rep", None, None, "seq", None),
        ),
        check_vma=False,
    )
```

```python
import jax
import jax.numpy as jnp
from jax import lax
from jax.experimental import pallas as pl
from jax.experimental.pallas import tpu as pltpu
from jax.sharding import PartitionSpec as P

DK = 128
DV = 128
KERNEL = 4
SPAN = 64
CAP = 2
RATIO = 2
TILE = 2 * SPAN
KROWS = 160
VROWS = 288
WIDE = 8
MOST = 16
EPSILON = 1e-06
F32 = jnp.float32
BF16 = jnp.bfloat16
VMEM_LIMIT = 56 * 1024 * 1024
ALL_VMEM = 63 * 1024 * 1024


def params(limit=VMEM_LIMIT):
    return pltpu.CompilerParams(vmem_limit_bytes=limit)


def iota(shape, dim):
    return lax.broadcasted_iota(jnp.int32, shape, dim)


def dot(left, right):
    return jnp.dot(left, right, preferred_element_type=F32)


def split(wide):
    high = wide.astype(BF16)
    return high, (wide - high.astype(F32)).astype(BF16)


def halves(shape):
    first = iota(shape, len(shape) - 1) < SPAN
    return jnp.where(first, 1.0, 0.0).astype(BF16), jnp.where(first, 0.0, 1.0).astype(BF16)


def corner(first, second):
    none = jnp.zeros_like(first)
    top = jnp.concatenate([first, none], axis=1)
    return jnp.concatenate([top, jnp.concatenate([none, second], axis=1)], axis=0)


def diagonal(packed, masks):
    squares = []
    for r in range(RATIO):
        one = packed[:, r * TILE : (r + 1) * TILE]
        squares.append(jnp.concatenate([one * masks[0], one * masks[1]], axis=0))
    return corner(*squares)


def block_dot(left, right, masks):
    return dot(left, diagonal(right, masks))


def parameter_lines(h, cw, alog, dtb):
    taps = cw[:, h].astype(F32)
    rows = [taps[tap : tap + 1, cg * 128 : (cg + 1) * 128] for tap in range(KERNEL) for cg in range(4)]
    rest = jnp.concatenate(
        [jnp.full((1, 128), ref[h * RATIO + r], F32) for ref in (alog, dtb) for r in range(RATIO)], axis=0
    )
    parts = []
    for _ in range(3):
        part = rest.astype(BF16).astype(F32)
        rest = rest - part
        parts.append(part)
    return jnp.concatenate(rows + parts + [jnp.zeros((4, 128), F32)], axis=0)


def parameters(lines):
    wide = lines.astype(F32)
    rest = wide[16:20] + wide[20:24] + wide[24:28]
    return wide[:16], rest[:RATIO], rest[RATIO:]


def pack_keys_kernel(mixed, dec, beta, cw, alog, dtb, kout, pout):
    row = iota((32, TILE), 0)
    own = pout.shape[0]
    lines = [parameter_lines(h, cw, alog, dtb) for h in range(own)]
    for t in range(mixed.shape[0]):
        kout[t, :DK] = mixed[t]
        rest = lines[t % own]
        d, b = dec[t].astype(F32), beta[t].astype(F32)
        for r in range(RATIO):
            rest = jnp.where(row == 28 + r, d[r : r + 1], rest)
            rest = jnp.where(row == 30 + r, b[r : r + 1], rest)
        kout[t, DK:] = rest.astype(BF16)

    @pl.when(pl.program_id(0) == 0)
    def first():
        for h in range(own):
            pout[h] = lines[h].astype(BF16)


def pack_keys(mixed, dec, beta, cw, alog, dtb):
    heads = mixed.shape[0]
    own = cw.shape[1]
    step = heads // 2
    smem = pl.BlockSpec(memory_space=pltpu.SMEM)
    return pl.pallas_call(
        pack_keys_kernel,
        grid=(heads // step,),
        in_specs=[
            pl.BlockSpec((step, DK, TILE), lambda g: (g, 1, 0)),
            pl.BlockSpec((step, RATIO, TILE), lambda g: (g, 0, 0)),
            pl.BlockSpec((step, RATIO, TILE), lambda g: (g, 0, 0)),
            pl.BlockSpec((KERNEL, own, 512), lambda g: (0, 0, 0)),
            smem,
            smem,
        ],
        out_specs=[
            pl.BlockSpec((step, KROWS, TILE), lambda g: (g, 0, 0)),
            pl.BlockSpec((own, 32, 128), lambda g: (0, 0, 0)),
        ],
        out_shape=[
            jax.ShapeDtypeStruct((heads, KROWS, TILE), BF16),
            jax.ShapeDtypeStruct((own, 32, 128), BF16),
        ],
        compiler_params=params(),
        cost_estimate=pl.CostEstimate(flops=10**6, bytes_accessed=2 << 20, transcendentals=0),
        name="pack_keys",
    )(mixed, dec, beta, cw, alog, dtb)


def pack_values_kernel(me, mixed, hout, *outs):
    step = pl.program_id(0)
    own = outs[0].shape[0]
    row, tok = iota((TILE, 128), 1), iota((TILE, 128), 0)
    place = row & 15
    picks = []
    for cg in range(4):
        hit = (row < 32) & (place < 12) & ((place & 3) == cg)
        hit = hit & (tok == (row >> 4) * SPAN + 61 + (place >> 2))
        picks.append(jnp.where(hit, 1.0, 0.0).astype(BF16))
    all_tails = []
    for h in range(mixed.shape[0]):
        tails = dot(mixed[h, :128], picks[0])
        for cg in range(1, 4):
            tails = tails + dot(mixed[h, cg * 128 : (cg + 1) * 128], picks[cg])
        all_tails.append(jnp.transpose(tails)[:32].astype(BF16))
        hout[h] = all_tails[h][16:]
    for i, out in enumerate(outs):

        @pl.when((step == i // 4) & ((me[0] & 3) == 0))
        def put0():
            put(mixed, all_tails, out, (i & 3) ^ 0, own)

        @pl.when((step == i // 4) & ((me[0] & 3) == 1))
        def put1():
            put(mixed, all_tails, out, (i & 3) ^ 1, own)

        @pl.when((step == i // 4) & ((me[0] & 3) == 2))
        def put2():
            put(mixed, all_tails, out, (i & 3) ^ 2, own)

        @pl.when((step == i // 4) & ((me[0] & 3) == 3))
        def put3():
            put(mixed, all_tails, out, (i & 3) ^ 3, own)


def put(mixed, all_tails, out, place, own):
    for h in range(own):
        out[h, :256] = mixed[place * own + h, 2 * DK :]
        out[h, 256:] = all_tails[place * own + h]


def pack_values(me, mixed, n):
    heads = mixed.shape[0]
    own = heads // n
    return pl.pallas_call(
        pack_values_kernel,
        grid_spec=pltpu.PrefetchScalarGridSpec(
            num_scalar_prefetch=1,
            grid=(n // 4,),
            in_specs=[pl.BlockSpec((4 * own, 512, TILE), lambda g, me: ((me[0] >> 2) ^ g, 0, 0))],
            out_specs=[pl.BlockSpec((4 * own, 16, TILE), lambda g, me: ((me[0] >> 2) ^ g, 0, 0))]
            + [pl.BlockSpec((own, VROWS, TILE), lambda g, me: (0, 0, 0))] * n,
        ),
        out_shape=[jax.ShapeDtypeStruct((heads, 16, TILE), BF16)]
        + [jax.ShapeDtypeStruct((own, VROWS, TILE), BF16)] * n,
        compiler_params=params(),
        cost_estimate=pl.CostEstimate(flops=10**8, bytes_accessed=4 << 20, transcendentals=0),
        name="pack_values",
    )(me, mixed)


def is_fresh(req, block):
    start = jnp.int32(0)
    fresh = jnp.bool_(False)
    for j in range(req.shape[1]):
        fresh = fresh | (start == block)
        start = start + req[0, j]
    return fresh


def tap_tables():
    row, part = iota((16, 4 * 128), 0), iota((16, 4 * 128), 1) >> 7
    hits = [((row & 3) == cg) & ((row >> 2) == part) for cg in range(4)]
    return [jnp.where(hit, 1.0, 0.0).astype(BF16) for hit in hits]


def halo_tables():
    row, lane = iota((48, 128), 0), iota((48, 128), 1)
    token = (row >> 2) % 3
    hits = [((row & 3) == cg) & (row < 36) & (token == lane) for cg in range(4)]
    return [jnp.where(hit, 1.0, 0.0).astype(BF16) for hit in hits]


def turned_dot(rows, table):
    return lax.dot_general(rows, table, (((0,), (0,)), ((), ())), preferred_element_type=F32)


def spread_taps(par, table):
    both = turned_dot(par, table)
    return [both[:, tap * 128 : (tap + 1) * 128] for tap in range(KERNEL)]


def halo_terms(halo, par, not_fresh0):
    x = [halo[4 * k : 4 * k + 4].astype(F32) * not_fresh0 for k in range(3)]
    w = [par[4 * k : 4 * k + 4] for k in range(3)]
    terms = jnp.concatenate(
        [w[0] * x[0] + w[1] * x[1] + w[2] * x[2], w[0] * x[1] + w[1] * x[2], w[0] * x[2]], axis=0
    )
    high = terms.astype(BF16).astype(F32)
    middle = (terms - high).astype(BF16).astype(F32)
    parts = [high, middle, terms - high - middle, jnp.zeros((12, 128), F32)]
    return jnp.concatenate(parts, axis=0).astype(BF16)


def convolve(raw, before, terms, taps, masks):
    lane = iota((1, TILE), 1)
    cur = raw.astype(F32)
    total = taps[KERNEL - 1] * cur
    if terms is not None:
        total = total + terms
    for back in range(1, KERNEL):
        moved = cur if before is None else jnp.where(lane >= TILE - back, before, cur)
        total = total + taps[KERNEL - 1 - back] * (pltpu.roll(moved, back, 1) * masks[back - 1])
    return (total / (1.0 + jnp.exp(-total))).astype(BF16)


def conv_masks(cut0, cut1):
    lane = iota((1, TILE), 1)
    masks = []
    for back in range(1, KERNEL):
        gone = ((lane < back) & cut0) | ((lane >= SPAN) & (lane < SPAN + back) & cut1)
        masks.append(jnp.where(gone, 0.0, 1.0))
    return masks


def row_prep(dec, beta, alog, dtb):
    lane = iota(dec.shape, 1)
    x = dec + dtb
    decay = -jnp.exp(alog) * (jnp.maximum(x, 0.0) + jnp.log1p(jnp.exp(-jnp.abs(x))))
    cum = decay
    for shift in (1, 2, 4, 8, 16, 32):
        cum = cum + jnp.where((lane & (SPAN - 1)) >= shift, pltpu.roll(cum, shift, 1), 0.0)
    strength = 1.0 / (1.0 + jnp.exp(-beta))
    grown = jnp.exp(cum)
    close0, close1 = cum[:, SPAN - 1 : SPAN], cum[:, TILE - 1 :]
    fade = jnp.exp(jnp.where(lane < SPAN, close0, close1) - cum)
    keep0 = jnp.exp(jnp.broadcast_to(close0, cum.shape))
    keep1 = jnp.exp(jnp.broadcast_to(close1, cum.shape))
    return cum, strength, grown, fade, keep0, keep1


def unit_inverses(systems):
    shape = (SPAN, RATIO * TILE)
    row, col = iota(shape, 0), iota(shape, 1) & (SPAN - 1)
    near = (row >> 4) == (col >> 4)
    eye = jnp.where(row == col, 1.0, 0.0)
    masks = halves((SPAN, TILE))

    def low(arrays):
        return [a.astype(BF16) for a in arrays]

    def stack(pair):
        return jnp.concatenate(pair, axis=0)

    total = [jnp.where(near, eye - a, 0.0) for a in systems]
    power = low([jnp.where(near, -a, 0.0) for a in systems])
    power = low([block_dot(p, p, masks) for p in power])
    for _ in range(2):
        both = [block_dot(stack([t, p]), p, masks) for t, p in zip(low(total), power)]
        total = [t + b[:SPAN] for t, b in zip(total, both)]
        power = low([b[SPAN:] for b in both])
    total = [t + block_dot(l, p, masks) for t, l, p in zip(total, low(total), power)]
    small = low(total)
    rest = low([jnp.where(near, 0.0, a) for a in systems])
    cross = low([block_dot(t, r, masks) for t, r in zip(small, rest)])
    total = [t - block_dot(x, l, masks) for t, x, l in zip(total, cross, small)]
    small = low(total)
    solved = []
    for a, x in zip(systems, small):
        wide = x.astype(F32)
        parts = block_dot(stack(split(a)), x, masks)
        miss = eye - wide - (parts[:SPAN] + parts[SPAN:])
        solved.append((wide + block_dot(x, miss.astype(BF16), masks)).astype(BF16))
    return solved


def both_blocks(square):
    none = jnp.zeros((SPAN, square.shape[1]), square.dtype)
    first = jnp.concatenate([square[:SPAN], none], axis=0)
    return jnp.concatenate([first, jnp.concatenate([none, square[SPAN:]], axis=0)], axis=1)


def unit_keys(convolved):
    wide = convolved.astype(F32)
    return (wide * lax.rsqrt(jnp.sum(wide * wide, axis=0, keepdims=True) + EPSILON)).astype(BF16)


def solve_tiles(keys, queries, prep):
    cum, strength, grown, fade, keep0, keep1 = prep
    row, lane = iota((SPAN, TILE), 0), iota((SPAN, TILE), 1)
    early = lane < SPAN
    seen = (lane & (SPAN - 1)) >= row
    later = (lane & (SPAN - 1)) > row
    columns = jnp.transpose(jnp.concatenate([cum, fade], axis=0))
    count = cum.shape[0]

    def beside(tall):
        return jnp.where(early, tall[:SPAN], tall[SPAN:])

    systems, faded, scores = [], [], []
    for t, k in enumerate(keys):
        turned = jnp.transpose(k.astype(F32))
        if queries is None:
            gram = beside(dot(turned.astype(BF16), k))
        else:
            prod = dot(turned.astype(BF16), jnp.concatenate([k, queries[t]], axis=1))
            gram, touch = beside(prod[:, :TILE]), beside(prod[:, TILE:])
        pair = []
        for r in range(RATIO):
            at = t * RATIO + r
            diff = cum[at : at + 1] - beside(columns[:, at : at + 1])
            ratio = jnp.where(seen, jnp.exp(jnp.where(seen, diff, 0.0)), 0.0)
            pair.append(jnp.where(later, strength[at : at + 1] * gram * ratio, 0.0))
            if queries is not None:
                scores.append((touch * ratio).astype(BF16))
            faded.append((turned * columns[:, count + at : count + at + 1]).astype(BF16))
        systems.append(jnp.concatenate(pair, axis=1))
    return unit_inverses(systems), faded, scores


def token_prep_kernel(req, me, mixed, dec, beta, halo, par_lines, wk, wv, sc, ft, qo, rows):
    fresh0, fresh1 = is_fresh(req, me[0] * 2), is_fresh(req, me[0] * 2 + 1)
    not_fresh0 = jnp.where(fresh0, 0.0, 1.0)
    masks = conv_masks(True, fresh1)
    tap_tab, halo_tab = tap_tables(), halo_tables()
    tiles = range(mixed.shape[0])
    par = [parameters(par_lines[t]) for t in tiles]

    def gather(pick):
        return jnp.concatenate([pick(t) for t in tiles], axis=0)

    prep = row_prep(
        gather(lambda t: dec[t].astype(F32)),
        gather(lambda t: beta[t].astype(F32)),
        jnp.concatenate([p[1] for p in par], axis=0),
        jnp.concatenate([p[2] for p in par], axis=0),
    )
    cum, strength, grown, fade, keep0, keep1 = prep
    keys, queries, values = [], [], []
    for t in tiles:
        terms = halo_terms(halo[t], par[t][0], not_fresh0)
        lines = par_lines[t, :16]
        q, k, v0, v1 = [
            convolve(
                mixed[t, c * 128 : (c + 1) * 128],
                None,
                turned_dot(terms, halo_tab[c]),
                spread_taps(lines, tap_tab[c]),
                masks,
            )
            for c in range(4)
        ]
        keys.append(unit_keys(k))
        queries.append(q)
        values.append((v0, v1))
        qo[t] = q
        rows[t] = jnp.concatenate(
            [keep0[2 * t : 2 * t + 2], grown[2 * t : 2 * t + 2], keep1[2 * t : 2 * t + 2], strength[2 * t : 2 * t + 2]],
            axis=0,
        )
    solved, faded, scores = solve_tiles(keys, queries, prep)
    sides = halves((SPAN, TILE))
    for t in tiles:
        stacks = []
        for r in range(RATIO):
            at = t * RATIO + r
            s, lift = strength[at : at + 1], strength[at : at + 1] * grown[at : at + 1]
            stacked = jnp.concatenate(
                [lift * keys[t].astype(F32), s * values[t][r].astype(F32)], axis=0
            )
            stacks.append(stacked.astype(BF16))
            sc[t, :, r * TILE : (r + 1) * TILE] = scores[at]
            ft[at] = faded[at]
        out = block_dot(jnp.concatenate(stacks, axis=1), solved[t], sides).astype(BF16)
        for r in range(RATIO):
            wk[t * RATIO + r] = out[:DK, r * TILE : (r + 1) * TILE]
            wv[t * RATIO + r] = out[DK:, r * TILE : (r + 1) * TILE]


def token_prep(req, me, mixed, dec, beta, halo, par):
    heads = mixed.shape[0]
    smem = pl.BlockSpec(memory_space=pltpu.SMEM)

    def tiles(count, *rest):
        return pl.BlockSpec((count,) + rest, lambda g: (g,) + (0,) * len(rest))

    square = jax.ShapeDtypeStruct((heads * RATIO, 128, 128), BF16)
    return pl.pallas_call(
        token_prep_kernel,
        grid=(heads // WIDE,),
        in_specs=[
            smem,
            smem,
            tiles(WIDE, 512, TILE),
            tiles(WIDE, RATIO, TILE),
            tiles(WIDE, RATIO, TILE),
            tiles(WIDE, 16, TILE),
            pl.BlockSpec((WIDE, 32, 128), lambda g: (g, 4, 0)),
        ],
        out_specs=[tiles(WIDE * RATIO, 128, 128)] * 2
        + [tiles(WIDE, SPAN, RATIO * TILE), tiles(WIDE * RATIO, 128, 128)]
        + [tiles(WIDE, 128, 128), tiles(WIDE, 8, 128)],
        out_shape=[square] * 2
        + [
            jax.ShapeDtypeStruct((heads, SPAN, RATIO * TILE), BF16),
            square,
            jax.ShapeDtypeStruct((heads, 128, 128), BF16),
            jax.ShapeDtypeStruct((heads, 8, 128), F32),
        ],
        compiler_params=params(),
        cost_estimate=pl.CostEstimate(flops=10**10, bytes_accessed=8 << 20, transcendentals=10**6),
        name="token_prep",
    )(req, me, mixed, dec, beta, halo, par)


def head_prep_kernel(req, kp, previous, par_lines, sol, ft, gs, rows):
    step = pl.program_id(0)
    depth, own = kp.shape[0], kp.shape[1]
    tap_tab = tap_tables()
    order = [(d, h) for d in range(depth) for h in range(own)]
    par = [parameters(par_lines[h]) for h in range(own)]

    small = [kp[d, h, DK:].astype(F32) for d, h in order]
    prep = row_prep(
        jnp.concatenate([s[28:30] for s in small], axis=0),
        jnp.concatenate([s[30:32] for s in small], axis=0),
        jnp.concatenate([par[h][1] for d, h in order], axis=0),
        jnp.concatenate([par[h][2] for d, h in order], axis=0),
    )
    cum, strength, grown, fade, keep0, keep1 = prep
    keys = []
    taps = [spread_taps(par_lines[h, :16], tap_tab[1]) for h in range(own)]
    for d in range(depth):
        block = (step * depth + d) * 2
        masks = conv_masks(is_fresh(req, block), is_fresh(req, block + 1))
        for h in range(own):
            before = (kp[d - 1, h, :DK] if d else previous[0, h]).astype(F32)
            keys.append(unit_keys(convolve(kp[d, h, :DK], before, None, taps[h], masks)))
    solved, faded, unused = solve_tiles(keys, None, prep)
    sides = halves((SPAN, TILE))
    for t, (d, h) in enumerate(order):
        rows[d, h] = jnp.concatenate(
            [keep0[2 * t : 2 * t + 2], keep1[2 * t : 2 * t + 2], strength[2 * t : 2 * t + 2], strength[2 * t : 2 * t + 2]],
            axis=0,
        )
        scaled = []
        for r in range(RATIO):
            at = t * RATIO + r
            lift = strength[at : at + 1] * grown[at : at + 1]
            scaled.append((lift * keys[t].astype(F32)).astype(BF16))
        wide = block_dot(jnp.concatenate(scaled, axis=1), solved[t], sides).astype(BF16)
        sol[d, h] = solved[t]
        for r in range(RATIO):
            at = t * RATIO + r
            drop = dot(wide[:, r * TILE : (r + 1) * TILE], both_blocks(faded[at])).astype(BF16)
            gs[d, h, r, 0] = drop[:, :DK]
            gs[d, h, r, 1] = drop[:, DK:]
            ft[d, h, r] = faded[at]


def head_prep(req, kp, par):
    n, own = kp.shape[:2]
    depth = MOST // own
    smem = pl.BlockSpec(memory_space=pltpu.SMEM)

    def tiles(*rest):
        return pl.BlockSpec((depth, own) + rest, lambda g: (g, 0) + (0,) * len(rest))

    square = jax.ShapeDtypeStruct((n, own, RATIO, 128, 128), BF16)
    return pl.pallas_call(
        head_prep_kernel,
        grid=(n // depth,),
        in_specs=[
            smem,
            tiles(KROWS, TILE),
            pl.BlockSpec((1, own, DK, TILE), lambda g: (jnp.maximum(g * depth - 1, 0), 0, 0, 0)),
            pl.BlockSpec((own, 32, 128), lambda g: (0, 0, 0)),
        ],
        out_specs=[
            tiles(SPAN, RATIO * TILE),
            tiles(RATIO, 128, 128),
            tiles(RATIO, 2, 128, 128),
            tiles(8, 128),
        ],
        out_shape=[
            jax.ShapeDtypeStruct((n, own, SPAN, RATIO * TILE), BF16),
            square,
            jax.ShapeDtypeStruct((n, own, RATIO, 2, 128, 128), BF16),
            jax.ShapeDtypeStruct((n, own, 8, 128), F32),
        ],
        compiler_params=params(),
        cost_estimate=pl.CostEstimate(flops=10**10, bytes_accessed=6 << 20, transcendentals=10**6),
        name="head_prep",
    )(req, kp, kp, par)


def head_chain_kernel(req, me, par_lines, sol, ft, gs, rows, *refs):
    n = refs[-6].shape[0]
    arrived, (sin, ends, tails, state, vp, spread) = refs[:n], refs[n:]
    step = pl.program_id(0)
    depth, own = sol.shape[0], sol.shape[1]

    @pl.when(step == 0)
    def first():
        for k, one in enumerate(arrived):
            vp[me[0] ^ k] = one[...]
            tails[me[0] ^ k] = one[:, 256:]
        tap_tab = tap_tables()
        for h in range(own):
            for r in range(RATIO):
                for tap, wide in enumerate(spread_taps(par_lines[h, :16], tap_tab[2 + r])):
                    spread[h * RATIO + r, tap] = wide

    sides = halves((SPAN, TILE))
    heads = [(h, r) for h in range(own) for r in range(RATIO)]
    taps = [[spread[v, tap] for tap in range(KERNEL)] for v in range(len(heads))]
    current = [state[v] for v in range(len(heads))]
    for d in range(depth):
        tile = step * depth + d
        past = jnp.maximum(tile - 1, 0)
        fresh = [is_fresh(req, tile * 2), is_fresh(req, tile * 2 + 1)]
        masks = conv_masks(fresh[0], fresh[1])
        gains = []
        for h in range(own):
            scaled = []
            for r in range(RATIO):
                raw = vp[tile, h, r * DV : (r + 1) * DV]
                before = vp[past, h, r * DV : (r + 1) * DV].astype(F32)
                value = convolve(raw, before, None, taps[h * RATIO + r], masks)
                scaled.append((rows[d, h, 4 + r : 5 + r] * value.astype(F32)).astype(BF16))
            wide = block_dot(jnp.concatenate(scaled, axis=1), sol[d, h], sides).astype(BF16)
            for r in range(RATIO):
                gains.append(dot(wide[:, r * TILE : (r + 1) * TILE], both_blocks(ft[d, h, r])))
        for half in range(2):
            for h in range(own):
                now = [jnp.where(fresh[half], 0.0, current[h * RATIO + r]) for r in range(RATIO)]
                lost = dot(
                    jnp.concatenate([x.astype(BF16) for x in now], axis=1),
                    corner(gs[d, h, 0, half], gs[d, h, 1, half]),
                )
                for r in range(RATIO):
                    v = h * RATIO + r
                    keep = rows[d, h, 2 * half + r : 2 * half + r + 1]
                    gain = gains[v][:, half * DV : (half + 1) * DV]
                    current[v] = keep * now[r] + (gain - lost[:, r * TILE : (r + 1) * TILE])
                    ends[d * 2 + half, v] = current[v].astype(BF16)
        onward = lax.rem(tile + 1, n)
        for v in range(len(heads)):
            sin[onward, v] = current[v].astype(BF16)
    for v in range(len(heads)):
        state[v] = current[v]


def head_chain(req, me, par, sol, ft, gs, rows, arrived):
    n, own = sol.shape[:2]
    depth = WIDE // own
    smem = pl.BlockSpec(memory_space=pltpu.SMEM)

    def tiles(*rest):
        return pl.BlockSpec((depth, own) + rest, lambda g: (g, 0) + (0,) * len(rest))

    return pl.pallas_call(
        head_chain_kernel,
        grid=(n // depth,),
        in_specs=[
            smem,
            smem,
            pl.BlockSpec((own, 32, 128), lambda g: (0, 0, 0)),
            tiles(SPAN, RATIO * TILE),
            tiles(RATIO, 128, 128),
            tiles(RATIO, 2, 128, 128),
            tiles(8, 128),
        ]
        + [pl.BlockSpec((own, VROWS, TILE), lambda g: (0, 0, 0))] * n,
        out_specs=[
            pl.BlockSpec((n, own * RATIO, 128, 128), lambda g: (0, 0, 0, 0)),
            pl.BlockSpec((2 * depth, own * RATIO, 128, 128), lambda g: (g, 0, 0, 0)),
            pl.BlockSpec((n, own, 32, TILE), lambda g: (0, 0, 0, 0)),
        ],
        out_shape=[
            jax.ShapeDtypeStruct((n, own * RATIO, 128, 128), BF16),
            jax.ShapeDtypeStruct((2 * n, own * RATIO, 128, 128), BF16),
            jax.ShapeDtypeStruct((n, own, 32, TILE), BF16),
        ],
        scratch_shapes=[
            pltpu.VMEM((own * RATIO, 128, 128), F32),
            pltpu.VMEM((n, own, VROWS, TILE), BF16),
            pltpu.VMEM((own * RATIO, KERNEL, 128, 128), F32),
        ],
        compiler_params=params(),
        cost_estimate=pl.CostEstimate(flops=3 * 10**9, bytes_accessed=8 << 20, transcendentals=10**6),
        name="head_chain",
    )(req, me, par, sol, ft, gs, rows, *arrived)


def choose_kernel(req, rep, fin, me, ends, kt, *refs):
    outs, counts = refs[:-1], refs[-1]
    own, heads = kt.shape[1], ends.shape[1]
    base = heads * 128
    for i, out in enumerate(outs):
        out[...] = jnp.zeros_like(out)
        counts[i] = 0
    end = jnp.int32(-1)
    for j in range(req.shape[1]):
        end = end + req[0, j]
        where = rep[0, j] ^ me[0]
        place = jnp.minimum(counts[where], CAP - 1)
        done = fin[0, j] > 0
        counts[where] = counts[where] + jnp.where(done, 1, 0)
        for i, out in enumerate(outs):

            @pl.when(done & (where == i))
            def take():
                for v in range(heads):
                    out[place, v * 128 : (v + 1) * 128] = ends[end, v]
                for h in range(own):
                    lines = kt[end >> 1, h].astype(F32)
                    lines = jnp.where((end & 1) > 0, lines[16:], lines[:16]).astype(BF16)
                    out[place, base + h * 16 : base + h * 16 + 16] = lines

    for i, out in enumerate(outs):
        number = jnp.full((16, 128), counts[i], jnp.int32).astype(F32).astype(BF16)
        for c in range(CAP):
            out[c, base + own * 16 :] = number


def choose(req, rep, fin, me, ends, tails, replicas):
    own = tails.shape[1]
    smem = pl.BlockSpec(memory_space=pltpu.SMEM)
    lines = own * RATIO * 128 + own * 16 + 16
    return pl.pallas_call(
        choose_kernel,
        grid=(1,),
        in_specs=[
            smem,
            smem,
            smem,
            smem,
            pl.BlockSpec(ends.shape, lambda g: (0, 0, 0, 0)),
            pl.BlockSpec(tails.shape, lambda g: (0, 0, 0, 0)),
        ],
        out_specs=[pl.BlockSpec((CAP, lines, 128), lambda g: (0, 0, 0))] * replicas,
        out_shape=[jax.ShapeDtypeStruct((CAP, lines, 128), BF16)] * replicas,
        scratch_shapes=[pltpu.SMEM((replicas,), jnp.int32)],
        compiler_params=params(),
        cost_estimate=pl.CostEstimate(flops=10**6, bytes_accessed=4 << 20, transcendentals=0),
        name="choose",
    )(req, rep, fin, me, ends, tails)


def token_out_kernel(req, me, sin, wk, wv, sc, ft, qs, rows, gate, norm_gain, out):
    gain = jnp.transpose(jnp.broadcast_to(norm_gain[...], (TILE, DV)))
    stay0 = jnp.where(is_fresh(req, me[0] * 2), 0.0, 1.0)
    stay1 = jnp.where(is_fresh(req, me[0] * 2 + 1), 0.0, 1.0)
    lane = iota((DV, TILE), 1)
    early = lane < SPAN
    sides = halves((SPAN, TILE))
    units = [(t, r) for t in range(qs.shape[0]) for r in range(RATIO)]
    both = [jnp.concatenate([wk[t * RATIO + r], qs[t]], axis=1) for t, r in units]
    enter = [sin[t * RATIO + r].astype(F32) * stay0 for t, r in units]
    first = [dot(e.astype(BF16), b) for e, b in zip(enter, both)]
    wide = [wv[t * RATIO + r].astype(F32) for t, r in units]
    new0 = [jnp.where(early, w - f[:, :TILE], 0.0) for w, f in zip(wide, first)]
    tiles = range(qs.shape[0])
    pairs = [
        dot(
            jnp.concatenate([new0[2 * t].astype(BF16), new0[2 * t + 1].astype(BF16)], axis=1),
            corner(ft[2 * t], ft[2 * t + 1]),
        )
        for t in tiles
    ]
    middle = [
        (rows[t, r : r + 1] * e + pairs[t][:, r * TILE : (r + 1) * TILE]) * stay1
        for (t, r), e in zip(units, enter)
    ]
    second = [dot(m.astype(BF16), b) for m, b in zip(middle, both)]
    new = [
        jnp.where(early, x, w - s[:, :TILE]).astype(BF16) for x, w, s in zip(new0, wide, second)
    ]
    near = [
        block_dot(jnp.concatenate([new[2 * t], new[2 * t + 1]], axis=1), sc[t], sides) for t in tiles
    ]
    for at, (t, r) in enumerate(units):
        core = rows[t, 2 + r : 3 + r] * jnp.where(early, first[at][:, TILE:], second[at][:, TILE:])
        core = (core + near[t][:, r * TILE : (r + 1) * TILE]).astype(BF16).astype(F32)
        inverse_rms = lax.rsqrt(jnp.mean(core * core, axis=0, keepdims=True) + EPSILON)
        z = gate[t, r * DV : (r + 1) * DV].astype(F32)
        result = core * inverse_rms * gain * (z / (1.0 + jnp.exp(-z)))
        out[t, r * DV : (r + 1) * DV] = result.astype(BF16)


def token_out(req, me, sin, wk, wv, sc, ft, qs, rows, gate, gain):
    heads = qs.shape[0]
    smem = pl.BlockSpec(memory_space=pltpu.SMEM)

    def tiles(count, *rest):
        return pl.BlockSpec((count,) + rest, lambda g: (g,) + (0,) * len(rest))

    return pl.pallas_call(
        token_out_kernel,
        grid=(heads // WIDE,),
        in_specs=[smem, smem]
        + [tiles(WIDE * RATIO, 128, 128)] * 3
        + [tiles(WIDE, SPAN, RATIO * TILE), tiles(WIDE * RATIO, 128, 128)]
        + [
            tiles(WIDE, 128, 128),
            tiles(WIDE, 8, 128),
            tiles(WIDE, 256, TILE),
            pl.BlockSpec((1, 128), lambda g: (0, 0)),
        ],
        out_specs=tiles(WIDE, 256, TILE),
        out_shape=jax.ShapeDtypeStruct((heads, 256, TILE), BF16),
        compiler_params=params(ALL_VMEM),
        cost_estimate=pl.CostEstimate(flops=10**9, bytes_accessed=8 << 20, transcendentals=10**6),
        name="token_out",
    )(req, me, sin, wk, wv, sc, ft, qs, rows, gate, gain)


def land_kernel(me, *refs):
    got, (states, tails, counts) = refs[:-3], refs[-3:]
    slot = pl.program_id(0)
    heads, own = states.shape[1], tails.shape[2]
    base = heads * 128

    @pl.when(slot == 0)
    def first():
        for i, one in enumerate(got):
            number = jnp.max(one[0, base + own * 16 :].astype(F32))
            counts[i] = number.astype(jnp.int32)

    start = jnp.int32(0)
    source, place = jnp.int32(-1), jnp.int32(0)
    for p in range(len(got)):
        away = me[0] ^ p
        number = counts[away]
        inside = (slot >= start) & (slot < start + number)
        source = jnp.where(inside, away, source)
        place = jnp.where(inside, slot - start, place)
        start = start + number
    place = jnp.clip(place, 0, CAP - 1)
    for i, one in enumerate(got):

        @pl.when(source == i)
        def take():
            for v in range(heads):
                states[0, v] = jnp.transpose(one[place, v * 128 : (v + 1) * 128]).astype(F32)
            lines = [one[place, base + h * 16 : base + h * 16 + 16].astype(F32) for h in range(own)]
            for k in range(KERNEL - 1):
                row = [
                    jnp.concatenate([x[4 * k + cg : 4 * k + cg + 1] for cg in range(4)], axis=1)
                    for x in lines
                ]
                tails[0, k] = jnp.concatenate(row, axis=0).astype(BF16)

    @pl.when(source < 0)
    def clear():
        states[...] = jnp.zeros_like(states)
        tails[...] = jnp.zeros_like(tails)


def land(me, got, heads, own):
    lines = got[0].shape[1]
    slots = len(got) * CAP
    smem = pl.BlockSpec(memory_space=pltpu.SMEM)
    return pl.pallas_call(
        land_kernel,
        grid=(slots,),
        in_specs=[smem] + [pl.BlockSpec((CAP, lines, 128), lambda g: (0, 0, 0))] * len(got),
        out_specs=[
            pl.BlockSpec((1, heads, 128, 128), lambda g: (g, 0, 0, 0)),
            pl.BlockSpec((1, KERNEL - 1, own, 512), lambda g: (g, 0, 0, 0)),
        ],
        out_shape=[
            jax.ShapeDtypeStruct((slots, heads, 128, 128), F32),
            jax.ShapeDtypeStruct((slots, KERNEL - 1, own, 512), BF16),
        ],
        scratch_shapes=[pltpu.SMEM((len(got),), jnp.int32)],
        compiler_params=params(ALL_VMEM),
        cost_estimate=pl.CostEstimate(flops=10**6, bytes_accessed=4 << 20, transcendentals=0),
        name="land",
    )(me, *got)


def exchange(parts, axis):
    count = len(parts)
    got = {0: parts[0]}
    for k in range(count - 1, 0, -1):
        got[k] = lax.ppermute(parts[k], axis, [(i, i ^ k) for i in range(count)])
    return [got[k] for k in range(count)]


def body(
    mixed,
    decay_in,
    beta_in,
    gate_z,
    conv_weight,
    a_log,
    dt_bias,
    norm_gain,
    req_blocks,
    replica_of,
    finished,
):
    n = lax.axis_size("seq")
    replicas = lax.axis_size("rep")
    heads = mixed.shape[1]
    own = heads // n
    me = lax.axis_index("seq").astype(jnp.int32).reshape(1)
    kpack, par = pack_keys(mixed[0], decay_in[0], beta_in[0], conv_weight, a_log, dt_bias)
    halo, *vpack = pack_values(me, mixed[0], n)
    kp = lax.all_to_all(kpack.reshape(n, own, KROWS, TILE), "seq", 0, 0, tiled=True)
    vp = exchange(vpack, "seq")
    hsol, hft, hgs, hrows = head_prep(req_blocks, kp, par)
    hrows, halo = lax.optimization_barrier((hrows, halo))
    halo = lax.ppermute(halo, "seq", [(i, i + 1) for i in range(n - 1)])
    hsol, halo = lax.optimization_barrier((hsol, halo))
    wk, wv, sc, ft, qs, rows = token_prep(
        req_blocks, me, mixed[0], decay_in[0], beta_in[0], halo, kp.reshape(heads, KROWS, TILE)
    )
    sin, ends, ktails = head_chain(req_blocks, me, par, hsol, hft, hgs, hrows, vp)
    sin = lax.all_to_all(sin, "seq", 0, 0, tiled=True)
    my_rep = lax.axis_index("rep").astype(jnp.int32).reshape(1)
    send = choose(req_blocks, replica_of, finished, my_rep, ends, ktails, replicas)
    got = exchange(send, "rep")
    states, tails = land(my_rep, got, own * RATIO, own)
    out = token_out(
        req_blocks,
        me,
        sin.reshape(heads * RATIO, 128, 128),
        wk,
        wv,
        sc,
        ft,
        qs,
        rows,
        gate_z[0],
        norm_gain.reshape(1, DV),
    )
    return (out[None], states[None], tails[None])


def solution(mesh):
    placed = (
        P("rep", None, None, "seq"),
        P("rep", None, None, "seq"),
        P("rep", None, None, "seq"),
        P("rep", None, None, "seq"),
        P(None, "seq", None),
        P("seq"),
        P("seq"),
        P(),
        P("rep", None),
        P("rep", None),
        P("rep", None),
    )
    return jax.shard_map(
        body,
        mesh=mesh,
        in_specs=placed,
        out_specs=(
            P("rep", None, None, "seq"),
            P("rep", None, "seq", None, None),
            P("rep", None, None, "seq", None),
        ),
        check_vma=False,
    )
```

```python
import jax
import jax.numpy as jnp
from jax import lax
from jax.experimental import pallas as pl
from jax.experimental.pallas import tpu as pltpu
from jax.sharding import PartitionSpec as P

DK = 128
DV = 128
KERNEL = 4
SPAN = 64
CAP = 2
RATIO = 2
TILE = 2 * SPAN
KROWS = 160
VROWS = 288
WIDE = 8
MOST = 16
EPSILON = 1e-06
F32 = jnp.float32
BF16 = jnp.bfloat16
VMEM_LIMIT = 56 * 1024 * 1024
ALL_VMEM = 63 * 1024 * 1024


def params(limit=VMEM_LIMIT):
    return pltpu.CompilerParams(vmem_limit_bytes=limit)


def iota(shape, dim):
    return lax.broadcasted_iota(jnp.int32, shape, dim)


def dot(left, right):
    return jnp.dot(left, right, preferred_element_type=F32)


def split(wide):
    high = wide.astype(BF16)
    return high, (wide - high.astype(F32)).astype(BF16)


def halves(shape):
    first = iota(shape, len(shape) - 1) < SPAN
    return jnp.where(first, 1.0, 0.0).astype(BF16), jnp.where(first, 0.0, 1.0).astype(BF16)


def corner(first, second):
    none = jnp.zeros_like(first)
    top = jnp.concatenate([first, none], axis=1)
    return jnp.concatenate([top, jnp.concatenate([none, second], axis=1)], axis=0)


def diagonal(packed, masks):
    squares = []
    for r in range(RATIO):
        one = packed[:, r * TILE : (r + 1) * TILE]
        squares.append(jnp.concatenate([one * masks[0], one * masks[1]], axis=0))
    return corner(*squares)


def block_dot(left, right, masks):
    return dot(left, diagonal(right, masks))


def parameter_lines(h, cw, alog, dtb):
    taps = cw[:, h].astype(F32)
    rows = [taps[tap : tap + 1, cg * 128 : (cg + 1) * 128] for tap in range(KERNEL) for cg in range(4)]
    rest = jnp.concatenate(
        [jnp.full((1, 128), ref[h * RATIO + r], F32) for ref in (alog, dtb) for r in range(RATIO)], axis=0
    )
    parts = []
    for _ in range(3):
        part = rest.astype(BF16).astype(F32)
        rest = rest - part
        parts.append(part)
    return jnp.concatenate(rows + parts + [jnp.zeros((4, 128), F32)], axis=0)


def parameters(lines):
    wide = lines.astype(F32)
    rest = wide[16:20] + wide[20:24] + wide[24:28]
    return wide[:16], rest[:RATIO], rest[RATIO:]


def pack_keys_kernel(mixed, dec, beta, cw, alog, dtb, kout, pout):
    row = iota((32, TILE), 0)
    own = pout.shape[0]
    lines = [parameter_lines(h, cw, alog, dtb) for h in range(own)]
    for t in range(mixed.shape[0]):
        kout[t, :DK] = mixed[t]
        rest = lines[t % own]
        d, b = dec[t].astype(F32), beta[t].astype(F32)
        for r in range(RATIO):
            rest = jnp.where(row == 28 + r, d[r : r + 1], rest)
            rest = jnp.where(row == 30 + r, b[r : r + 1], rest)
        kout[t, DK:] = rest.astype(BF16)

    @pl.when(pl.program_id(0) == 0)
    def first():
        for h in range(own):
            pout[h] = lines[h].astype(BF16)


def pack_keys(mixed, dec, beta, cw, alog, dtb):
    heads = mixed.shape[0]
    own = cw.shape[1]
    step = heads // 2
    smem = pl.BlockSpec(memory_space=pltpu.SMEM)
    return pl.pallas_call(
        pack_keys_kernel,
        grid=(heads // step,),
        in_specs=[
            pl.BlockSpec((step, DK, TILE), lambda g: (g, 1, 0)),
            pl.BlockSpec((step, RATIO, TILE), lambda g: (g, 0, 0)),
            pl.BlockSpec((step, RATIO, TILE), lambda g: (g, 0, 0)),
            pl.BlockSpec((KERNEL, own, 512), lambda g: (0, 0, 0)),
            smem,
            smem,
        ],
        out_specs=[
            pl.BlockSpec((step, KROWS, TILE), lambda g: (g, 0, 0)),
            pl.BlockSpec((own, 32, 128), lambda g: (0, 0, 0)),
        ],
        out_shape=[
            jax.ShapeDtypeStruct((heads, KROWS, TILE), BF16),
            jax.ShapeDtypeStruct((own, 32, 128), BF16),
        ],
        compiler_params=params(),
        cost_estimate=pl.CostEstimate(flops=10**6, bytes_accessed=2 << 20, transcendentals=0),
        name="pack_keys",
    )(mixed, dec, beta, cw, alog, dtb)


def pack_values_kernel(me, mixed, hout, *outs):
    step = pl.program_id(0)
    own = outs[0].shape[0]
    row, tok = iota((TILE, 128), 1), iota((TILE, 128), 0)
    place = row & 15
    picks = []
    for cg in range(4):
        hit = (row < 32) & (place < 12) & ((place & 3) == cg)
        hit = hit & (tok == (row >> 4) * SPAN + 61 + (place >> 2))
        picks.append(jnp.where(hit, 1.0, 0.0).astype(BF16))
    all_tails = []
    for h in range(mixed.shape[0]):
        tails = dot(mixed[h, :128], picks[0])
        for cg in range(1, 4):
            tails = tails + dot(mixed[h, cg * 128 : (cg + 1) * 128], picks[cg])
        all_tails.append(jnp.transpose(tails)[:32].astype(BF16))
        hout[h] = all_tails[h][16:]
    for i, out in enumerate(outs):

        @pl.when((step == i // 4) & ((me[0] & 3) == 0))
        def put0():
            put(mixed, all_tails, out, (i & 3) ^ 0, own)

        @pl.when((step == i // 4) & ((me[0] & 3) == 1))
        def put1():
            put(mixed, all_tails, out, (i & 3) ^ 1, own)

        @pl.when((step == i // 4) & ((me[0] & 3) == 2))
        def put2():
            put(mixed, all_tails, out, (i & 3) ^ 2, own)

        @pl.when((step == i // 4) & ((me[0] & 3) == 3))
        def put3():
            put(mixed, all_tails, out, (i & 3) ^ 3, own)


def put(mixed, all_tails, out, place, own):
    for h in range(own):
        out[h, :256] = mixed[place * own + h, 2 * DK :]
        out[h, 256:] = all_tails[place * own + h]


def pack_values(me, mixed, n):
    heads = mixed.shape[0]
    own = heads // n
    return pl.pallas_call(
        pack_values_kernel,
        grid_spec=pltpu.PrefetchScalarGridSpec(
            num_scalar_prefetch=1,
            grid=(n // 4,),
            in_specs=[pl.BlockSpec((4 * own, 512, TILE), lambda g, me: ((me[0] >> 2) ^ g, 0, 0))],
            out_specs=[pl.BlockSpec((4 * own, 16, TILE), lambda g, me: ((me[0] >> 2) ^ g, 0, 0))]
            + [pl.BlockSpec((own, VROWS, TILE), lambda g, me: (0, 0, 0))] * n,
        ),
        out_shape=[jax.ShapeDtypeStruct((heads, 16, TILE), BF16)]
        + [jax.ShapeDtypeStruct((own, VROWS, TILE), BF16)] * n,
        compiler_params=params(),
        cost_estimate=pl.CostEstimate(flops=10**8, bytes_accessed=4 << 20, transcendentals=0),
        name="pack_values",
    )(me, mixed)


def is_fresh(req, block):
    start = jnp.int32(0)
    fresh = jnp.bool_(False)
    for j in range(req.shape[1]):
        fresh = fresh | (start == block)
        start = start + req[0, j]
    return fresh


def tap_tables():
    row, part = iota((16, 4 * 128), 0), iota((16, 4 * 128), 1) >> 7
    hits = [((row & 3) == cg) & ((row >> 2) == part) for cg in range(4)]
    return [jnp.where(hit, 1.0, 0.0).astype(BF16) for hit in hits]


def halo_tables():
    row, lane = iota((48, 128), 0), iota((48, 128), 1)
    token = (row >> 2) % 3
    hits = [((row & 3) == cg) & (row < 36) & (token == lane) for cg in range(4)]
    return [jnp.where(hit, 1.0, 0.0).astype(BF16) for hit in hits]


def turned_dot(rows, table):
    return lax.dot_general(rows, table, (((0,), (0,)), ((), ())), preferred_element_type=F32)


def spread_taps(par, table):
    both = turned_dot(par, table)
    return [both[:, tap * 128 : (tap + 1) * 128] for tap in range(KERNEL)]


def halo_terms(halo, par, not_fresh0):
    x = [halo[4 * k : 4 * k + 4].astype(F32) * not_fresh0 for k in range(3)]
    w = [par[4 * k : 4 * k + 4] for k in range(3)]
    terms = jnp.concatenate(
        [w[0] * x[0] + w[1] * x[1] + w[2] * x[2], w[0] * x[1] + w[1] * x[2], w[0] * x[2]], axis=0
    )
    high = terms.astype(BF16).astype(F32)
    middle = (terms - high).astype(BF16).astype(F32)
    parts = [high, middle, terms - high - middle, jnp.zeros((12, 128), F32)]
    return jnp.concatenate(parts, axis=0).astype(BF16)


def convolve(raw, before, terms, taps, masks):
    lane = iota((1, TILE), 1)
    cur = raw.astype(F32)
    total = taps[KERNEL - 1] * cur
    if terms is not None:
        total = total + terms
    for back in range(1, KERNEL):
        moved = cur if before is None else jnp.where(lane >= TILE - back, before, cur)
        total = total + taps[KERNEL - 1 - back] * (pltpu.roll(moved, back, 1) * masks[back - 1])
    return (total / (1.0 + jnp.exp(-total))).astype(BF16)


def conv_masks(cut0, cut1):
    lane = iota((1, TILE), 1)
    masks = []
    for back in range(1, KERNEL):
        gone = ((lane < back) & cut0) | ((lane >= SPAN) & (lane < SPAN + back) & cut1)
        masks.append(jnp.where(gone, 0.0, 1.0))
    return masks


def row_prep(dec, beta, alog, dtb):
    lane = iota(dec.shape, 1)
    x = dec + dtb
    decay = -jnp.exp(alog) * (jnp.maximum(x, 0.0) + jnp.log1p(jnp.exp(-jnp.abs(x))))
    cum = decay
    for shift in (1, 2, 4, 8, 16, 32):
        cum = cum + jnp.where((lane & (SPAN - 1)) >= shift, pltpu.roll(cum, shift, 1), 0.0)
    strength = 1.0 / (1.0 + jnp.exp(-beta))
    grown = jnp.exp(cum)
    close0, close1 = cum[:, SPAN - 1 : SPAN], cum[:, TILE - 1 :]
    fade = jnp.exp(jnp.where(lane < SPAN, close0, close1) - cum)
    keep0 = jnp.exp(jnp.broadcast_to(close0, cum.shape))
    keep1 = jnp.exp(jnp.broadcast_to(close1, cum.shape))
    return cum, strength, grown, fade, keep0, keep1


def unit_inverses(systems):
    shape = (SPAN, RATIO * TILE)
    row, col = iota(shape, 0), iota(shape, 1) & (SPAN - 1)
    near = (row >> 4) == (col >> 4)
    eye = jnp.where(row == col, 1.0, 0.0)
    masks = halves((SPAN, TILE))

    def low(arrays):
        return [a.astype(BF16) for a in arrays]

    def stack(pair):
        return jnp.concatenate(pair, axis=0)

    total = [jnp.where(near, eye - a, 0.0) for a in systems]
    power = low([jnp.where(near, -a, 0.0) for a in systems])
    power = low([block_dot(p, p, masks) for p in power])
    for _ in range(2):
        both = [block_dot(stack([t, p]), p, masks) for t, p in zip(low(total), power)]
        total = [t + b[:SPAN] for t, b in zip(total, both)]
        power = low([b[SPAN:] for b in both])
    total = [t + block_dot(l, p, masks) for t, l, p in zip(total, low(total), power)]
    small = low(total)
    rest = low([jnp.where(near, 0.0, a) for a in systems])
    cross = low([block_dot(t, r, masks) for t, r in zip(small, rest)])
    total = [t - block_dot(x, l, masks) for t, x, l in zip(total, cross, small)]
    small = low(total)
    solved = []
    for a, x in zip(systems, small):
        wide = x.astype(F32)
        parts = block_dot(stack(split(a)), x, masks)
        miss = eye - wide - (parts[:SPAN] + parts[SPAN:])
        solved.append((wide + block_dot(x, miss.astype(BF16), masks)).astype(BF16))
    return solved


def both_blocks(square):
    none = jnp.zeros((SPAN, square.shape[1]), square.dtype)
    first = jnp.concatenate([square[:SPAN], none], axis=0)
    return jnp.concatenate([first, jnp.concatenate([none, square[SPAN:]], axis=0)], axis=1)


def unit_keys(convolved):
    wide = convolved.astype(F32)
    return (wide * lax.rsqrt(jnp.sum(wide * wide, axis=0, keepdims=True) + EPSILON)).astype(BF16)


def solve_tiles(keys, queries, prep):
    cum, strength, grown, fade, keep0, keep1 = prep
    row, lane = iota((SPAN, TILE), 0), iota((SPAN, TILE), 1)
    early = lane < SPAN
    seen = (lane & (SPAN - 1)) >= row
    later = (lane & (SPAN - 1)) > row
    columns = jnp.transpose(jnp.concatenate([cum, fade], axis=0))
    count = cum.shape[0]

    def beside(tall):
        return jnp.where(early, tall[:SPAN], tall[SPAN:])

    systems, faded, scores = [], [], []
    for t, k in enumerate(keys):
        turned = jnp.transpose(k.astype(F32))
        if queries is None:
            gram = beside(dot(turned.astype(BF16), k))
        else:
            prod = dot(turned.astype(BF16), jnp.concatenate([k, queries[t]], axis=1))
            gram, touch = beside(prod[:, :TILE]), beside(prod[:, TILE:])
        pair = []
        for r in range(RATIO):
            at = t * RATIO + r
            diff = cum[at : at + 1] - beside(columns[:, at : at + 1])
            ratio = jnp.where(seen, jnp.exp(jnp.where(seen, diff, 0.0)), 0.0)
            pair.append(jnp.where(later, strength[at : at + 1] * gram * ratio, 0.0))
            if queries is not None:
                scores.append((touch * ratio).astype(BF16))
            faded.append((turned * columns[:, count + at : count + at + 1]).astype(BF16))
        systems.append(jnp.concatenate(pair, axis=1))
    return unit_inverses(systems), faded, scores


def token_prep_kernel(req, me, mixed, dec, beta, halo, par_lines, wk, wv, sc, ft, qo, rows):
    fresh0, fresh1 = is_fresh(req, me[0] * 2), is_fresh(req, me[0] * 2 + 1)
    not_fresh0 = jnp.where(fresh0, 0.0, 1.0)
    masks = conv_masks(True, fresh1)
    tap_tab, halo_tab = tap_tables(), halo_tables()
    tiles = range(mixed.shape[0])
    par = [parameters(par_lines[t]) for t in tiles]

    def gather(pick):
        return jnp.concatenate([pick(t) for t in tiles], axis=0)

    prep = row_prep(
        gather(lambda t: dec[t].astype(F32)),
        gather(lambda t: beta[t].astype(F32)),
        jnp.concatenate([p[1] for p in par], axis=0),
        jnp.concatenate([p[2] for p in par], axis=0),
    )
    cum, strength, grown, fade, keep0, keep1 = prep
    keys, queries, values = [], [], []
    for t in tiles:
        terms = halo_terms(halo[t], par[t][0], not_fresh0)
        lines = par_lines[t, :16]
        q, k, v0, v1 = [
            convolve(
                mixed[t, c * 128 : (c + 1) * 128],
                None,
                turned_dot(terms, halo_tab[c]),
                spread_taps(lines, tap_tab[c]),
                masks,
            )
            for c in range(4)
        ]
        keys.append(unit_keys(k))
        queries.append(q)
        values.append((v0, v1))
        qo[t] = q
        rows[t] = jnp.concatenate(
            [keep0[2 * t : 2 * t + 2], grown[2 * t : 2 * t + 2], keep1[2 * t : 2 * t + 2], strength[2 * t : 2 * t + 2]],
            axis=0,
        )
    solved, faded, scores = solve_tiles(keys, queries, prep)
    sides = halves((SPAN, TILE))
    for t in tiles:
        stacks = []
        for r in range(RATIO):
            at = t * RATIO + r
            s, lift = strength[at : at + 1], strength[at : at + 1] * grown[at : at + 1]
            stacked = jnp.concatenate(
                [lift * keys[t].astype(F32), s * values[t][r].astype(F32)], axis=0
            )
            stacks.append(stacked.astype(BF16))
            sc[t, :, r * TILE : (r + 1) * TILE] = scores[at]
            ft[at] = faded[at]
        out = block_dot(jnp.concatenate(stacks, axis=1), solved[t], sides).astype(BF16)
        for r in range(RATIO):
            wk[t * RATIO + r] = out[:DK, r * TILE : (r + 1) * TILE]
            wv[t * RATIO + r] = out[DK:, r * TILE : (r + 1) * TILE]


def token_prep(req, me, mixed, dec, beta, halo, par):
    heads = mixed.shape[0]
    smem = pl.BlockSpec(memory_space=pltpu.SMEM)

    def tiles(count, *rest):
        return pl.BlockSpec((count,) + rest, lambda g: (g,) + (0,) * len(rest))

    square = jax.ShapeDtypeStruct((heads * RATIO, 128, 128), BF16)
    return pl.pallas_call(
        token_prep_kernel,
        grid=(heads // WIDE,),
        in_specs=[
            smem,
            smem,
            tiles(WIDE, 512, TILE),
            tiles(WIDE, RATIO, TILE),
            tiles(WIDE, RATIO, TILE),
            tiles(WIDE, 16, TILE),
            pl.BlockSpec((WIDE, 32, 128), lambda g: (g, 4, 0)),
        ],
        out_specs=[tiles(WIDE * RATIO, 128, 128)] * 2
        + [tiles(WIDE, SPAN, RATIO * TILE), tiles(WIDE * RATIO, 128, 128)]
        + [tiles(WIDE, 128, 128), tiles(WIDE, 8, 128)],
        out_shape=[square] * 2
        + [
            jax.ShapeDtypeStruct((heads, SPAN, RATIO * TILE), BF16),
            square,
            jax.ShapeDtypeStruct((heads, 128, 128), BF16),
            jax.ShapeDtypeStruct((heads, 8, 128), F32),
        ],
        compiler_params=params(),
        cost_estimate=pl.CostEstimate(flops=10**10, bytes_accessed=8 << 20, transcendentals=10**6),
        name="token_prep",
    )(req, me, mixed, dec, beta, halo, par)


def head_prep_kernel(req, kp, previous, par_lines, sol, ft, gs, rows):
    step = pl.program_id(0)
    depth, own = kp.shape[0], kp.shape[1]
    tap_tab = tap_tables()
    order = [(d, h) for d in range(depth) for h in range(own)]
    par = [parameters(par_lines[h]) for h in range(own)]

    small = [kp[d, h, DK:].astype(F32) for d, h in order]
    prep = row_prep(
        jnp.concatenate([s[28:30] for s in small], axis=0),
        jnp.concatenate([s[30:32] for s in small], axis=0),
        jnp.concatenate([par[h][1] for d, h in order], axis=0),
        jnp.concatenate([par[h][2] for d, h in order], axis=0),
    )
    cum, strength, grown, fade, keep0, keep1 = prep
    keys = []
    taps = [spread_taps(par_lines[h, :16], tap_tab[1]) for h in range(own)]
    for d in range(depth):
        block = (step * depth + d) * 2
        masks = conv_masks(is_fresh(req, block), is_fresh(req, block + 1))
        for h in range(own):
            before = (kp[d - 1, h, :DK] if d else previous[0, h]).astype(F32)
            keys.append(unit_keys(convolve(kp[d, h, :DK], before, None, taps[h], masks)))
    solved, faded, unused = solve_tiles(keys, None, prep)
    sides = halves((SPAN, TILE))
    for t, (d, h) in enumerate(order):
        rows[d, h] = jnp.concatenate(
            [keep0[2 * t : 2 * t + 2], keep1[2 * t : 2 * t + 2], strength[2 * t : 2 * t + 2], strength[2 * t : 2 * t + 2]],
            axis=0,
        )
        scaled = []
        for r in range(RATIO):
            at = t * RATIO + r
            lift = strength[at : at + 1] * grown[at : at + 1]
            scaled.append((lift * keys[t].astype(F32)).astype(BF16))
        wide = block_dot(jnp.concatenate(scaled, axis=1), solved[t], sides).astype(BF16)
        sol[d, h] = solved[t]
        for r in range(RATIO):
            at = t * RATIO + r
            drop = dot(wide[:, r * TILE : (r + 1) * TILE], both_blocks(faded[at])).astype(BF16)
            gs[d, h, r, 0] = drop[:, :DK]
            gs[d, h, r, 1] = drop[:, DK:]
            ft[d, h, r] = faded[at]


def head_prep(req, kp, par):
    n, own = kp.shape[:2]
    depth = MOST // own
    smem = pl.BlockSpec(memory_space=pltpu.SMEM)

    def tiles(*rest):
        return pl.BlockSpec((depth, own) + rest, lambda g: (g, 0) + (0,) * len(rest))

    square = jax.ShapeDtypeStruct((n, own, RATIO, 128, 128), BF16)
    return pl.pallas_call(
        head_prep_kernel,
        grid=(n // depth,),
        in_specs=[
            smem,
            tiles(KROWS, TILE),
            pl.BlockSpec((1, own, DK, TILE), lambda g: (jnp.maximum(g * depth - 1, 0), 0, 0, 0)),
            pl.BlockSpec((own, 32, 128), lambda g: (0, 0, 0)),
        ],
        out_specs=[
            tiles(SPAN, RATIO * TILE),
            tiles(RATIO, 128, 128),
            tiles(RATIO, 2, 128, 128),
            tiles(8, 128),
        ],
        out_shape=[
            jax.ShapeDtypeStruct((n, own, SPAN, RATIO * TILE), BF16),
            square,
            jax.ShapeDtypeStruct((n, own, RATIO, 2, 128, 128), BF16),
            jax.ShapeDtypeStruct((n, own, 8, 128), F32),
        ],
        compiler_params=params(),
        cost_estimate=pl.CostEstimate(flops=10**10, bytes_accessed=6 << 20, transcendentals=10**6),
        name="head_prep",
    )(req, kp, kp, par)


def head_chain_kernel(req, me, par_lines, sol, ft, gs, rows, *refs):
    n = refs[-6].shape[0]
    arrived, (sin, ends, tails, state, vp, spread) = refs[:n], refs[n:]
    step = pl.program_id(0)
    depth, own = sol.shape[0], sol.shape[1]

    @pl.when(step == 0)
    def first():
        for k, one in enumerate(arrived):
            vp[me[0] ^ k] = one[...]
            tails[me[0] ^ k] = one[:, 256:]
        tap_tab = tap_tables()
        for h in range(own):
            for r in range(RATIO):
                for tap, wide in enumerate(spread_taps(par_lines[h, :16], tap_tab[2 + r])):
                    spread[h * RATIO + r, tap] = wide

    sides = halves((SPAN, TILE))
    heads = [(h, r) for h in range(own) for r in range(RATIO)]
    taps = [[spread[v, tap] for tap in range(KERNEL)] for v in range(len(heads))]
    current = [state[v] for v in range(len(heads))]
    for d in range(depth):
        tile = step * depth + d
        past = jnp.maximum(tile - 1, 0)
        fresh = [is_fresh(req, tile * 2), is_fresh(req, tile * 2 + 1)]
        masks = conv_masks(fresh[0], fresh[1])
        gains = []
        for h in range(own):
            scaled = []
            for r in range(RATIO):
                raw = vp[tile, h, r * DV : (r + 1) * DV]
                before = vp[past, h, r * DV : (r + 1) * DV].astype(F32)
                value = convolve(raw, before, None, taps[h * RATIO + r], masks)
                scaled.append((rows[d, h, 4 + r : 5 + r] * value.astype(F32)).astype(BF16))
            wide = block_dot(jnp.concatenate(scaled, axis=1), sol[d, h], sides).astype(BF16)
            for r in range(RATIO):
                gains.append(dot(wide[:, r * TILE : (r + 1) * TILE], both_blocks(ft[d, h, r])))
        for half in range(2):
            for h in range(own):
                now = [jnp.where(fresh[half], 0.0, current[h * RATIO + r]) for r in range(RATIO)]
                lost = dot(
                    jnp.concatenate([x.astype(BF16) for x in now], axis=1),
                    corner(gs[d, h, 0, half], gs[d, h, 1, half]),
                )
                for r in range(RATIO):
                    v = h * RATIO + r
                    keep = rows[d, h, 2 * half + r : 2 * half + r + 1]
                    gain = gains[v][:, half * DV : (half + 1) * DV]
                    current[v] = keep * now[r] + (gain - lost[:, r * TILE : (r + 1) * TILE])
                    ends[d * 2 + half, v] = current[v].astype(BF16)
        onward = lax.rem(tile + 1, n)
        for v in range(len(heads)):
            sin[onward, v] = current[v].astype(BF16)
    for v in range(len(heads)):
        state[v] = current[v]


def head_chain(req, me, par, sol, ft, gs, rows, arrived):
    n, own = sol.shape[:2]
    depth = WIDE // own
    smem = pl.BlockSpec(memory_space=pltpu.SMEM)

    def tiles(*rest):
        return pl.BlockSpec((depth, own) + rest, lambda g: (g, 0) + (0,) * len(rest))

    return pl.pallas_call(
        head_chain_kernel,
        grid=(n // depth,),
        in_specs=[
            smem,
            smem,
            pl.BlockSpec((own, 32, 128), lambda g: (0, 0, 0)),
            tiles(SPAN, RATIO * TILE),
            tiles(RATIO, 128, 128),
            tiles(RATIO, 2, 128, 128),
            tiles(8, 128),
        ]
        + [pl.BlockSpec((own, VROWS, TILE), lambda g: (0, 0, 0))] * n,
        out_specs=[
            pl.BlockSpec((n, own * RATIO, 128, 128), lambda g: (0, 0, 0, 0)),
            pl.BlockSpec((2 * depth, own * RATIO, 128, 128), lambda g: (g, 0, 0, 0)),
            pl.BlockSpec((n, own, 32, TILE), lambda g: (0, 0, 0, 0)),
        ],
        out_shape=[
            jax.ShapeDtypeStruct((n, own * RATIO, 128, 128), BF16),
            jax.ShapeDtypeStruct((2 * n, own * RATIO, 128, 128), BF16),
            jax.ShapeDtypeStruct((n, own, 32, TILE), BF16),
        ],
        scratch_shapes=[
            pltpu.VMEM((own * RATIO, 128, 128), F32),
            pltpu.VMEM((n, own, VROWS, TILE), BF16),
            pltpu.VMEM((own * RATIO, KERNEL, 128, 128), F32),
        ],
        compiler_params=params(),
        cost_estimate=pl.CostEstimate(flops=3 * 10**9, bytes_accessed=8 << 20, transcendentals=10**6),
        name="head_chain",
    )(req, me, par, sol, ft, gs, rows, *arrived)


def choose_kernel(req, rep, fin, me, ends, kt, *refs):
    outs, counts = refs[:-1], refs[-1]
    own, heads = kt.shape[1], ends.shape[1]
    base = heads * 128
    for i, out in enumerate(outs):
        out[...] = jnp.zeros_like(out)
        counts[i] = 0
    end = jnp.int32(-1)
    for j in range(req.shape[1]):
        end = end + req[0, j]
        where = rep[0, j] ^ me[0]
        place = jnp.minimum(counts[where], CAP - 1)
        done = fin[0, j] > 0
        counts[where] = counts[where] + jnp.where(done, 1, 0)
        for i, out in enumerate(outs):

            @pl.when(done & (where == i))
            def take():
                for v in range(heads):
                    out[place, v * 128 : (v + 1) * 128] = ends[end, v]
                for h in range(own):
                    lines = kt[end >> 1, h].astype(F32)
                    lines = jnp.where((end & 1) > 0, lines[16:], lines[:16]).astype(BF16)
                    out[place, base + h * 16 : base + h * 16 + 16] = lines

    for i, out in enumerate(outs):
        number = jnp.full((16, 128), counts[i], jnp.int32).astype(F32).astype(BF16)
        for c in range(CAP):
            out[c, base + own * 16 :] = number


def choose(req, rep, fin, me, ends, tails, replicas):
    own = tails.shape[1]
    smem = pl.BlockSpec(memory_space=pltpu.SMEM)
    lines = own * RATIO * 128 + own * 16 + 16
    return pl.pallas_call(
        choose_kernel,
        grid=(1,),
        in_specs=[
            smem,
            smem,
            smem,
            smem,
            pl.BlockSpec(ends.shape, lambda g: (0, 0, 0, 0)),
            pl.BlockSpec(tails.shape, lambda g: (0, 0, 0, 0)),
        ],
        out_specs=[pl.BlockSpec((CAP, lines, 128), lambda g: (0, 0, 0))] * replicas,
        out_shape=[jax.ShapeDtypeStruct((CAP, lines, 128), BF16)] * replicas,
        scratch_shapes=[pltpu.SMEM((replicas,), jnp.int32)],
        compiler_params=params(),
        cost_estimate=pl.CostEstimate(flops=10**6, bytes_accessed=4 << 20, transcendentals=0),
        name="choose",
    )(req, rep, fin, me, ends, tails)


def token_out_kernel(req, me, sin, wk, wv, sc, ft, qs, rows, gate, norm_gain, out):
    gain = jnp.transpose(jnp.broadcast_to(norm_gain[...], (TILE, DV)))
    stay0 = jnp.where(is_fresh(req, me[0] * 2), 0.0, 1.0)
    stay1 = jnp.where(is_fresh(req, me[0] * 2 + 1), 0.0, 1.0)
    lane = iota((DV, TILE), 1)
    early = lane < SPAN
    sides = halves((SPAN, TILE))
    units = [(t, r) for t in range(qs.shape[0]) for r in range(RATIO)]
    both = [jnp.concatenate([wk[t * RATIO + r], qs[t]], axis=1) for t, r in units]
    enter = [sin[t * RATIO + r].astype(F32) * stay0 for t, r in units]
    first = [dot(e.astype(BF16), b) for e, b in zip(enter, both)]
    wide = [wv[t * RATIO + r].astype(F32) for t, r in units]
    new0 = [jnp.where(early, w - f[:, :TILE], 0.0) for w, f in zip(wide, first)]
    tiles = range(qs.shape[0])
    pairs = [
        dot(
            jnp.concatenate([new0[2 * t].astype(BF16), new0[2 * t + 1].astype(BF16)], axis=1),
            corner(ft[2 * t], ft[2 * t + 1]),
        )
        for t in tiles
    ]
    middle = [
        (rows[t, r : r + 1] * e + pairs[t][:, r * TILE : (r + 1) * TILE]) * stay1
        for (t, r), e in zip(units, enter)
    ]
    second = [dot(m.astype(BF16), b) for m, b in zip(middle, both)]
    new = [
        jnp.where(early, x, w - s[:, :TILE]).astype(BF16) for x, w, s in zip(new0, wide, second)
    ]
    near = [
        block_dot(jnp.concatenate([new[2 * t], new[2 * t + 1]], axis=1), sc[t], sides) for t in tiles
    ]
    for at, (t, r) in enumerate(units):
        core = rows[t, 2 + r : 3 + r] * jnp.where(early, first[at][:, TILE:], second[at][:, TILE:])
        core = (core + near[t][:, r * TILE : (r + 1) * TILE]).astype(BF16).astype(F32)
        inverse_rms = lax.rsqrt(jnp.mean(core * core, axis=0, keepdims=True) + EPSILON)
        z = gate[t, r * DV : (r + 1) * DV].astype(F32)
        result = core * inverse_rms * gain * (z / (1.0 + jnp.exp(-z)))
        out[t, r * DV : (r + 1) * DV] = result.astype(BF16)


def token_out(req, me, sin, wk, wv, sc, ft, qs, rows, gate, gain):
    heads = qs.shape[0]
    smem = pl.BlockSpec(memory_space=pltpu.SMEM)

    def tiles(count, *rest):
        return pl.BlockSpec((count,) + rest, lambda g: (g,) + (0,) * len(rest))

    return pl.pallas_call(
        token_out_kernel,
        grid=(heads // WIDE,),
        in_specs=[smem, smem]
        + [tiles(WIDE * RATIO, 128, 128)] * 3
        + [tiles(WIDE, SPAN, RATIO * TILE), tiles(WIDE * RATIO, 128, 128)]
        + [
            tiles(WIDE, 128, 128),
            tiles(WIDE, 8, 128),
            tiles(WIDE, 256, TILE),
            pl.BlockSpec((1, 128), lambda g: (0, 0)),
        ],
        out_specs=tiles(WIDE, 256, TILE),
        out_shape=jax.ShapeDtypeStruct((heads, 256, TILE), BF16),
        compiler_params=params(ALL_VMEM),
        cost_estimate=pl.CostEstimate(flops=10**9, bytes_accessed=8 << 20, transcendentals=10**6),
        name="token_out",
    )(req, me, sin, wk, wv, sc, ft, qs, rows, gate, gain)


def land_kernel(me, *refs):
    got, (states, tails, counts) = refs[:-3], refs[-3:]
    slot = pl.program_id(0)
    heads, own = states.shape[1], tails.shape[2]
    base = heads * 128

    @pl.when(slot == 0)
    def first():
        for i, one in enumerate(got):
            number = jnp.max(one[0, base + own * 16 :].astype(F32))
            counts[i] = number.astype(jnp.int32)

    start = jnp.int32(0)
    source, place = jnp.int32(-1), jnp.int32(0)
    for p in range(len(got)):
        away = me[0] ^ p
        number = counts[away]
        inside = (slot >= start) & (slot < start + number)
        source = jnp.where(inside, away, source)
        place = jnp.where(inside, slot - start, place)
        start = start + number
    place = jnp.clip(place, 0, CAP - 1)
    for i, one in enumerate(got):

        @pl.when(source == i)
        def take():
            for v in range(heads):
                states[0, v] = jnp.transpose(one[place, v * 128 : (v + 1) * 128]).astype(F32)
            lines = [one[place, base + h * 16 : base + h * 16 + 16].astype(F32) for h in range(own)]
            for k in range(KERNEL - 1):
                row = [
                    jnp.concatenate([x[4 * k + cg : 4 * k + cg + 1] for cg in range(4)], axis=1)
                    for x in lines
                ]
                tails[0, k] = jnp.concatenate(row, axis=0).astype(BF16)

    @pl.when(source < 0)
    def clear():
        states[...] = jnp.zeros_like(states)
        tails[...] = jnp.zeros_like(tails)


def land(me, got, heads, own):
    lines = got[0].shape[1]
    slots = len(got) * CAP
    smem = pl.BlockSpec(memory_space=pltpu.SMEM)
    return pl.pallas_call(
        land_kernel,
        grid=(slots,),
        in_specs=[smem] + [pl.BlockSpec((CAP, lines, 128), lambda g: (0, 0, 0))] * len(got),
        out_specs=[
            pl.BlockSpec((1, heads, 128, 128), lambda g: (g, 0, 0, 0)),
            pl.BlockSpec((1, KERNEL - 1, own, 512), lambda g: (g, 0, 0, 0)),
        ],
        out_shape=[
            jax.ShapeDtypeStruct((slots, heads, 128, 128), F32),
            jax.ShapeDtypeStruct((slots, KERNEL - 1, own, 512), BF16),
        ],
        scratch_shapes=[pltpu.SMEM((len(got),), jnp.int32)],
        compiler_params=params(ALL_VMEM),
        cost_estimate=pl.CostEstimate(flops=10**6, bytes_accessed=4 << 20, transcendentals=0),
        name="land",
    )(me, *got)


def exchange(parts, axis):
    count = len(parts)
    got = {0: parts[0]}
    for k in range(count - 1, 0, -1):
        got[k] = lax.ppermute(parts[k], axis, [(i, i ^ k) for i in range(count)])
    return [got[k] for k in range(count)]


def body(
    mixed,
    decay_in,
    beta_in,
    gate_z,
    conv_weight,
    a_log,
    dt_bias,
    norm_gain,
    req_blocks,
    replica_of,
    finished,
):
    n = lax.axis_size("seq")
    replicas = lax.axis_size("rep")
    heads = mixed.shape[1]
    own = heads // n
    me = lax.axis_index("seq").astype(jnp.int32).reshape(1)
    kpack, par = pack_keys(mixed[0], decay_in[0], beta_in[0], conv_weight, a_log, dt_bias)
    halo, *vpack = pack_values(me, mixed[0], n)
    kp = lax.all_to_all(kpack.reshape(n, own, KROWS, TILE), "seq", 0, 0, tiled=True)
    halo = lax.ppermute(halo, "seq", [(i, i + 1) for i in range(n - 1)])
    vp = exchange(vpack, "seq")
    hsol, hft, hgs, hrows = head_prep(req_blocks, kp, par)
    sin, ends, ktails = head_chain(req_blocks, me, par, hsol, hft, hgs, hrows, vp)
    sin, halo = lax.optimization_barrier((sin, halo))
    sin = lax.all_to_all(sin, "seq", 0, 0, tiled=True)
    wk, wv, sc, ft, qs, rows = token_prep(
        req_blocks, me, mixed[0], decay_in[0], beta_in[0], halo, kp.reshape(heads, KROWS, TILE)
    )
    my_rep = lax.axis_index("rep").astype(jnp.int32).reshape(1)
    send = choose(req_blocks, replica_of, finished, my_rep, ends, ktails, replicas)
    got = exchange(send, "rep")
    states, tails = land(my_rep, got, own * RATIO, own)
    out = token_out(
        req_blocks,
        me,
        sin.reshape(heads * RATIO, 128, 128),
        wk,
        wv,
        sc,
        ft,
        qs,
        rows,
        gate_z[0],
        norm_gain.reshape(1, DV),
    )
    return (out[None], states[None], tails[None])


def solution(mesh):
    placed = (
        P("rep", None, None, "seq"),
        P("rep", None, None, "seq"),
        P("rep", None, None, "seq"),
        P("rep", None, None, "seq"),
        P(None, "seq", None),
        P("seq"),
        P("seq"),
        P(),
        P("rep", None),
        P("rep", None),
        P("rep", None),
    )
    return jax.shard_map(
        body,
        mesh=mesh,
        in_specs=placed,
        out_specs=(
            P("rep", None, None, "seq"),
            P("rep", None, "seq", None, None),
            P("rep", None, None, "seq", None),
        ),
        check_vma=False,
    )
```

```python
import jax
import jax.numpy as jnp
from jax import lax
from jax.experimental import pallas as pl
from jax.experimental.pallas import tpu as pltpu
from jax.sharding import PartitionSpec as P

DK = 128
DV = 128
KERNEL = 4
SPAN = 64
CAP = 2
RATIO = 2
TILE = 2 * SPAN
KROWS = 160
VROWS = 288
WIDE = 8
MOST = 16
EPSILON = 1e-06
F32 = jnp.float32
BF16 = jnp.bfloat16
VMEM_LIMIT = 56 * 1024 * 1024
ALL_VMEM = 63 * 1024 * 1024
SOME_VMEM = 24 * 1024 * 1024


def params(limit=VMEM_LIMIT):
    return pltpu.CompilerParams(vmem_limit_bytes=limit)


def iota(shape, dim):
    return lax.broadcasted_iota(jnp.int32, shape, dim)


def dot(left, right):
    return jnp.dot(left, right, preferred_element_type=F32)


def split(wide):
    high = wide.astype(BF16)
    return high, (wide - high.astype(F32)).astype(BF16)


def halves(shape):
    first = iota(shape, len(shape) - 1) < SPAN
    return jnp.where(first, 1.0, 0.0).astype(BF16), jnp.where(first, 0.0, 1.0).astype(BF16)


def corner(first, second):
    none = jnp.zeros_like(first)
    top = jnp.concatenate([first, none], axis=1)
    return jnp.concatenate([top, jnp.concatenate([none, second], axis=1)], axis=0)


def diagonal(packed, masks):
    squares = []
    for r in range(RATIO):
        one = packed[:, r * TILE : (r + 1) * TILE]
        squares.append(jnp.concatenate([one * masks[0], one * masks[1]], axis=0))
    return corner(*squares)


def block_dot(left, right, masks):
    return dot(left, diagonal(right, masks))


def parameter_lines(h, cw, alog, dtb):
    taps = cw[:, h].astype(F32)
    rows = [taps[tap : tap + 1, cg * 128 : (cg + 1) * 128] for tap in range(KERNEL) for cg in range(4)]
    rest = jnp.concatenate(
        [jnp.full((1, 128), ref[h * RATIO + r], F32) for ref in (alog, dtb) for r in range(RATIO)], axis=0
    )
    parts = []
    for _ in range(3):
        part = rest.astype(BF16).astype(F32)
        rest = rest - part
        parts.append(part)
    return jnp.concatenate(rows + parts + [jnp.zeros((4, 128), F32)], axis=0)


def parameters(lines):
    wide = lines.astype(F32)
    rest = wide[16:20] + wide[20:24] + wide[24:28]
    return wide[:16], rest[:RATIO], rest[RATIO:]


def pack_keys_kernel(mixed, dec, beta, cw, alog, dtb, kout, pout):
    row = iota((32, TILE), 0)
    own = pout.shape[0]
    lines = [parameter_lines(h, cw, alog, dtb) for h in range(own)]
    for t in range(mixed.shape[0]):
        kout[t, :DK] = mixed[t]
        rest = lines[t % own]
        d, b = dec[t].astype(F32), beta[t].astype(F32)
        for r in range(RATIO):
            rest = jnp.where(row == 28 + r, d[r : r + 1], rest)
            rest = jnp.where(row == 30 + r, b[r : r + 1], rest)
        kout[t, DK:] = rest.astype(BF16)

    @pl.when(pl.program_id(0) == 0)
    def first():
        for h in range(own):
            pout[h] = lines[h].astype(BF16)


def pack_keys(mixed, dec, beta, cw, alog, dtb):
    heads = mixed.shape[0]
    own = cw.shape[1]
    step = heads // 2
    smem = pl.BlockSpec(memory_space=pltpu.SMEM)
    return pl.pallas_call(
        pack_keys_kernel,
        grid=(heads // step,),
        in_specs=[
            pl.BlockSpec((step, DK, TILE), lambda g: (g, 1, 0)),
            pl.BlockSpec((step, RATIO, TILE), lambda g: (g, 0, 0)),
            pl.BlockSpec((step, RATIO, TILE), lambda g: (g, 0, 0)),
            pl.BlockSpec((KERNEL, own, 512), lambda g: (0, 0, 0)),
            smem,
            smem,
        ],
        out_specs=[
            pl.BlockSpec((step, KROWS, TILE), lambda g: (g, 0, 0)),
            pl.BlockSpec((own, 32, 128), lambda g: (0, 0, 0)),
        ],
        out_shape=[
            jax.ShapeDtypeStruct((heads, KROWS, TILE), BF16),
            jax.ShapeDtypeStruct((own, 32, 128), BF16),
        ],
        compiler_params=params(),
        cost_estimate=pl.CostEstimate(flops=10**6, bytes_accessed=2 << 20, transcendentals=0),
        name="pack_keys",
    )(mixed, dec, beta, cw, alog, dtb)


def pack_values_kernel(me, mixed, hout, *outs):
    step = pl.program_id(0)
    own = outs[0].shape[0]
    row, tok = iota((TILE, 128), 1), iota((TILE, 128), 0)
    place = row & 15
    picks = []
    for cg in range(4):
        hit = (row < 32) & (place < 12) & ((place & 3) == cg)
        hit = hit & (tok == (row >> 4) * SPAN + 61 + (place >> 2))
        picks.append(jnp.where(hit, 1.0, 0.0).astype(BF16))
    all_tails = []
    for h in range(mixed.shape[0]):
        tails = dot(mixed[h, :128], picks[0])
        for cg in range(1, 4):
            tails = tails + dot(mixed[h, cg * 128 : (cg + 1) * 128], picks[cg])
        all_tails.append(jnp.transpose(tails)[:32].astype(BF16))
        hout[h] = all_tails[h][16:]
    for i, out in enumerate(outs):

        @pl.when((step == i // 4) & ((me[0] & 3) == 0))
        def put0():
            put(mixed, all_tails, out, (i & 3) ^ 0, own)

        @pl.when((step == i // 4) & ((me[0] & 3) == 1))
        def put1():
            put(mixed, all_tails, out, (i & 3) ^ 1, own)

        @pl.when((step == i // 4) & ((me[0] & 3) == 2))
        def put2():
            put(mixed, all_tails, out, (i & 3) ^ 2, own)

        @pl.when((step == i // 4) & ((me[0] & 3) == 3))
        def put3():
            put(mixed, all_tails, out, (i & 3) ^ 3, own)


def put(mixed, all_tails, out, place, own):
    for h in range(own):
        out[h, :256] = mixed[place * own + h, 2 * DK :]
        out[h, 256:] = all_tails[place * own + h]


def pack_values(me, mixed, n):
    heads = mixed.shape[0]
    own = heads // n
    return pl.pallas_call(
        pack_values_kernel,
        grid_spec=pltpu.PrefetchScalarGridSpec(
            num_scalar_prefetch=1,
            grid=(n // 4,),
            in_specs=[pl.BlockSpec((4 * own, 512, TILE), lambda g, me: ((me[0] >> 2) ^ g, 0, 0))],
            out_specs=[pl.BlockSpec((4 * own, 16, TILE), lambda g, me: ((me[0] >> 2) ^ g, 0, 0))]
            + [pl.BlockSpec((own, VROWS, TILE), lambda g, me: (0, 0, 0))] * n,
        ),
        out_shape=[jax.ShapeDtypeStruct((heads, 16, TILE), BF16)]
        + [jax.ShapeDtypeStruct((own, VROWS, TILE), BF16)] * n,
        compiler_params=params(),
        cost_estimate=pl.CostEstimate(flops=10**8, bytes_accessed=4 << 20, transcendentals=0),
        name="pack_values",
    )(me, mixed)


def is_fresh(req, block):
    start = jnp.int32(0)
    fresh = jnp.bool_(False)
    for j in range(req.shape[1]):
        fresh = fresh | (start == block)
        start = start + req[0, j]
    return fresh


def tap_tables():
    row, part = iota((16, 4 * 128), 0), iota((16, 4 * 128), 1) >> 7
    hits = [((row & 3) == cg) & ((row >> 2) == part) for cg in range(4)]
    return [jnp.where(hit, 1.0, 0.0).astype(BF16) for hit in hits]


def halo_tables():
    row, lane = iota((48, 128), 0), iota((48, 128), 1)
    token = (row >> 2) % 3
    hits = [((row & 3) == cg) & (row < 36) & (token == lane) for cg in range(4)]
    return [jnp.where(hit, 1.0, 0.0).astype(BF16) for hit in hits]


def turned_dot(rows, table):
    return lax.dot_general(rows, table, (((0,), (0,)), ((), ())), preferred_element_type=F32)


def spread_taps(par, table):
    both = turned_dot(par, table)
    return [both[:, tap * 128 : (tap + 1) * 128] for tap in range(KERNEL)]


def halo_terms(halo, par, not_fresh0):
    x = [halo[4 * k : 4 * k + 4].astype(F32) * not_fresh0 for k in range(3)]
    w = [par[4 * k : 4 * k + 4] for k in range(3)]
    terms = jnp.concatenate(
        [w[0] * x[0] + w[1] * x[1] + w[2] * x[2], w[0] * x[1] + w[1] * x[2], w[0] * x[2]], axis=0
    )
    high = terms.astype(BF16).astype(F32)
    middle = (terms - high).astype(BF16).astype(F32)
    parts = [high, middle, terms - high - middle, jnp.zeros((12, 128), F32)]
    return jnp.concatenate(parts, axis=0).astype(BF16)


def convolve(raw, before, terms, taps, masks):
    lane = iota((1, TILE), 1)
    cur = raw.astype(F32)
    total = taps[KERNEL - 1] * cur
    if terms is not None:
        total = total + terms
    for back in range(1, KERNEL):
        moved = cur if before is None else jnp.where(lane >= TILE - back, before, cur)
        total = total + taps[KERNEL - 1 - back] * (pltpu.roll(moved, back, 1) * masks[back - 1])
    return (total / (1.0 + jnp.exp(-total))).astype(BF16)


def conv_masks(cut0, cut1):
    lane = iota((1, TILE), 1)
    masks = []
    for back in range(1, KERNEL):
        gone = ((lane < back) & cut0) | ((lane >= SPAN) & (lane < SPAN + back) & cut1)
        masks.append(jnp.where(gone, 0.0, 1.0))
    return masks


def row_prep(dec, beta, alog, dtb):
    lane = iota(dec.shape, 1)
    x = dec + dtb
    decay = -jnp.exp(alog) * (jnp.maximum(x, 0.0) + jnp.log1p(jnp.exp(-jnp.abs(x))))
    cum = decay
    for shift in (1, 2, 4, 8, 16, 32):
        cum = cum + jnp.where((lane & (SPAN - 1)) >= shift, pltpu.roll(cum, shift, 1), 0.0)
    strength = 1.0 / (1.0 + jnp.exp(-beta))
    grown = jnp.exp(cum)
    close0, close1 = cum[:, SPAN - 1 : SPAN], cum[:, TILE - 1 :]
    fade = jnp.exp(jnp.where(lane < SPAN, close0, close1) - cum)
    keep0 = jnp.exp(jnp.broadcast_to(close0, cum.shape))
    keep1 = jnp.exp(jnp.broadcast_to(close1, cum.shape))
    return cum, strength, grown, fade, keep0, keep1


def unit_inverses(systems):
    shape = (SPAN, RATIO * TILE)
    row, col = iota(shape, 0), iota(shape, 1) & (SPAN - 1)
    near = (row >> 4) == (col >> 4)
    eye = jnp.where(row == col, 1.0, 0.0)
    masks = halves((SPAN, TILE))

    def low(arrays):
        return [a.astype(BF16) for a in arrays]

    def stack(pair):
        return jnp.concatenate(pair, axis=0)

    total = [jnp.where(near, eye - a, 0.0) for a in systems]
    power = low([jnp.where(near, -a, 0.0) for a in systems])
    power = low([block_dot(p, p, masks) for p in power])
    for _ in range(2):
        both = [block_dot(stack([t, p]), p, masks) for t, p in zip(low(total), power)]
        total = [t + b[:SPAN] for t, b in zip(total, both)]
        power = low([b[SPAN:] for b in both])
    total = [t + block_dot(l, p, masks) for t, l, p in zip(total, low(total), power)]
    small = low(total)
    rest = low([jnp.where(near, 0.0, a) for a in systems])
    cross = low([block_dot(t, r, masks) for t, r in zip(small, rest)])
    total = [t - block_dot(x, l, masks) for t, x, l in zip(total, cross, small)]
    small = low(total)
    solved = []
    for a, x in zip(systems, small):
        wide = x.astype(F32)
        parts = block_dot(stack(split(a)), x, masks)
        miss = eye - wide - (parts[:SPAN] + parts[SPAN:])
        solved.append((wide + block_dot(x, miss.astype(BF16), masks)).astype(BF16))
    return solved


def both_blocks(square):
    none = jnp.zeros((SPAN, square.shape[1]), square.dtype)
    first = jnp.concatenate([square[:SPAN], none], axis=0)
    return jnp.concatenate([first, jnp.concatenate([none, square[SPAN:]], axis=0)], axis=1)


def unit_keys(convolved):
    wide = convolved.astype(F32)
    return (wide * lax.rsqrt(jnp.sum(wide * wide, axis=0, keepdims=True) + EPSILON)).astype(BF16)


def solve_tiles(keys, queries, prep):
    cum, strength, grown, fade, keep0, keep1 = prep
    row, lane = iota((SPAN, TILE), 0), iota((SPAN, TILE), 1)
    early = lane < SPAN
    seen = (lane & (SPAN - 1)) >= row
    later = (lane & (SPAN - 1)) > row
    columns = jnp.transpose(jnp.concatenate([cum, fade], axis=0))
    count = cum.shape[0]

    def beside(tall):
        return jnp.where(early, tall[:SPAN], tall[SPAN:])

    systems, faded, scores = [], [], []
    for t, k in enumerate(keys):
        turned = jnp.transpose(k.astype(F32))
        if queries is None:
            gram = beside(dot(turned.astype(BF16), k))
        else:
            prod = dot(turned.astype(BF16), jnp.concatenate([k, queries[t]], axis=1))
            gram, touch = beside(prod[:, :TILE]), beside(prod[:, TILE:])
        pair = []
        for r in range(RATIO):
            at = t * RATIO + r
            diff = cum[at : at + 1] - beside(columns[:, at : at + 1])
            ratio = jnp.where(seen, jnp.exp(jnp.where(seen, diff, 0.0)), 0.0)
            pair.append(jnp.where(later, strength[at : at + 1] * gram * ratio, 0.0))
            if queries is not None:
                scores.append((touch * ratio).astype(BF16))
            faded.append((turned * columns[:, count + at : count + at + 1]).astype(BF16))
        systems.append(jnp.concatenate(pair, axis=1))
    return unit_inverses(systems), faded, scores


def token_prep_kernel(req, me, mixed, dec, beta, halo, par_lines, wk, wv, sc, ft, qo, rows):
    fresh0, fresh1 = is_fresh(req, me[0] * 2), is_fresh(req, me[0] * 2 + 1)
    not_fresh0 = jnp.where(fresh0, 0.0, 1.0)
    masks = conv_masks(True, fresh1)
    tap_tab, halo_tab = tap_tables(), halo_tables()
    tiles = range(mixed.shape[0])
    par = [parameters(par_lines[t]) for t in tiles]

    def gather(pick):
        return jnp.concatenate([pick(t) for t in tiles], axis=0)

    prep = row_prep(
        gather(lambda t: dec[t].astype(F32)),
        gather(lambda t: beta[t].astype(F32)),
        jnp.concatenate([p[1] for p in par], axis=0),
        jnp.concatenate([p[2] for p in par], axis=0),
    )
    cum, strength, grown, fade, keep0, keep1 = prep
    keys, queries, values = [], [], []
    for t in tiles:
        terms = halo_terms(halo[t], par[t][0], not_fresh0)
        lines = par_lines[t, :16]
        q, k, v0, v1 = [
            convolve(
                mixed[t, c * 128 : (c + 1) * 128],
                None,
                turned_dot(terms, halo_tab[c]),
                spread_taps(lines, tap_tab[c]),
                masks,
            )
            for c in range(4)
        ]
        keys.append(unit_keys(k))
        queries.append(q)
        values.append((v0, v1))
        qo[t] = q
        rows[t] = jnp.concatenate(
            [keep0[2 * t : 2 * t + 2], grown[2 * t : 2 * t + 2], keep1[2 * t : 2 * t + 2], strength[2 * t : 2 * t + 2]],
            axis=0,
        )
    solved, faded, scores = solve_tiles(keys, queries, prep)
    sides = halves((SPAN, TILE))
    for t in tiles:
        stacks = []
        for r in range(RATIO):
            at = t * RATIO + r
            s, lift = strength[at : at + 1], strength[at : at + 1] * grown[at : at + 1]
            stacked = jnp.concatenate(
                [lift * keys[t].astype(F32), s * values[t][r].astype(F32)], axis=0
            )
            stacks.append(stacked.astype(BF16))
            sc[t, :, r * TILE : (r + 1) * TILE] = scores[at]
            ft[at] = faded[at]
        out = block_dot(jnp.concatenate(stacks, axis=1), solved[t], sides).astype(BF16)
        for r in range(RATIO):
            wk[t * RATIO + r] = out[:DK, r * TILE : (r + 1) * TILE]
            wv[t * RATIO + r] = out[DK:, r * TILE : (r + 1) * TILE]


def token_prep(req, me, mixed, dec, beta, halo, par):
    heads = mixed.shape[0]
    smem = pl.BlockSpec(memory_space=pltpu.SMEM)

    def tiles(count, *rest):
        return pl.BlockSpec((count,) + rest, lambda g: (g,) + (0,) * len(rest))

    square = jax.ShapeDtypeStruct((heads * RATIO, 128, 128), BF16)
    return pl.pallas_call(
        token_prep_kernel,
        grid=(heads // WIDE,),
        in_specs=[
            smem,
            smem,
            tiles(WIDE, 512, TILE),
            tiles(WIDE, RATIO, TILE),
            tiles(WIDE, RATIO, TILE),
            tiles(WIDE, 16, TILE),
            pl.BlockSpec((WIDE, 32, 128), lambda g: (g, 4, 0)),
        ],
        out_specs=[tiles(WIDE * RATIO, 128, 128)] * 2
        + [tiles(WIDE, SPAN, RATIO * TILE), tiles(WIDE * RATIO, 128, 128)]
        + [tiles(WIDE, 128, 128), tiles(WIDE, 8, 128)],
        out_shape=[square] * 2
        + [
            jax.ShapeDtypeStruct((heads, SPAN, RATIO * TILE), BF16),
            square,
            jax.ShapeDtypeStruct((heads, 128, 128), BF16),
            jax.ShapeDtypeStruct((heads, 8, 128), F32),
        ],
        compiler_params=params(),
        cost_estimate=pl.CostEstimate(flops=10**10, bytes_accessed=8 << 20, transcendentals=10**6),
        name="token_prep",
    )(req, me, mixed, dec, beta, halo, par)


def head_prep_kernel(req, kp, previous, par_lines, sol, ft, gs, rows):
    step = pl.program_id(0)
    depth, own = kp.shape[0], kp.shape[1]
    tap_tab = tap_tables()
    order = [(d, h) for d in range(depth) for h in range(own)]
    par = [parameters(par_lines[h]) for h in range(own)]

    small = [kp[d, h, DK:].astype(F32) for d, h in order]
    prep = row_prep(
        jnp.concatenate([s[28:30] for s in small], axis=0),
        jnp.concatenate([s[30:32] for s in small], axis=0),
        jnp.concatenate([par[h][1] for d, h in order], axis=0),
        jnp.concatenate([par[h][2] for d, h in order], axis=0),
    )
    cum, strength, grown, fade, keep0, keep1 = prep
    keys = []
    taps = [spread_taps(par_lines[h, :16], tap_tab[1]) for h in range(own)]
    for d in range(depth):
        block = (step * depth + d) * 2
        masks = conv_masks(is_fresh(req, block), is_fresh(req, block + 1))
        for h in range(own):
            before = (kp[d - 1, h, :DK] if d else previous[0, h]).astype(F32)
            keys.append(unit_keys(convolve(kp[d, h, :DK], before, None, taps[h], masks)))
    solved, faded, unused = solve_tiles(keys, None, prep)
    sides = halves((SPAN, TILE))
    for t, (d, h) in enumerate(order):
        rows[d, h] = jnp.concatenate(
            [keep0[2 * t : 2 * t + 2], keep1[2 * t : 2 * t + 2], strength[2 * t : 2 * t + 2], strength[2 * t : 2 * t + 2]],
            axis=0,
        )
        scaled = []
        for r in range(RATIO):
            at = t * RATIO + r
            lift = strength[at : at + 1] * grown[at : at + 1]
            scaled.append((lift * keys[t].astype(F32)).astype(BF16))
        wide = block_dot(jnp.concatenate(scaled, axis=1), solved[t], sides).astype(BF16)
        sol[d, h] = solved[t]
        for r in range(RATIO):
            at = t * RATIO + r
            drop = dot(wide[:, r * TILE : (r + 1) * TILE], both_blocks(faded[at])).astype(BF16)
            gs[d, h, r, 0] = drop[:, :DK]
            gs[d, h, r, 1] = drop[:, DK:]
            ft[d, h, r] = faded[at]


def head_prep(req, kp, par):
    n, own = kp.shape[:2]
    depth = MOST // own
    smem = pl.BlockSpec(memory_space=pltpu.SMEM)

    def tiles(*rest):
        return pl.BlockSpec((depth, own) + rest, lambda g: (g, 0) + (0,) * len(rest))

    square = jax.ShapeDtypeStruct((n, own, RATIO, 128, 128), BF16)
    return pl.pallas_call(
        head_prep_kernel,
        grid=(n // depth,),
        in_specs=[
            smem,
            tiles(KROWS, TILE),
            pl.BlockSpec((1, own, DK, TILE), lambda g: (jnp.maximum(g * depth - 1, 0), 0, 0, 0)),
            pl.BlockSpec((own, 32, 128), lambda g: (0, 0, 0)),
        ],
        out_specs=[
            tiles(SPAN, RATIO * TILE),
            tiles(RATIO, 128, 128),
            tiles(RATIO, 2, 128, 128),
            tiles(8, 128),
        ],
        out_shape=[
            jax.ShapeDtypeStruct((n, own, SPAN, RATIO * TILE), BF16),
            square,
            jax.ShapeDtypeStruct((n, own, RATIO, 2, 128, 128), BF16),
            jax.ShapeDtypeStruct((n, own, 8, 128), F32),
        ],
        compiler_params=params(),
        cost_estimate=pl.CostEstimate(flops=10**10, bytes_accessed=6 << 20, transcendentals=10**6),
        name="head_prep",
    )(req, kp, kp, par)


def head_chain_kernel(req, me, par_lines, sol, ft, gs, rows, *refs):
    n = refs[-6].shape[0]
    arrived, (sin, ends, tails, state, vp, spread) = refs[:n], refs[n:]
    step = pl.program_id(0)
    depth, own = sol.shape[0], sol.shape[1]

    @pl.when(step == 0)
    def first():
        for k, one in enumerate(arrived):
            vp[me[0] ^ k] = one[...]
            tails[me[0] ^ k] = one[:, 256:]
        tap_tab = tap_tables()
        for h in range(own):
            for r in range(RATIO):
                for tap, wide in enumerate(spread_taps(par_lines[h, :16], tap_tab[2 + r])):
                    spread[h * RATIO + r, tap] = wide

    sides = halves((SPAN, TILE))
    heads = [(h, r) for h in range(own) for r in range(RATIO)]
    taps = [[spread[v, tap] for tap in range(KERNEL)] for v in range(len(heads))]
    current = [state[v] for v in range(len(heads))]
    for d in range(depth):
        tile = step * depth + d
        past = jnp.maximum(tile - 1, 0)
        fresh = [is_fresh(req, tile * 2), is_fresh(req, tile * 2 + 1)]
        masks = conv_masks(fresh[0], fresh[1])
        gains = []
        for h in range(own):
            scaled = []
            for r in range(RATIO):
                raw = vp[tile, h, r * DV : (r + 1) * DV]
                before = vp[past, h, r * DV : (r + 1) * DV].astype(F32)
                value = convolve(raw, before, None, taps[h * RATIO + r], masks)
                scaled.append((rows[d, h, 4 + r : 5 + r] * value.astype(F32)).astype(BF16))
            wide = block_dot(jnp.concatenate(scaled, axis=1), sol[d, h], sides).astype(BF16)
            for r in range(RATIO):
                gains.append(dot(wide[:, r * TILE : (r + 1) * TILE], both_blocks(ft[d, h, r])))
        for half in range(2):
            for h in range(own):
                now = [jnp.where(fresh[half], 0.0, current[h * RATIO + r]) for r in range(RATIO)]
                lost = dot(
                    jnp.concatenate([x.astype(BF16) for x in now], axis=1),
                    corner(gs[d, h, 0, half], gs[d, h, 1, half]),
                )
                for r in range(RATIO):
                    v = h * RATIO + r
                    keep = rows[d, h, 2 * half + r : 2 * half + r + 1]
                    gain = gains[v][:, half * DV : (half + 1) * DV]
                    current[v] = keep * now[r] + (gain - lost[:, r * TILE : (r + 1) * TILE])
                    ends[d * 2 + half, v] = current[v].astype(BF16)
        onward = lax.rem(tile + 1, n)
        for v in range(len(heads)):
            sin[onward, v] = current[v].astype(BF16)
    for v in range(len(heads)):
        state[v] = current[v]


def head_chain(req, me, par, sol, ft, gs, rows, arrived):
    n, own = sol.shape[:2]
    depth = WIDE // own
    smem = pl.BlockSpec(memory_space=pltpu.SMEM)

    def tiles(*rest):
        return pl.BlockSpec((depth, own) + rest, lambda g: (g, 0) + (0,) * len(rest))

    return pl.pallas_call(
        head_chain_kernel,
        grid=(n // depth,),
        in_specs=[
            smem,
            smem,
            pl.BlockSpec((own, 32, 128), lambda g: (0, 0, 0)),
            tiles(SPAN, RATIO * TILE),
            tiles(RATIO, 128, 128),
            tiles(RATIO, 2, 128, 128),
            tiles(8, 128),
        ]
        + [pl.BlockSpec((own, VROWS, TILE), lambda g: (0, 0, 0))] * n,
        out_specs=[
            pl.BlockSpec((n, own * RATIO, 128, 128), lambda g: (0, 0, 0, 0)),
            pl.BlockSpec((2 * depth, own * RATIO, 128, 128), lambda g: (g, 0, 0, 0)),
            pl.BlockSpec((n, own, 32, TILE), lambda g: (0, 0, 0, 0)),
        ],
        out_shape=[
            jax.ShapeDtypeStruct((n, own * RATIO, 128, 128), BF16),
            jax.ShapeDtypeStruct((2 * n, own * RATIO, 128, 128), BF16),
            jax.ShapeDtypeStruct((n, own, 32, TILE), BF16),
        ],
        scratch_shapes=[
            pltpu.VMEM((own * RATIO, 128, 128), F32),
            pltpu.VMEM((n, own, VROWS, TILE), BF16),
            pltpu.VMEM((own * RATIO, KERNEL, 128, 128), F32),
        ],
        compiler_params=params(SOME_VMEM),
        cost_estimate=pl.CostEstimate(flops=3 * 10**9, bytes_accessed=8 << 20, transcendentals=10**6),
        name="head_chain",
    )(req, me, par, sol, ft, gs, rows, *arrived)


def choose_kernel(req, rep, fin, me, ends, kt, *refs):
    outs, counts = refs[:-1], refs[-1]
    own, heads = kt.shape[1], ends.shape[1]
    base = heads * 128
    for i, out in enumerate(outs):
        out[...] = jnp.zeros_like(out)
        counts[i] = 0
    end = jnp.int32(-1)
    for j in range(req.shape[1]):
        end = end + req[0, j]
        where = rep[0, j] ^ me[0]
        place = jnp.minimum(counts[where], CAP - 1)
        done = fin[0, j] > 0
        counts[where] = counts[where] + jnp.where(done, 1, 0)
        for i, out in enumerate(outs):

            @pl.when(done & (where == i))
            def take():
                for v in range(heads):
                    out[place, v * 128 : (v + 1) * 128] = ends[end, v]
                for h in range(own):
                    lines = kt[end >> 1, h].astype(F32)
                    lines = jnp.where((end & 1) > 0, lines[16:], lines[:16]).astype(BF16)
                    out[place, base + h * 16 : base + h * 16 + 16] = lines

    for i, out in enumerate(outs):
        number = jnp.full((16, 128), counts[i], jnp.int32).astype(F32).astype(BF16)
        for c in range(CAP):
            out[c, base + own * 16 :] = number


def choose(req, rep, fin, me, ends, tails, replicas):
    own = tails.shape[1]
    smem = pl.BlockSpec(memory_space=pltpu.SMEM)
    lines = own * RATIO * 128 + own * 16 + 16
    return pl.pallas_call(
        choose_kernel,
        grid=(1,),
        in_specs=[
            smem,
            smem,
            smem,
            smem,
            pl.BlockSpec(ends.shape, lambda g: (0, 0, 0, 0)),
            pl.BlockSpec(tails.shape, lambda g: (0, 0, 0, 0)),
        ],
        out_specs=[pl.BlockSpec((CAP, lines, 128), lambda g: (0, 0, 0))] * replicas,
        out_shape=[jax.ShapeDtypeStruct((CAP, lines, 128), BF16)] * replicas,
        scratch_shapes=[pltpu.SMEM((replicas,), jnp.int32)],
        compiler_params=params(),
        cost_estimate=pl.CostEstimate(flops=10**6, bytes_accessed=4 << 20, transcendentals=0),
        name="choose",
    )(req, rep, fin, me, ends, tails)


def token_out_kernel(req, me, sin, wk, wv, sc, ft, qs, rows, gate, norm_gain, out):
    gain = jnp.transpose(jnp.broadcast_to(norm_gain[...], (TILE, DV)))
    stay0 = jnp.where(is_fresh(req, me[0] * 2), 0.0, 1.0)
    stay1 = jnp.where(is_fresh(req, me[0] * 2 + 1), 0.0, 1.0)
    lane = iota((DV, TILE), 1)
    early = lane < SPAN
    sides = halves((SPAN, TILE))
    units = [(t, r) for t in range(qs.shape[0]) for r in range(RATIO)]
    both = [jnp.concatenate([wk[t * RATIO + r], qs[t]], axis=1) for t, r in units]
    enter = [sin[t * RATIO + r].astype(F32) * stay0 for t, r in units]
    first = [dot(e.astype(BF16), b) for e, b in zip(enter, both)]
    wide = [wv[t * RATIO + r].astype(F32) for t, r in units]
    new0 = [jnp.where(early, w - f[:, :TILE], 0.0) for w, f in zip(wide, first)]
    tiles = range(qs.shape[0])
    pairs = [
        dot(
            jnp.concatenate([new0[2 * t].astype(BF16), new0[2 * t + 1].astype(BF16)], axis=1),
            corner(ft[2 * t], ft[2 * t + 1]),
        )
        for t in tiles
    ]
    middle = [
        (rows[t, r : r + 1] * e + pairs[t][:, r * TILE : (r + 1) * TILE]) * stay1
        for (t, r), e in zip(units, enter)
    ]
    second = [dot(m.astype(BF16), b) for m, b in zip(middle, both)]
    new = [
        jnp.where(early, x, w - s[:, :TILE]).astype(BF16) for x, w, s in zip(new0, wide, second)
    ]
    near = [
        block_dot(jnp.concatenate([new[2 * t], new[2 * t + 1]], axis=1), sc[t], sides) for t in tiles
    ]
    for at, (t, r) in enumerate(units):
        core = rows[t, 2 + r : 3 + r] * jnp.where(early, first[at][:, TILE:], second[at][:, TILE:])
        core = (core + near[t][:, r * TILE : (r + 1) * TILE]).astype(BF16).astype(F32)
        inverse_rms = lax.rsqrt(jnp.mean(core * core, axis=0, keepdims=True) + EPSILON)
        z = gate[t, r * DV : (r + 1) * DV].astype(F32)
        result = core * inverse_rms * gain * (z / (1.0 + jnp.exp(-z)))
        out[t, r * DV : (r + 1) * DV] = result.astype(BF16)


def token_out(req, me, sin, wk, wv, sc, ft, qs, rows, gate, gain):
    heads = qs.shape[0]
    smem = pl.BlockSpec(memory_space=pltpu.SMEM)

    def tiles(count, *rest):
        return pl.BlockSpec((count,) + rest, lambda g: (g,) + (0,) * len(rest))

    return pl.pallas_call(
        token_out_kernel,
        grid=(heads // WIDE,),
        in_specs=[smem, smem]
        + [tiles(WIDE * RATIO, 128, 128)] * 3
        + [tiles(WIDE, SPAN, RATIO * TILE), tiles(WIDE * RATIO, 128, 128)]
        + [
            tiles(WIDE, 128, 128),
            tiles(WIDE, 8, 128),
            tiles(WIDE, 256, TILE),
            pl.BlockSpec((1, 128), lambda g: (0, 0)),
        ],
        out_specs=tiles(WIDE, 256, TILE),
        out_shape=jax.ShapeDtypeStruct((heads, 256, TILE), BF16),
        compiler_params=params(ALL_VMEM),
        cost_estimate=pl.CostEstimate(flops=10**9, bytes_accessed=8 << 20, transcendentals=10**6),
        name="token_out",
    )(req, me, sin, wk, wv, sc, ft, qs, rows, gate, gain)


def land_kernel(me, *refs):
    got, (states, tails, counts) = refs[:-3], refs[-3:]
    slot = pl.program_id(0)
    heads, own = states.shape[1], tails.shape[2]
    base = heads * 128

    @pl.when(slot == 0)
    def first():
        for i, one in enumerate(got):
            number = jnp.max(one[0, base + own * 16 :].astype(F32))
            counts[i] = number.astype(jnp.int32)

    start = jnp.int32(0)
    source, place = jnp.int32(-1), jnp.int32(0)
    for p in range(len(got)):
        away = me[0] ^ p
        number = counts[away]
        inside = (slot >= start) & (slot < start + number)
        source = jnp.where(inside, away, source)
        place = jnp.where(inside, slot - start, place)
        start = start + number
    place = jnp.clip(place, 0, CAP - 1)
    for i, one in enumerate(got):

        @pl.when(source == i)
        def take():
            for v in range(heads):
                states[0, v] = jnp.transpose(one[place, v * 128 : (v + 1) * 128]).astype(F32)
            lines = [one[place, base + h * 16 : base + h * 16 + 16].astype(F32) for h in range(own)]
            for k in range(KERNEL - 1):
                row = [
                    jnp.concatenate([x[4 * k + cg : 4 * k + cg + 1] for cg in range(4)], axis=1)
                    for x in lines
                ]
                tails[0, k] = jnp.concatenate(row, axis=0).astype(BF16)

    @pl.when(source < 0)
    def clear():
        states[...] = jnp.zeros_like(states)
        tails[...] = jnp.zeros_like(tails)


def land(me, got, heads, own):
    lines = got[0].shape[1]
    slots = len(got) * CAP
    smem = pl.BlockSpec(memory_space=pltpu.SMEM)
    return pl.pallas_call(
        land_kernel,
        grid=(slots,),
        in_specs=[smem] + [pl.BlockSpec((CAP, lines, 128), lambda g: (0, 0, 0))] * len(got),
        out_specs=[
            pl.BlockSpec((1, heads, 128, 128), lambda g: (g, 0, 0, 0)),
            pl.BlockSpec((1, KERNEL - 1, own, 512), lambda g: (g, 0, 0, 0)),
        ],
        out_shape=[
            jax.ShapeDtypeStruct((slots, heads, 128, 128), F32),
            jax.ShapeDtypeStruct((slots, KERNEL - 1, own, 512), BF16),
        ],
        scratch_shapes=[pltpu.SMEM((len(got),), jnp.int32)],
        compiler_params=params(SOME_VMEM),
        cost_estimate=pl.CostEstimate(flops=10**6, bytes_accessed=4 << 20, transcendentals=0),
        name="land",
    )(me, *got)


def exchange(parts, axis):
    count = len(parts)
    got = {0: parts[0]}
    for k in range(count - 1, 0, -1):
        got[k] = lax.ppermute(parts[k], axis, [(i, i ^ k) for i in range(count)])
    return [got[k] for k in range(count)]


def body(
    mixed,
    decay_in,
    beta_in,
    gate_z,
    conv_weight,
    a_log,
    dt_bias,
    norm_gain,
    req_blocks,
    replica_of,
    finished,
):
    n = lax.axis_size("seq")
    replicas = lax.axis_size("rep")
    heads = mixed.shape[1]
    own = heads // n
    me = lax.axis_index("seq").astype(jnp.int32).reshape(1)
    kpack, par = pack_keys(mixed[0], decay_in[0], beta_in[0], conv_weight, a_log, dt_bias)
    halo, *vpack = pack_values(me, mixed[0], n)
    kp = lax.all_to_all(kpack.reshape(n, own, KROWS, TILE), "seq", 0, 0, tiled=True)
    halo = lax.ppermute(halo, "seq", [(i, i + 1) for i in range(n - 1)])
    vp = exchange(vpack, "seq")
    hsol, hft, hgs, hrows = head_prep(req_blocks, kp, par)
    sin, ends, ktails = head_chain(req_blocks, me, par, hsol, hft, hgs, hrows, vp)
    sin, halo = lax.optimization_barrier((sin, halo))
    sin = lax.all_to_all(sin, "seq", 0, 0, tiled=True)
    wk, wv, sc, ft, qs, rows = token_prep(
        req_blocks, me, mixed[0], decay_in[0], beta_in[0], halo, kp.reshape(heads, KROWS, TILE)
    )
    my_rep = lax.axis_index("rep").astype(jnp.int32).reshape(1)
    send = choose(req_blocks, replica_of, finished, my_rep, ends, ktails, replicas)
    got = exchange(send, "rep")
    states, tails = land(my_rep, got, own * RATIO, own)
    out = token_out(
        req_blocks,
        me,
        sin.reshape(heads * RATIO, 128, 128),
        wk,
        wv,
        sc,
        ft,
        qs,
        rows,
        gate_z[0],
        norm_gain.reshape(1, DV),
    )
    return (out[None], states[None], tails[None])


def solution(mesh):
    placed = (
        P("rep", None, None, "seq"),
        P("rep", None, None, "seq"),
        P("rep", None, None, "seq"),
        P("rep", None, None, "seq"),
        P(None, "seq", None),
        P("seq"),
        P("seq"),
        P(),
        P("rep", None),
        P("rep", None),
        P("rep", None),
    )
    return jax.shard_map(
        body,
        mesh=mesh,
        in_specs=placed,
        out_specs=(
            P("rep", None, None, "seq"),
            P("rep", None, "seq", None, None),
            P("rep", None, None, "seq", None),
        ),
        check_vma=False,
    )
```

```python
import jax
import jax.numpy as jnp
from jax import lax
from jax.experimental import pallas as pl
from jax.experimental.pallas import tpu as pltpu
from jax.sharding import PartitionSpec as P

DK = 128
DV = 128
KERNEL = 4
SPAN = 64
CAP = 2
RATIO = 2
TILE = 2 * SPAN
KROWS = 160
VROWS = 288
WIDE = 8
MOST = 16
EPSILON = 1e-06
F32 = jnp.float32
BF16 = jnp.bfloat16
VMEM_LIMIT = 56 * 1024 * 1024
ALL_VMEM = 63 * 1024 * 1024
SOME_VMEM = 53 * 1024 * 1024


def params(limit=VMEM_LIMIT):
    return pltpu.CompilerParams(vmem_limit_bytes=limit)


def iota(shape, dim):
    return lax.broadcasted_iota(jnp.int32, shape, dim)


def dot(left, right):
    return jnp.dot(left, right, preferred_element_type=F32)


def split(wide):
    high = wide.astype(BF16)
    return high, (wide - high.astype(F32)).astype(BF16)


def halves(shape):
    first = iota(shape, len(shape) - 1) < SPAN
    return jnp.where(first, 1.0, 0.0).astype(BF16), jnp.where(first, 0.0, 1.0).astype(BF16)


def corner(first, second):
    none = jnp.zeros_like(first)
    top = jnp.concatenate([first, none], axis=1)
    return jnp.concatenate([top, jnp.concatenate([none, second], axis=1)], axis=0)


def diagonal(packed, masks):
    squares = []
    for r in range(RATIO):
        one = packed[:, r * TILE : (r + 1) * TILE]
        squares.append(jnp.concatenate([one * masks[0], one * masks[1]], axis=0))
    return corner(*squares)


def block_dot(left, right, masks):
    return dot(left, diagonal(right, masks))


def parameter_lines(h, cw, alog, dtb):
    taps = cw[:, h].astype(F32)
    rows = [taps[tap : tap + 1, cg * 128 : (cg + 1) * 128] for tap in range(KERNEL) for cg in range(4)]
    rest = jnp.concatenate(
        [jnp.full((1, 128), ref[h * RATIO + r], F32) for ref in (alog, dtb) for r in range(RATIO)], axis=0
    )
    parts = []
    for _ in range(3):
        part = rest.astype(BF16).astype(F32)
        rest = rest - part
        parts.append(part)
    return jnp.concatenate(rows + parts + [jnp.zeros((4, 128), F32)], axis=0)


def parameters(lines):
    wide = lines.astype(F32)
    rest = wide[16:20] + wide[20:24] + wide[24:28]
    return wide[:16], rest[:RATIO], rest[RATIO:]


def pack_keys_kernel(mixed, dec, beta, cw, alog, dtb, kout, pout):
    row = iota((32, TILE), 0)
    own = pout.shape[0]
    lines = [parameter_lines(h, cw, alog, dtb) for h in range(own)]
    for t in range(mixed.shape[0]):
        kout[t, :DK] = mixed[t]
        rest = lines[t % own]
        d, b = dec[t].astype(F32), beta[t].astype(F32)
        for r in range(RATIO):
            rest = jnp.where(row == 28 + r, d[r : r + 1], rest)
            rest = jnp.where(row == 30 + r, b[r : r + 1], rest)
        kout[t, DK:] = rest.astype(BF16)

    @pl.when(pl.program_id(0) == 0)
    def first():
        for h in range(own):
            pout[h] = lines[h].astype(BF16)


def pack_keys(mixed, dec, beta, cw, alog, dtb):
    heads = mixed.shape[0]
    own = cw.shape[1]
    step = heads // 2
    smem = pl.BlockSpec(memory_space=pltpu.SMEM)
    return pl.pallas_call(
        pack_keys_kernel,
        grid=(heads // step,),
        in_specs=[
            pl.BlockSpec((step, DK, TILE), lambda g: (g, 1, 0)),
            pl.BlockSpec((step, RATIO, TILE), lambda g: (g, 0, 0)),
            pl.BlockSpec((step, RATIO, TILE), lambda g: (g, 0, 0)),
            pl.BlockSpec((KERNEL, own, 512), lambda g: (0, 0, 0)),
            smem,
            smem,
        ],
        out_specs=[
            pl.BlockSpec((step, KROWS, TILE), lambda g: (g, 0, 0)),
            pl.BlockSpec((own, 32, 128), lambda g: (0, 0, 0)),
        ],
        out_shape=[
            jax.ShapeDtypeStruct((heads, KROWS, TILE), BF16),
            jax.ShapeDtypeStruct((own, 32, 128), BF16),
        ],
        compiler_params=params(),
        cost_estimate=pl.CostEstimate(flops=10**6, bytes_accessed=2 << 20, transcendentals=0),
        name="pack_keys",
    )(mixed, dec, beta, cw, alog, dtb)


def pack_values_kernel(me, mixed, hout, *outs):
    step = pl.program_id(0)
    own = outs[0].shape[0]
    row, tok = iota((TILE, 128), 1), iota((TILE, 128), 0)
    place = row & 15
    picks = []
    for cg in range(4):
        hit = (row < 32) & (place < 12) & ((place & 3) == cg)
        hit = hit & (tok == (row >> 4) * SPAN + 61 + (place >> 2))
        picks.append(jnp.where(hit, 1.0, 0.0).astype(BF16))
    all_tails = []
    for h in range(mixed.shape[0]):
        tails = dot(mixed[h, :128], picks[0])
        for cg in range(1, 4):
            tails = tails + dot(mixed[h, cg * 128 : (cg + 1) * 128], picks[cg])
        all_tails.append(jnp.transpose(tails)[:32].astype(BF16))
        hout[h] = all_tails[h][16:]
    for i, out in enumerate(outs):

        @pl.when((step == i // 4) & ((me[0] & 3) == 0))
        def put0():
            put(mixed, all_tails, out, (i & 3) ^ 0, own)

        @pl.when((step == i // 4) & ((me[0] & 3) == 1))
        def put1():
            put(mixed, all_tails, out, (i & 3) ^ 1, own)

        @pl.when((step == i // 4) & ((me[0] & 3) == 2))
        def put2():
            put(mixed, all_tails, out, (i & 3) ^ 2, own)

        @pl.when((step == i // 4) & ((me[0] & 3) == 3))
        def put3():
            put(mixed, all_tails, out, (i & 3) ^ 3, own)


def put(mixed, all_tails, out, place, own):
    for h in range(own):
        out[h, :256] = mixed[place * own + h, 2 * DK :]
        out[h, 256:] = all_tails[place * own + h]


def pack_values(me, mixed, n):
    heads = mixed.shape[0]
    own = heads // n
    return pl.pallas_call(
        pack_values_kernel,
        grid_spec=pltpu.PrefetchScalarGridSpec(
            num_scalar_prefetch=1,
            grid=(n // 4,),
            in_specs=[pl.BlockSpec((4 * own, 512, TILE), lambda g, me: ((me[0] >> 2) ^ g, 0, 0))],
            out_specs=[pl.BlockSpec((4 * own, 16, TILE), lambda g, me: ((me[0] >> 2) ^ g, 0, 0))]
            + [pl.BlockSpec((own, VROWS, TILE), lambda g, me: (0, 0, 0))] * n,
        ),
        out_shape=[jax.ShapeDtypeStruct((heads, 16, TILE), BF16)]
        + [jax.ShapeDtypeStruct((own, VROWS, TILE), BF16)] * n,
        compiler_params=params(),
        cost_estimate=pl.CostEstimate(flops=10**8, bytes_accessed=4 << 20, transcendentals=0),
        name="pack_values",
    )(me, mixed)


def is_fresh(req, block):
    start = jnp.int32(0)
    fresh = jnp.bool_(False)
    for j in range(req.shape[1]):
        fresh = fresh | (start == block)
        start = start + req[0, j]
    return fresh


def tap_tables():
    row, part = iota((16, 4 * 128), 0), iota((16, 4 * 128), 1) >> 7
    hits = [((row & 3) == cg) & ((row >> 2) == part) for cg in range(4)]
    return [jnp.where(hit, 1.0, 0.0).astype(BF16) for hit in hits]


def halo_tables():
    row, lane = iota((48, 128), 0), iota((48, 128), 1)
    token = (row >> 2) % 3
    hits = [((row & 3) == cg) & (row < 36) & (token == lane) for cg in range(4)]
    return [jnp.where(hit, 1.0, 0.0).astype(BF16) for hit in hits]


def turned_dot(rows, table):
    return lax.dot_general(rows, table, (((0,), (0,)), ((), ())), preferred_element_type=F32)


def spread_taps(par, table):
    both = turned_dot(par, table)
    return [both[:, tap * 128 : (tap + 1) * 128] for tap in range(KERNEL)]


def halo_terms(halo, par, not_fresh0):
    x = [halo[4 * k : 4 * k + 4].astype(F32) * not_fresh0 for k in range(3)]
    w = [par[4 * k : 4 * k + 4] for k in range(3)]
    terms = jnp.concatenate(
        [w[0] * x[0] + w[1] * x[1] + w[2] * x[2], w[0] * x[1] + w[1] * x[2], w[0] * x[2]], axis=0
    )
    high = terms.astype(BF16).astype(F32)
    middle = (terms - high).astype(BF16).astype(F32)
    parts = [high, middle, terms - high - middle, jnp.zeros((12, 128), F32)]
    return jnp.concatenate(parts, axis=0).astype(BF16)


def convolve(raw, before, terms, taps, masks):
    lane = iota((1, TILE), 1)
    cur = raw.astype(F32)
    total = taps[KERNEL - 1] * cur
    if terms is not None:
        total = total + terms
    for back in range(1, KERNEL):
        moved = cur if before is None else jnp.where(lane >= TILE - back, before, cur)
        total = total + taps[KERNEL - 1 - back] * (pltpu.roll(moved, back, 1) * masks[back - 1])
    return (total / (1.0 + jnp.exp(-total))).astype(BF16)


def conv_masks(cut0, cut1):
    lane = iota((1, TILE), 1)
    masks = []
    for back in range(1, KERNEL):
        gone = ((lane < back) & cut0) | ((lane >= SPAN) & (lane < SPAN + back) & cut1)
        masks.append(jnp.where(gone, 0.0, 1.0))
    return masks


def row_prep(dec, beta, alog, dtb):
    lane = iota(dec.shape, 1)
    x = dec + dtb
    decay = -jnp.exp(alog) * (jnp.maximum(x, 0.0) + jnp.log1p(jnp.exp(-jnp.abs(x))))
    cum = decay
    for shift in (1, 2, 4, 8, 16, 32):
        cum = cum + jnp.where((lane & (SPAN - 1)) >= shift, pltpu.roll(cum, shift, 1), 0.0)
    strength = 1.0 / (1.0 + jnp.exp(-beta))
    grown = jnp.exp(cum)
    close0, close1 = cum[:, SPAN - 1 : SPAN], cum[:, TILE - 1 :]
    fade = jnp.exp(jnp.where(lane < SPAN, close0, close1) - cum)
    keep0 = jnp.exp(jnp.broadcast_to(close0, cum.shape))
    keep1 = jnp.exp(jnp.broadcast_to(close1, cum.shape))
    return cum, strength, grown, fade, keep0, keep1


def unit_inverses(systems):
    shape = (SPAN, RATIO * TILE)
    row, col = iota(shape, 0), iota(shape, 1) & (SPAN - 1)
    near = (row >> 4) == (col >> 4)
    eye = jnp.where(row == col, 1.0, 0.0)
    masks = halves((SPAN, TILE))

    def low(arrays):
        return [a.astype(BF16) for a in arrays]

    def stack(pair):
        return jnp.concatenate(pair, axis=0)

    total = [jnp.where(near, eye - a, 0.0) for a in systems]
    power = low([jnp.where(near, -a, 0.0) for a in systems])
    power = low([block_dot(p, p, masks) for p in power])
    for _ in range(2):
        both = [block_dot(stack([t, p]), p, masks) for t, p in zip(low(total), power)]
        total = [t + b[:SPAN] for t, b in zip(total, both)]
        power = low([b[SPAN:] for b in both])
    total = [t + block_dot(l, p, masks) for t, l, p in zip(total, low(total), power)]
    small = low(total)
    rest = low([jnp.where(near, 0.0, a) for a in systems])
    cross = low([block_dot(t, r, masks) for t, r in zip(small, rest)])
    total = [t - block_dot(x, l, masks) for t, x, l in zip(total, cross, small)]
    small = low(total)
    solved = []
    for a, x in zip(systems, small):
        wide = x.astype(F32)
        parts = block_dot(stack(split(a)), x, masks)
        miss = eye - wide - (parts[:SPAN] + parts[SPAN:])
        solved.append((wide + block_dot(x, miss.astype(BF16), masks)).astype(BF16))
    return solved


def both_blocks(square):
    none = jnp.zeros((SPAN, square.shape[1]), square.dtype)
    first = jnp.concatenate([square[:SPAN], none], axis=0)
    return jnp.concatenate([first, jnp.concatenate([none, square[SPAN:]], axis=0)], axis=1)


def unit_keys(convolved):
    wide = convolved.astype(F32)
    return (wide * lax.rsqrt(jnp.sum(wide * wide, axis=0, keepdims=True) + EPSILON)).astype(BF16)


def solve_tiles(keys, queries, prep):
    cum, strength, grown, fade, keep0, keep1 = prep
    row, lane = iota((SPAN, TILE), 0), iota((SPAN, TILE), 1)
    early = lane < SPAN
    seen = (lane & (SPAN - 1)) >= row
    later = (lane & (SPAN - 1)) > row
    columns = jnp.transpose(jnp.concatenate([cum, fade], axis=0))
    count = cum.shape[0]

    def beside(tall):
        return jnp.where(early, tall[:SPAN], tall[SPAN:])

    systems, faded, scores = [], [], []
    for t, k in enumerate(keys):
        turned = jnp.transpose(k.astype(F32))
        if queries is None:
            gram = beside(dot(turned.astype(BF16), k))
        else:
            prod = dot(turned.astype(BF16), jnp.concatenate([k, queries[t]], axis=1))
            gram, touch = beside(prod[:, :TILE]), beside(prod[:, TILE:])
        pair = []
        for r in range(RATIO):
            at = t * RATIO + r
            diff = cum[at : at + 1] - beside(columns[:, at : at + 1])
            ratio = jnp.where(seen, jnp.exp(jnp.where(seen, diff, 0.0)), 0.0)
            pair.append(jnp.where(later, strength[at : at + 1] * gram * ratio, 0.0))
            if queries is not None:
                scores.append((touch * ratio).astype(BF16))
            faded.append((turned * columns[:, count + at : count + at + 1]).astype(BF16))
        systems.append(jnp.concatenate(pair, axis=1))
    return unit_inverses(systems), faded, scores


def token_prep_kernel(req, me, mixed, dec, beta, halo, par_lines, wk, wv, sc, ft, qo, rows):
    fresh0, fresh1 = is_fresh(req, me[0] * 2), is_fresh(req, me[0] * 2 + 1)
    not_fresh0 = jnp.where(fresh0, 0.0, 1.0)
    masks = conv_masks(True, fresh1)
    tap_tab, halo_tab = tap_tables(), halo_tables()
    tiles = range(mixed.shape[0])
    par = [parameters(par_lines[t]) for t in tiles]

    def gather(pick):
        return jnp.concatenate([pick(t) for t in tiles], axis=0)

    prep = row_prep(
        gather(lambda t: dec[t].astype(F32)),
        gather(lambda t: beta[t].astype(F32)),
        jnp.concatenate([p[1] for p in par], axis=0),
        jnp.concatenate([p[2] for p in par], axis=0),
    )
    cum, strength, grown, fade, keep0, keep1 = prep
    keys, queries, values = [], [], []
    for t in tiles:
        terms = halo_terms(halo[t], par[t][0], not_fresh0)
        lines = par_lines[t, :16]
        q, k, v0, v1 = [
            convolve(
                mixed[t, c * 128 : (c + 1) * 128],
                None,
                turned_dot(terms, halo_tab[c]),
                spread_taps(lines, tap_tab[c]),
                masks,
            )
            for c in range(4)
        ]
        keys.append(unit_keys(k))
        queries.append(q)
        values.append((v0, v1))
        qo[t] = q
        rows[t] = jnp.concatenate(
            [keep0[2 * t : 2 * t + 2], grown[2 * t : 2 * t + 2], keep1[2 * t : 2 * t + 2], strength[2 * t : 2 * t + 2]],
            axis=0,
        )
    solved, faded, scores = solve_tiles(keys, queries, prep)
    sides = halves((SPAN, TILE))
    for t in tiles:
        stacks = []
        for r in range(RATIO):
            at = t * RATIO + r
            s, lift = strength[at : at + 1], strength[at : at + 1] * grown[at : at + 1]
            stacked = jnp.concatenate(
                [lift * keys[t].astype(F32), s * values[t][r].astype(F32)], axis=0
            )
            stacks.append(stacked.astype(BF16))
            sc[t, :, r * TILE : (r + 1) * TILE] = scores[at]
            ft[at] = faded[at]
        out = block_dot(jnp.concatenate(stacks, axis=1), solved[t], sides).astype(BF16)
        for r in range(RATIO):
            wk[t * RATIO + r] = out[:DK, r * TILE : (r + 1) * TILE]
            wv[t * RATIO + r] = out[DK:, r * TILE : (r + 1) * TILE]


def token_prep(req, me, mixed, dec, beta, halo, par):
    heads = mixed.shape[0]
    smem = pl.BlockSpec(memory_space=pltpu.SMEM)

    def tiles(count, *rest):
        return pl.BlockSpec((count,) + rest, lambda g: (g,) + (0,) * len(rest))

    square = jax.ShapeDtypeStruct((heads * RATIO, 128, 128), BF16)
    return pl.pallas_call(
        token_prep_kernel,
        grid=(heads // WIDE,),
        in_specs=[
            smem,
            smem,
            tiles(WIDE, 512, TILE),
            tiles(WIDE, RATIO, TILE),
            tiles(WIDE, RATIO, TILE),
            tiles(WIDE, 16, TILE),
            pl.BlockSpec((WIDE, 32, 128), lambda g: (g, 4, 0)),
        ],
        out_specs=[tiles(WIDE * RATIO, 128, 128)] * 2
        + [tiles(WIDE, SPAN, RATIO * TILE), tiles(WIDE * RATIO, 128, 128)]
        + [tiles(WIDE, 128, 128), tiles(WIDE, 8, 128)],
        out_shape=[square] * 2
        + [
            jax.ShapeDtypeStruct((heads, SPAN, RATIO * TILE), BF16),
            square,
            jax.ShapeDtypeStruct((heads, 128, 128), BF16),
            jax.ShapeDtypeStruct((heads, 8, 128), F32),
        ],
        compiler_params=params(),
        cost_estimate=pl.CostEstimate(flops=10**10, bytes_accessed=8 << 20, transcendentals=10**6),
        name="token_prep",
    )(req, me, mixed, dec, beta, halo, par)


def head_prep_kernel(req, kp, previous, par_lines, sol, ft, gs, rows):
    step = pl.program_id(0)
    depth, own = kp.shape[0], kp.shape[1]
    tap_tab = tap_tables()
    order = [(d, h) for d in range(depth) for h in range(own)]
    par = [parameters(par_lines[h]) for h in range(own)]

    small = [kp[d, h, DK:].astype(F32) for d, h in order]
    prep = row_prep(
        jnp.concatenate([s[28:30] for s in small], axis=0),
        jnp.concatenate([s[30:32] for s in small], axis=0),
        jnp.concatenate([par[h][1] for d, h in order], axis=0),
        jnp.concatenate([par[h][2] for d, h in order], axis=0),
    )
    cum, strength, grown, fade, keep0, keep1 = prep
    keys = []
    taps = [spread_taps(par_lines[h, :16], tap_tab[1]) for h in range(own)]
    for d in range(depth):
        block = (step * depth + d) * 2
        masks = conv_masks(is_fresh(req, block), is_fresh(req, block + 1))
        for h in range(own):
            before = (kp[d - 1, h, :DK] if d else previous[0, h]).astype(F32)
            keys.append(unit_keys(convolve(kp[d, h, :DK], before, None, taps[h], masks)))
    solved, faded, unused = solve_tiles(keys, None, prep)
    sides = halves((SPAN, TILE))
    for t, (d, h) in enumerate(order):
        rows[d, h] = jnp.concatenate(
            [keep0[2 * t : 2 * t + 2], keep1[2 * t : 2 * t + 2], strength[2 * t : 2 * t + 2], strength[2 * t : 2 * t + 2]],
            axis=0,
        )
        scaled = []
        for r in range(RATIO):
            at = t * RATIO + r
            lift = strength[at : at + 1] * grown[at : at + 1]
            scaled.append((lift * keys[t].astype(F32)).astype(BF16))
        wide = block_dot(jnp.concatenate(scaled, axis=1), solved[t], sides).astype(BF16)
        sol[d, h] = solved[t]
        for r in range(RATIO):
            at = t * RATIO + r
            drop = dot(wide[:, r * TILE : (r + 1) * TILE], both_blocks(faded[at])).astype(BF16)
            gs[d, h, r, 0] = drop[:, :DK]
            gs[d, h, r, 1] = drop[:, DK:]
            ft[d, h, r] = faded[at]


def head_prep(req, kp, par):
    n, own = kp.shape[:2]
    depth = MOST // own
    smem = pl.BlockSpec(memory_space=pltpu.SMEM)

    def tiles(*rest):
        return pl.BlockSpec((depth, own) + rest, lambda g: (g, 0) + (0,) * len(rest))

    square = jax.ShapeDtypeStruct((n, own, RATIO, 128, 128), BF16)
    return pl.pallas_call(
        head_prep_kernel,
        grid=(n // depth,),
        in_specs=[
            smem,
            tiles(KROWS, TILE),
            pl.BlockSpec((1, own, DK, TILE), lambda g: (jnp.maximum(g * depth - 1, 0), 0, 0, 0)),
            pl.BlockSpec((own, 32, 128), lambda g: (0, 0, 0)),
        ],
        out_specs=[
            tiles(SPAN, RATIO * TILE),
            tiles(RATIO, 128, 128),
            tiles(RATIO, 2, 128, 128),
            tiles(8, 128),
        ],
        out_shape=[
            jax.ShapeDtypeStruct((n, own, SPAN, RATIO * TILE), BF16),
            square,
            jax.ShapeDtypeStruct((n, own, RATIO, 2, 128, 128), BF16),
            jax.ShapeDtypeStruct((n, own, 8, 128), F32),
        ],
        compiler_params=params(),
        cost_estimate=pl.CostEstimate(flops=10**10, bytes_accessed=6 << 20, transcendentals=10**6),
        name="head_prep",
    )(req, kp, kp, par)


def head_chain_kernel(req, me, par_lines, sol, ft, gs, rows, *refs):
    n = refs[-6].shape[0]
    arrived, (sin, ends, tails, state, vp, spread) = refs[:n], refs[n:]
    step = pl.program_id(0)
    depth, own = sol.shape[0], sol.shape[1]

    @pl.when(step == 0)
    def first():
        for k, one in enumerate(arrived):
            vp[me[0] ^ k] = one[...]
            tails[me[0] ^ k] = one[:, 256:]
        tap_tab = tap_tables()
        for h in range(own):
            for r in range(RATIO):
                for tap, wide in enumerate(spread_taps(par_lines[h, :16], tap_tab[2 + r])):
                    spread[h * RATIO + r, tap] = wide

    sides = halves((SPAN, TILE))
    heads = [(h, r) for h in range(own) for r in range(RATIO)]
    taps = [[spread[v, tap] for tap in range(KERNEL)] for v in range(len(heads))]
    current = [state[v] for v in range(len(heads))]
    for d in range(depth):
        tile = step * depth + d
        past = jnp.maximum(tile - 1, 0)
        fresh = [is_fresh(req, tile * 2), is_fresh(req, tile * 2 + 1)]
        masks = conv_masks(fresh[0], fresh[1])
        gains = []
        for h in range(own):
            scaled = []
            for r in range(RATIO):
                raw = vp[tile, h, r * DV : (r + 1) * DV]
                before = vp[past, h, r * DV : (r + 1) * DV].astype(F32)
                value = convolve(raw, before, None, taps[h * RATIO + r], masks)
                scaled.append((rows[d, h, 4 + r : 5 + r] * value.astype(F32)).astype(BF16))
            wide = block_dot(jnp.concatenate(scaled, axis=1), sol[d, h], sides).astype(BF16)
            for r in range(RATIO):
                gains.append(dot(wide[:, r * TILE : (r + 1) * TILE], both_blocks(ft[d, h, r])))
        for half in range(2):
            for h in range(own):
                now = [jnp.where(fresh[half], 0.0, current[h * RATIO + r]) for r in range(RATIO)]
                lost = dot(
                    jnp.concatenate([x.astype(BF16) for x in now], axis=1),
                    corner(gs[d, h, 0, half], gs[d, h, 1, half]),
                )
                for r in range(RATIO):
                    v = h * RATIO + r
                    keep = rows[d, h, 2 * half + r : 2 * half + r + 1]
                    gain = gains[v][:, half * DV : (half + 1) * DV]
                    current[v] = keep * now[r] + (gain - lost[:, r * TILE : (r + 1) * TILE])
                    ends[d * 2 + half, v] = current[v].astype(BF16)
        onward = lax.rem(tile + 1, n)
        for v in range(len(heads)):
            sin[onward, v] = current[v].astype(BF16)
    for v in range(len(heads)):
        state[v] = current[v]


def head_chain(req, me, par, sol, ft, gs, rows, arrived):
    n, own = sol.shape[:2]
    depth = WIDE // own
    smem = pl.BlockSpec(memory_space=pltpu.SMEM)

    def tiles(*rest):
        return pl.BlockSpec((depth, own) + rest, lambda g: (g, 0) + (0,) * len(rest))

    return pl.pallas_call(
        head_chain_kernel,
        grid=(n // depth,),
        in_specs=[
            smem,
            smem,
            pl.BlockSpec((own, 32, 128), lambda g: (0, 0, 0)),
            tiles(SPAN, RATIO * TILE),
            tiles(RATIO, 128, 128),
            tiles(RATIO, 2, 128, 128),
            tiles(8, 128),
        ]
        + [pl.BlockSpec((own, VROWS, TILE), lambda g: (0, 0, 0))] * n,
        out_specs=[
            pl.BlockSpec((n, own * RATIO, 128, 128), lambda g: (0, 0, 0, 0)),
            pl.BlockSpec((2 * depth, own * RATIO, 128, 128), lambda g: (g, 0, 0, 0)),
            pl.BlockSpec((n, own, 32, TILE), lambda g: (0, 0, 0, 0)),
        ],
        out_shape=[
            jax.ShapeDtypeStruct((n, own * RATIO, 128, 128), BF16),
            jax.ShapeDtypeStruct((2 * n, own * RATIO, 128, 128), BF16),
            jax.ShapeDtypeStruct((n, own, 32, TILE), BF16),
        ],
        scratch_shapes=[
            pltpu.VMEM((own * RATIO, 128, 128), F32),
            pltpu.VMEM((n, own, VROWS, TILE), BF16),
            pltpu.VMEM((own * RATIO, KERNEL, 128, 128), F32),
        ],
        compiler_params=params(SOME_VMEM),
        cost_estimate=pl.CostEstimate(flops=3 * 10**9, bytes_accessed=8 << 20, transcendentals=10**6),
        name="head_chain",
    )(req, me, par, sol, ft, gs, rows, *arrived)


def choose_kernel(req, rep, fin, me, ends, kt, *refs):
    outs, counts = refs[:-1], refs[-1]
    own, heads = kt.shape[1], ends.shape[1]
    base = heads * 128
    for i, out in enumerate(outs):
        out[...] = jnp.zeros_like(out)
        counts[i] = 0
    end = jnp.int32(-1)
    for j in range(req.shape[1]):
        end = end + req[0, j]
        where = rep[0, j] ^ me[0]
        place = jnp.minimum(counts[where], CAP - 1)
        done = fin[0, j] > 0
        counts[where] = counts[where] + jnp.where(done, 1, 0)
        for i, out in enumerate(outs):

            @pl.when(done & (where == i))
            def take():
                for v in range(heads):
                    out[place, v * 128 : (v + 1) * 128] = ends[end, v]
                for h in range(own):
                    lines = kt[end >> 1, h].astype(F32)
                    lines = jnp.where((end & 1) > 0, lines[16:], lines[:16]).astype(BF16)
                    out[place, base + h * 16 : base + h * 16 + 16] = lines

    for i, out in enumerate(outs):
        number = jnp.full((16, 128), counts[i], jnp.int32).astype(F32).astype(BF16)
        for c in range(CAP):
            out[c, base + own * 16 :] = number


def choose(req, rep, fin, me, ends, tails, replicas):
    own = tails.shape[1]
    smem = pl.BlockSpec(memory_space=pltpu.SMEM)
    lines = own * RATIO * 128 + own * 16 + 16
    return pl.pallas_call(
        choose_kernel,
        grid=(1,),
        in_specs=[
            smem,
            smem,
            smem,
            smem,
            pl.BlockSpec(ends.shape, lambda g: (0, 0, 0, 0)),
            pl.BlockSpec(tails.shape, lambda g: (0, 0, 0, 0)),
        ],
        out_specs=[pl.BlockSpec((CAP, lines, 128), lambda g: (0, 0, 0))] * replicas,
        out_shape=[jax.ShapeDtypeStruct((CAP, lines, 128), BF16)] * replicas,
        scratch_shapes=[pltpu.SMEM((replicas,), jnp.int32)],
        compiler_params=params(),
        cost_estimate=pl.CostEstimate(flops=10**6, bytes_accessed=4 << 20, transcendentals=0),
        name="choose",
    )(req, rep, fin, me, ends, tails)


def token_out_kernel(req, me, sin, wk, wv, sc, ft, qs, rows, gate, norm_gain, out):
    gain = jnp.transpose(jnp.broadcast_to(norm_gain[...], (TILE, DV)))
    stay0 = jnp.where(is_fresh(req, me[0] * 2), 0.0, 1.0)
    stay1 = jnp.where(is_fresh(req, me[0] * 2 + 1), 0.0, 1.0)
    lane = iota((DV, TILE), 1)
    early = lane < SPAN
    sides = halves((SPAN, TILE))
    units = [(t, r) for t in range(qs.shape[0]) for r in range(RATIO)]
    both = [jnp.concatenate([wk[t * RATIO + r], qs[t]], axis=1) for t, r in units]
    enter = [sin[t * RATIO + r].astype(F32) * stay0 for t, r in units]
    first = [dot(e.astype(BF16), b) for e, b in zip(enter, both)]
    wide = [wv[t * RATIO + r].astype(F32) for t, r in units]
    new0 = [jnp.where(early, w - f[:, :TILE], 0.0) for w, f in zip(wide, first)]
    tiles = range(qs.shape[0])
    pairs = [
        dot(
            jnp.concatenate([new0[2 * t].astype(BF16), new0[2 * t + 1].astype(BF16)], axis=1),
            corner(ft[2 * t], ft[2 * t + 1]),
        )
        for t in tiles
    ]
    middle = [
        (rows[t, r : r + 1] * e + pairs[t][:, r * TILE : (r + 1) * TILE]) * stay1
        for (t, r), e in zip(units, enter)
    ]
    second = [dot(m.astype(BF16), b) for m, b in zip(middle, both)]
    new = [
        jnp.where(early, x, w - s[:, :TILE]).astype(BF16) for x, w, s in zip(new0, wide, second)
    ]
    near = [
        block_dot(jnp.concatenate([new[2 * t], new[2 * t + 1]], axis=1), sc[t], sides) for t in tiles
    ]
    for at, (t, r) in enumerate(units):
        core = rows[t, 2 + r : 3 + r] * jnp.where(early, first[at][:, TILE:], second[at][:, TILE:])
        core = (core + near[t][:, r * TILE : (r + 1) * TILE]).astype(BF16).astype(F32)
        inverse_rms = lax.rsqrt(jnp.mean(core * core, axis=0, keepdims=True) + EPSILON)
        z = gate[t, r * DV : (r + 1) * DV].astype(F32)
        result = core * inverse_rms * gain * (z / (1.0 + jnp.exp(-z)))
        out[t, r * DV : (r + 1) * DV] = result.astype(BF16)


def token_out(req, me, sin, wk, wv, sc, ft, qs, rows, gate, gain):
    heads = qs.shape[0]
    smem = pl.BlockSpec(memory_space=pltpu.SMEM)

    def tiles(count, *rest):
        return pl.BlockSpec((count,) + rest, lambda g: (g,) + (0,) * len(rest))

    return pl.pallas_call(
        token_out_kernel,
        grid=(heads // WIDE,),
        in_specs=[smem, smem]
        + [tiles(WIDE * RATIO, 128, 128)] * 3
        + [tiles(WIDE, SPAN, RATIO * TILE), tiles(WIDE * RATIO, 128, 128)]
        + [
            tiles(WIDE, 128, 128),
            tiles(WIDE, 8, 128),
            tiles(WIDE, 256, TILE),
            pl.BlockSpec((1, 128), lambda g: (0, 0)),
        ],
        out_specs=tiles(WIDE, 256, TILE),
        out_shape=jax.ShapeDtypeStruct((heads, 256, TILE), BF16),
        compiler_params=params(ALL_VMEM),
        cost_estimate=pl.CostEstimate(flops=10**9, bytes_accessed=8 << 20, transcendentals=10**6),
        name="token_out",
    )(req, me, sin, wk, wv, sc, ft, qs, rows, gate, gain)


def land_kernel(me, *refs):
    got, (states, tails, counts) = refs[:-3], refs[-3:]
    slot = pl.program_id(0)
    heads, own = states.shape[1], tails.shape[2]
    base = heads * 128

    @pl.when(slot == 0)
    def first():
        for i, one in enumerate(got):
            number = jnp.max(one[0, base + own * 16 :].astype(F32))
            counts[i] = number.astype(jnp.int32)

    start = jnp.int32(0)
    source, place = jnp.int32(-1), jnp.int32(0)
    for p in range(len(got)):
        away = me[0] ^ p
        number = counts[away]
        inside = (slot >= start) & (slot < start + number)
        source = jnp.where(inside, away, source)
        place = jnp.where(inside, slot - start, place)
        start = start + number
    place = jnp.clip(place, 0, CAP - 1)
    for i, one in enumerate(got):

        @pl.when(source == i)
        def take():
            for v in range(heads):
                states[0, v] = jnp.transpose(one[place, v * 128 : (v + 1) * 128]).astype(F32)
            lines = [one[place, base + h * 16 : base + h * 16 + 16].astype(F32) for h in range(own)]
            for k in range(KERNEL - 1):
                row = [
                    jnp.concatenate([x[4 * k + cg : 4 * k + cg + 1] for cg in range(4)], axis=1)
                    for x in lines
                ]
                tails[0, k] = jnp.concatenate(row, axis=0).astype(BF16)

    @pl.when(source < 0)
    def clear():
        states[...] = jnp.zeros_like(states)
        tails[...] = jnp.zeros_like(tails)


def land(me, got, heads, own):
    lines = got[0].shape[1]
    slots = len(got) * CAP
    smem = pl.BlockSpec(memory_space=pltpu.SMEM)
    return pl.pallas_call(
        land_kernel,
        grid=(slots,),
        in_specs=[smem] + [pl.BlockSpec((CAP, lines, 128), lambda g: (0, 0, 0))] * len(got),
        out_specs=[
            pl.BlockSpec((1, heads, 128, 128), lambda g: (g, 0, 0, 0)),
            pl.BlockSpec((1, KERNEL - 1, own, 512), lambda g: (g, 0, 0, 0)),
        ],
        out_shape=[
            jax.ShapeDtypeStruct((slots, heads, 128, 128), F32),
            jax.ShapeDtypeStruct((slots, KERNEL - 1, own, 512), BF16),
        ],
        scratch_shapes=[pltpu.SMEM((len(got),), jnp.int32)],
        compiler_params=params(SOME_VMEM),
        cost_estimate=pl.CostEstimate(flops=10**6, bytes_accessed=4 << 20, transcendentals=0),
        name="land",
    )(me, *got)


def exchange(parts, axis):
    count = len(parts)
    got = {0: parts[0]}
    for k in range(count - 1, 0, -1):
        got[k] = lax.ppermute(parts[k], axis, [(i, i ^ k) for i in range(count)])
    return [got[k] for k in range(count)]


def body(
    mixed,
    decay_in,
    beta_in,
    gate_z,
    conv_weight,
    a_log,
    dt_bias,
    norm_gain,
    req_blocks,
    replica_of,
    finished,
):
    n = lax.axis_size("seq")
    replicas = lax.axis_size("rep")
    heads = mixed.shape[1]
    own = heads // n
    me = lax.axis_index("seq").astype(jnp.int32).reshape(1)
    kpack, par = pack_keys(mixed[0], decay_in[0], beta_in[0], conv_weight, a_log, dt_bias)
    halo, *vpack = pack_values(me, mixed[0], n)
    kp = lax.all_to_all(kpack.reshape(n, own, KROWS, TILE), "seq", 0, 0, tiled=True)
    halo = lax.ppermute(halo, "seq", [(i, i + 1) for i in range(n - 1)])
    vp = exchange(vpack, "seq")
    hsol, hft, hgs, hrows = head_prep(req_blocks, kp, par)
    sin, ends, ktails = head_chain(req_blocks, me, par, hsol, hft, hgs, hrows, vp)
    sin, halo = lax.optimization_barrier((sin, halo))
    sin = lax.all_to_all(sin, "seq", 0, 0, tiled=True)
    wk, wv, sc, ft, qs, rows = token_prep(
        req_blocks, me, mixed[0], decay_in[0], beta_in[0], halo, kp.reshape(heads, KROWS, TILE)
    )
    my_rep = lax.axis_index("rep").astype(jnp.int32).reshape(1)
    send = choose(req_blocks, replica_of, finished, my_rep, ends, ktails, replicas)
    got = exchange(send, "rep")
    states, tails = land(my_rep, got, own * RATIO, own)
    out = token_out(
        req_blocks,
        me,
        sin.reshape(heads * RATIO, 128, 128),
        wk,
        wv,
        sc,
        ft,
        qs,
        rows,
        gate_z[0],
        norm_gain.reshape(1, DV),
    )
    return (out[None], states[None], tails[None])


def solution(mesh):
    placed = (
        P("rep", None, None, "seq"),
        P("rep", None, None, "seq"),
        P("rep", None, None, "seq"),
        P("rep", None, None, "seq"),
        P(None, "seq", None),
        P("seq"),
        P("seq"),
        P(),
        P("rep", None),
        P("rep", None),
        P("rep", None),
    )
    return jax.shard_map(
        body,
        mesh=mesh,
        in_specs=placed,
        out_specs=(
            P("rep", None, None, "seq"),
            P("rep", None, "seq", None, None),
            P("rep", None, None, "seq", None),
        ),
        check_vma=False,
    )
```
